32 devices in a mesh: rep: 4 (over x, core), fsdp: 8 (over z, y).
Axes of the slice: x: 2, y: 2, z: 4, core: 2. Of those that a mesh axis runs over, the one named last changes fastest.
Arguments:
- tokens: bfloat16 [32, 592, 768], P(('rep', 'fsdp')), may hold values from -6 to 6
- slot_kinds: int32 [32], P(('rep', 'fsdp')), may hold values from 0 to 1
- small_index: int32 [197, 197], replicated, may hold values from 0 to 2239, as said below
- large_index: int32 [577, 577], replicated, may hold values from 0 to 2239, as said below
- first_gain: bfloat16 [1, 768], P(None, 'fsdp'), may hold values from 0.5 to 1.5
- first_shift: bfloat16 [1, 768], P(None, 'fsdp'), may hold values from -2 to 2
- triple_weight: bfloat16 [1, 768, 2304], P(None, 'fsdp'), may hold values from -0.21875 to 0.21875
- query_bias: bfloat16 [1, 768], P(None, 'fsdp'), may hold values from -2 to 2
- value_bias: bfloat16 [1, 768], P(None, 'fsdp'), may hold values from -2 to 2
- bias_table: bfloat16 [1, 2240, 12], P(None, 'fsdp'), may hold values from -4 to 4
- output_weight: bfloat16 [1, 768, 768], P(None, 'fsdp'), may hold values from -2 to 2
- output_bias: bfloat16 [1, 768], P(None, 'fsdp'), may hold values from -2 to 2
- attend_scale: bfloat16 [1, 768], P(None, 'fsdp'), may hold values from 0.5 to 1.5
- second_gain: bfloat16 [1, 768], P(None, 'fsdp'), may hold values from 0.5 to 1.5
- second_shift: bfloat16 [1, 768], P(None, 'fsdp'), may hold values from -2 to 2
- expand_weight: bfloat16 [1, 768, 3072], P(None, 'fsdp'), may hold values from -0.21875 to 0.21875
- expand_bias: bfloat16 [1, 3072], P(None, 'fsdp'), may hold values from -2 to 2
- reduce_weight: bfloat16 [1, 3072, 768], P(None, 'fsdp'), may hold values from -0.15625 to 0.15625
- reduce_bias: bfloat16 [1, 768], P(None, 'fsdp'), may hold values from -2 to 2
- feed_scale: bfloat16 [1, 768], P(None, 'fsdp'), may hold values from 0.5 to 1.5
- cotangent: bfloat16 [32, 592, 768], P(('rep', 'fsdp')), may hold values from -6 to 6
Outputs:
- block_output: bfloat16 [32, 592, 768], P(('rep', 'fsdp'))
- token_grad: bfloat16 [32, 592, 768], P(('rep', 'fsdp'))
- first_gain_grad: float32 [1, 768], P(None, 'fsdp')
- first_shift_grad: float32 [1, 768], P(None, 'fsdp')
- triple_weight_grad: float32 [1, 768, 2304], P(None, 'fsdp')
- query_bias_grad: float32 [1, 768], P(None, 'fsdp')
- value_bias_grad: float32 [1, 768], P(None, 'fsdp')
- bias_table_grad: float32 [1, 2240, 12], P(None, 'fsdp')
- output_weight_grad: float32 [1, 768, 768], P(None, 'fsdp')
- output_bias_grad: float32 [1, 768], P(None, 'fsdp')
- attend_scale_grad: float32 [1, 768], P(None, 'fsdp')
- second_gain_grad: float32 [1, 768], P(None, 'fsdp')
- second_shift_grad: float32 [1, 768], P(None, 'fsdp')
- expand_weight_grad: float32 [1, 768, 3072], P(None, 'fsdp')
- expand_bias_grad: float32 [1, 3072], P(None, 'fsdp')
- reduce_weight_grad: float32 [1, 3072, 768], P(None, 'fsdp')
- reduce_bias_grad: float32 [1, 768], P(None, 'fsdp')
- feed_scale_grad: float32 [1, 768], P(None, 'fsdp')
The draws below stay inside these ranges and needn't reach their ends.
Inputs may be any that keep to these rules, and one draw needn't show every extreme that they name: small_index[r, s] is the bias table row of tokens r and s of a 14 x 14 image, token 0 the class token and token 1 + 14 i + j the patch in row i, column j; large_index likewise for a 24 x 24 image. In both tables two patch pairs share a row exactly when their offsets on the patch grid agree, and the class-to-patch, patch-to-class and class-to-class pairs have three rows of their own; equal offsets and equal pair kinds take the same row in both tables. `large_index`: as for small_index.
All inputs are finite; a program needn't handle non-finite values.
Results may differ from the reference program's by a relative error of at most 0.012.
Values may be sent and summed in bfloat16 or wider, within the bound.
A program may use at most 576 MiB of HBM per device.

```python
import jax
import jax.numpy as jnp
from jax import lax

D = 768
HEADS = 12
FF = 3072
HEAD_DIM = 64
NB = 2240
GRID_S = 14
GRID_L = 24
TOK_S = 197
TOK_L = 577
SLOT = 592
LAYERS = 1
SLOTS = 32


def bucket_labels(key):
    width_span = 2 * GRID_L - 1
    corner_id = width_span * width_span + 2
    labels = jax.random.permutation(key, NB).astype(jnp.int32)
    swapped = labels[corner_id]
    labels = jnp.where(labels == NB - 1, swapped, labels)
    return labels.at[corner_id].set(NB - 1)


def grid_buckets(grid_side):
    width_span = 2 * GRID_L - 1
    drawn_count = width_span * width_span
    cell_count = grid_side * grid_side
    patch_ids = jnp.arange(cell_count, dtype=jnp.int32)
    row_pos = patch_ids // grid_side
    col_pos = patch_ids % grid_side
    offsets = (row_pos[:, None] - row_pos[None, :] + GRID_L - 1) * width_span + (col_pos[:, None] - col_pos[None, :] + GRID_L - 1)
    top_rows = jnp.concatenate([jnp.full((1, 1), drawn_count + 2, jnp.int32), jnp.full((1, cell_count), drawn_count, jnp.int32)], axis=1)
    lower_rows = jnp.concatenate([jnp.full((cell_count, 1), drawn_count + 1, jnp.int32), offsets.astype(jnp.int32)], axis=1)
    return jnp.concatenate([top_rows, lower_rows], axis=0)


def draw_small_index(key, part):
    labels = bucket_labels(key)
    return labels[grid_buckets(GRID_S)]


def draw_large_index(key, part):
    labels = bucket_labels(key)
    return labels[grid_buckets(GRID_L)]


def with_ends(entries, own_key, low, top_value):
    dims = entries.shape
    place = [jax.random.randint(jax.random.fold_in(own_key, axis), (), 0, dims[axis]) for axis in range(len(dims))]
    entries = entries.at[tuple(place)].set(low)
    longest = dims.index(max(dims))
    place[longest] = (place[longest] + 1) % dims[longest]
    return entries.at[tuple(place)].set(top_value)


def steps_of(stream_key, dims, cuts, smallest, high):
    level = 1.0
    for position, shards_of in cuts:
        heights = jax.random.uniform(jax.random.fold_in(jax.random.fold_in(stream_key, 6), position), (shards_of,), jnp.float32, smallest / len(cuts), high / len(cuts))
        level = level * jnp.repeat(jnp.exp(heights), dims[position] // shards_of).reshape((-1,) + (1,) * (len(dims) - 1 - position))
    return level


def noise(rng, shape, spread, most, shards=(), kind=jnp.bfloat16):
    loudness = steps_of(rng, shape, shards, -0.22, 0.18) if shards else 1.0
    values = jax.random.normal(rng, shape, jnp.float32) * spread * loudness
    return jnp.minimum(jnp.maximum(values, -most), most).astype(kind)


def setup_inputs(seed: int = 0) -> dict:
    seeds = jax.random.split(jax.random.key(seed), 22)
    tokens = noise(seeds[0], (SLOTS, SLOT, D), 1.0, 6.0, ((0, 32),))
    slot_kinds = with_ends(jax.random.randint(seeds[1], (SLOTS,), 0, 2), jax.random.fold_in(seeds[1], 1), 0, 1).astype(jnp.int32)
    small_index = draw_small_index(jax.random.fold_in(seeds[21], 71), 0)
    large_index = draw_large_index(jax.random.fold_in(seeds[21], 71), 0)
    first_gain = jnp.clip(1.0 + 0.1 * jax.random.normal(seeds[4], (LAYERS, D), jnp.float32), 0.5, 1.5).astype(jnp.bfloat16)
    first_shift = noise(seeds[5], (LAYERS, D), 0.3, 2.0, ((1, 8),))
    triple_weight = noise(seeds[6], (LAYERS, D, 3 * D), D ** -0.5, 0.21875, ((1, 8),))
    query_bias = noise(seeds[7], (LAYERS, D), 0.3, 2.0, ((1, 8),))
    value_bias = noise(seeds[8], (LAYERS, D), 0.3, 2.0, ((1, 8),))
    bias_table = noise(seeds[9], (LAYERS, NB, HEADS), 1.0, 4.0, ((1, 8),))
    output_weight = noise(seeds[10], (LAYERS, D, D), (max(D // 96, 8)) ** -0.5, 2.0, ((1, 8),))
    output_bias = noise(seeds[11], (LAYERS, D), 0.3, 2.0, ((1, 8),))
    attend_scale = jnp.clip(0.5 + 1.0 * jax.random.uniform(seeds[12], (LAYERS, D), jnp.float32) ** steps_of(seeds[12], (LAYERS, D), ((1, 8),), -0.2, 0.2), 0.5, 1.5).astype(jnp.bfloat16)
    second_gain = jnp.clip(1.0 + 0.1 * jax.random.normal(seeds[13], (LAYERS, D), jnp.float32), 0.5, 1.5).astype(jnp.bfloat16)
    second_shift = noise(seeds[14], (LAYERS, D), 0.3, 2.0, ((1, 8),))
    expand_weight = noise(seeds[15], (LAYERS, D, FF), D ** -0.5, 0.21875, ((1, 8),))
    expand_bias = noise(seeds[16], (LAYERS, FF), 0.3, 2.0, ((1, 8),))
    reduce_weight = noise(seeds[17], (LAYERS, FF, D), (FF // 2) ** -0.5, 0.15625, ((1, 8),))
    reduce_bias = noise(seeds[18], (LAYERS, D), 0.3, 2.0, ((1, 8),))
    feed_scale = jnp.clip(0.5 + 1.0 * jax.random.uniform(seeds[19], (LAYERS, D), jnp.float32) ** steps_of(seeds[19], (LAYERS, D), ((1, 8),), -0.2, 0.2), 0.5, 1.5).astype(jnp.bfloat16)
    cotangent = noise(seeds[20], (SLOTS, SLOT, D), 1.0, 6.0, ((0, 32),))
    return dict(tokens=tokens, slot_kinds=slot_kinds, small_index=small_index, large_index=large_index, first_gain=first_gain, first_shift=first_shift, triple_weight=triple_weight, query_bias=query_bias, value_bias=value_bias, bias_table=bias_table, output_weight=output_weight, output_bias=output_bias, attend_scale=attend_scale, second_gain=second_gain, second_shift=second_shift, expand_weight=expand_weight, expand_bias=expand_bias, reduce_weight=reduce_weight, reduce_bias=reduce_bias, feed_scale=feed_scale, cotangent=cotangent)


@jax.custom_vjp
def low(v):
    return lax.optimization_barrier(v.astype(jnp.bfloat16)).astype(jnp.float32)

@jax.custom_vjp
def low_back(v):
    return v

def low_keep(v):
    return (low(v), None)

def low_pass(kept, grad):
    return (grad,)

def back_keep(v):
    return (v, None)

def back_low(kept, grad):
    return (low(grad),)
low.defvjp(low_keep, low_pass)
low_back.defvjp(back_keep, back_low)
norm_eps = 1e-06
neg_fill = -1000000000.0

def matmul_high(left_arr, right_arr):
    return jnp.dot(left_arr, right_arr, precision=lax.Precision.HIGHEST)

def layer_norm(values_in, gain_vec, shift_vec):
    row_mean = lax.optimization_barrier(jnp.mean(values_in, axis=-1, keepdims=True))
    centred = values_in - row_mean
    row_var = lax.optimization_barrier(jnp.mean(centred * centred, axis=-1, keepdims=True))
    return centred * lax.rsqrt(row_var + norm_eps) * gain_vec + shift_vec

def segment_of(kind_value):
    row_ids = jnp.arange(SLOT, dtype=jnp.int32)
    small_seg = jnp.where(row_ids < 3 * TOK_S, row_ids // TOK_S, 3)
    large_seg = jnp.where(row_ids < TOK_L, 0, 3)
    return jnp.where(kind_value == 1, large_seg, small_seg)

def slot_bias(table_vals, small_index, large_index, kind_value):
    head_count = table_vals.shape[1]
    large_part = jnp.transpose(jnp.take(table_vals, large_index, axis=0), (2, 0, 1))
    small_part = jnp.transpose(jnp.take(table_vals, small_index, axis=0), (2, 0, 1))
    full_large = jnp.zeros((head_count, SLOT, SLOT), table_vals.dtype).at[:, :TOK_L, :TOK_L].set(large_part)
    full_small = jnp.zeros((head_count, SLOT, SLOT), table_vals.dtype)
    for block_idx in range(3):
        first_row = block_idx * TOK_S
        full_small = full_small.at[:, first_row:first_row + TOK_S, first_row:first_row + TOK_S].set(small_part)
    return jnp.where(kind_value == 1, full_large, full_small)

def layer_forward(params, hidden_in, allowed, kind_value, small_index, large_index):
    first_gain, first_shift, triple_weight, query_bias, value_bias, bias_table, output_weight, output_bias, attend_scale, second_gain, second_shift, expand_weight, expand_bias, reduce_weight, reduce_bias, feed_scale = params
    normed = low(layer_norm(hidden_in, first_gain, first_shift))
    triple = matmul_high(normed, triple_weight)
    query_rows = low(low_back(triple[:, :D] + query_bias)).reshape(SLOT, HEADS, HEAD_DIM)
    key_rows = low(low_back(triple[:, D:2 * D])).reshape(SLOT, HEADS, HEAD_DIM)
    value_rows = low(low_back(triple[:, 2 * D:] + value_bias)).reshape(SLOT, HEADS, HEAD_DIM)
    pair_bias = slot_bias(bias_table, small_index, large_index, kind_value)
    scores = jnp.einsum('qhd,khd->hqk', query_rows, key_rows, precision=lax.Precision.HIGHEST) * HEAD_DIM ** (-0.5) + pair_bias
    scores = jnp.where(allowed[None], low_back(scores), neg_fill)
    row_max = lax.optimization_barrier(jnp.max(scores, axis=-1, keepdims=True))
    exp_scores = jnp.exp(scores - row_max)
    soft_probs = low(exp_scores / lax.optimization_barrier(jnp.sum(exp_scores, axis=-1, keepdims=True)))
    mixed_heads = jnp.einsum('hqk,khd->qhd', soft_probs, value_rows, precision=lax.Precision.HIGHEST).reshape(SLOT, D)
    mixed_heads = low(low_back(mixed_heads))
    branch = low_back(matmul_high(mixed_heads, output_weight) + output_bias)
    middle = hidden_in + attend_scale * branch
    second = low(layer_norm(middle, second_gain, second_shift))
    pre_act = low_back(matmul_high(second, expand_weight) + expand_bias)
    activated = low(jax.nn.gelu(pre_act, approximate=False))
    feed_out = low_back(matmul_high(activated, reduce_weight) + reduce_bias)
    return middle + feed_scale * feed_out

def reference(tokens, slot_kinds, small_index, large_index, first_gain, first_shift, triple_weight, query_bias, value_bias, bias_table, output_weight, output_bias, attend_scale, second_gain, second_shift, expand_weight, expand_bias, reduce_weight, reduce_bias, feed_scale, cotangent):
    weights = tuple((weight_arr.astype(jnp.float32) for weight_arr in (first_gain, first_shift, triple_weight, query_bias, value_bias, bias_table, output_weight, output_bias, attend_scale, second_gain, second_shift, expand_weight, expand_bias, reduce_weight, reduce_bias, feed_scale)))

    def one_slot(carry_grads, slot_item):
        slot_tokens, kind_value, slot_cot = slot_item
        segment = segment_of(kind_value)
        allowed = segment[:, None] == segment[None, :]
        live_rows = (segment < 3).astype(jnp.float32)

        def forward(params, start_tokens):
            hidden_now = start_tokens
            for layer_idx in range(LAYERS):
                layer_params = tuple((param_arr[layer_idx] for param_arr in params))
                hidden_now = layer_forward(layer_params, hidden_now, allowed, kind_value, small_index, large_index)
            return hidden_now
        result, pull_back = jax.vjp(forward, weights, slot_tokens.astype(jnp.float32))
        weight_grads, input_grad = pull_back(slot_cot.astype(jnp.float32) * live_rows[:, None])
        carry_grads = jax.tree.map(lambda acc_arr, new_arr: acc_arr + new_arr, carry_grads, weight_grads)
        return (carry_grads, (result.astype(jnp.bfloat16), input_grad.astype(jnp.bfloat16)))
    start_grads = tuple((jnp.zeros(weight_arr.shape, jnp.float32) for weight_arr in weights))
    grads, (outputs, input_grads) = lax.scan(one_slot, start_grads, (tokens, slot_kinds, cotangent))
    return (outputs, input_grads, grads[0], grads[1], grads[2], grads[3], grads[4], grads[5], grads[6], grads[7], grads[8], grads[9], grads[10], grads[11], grads[12], grads[13], grads[14], grads[15])
```

```python
import functools

import jax
import jax.numpy as jnp
import numpy as np
from jax import lax
from jax.experimental import pallas as pl
from jax.experimental.pallas import tpu as pltpu
from jax.sharding import PartitionSpec as P

f32 = jnp.float32
bf16 = jnp.bfloat16
norm_eps = 1e-06
neg_fill = -1000000000.0
vmem_bytes = 60 << 20

NN = (((1,), (0,)), ((), ()))
NT = (((1,), (1,)), ((), ()))
TN = (((0,), (0,)), ((), ()))


def mm(left, right, dims=NN):
    return lax.dot_general(left, right, dims, preferred_element_type=f32)


def round_up(value, unit):
    return -(-value // unit) * unit


class Plan:
    def __init__(self, small_len, large_len, rows):
        self.rows = rows
        self.small_len, self.large_len = small_len, large_len
        self.gs = int(round((small_len - 1) ** 0.5))
        self.gl = int(round((large_len - 1) ** 0.5))
        gl, gs = self.gl, self.gs
        self.strip_l = round_up(2 * gl * gl, 128)
        self.strip_s = round_up(2 * gs * (2 * gs - 1) + gs, 128)
        self.line = 2 * self.strip_l
        self.lanes = self.line + 128
        self.pad_cols = round_up(2 * gs * gs + 1, 128)
        self.pad_rows = 16 * gs
        self.cls_col = 2 * gs * gs
        self.cls_row = gs

    def place(self, di, dj, limit):
        gl = self.gl
        good = (np.abs(di) < limit) & (np.abs(dj) < limit)
        row = 1 + gl * np.maximum(di, 0) + np.maximum(dj, 0)
        col = 1 + gl * np.maximum(-di, 0) + np.maximum(-dj, 0)
        return np.where(good, row, 0), np.where(good, col, 0), good

    def positions(self):
        gl, gs = self.gl, self.gs
        x = np.arange(self.strip_l)
        rows, cols, goods = [], [], []
        for parity in range(2):
            m = 2 * ((x + gl) // (2 * gl)) if parity == 0 else 2 * (x // (2 * gl)) + 1
            t = x - gl * m
            r, c, g = self.place(gl - m, -t, gl)
            rows.append(r), cols.append(c), goods.append(g)
        large = [np.concatenate(v) for v in (rows, cols, goods)]
        x = np.arange(self.strip_s)
        m = x // (2 * gs)
        t = x - 2 * gs * m - gs
        small = [np.resize(np.zeros(1, v.dtype), self.line) for v in large]
        for dst, src in zip(small, self.place(gs - 1 - m, -t, gs)):
            dst[: self.strip_s] = src
        tail_r, tail_c, tail_g = np.zeros(128, int), np.zeros(128, int), np.zeros(128, bool)
        tail_r[:3], tail_c[:3], tail_g[:3] = (0, 1, 0), (1, 0, 0), True
        out = []
        for base in (large, small):
            out.append([np.concatenate(v) for v in zip(base, (tail_r, tail_c, tail_g))])
        return out

    def selectors(self):
        gs = self.gs
        rows = np.zeros((self.rows, self.pad_rows), np.float32)
        cols = np.zeros((self.pad_cols, self.rows), np.float32)
        for image in range(3):
            for tok in range(self.small_len):
                r = image * self.small_len + tok
                i, j = divmod(tok - 1, gs)
                rows[r, self.cls_row if tok == 0 else 16 * i + j] = 1
                cols[self.cls_col if tok == 0 else 2 * gs * i + j, r] = 1
        return jnp.asarray(rows, bf16), jnp.asarray(cols, bf16)


def table_labels(plan, large_index, kind):
    (lr, lc, lg), (sr, sc, sg) = plan.positions()
    is_large = kind == 1
    row = jnp.where(is_large, jnp.asarray(lr, jnp.int32), jnp.asarray(sr, jnp.int32))
    col = jnp.where(is_large, jnp.asarray(lc, jnp.int32), jnp.asarray(sc, jnp.int32))
    good = jnp.where(is_large, jnp.asarray(lg), jnp.asarray(sg))
    return jnp.where(good, large_index[row, col], -1).reshape(1, plan.lanes)


def iota(shape, dim):
    return lax.broadcasted_iota(jnp.int32, shape, dim)


def one_hot(lab_ref, chunk, buckets):
    lab = lab_ref[:, chunk * 128 : (chunk + 1) * 128]
    return jnp.where(iota((buckets, 128), 0) == lab, 1.0, 0.0).astype(bf16)


def row_roll(value, first, step, span):
    shape = value.shape
    out = pltpu.roll(value, first % span, axis=1) if first % span else value
    bit = 1
    while bit < shape[0]:
        moved = pltpu.roll(out, (step * bit) % span, axis=1)
        out = jnp.where((iota(shape, 0) & bit) != 0, moved, out)
        bit *= 2
    return out


def bias_large(plan, line_ref, h, out_ref):
    gl, rows, span = plan.gl, plan.rows, plan.strip_l
    f0 = jnp.broadcast_to(line_ref[h, :, 0:span], (gl, span))
    f1 = jnp.broadcast_to(line_ref[h, :, span : 2 * span], (gl, span))
    tail = line_ref[h, :, 2 * span : 2 * span + 128]
    r0 = row_roll(f0, -1, 1, span)
    r1 = row_roll(f1, -1, 1, span)
    odd = (iota((gl, span), 1) // gl) % 2
    odd = jnp.where(iota((gl, span), 0) == 0, 1 - odd, odd)
    strip = jnp.where(odd == 1, r1, r0)
    strip = jnp.concatenate([jnp.zeros((gl, 128), f32), strip, jnp.zeros((gl, 128), f32)], axis=1)
    wide = round_up(rows, 128)
    col = iota((2 * gl, wide), 1)
    bands = -(-rows // gl)
    for pair in range(-(-bands // 2)):
        parts = []
        for a in range(2 * pair, 2 * pair + 2):
            if a >= bands:
                parts.append(jnp.zeros((gl, wide), f32))
                continue
            move = 127 + gl * (gl - a)
            low = move // 128 * 128
            piece = strip[:, low : low + wide + 128]
            parts.append(pltpu.roll(piece, (wide + 128 - (move - low)) % (wide + 128), axis=1)[:, :wide])
        block = jnp.concatenate(parts, axis=0)
        row = iota((2 * gl, wide), 0) + 2 * gl * pair
        block = jnp.where(col == 0, tail[:, 1:2], block)
        if pair == 0:
            block = jnp.where(row == 0, jnp.where(col == 0, tail[:, 2:3], tail[:, 0:1]), block)
        block = jnp.where((row < plan.large_len) == (col < plan.large_len), block, neg_fill)
        block = jnp.where((row < plan.large_len) | (col < plan.large_len), block, 0.0)
        first = 2 * gl * pair
        count = min(2 * gl, rows - first)
        out_ref[0, first : first + count, :] = block[:count, :rows].astype(bf16)


def segment(plan, ids):
    n = plan.small_len
    return (
        jnp.where(ids >= n, 1, 0) + jnp.where(ids >= 2 * n, 1, 0) + jnp.where(ids >= 3 * n, 1, 0)
    )


def bias_small(plan, line_ref, rowsel_ref, colsel_ref, h, out_ref):
    gs, span, rows = plan.gs, plan.strip_s, plan.rows
    line = jnp.broadcast_to(line_ref[h, :, 0:span], (16, span))
    tail = line_ref[h, :, plan.line : plan.line + 128]
    strip = row_roll(line, -gs, 1, span)
    col = iota((16, plan.pad_cols), 1)
    row = iota((16, plan.pad_cols), 0)
    bands = []
    for i in range(gs):
        band = pltpu.roll(strip, (span - 2 * gs * (gs - 1 - i)) % span, axis=1)[:, : plan.pad_cols]
        band = jnp.where(col == plan.cls_col, tail[:, 1:2], band)
        if i == 0:
            edge = jnp.where(col == plan.cls_col, tail[:, 2:3], tail[:, 0:1])
            band = jnp.where(row == plan.cls_row, edge, band)
        bands.append(band)
    padded = jnp.concatenate(bands, axis=0).astype(bf16)
    cols = mm(padded, colsel_ref[...]).astype(bf16)
    full = mm(rowsel_ref[...], cols)
    same = segment(plan, iota((rows, rows), 0)) == segment(plan, iota((rows, rows), 1))
    out_ref[0] = jnp.where(same, full, neg_fill).astype(bf16)


def bias_kernel(plan, kind_ref, lab_ref, tab_ref, rowsel_ref, colsel_ref, out_ref, line_ref):
    h = pl.program_id(0)

    @pl.when(h == 0)
    def _():
        for chunk in range(plan.lanes // 128):
            part = mm(tab_ref[...], one_hot(lab_ref, chunk, tab_ref.shape[1]))
            for i in range(line_ref.shape[0]):
                line_ref[i, :, chunk * 128 : (chunk + 1) * 128] = part[i : i + 1]

    @pl.when(kind_ref[0] == 1)
    def _():
        bias_large(plan, line_ref, h, out_ref)

    @pl.when(kind_ref[0] != 1)
    def _():
        bias_small(plan, line_ref, rowsel_ref, colsel_ref, h, out_ref)


def whole(shape):
    zeros = (0,) * len(shape)
    return pl.BlockSpec(shape, lambda i: zeros)


smem_spec = pl.BlockSpec(memory_space=pltpu.SMEM)
params = pltpu.CompilerParams(vmem_limit_bytes=vmem_bytes)


def pair_bias(plan, kind, labels, table, rowsel, colsel):
    heads, buckets = table.shape
    table = jnp.pad(table, ((0, 16 - heads), (0, 0)))
    rows = plan.rows
    return pl.pallas_call(
        functools.partial(bias_kernel, plan),
        grid=(heads,),
        in_specs=[
            smem_spec,
            whole(labels.shape),
            whole(table.shape),
            whole(rowsel.shape),
            whole(colsel.shape),
        ],
        out_specs=pl.BlockSpec((1, rows, rows), lambda i: (i, 0, 0)),
        out_shape=jax.ShapeDtypeStruct((heads, rows, rows), bf16),
        scratch_shapes=[pltpu.VMEM((16, 1, plan.lanes), f32)],
        compiler_params=params,
        name="pair_bias",
    )(kind, labels, table, rowsel, colsel)


def fold_large(plan, ds_ref, h, line_ref):
    gl, rows, span = plan.gl, plan.rows, plan.strip_l
    wide = round_up(rows, 128)
    total = jnp.zeros((gl, span + 256), f32)
    pieces = {}
    bands = -(-rows // gl)
    side = jnp.zeros((1, 1), f32)
    for pair in range(-(-bands // 2)):
        first = 2 * gl * pair
        count = min(2 * gl, rows - first)
        block = ds_ref[0, first : first + count, :].astype(f32)
        block = jnp.concatenate([block, jnp.zeros((count, wide - rows), f32)], axis=1)
        if count < 2 * gl:
            block = jnp.concatenate([block, jnp.zeros((2 * gl - count, wide), f32)], axis=0)
        shape = (2 * gl, wide)
        col = iota(shape, 1)
        if pair == 0:
            row = iota(shape, 0)
            corner = jnp.sum(jnp.where((row == 0) & (col == 0), block, 0.0), keepdims=True)
            top = jnp.sum(jnp.where((row == 0) & (col > 0), block, 0.0), keepdims=True)
            block = jnp.where(row == 0, 0.0, block)
        side = side + jnp.sum(block[:, 0:1], keepdims=True)
        block = jnp.where(col == 0, 0.0, block)
        for half in range(2):
            a = 2 * pair + half
            if a >= bands:
                continue
            move = 127 + gl * (gl - a)
            low = move // 128 * 128
            piece = block[half * gl : (half + 1) * gl]
            piece = jnp.concatenate([piece, jnp.zeros((gl, 128), f32)], axis=1)
            piece = pltpu.roll(piece, move - low, axis=1) if move > low else piece
            pieces[low] = piece if low not in pieces else pieces[low] + piece
    for low, piece in pieces.items():
        parts = [piece]
        if low:
            parts.insert(0, jnp.zeros((gl, low), f32))
        rest = span + 256 - low - wide - 128
        if rest > 0:
            parts.append(jnp.zeros((gl, rest), f32))
        total = total + jnp.concatenate(parts, axis=1)[:, : span + 256]
    strip = total[:, 128 : 128 + span]
    odd = (iota((gl, span), 1) // gl) % 2
    odd = jnp.where(iota((gl, span), 0) == 0, 1 - odd, odd)
    for parity in range(2):
        part = jnp.where(odd == parity, strip, 0.0)
        part = row_roll(part, 1, -1, span)
        line_ref[h, :, parity * span : (parity + 1) * span] = jnp.sum(
            part, axis=0, keepdims=True
        )
    store_tail(plan, line_ref, h, top, side, corner)


def store_tail(plan, line_ref, h, top, side, corner):
    lane = iota((1, 128), 1)
    tail = jnp.where(lane == 0, top, jnp.where(lane == 1, side, jnp.where(lane == 2, corner, 0.0)))
    line_ref[h, :, plan.line : plan.line + 128] = tail


def fold_small(plan, ds_ref, rowsel_ref, colsel_ref, h, line_ref):
    gs, span = plan.gs, plan.strip_s
    cols = mm(ds_ref[0], colsel_ref[...], NT).astype(bf16)
    padded = mm(rowsel_ref[...], cols, TN)
    row = iota((16, plan.pad_cols), 0)
    col = iota((16, plan.pad_cols), 1)
    total = jnp.zeros((16, span), f32)
    side = jnp.zeros((1, 1), f32)
    for i in range(gs):
        band = padded[16 * i : 16 * (i + 1)]
        if i == 0:
            is_top = row == plan.cls_row
            corner = jnp.sum(jnp.where(is_top & (col == plan.cls_col), band, 0.0), keepdims=True)
            top = jnp.sum(jnp.where(is_top & (col < plan.cls_col), band, 0.0), keepdims=True)
            band = jnp.where(is_top, 0.0, band)
        side = side + jnp.sum(jnp.where(col == plan.cls_col, band, 0.0), keepdims=True)
        band = jnp.where(col < plan.cls_col, band, 0.0)
        band = jnp.concatenate([band, jnp.zeros((16, span - plan.pad_cols), f32)], axis=1)
        move = 2 * gs * (gs - 1 - i)
        total = total + (pltpu.roll(band, move, axis=1) if move else band)
    total = row_roll(total, gs, -1, span)
    line_ref[h, :, 0 : plan.line] = jnp.zeros((1, plan.line), f32)
    line_ref[h, :, 0:span] = jnp.sum(total, axis=0, keepdims=True)
    store_tail(plan, line_ref, h, top, side, corner)


def fold_kernel(plan, kind_ref, ds_ref, lab_ref, rowsel_ref, colsel_ref, out_ref, line_ref):
    h = pl.program_id(0)

    @pl.when(h == 0)
    def _():
        line_ref[...] = jnp.zeros_like(line_ref)

    @pl.when(kind_ref[0] == 1)
    def _():
        fold_large(plan, ds_ref, h, line_ref)

    @pl.when(kind_ref[0] != 1)
    def _():
        fold_small(plan, ds_ref, rowsel_ref, colsel_ref, h, line_ref)

    @pl.when(h == pl.num_programs(0) - 1)
    def _():
        buckets = out_ref.shape[1]
        total = jnp.zeros(out_ref.shape, f32)
        for chunk in range(plan.lanes // 128):
            hot = one_hot(lab_ref, chunk, buckets)
            part = jnp.concatenate(
                [line_ref[i, :, chunk * 128 : (chunk + 1) * 128] for i in range(16)], axis=0
            )
            high = part.astype(bf16)
            low = (part - high.astype(f32)).astype(bf16)
            total = total + mm(high, hot, NT) + mm(low, hot, NT)
        out_ref[...] = total


def table_gradient(plan, kind, d_scores, labels, rowsel, colsel, buckets):
    heads, rows, _ = d_scores.shape
    return pl.pallas_call(
        functools.partial(fold_kernel, plan),
        grid=(heads,),
        in_specs=[
            smem_spec,
            pl.BlockSpec((1, rows, rows), lambda i: (i, 0, 0)),
            whole(labels.shape),
            whole(rowsel.shape),
            whole(colsel.shape),
        ],
        out_specs=whole((16, buckets)),
        out_shape=jax.ShapeDtypeStruct((16, buckets), f32),
        scratch_shapes=[pltpu.VMEM((16, 1, plan.lanes), f32)],
        compiler_params=params,
        name="table_gradient",
    )(kind, d_scores, labels, rowsel, colsel)


def norm_stats(values):
    mean = jnp.mean(values, axis=1, keepdims=True)
    centred = values - mean
    var = jnp.mean(centred * centred, axis=1, keepdims=True)
    inv = lax.rsqrt(var + norm_eps)
    return centred * inv, inv


def norm_back(d_out, gain, normal, inv):
    d_normal = d_out * gain
    mean_d = jnp.mean(d_normal, axis=1, keepdims=True)
    mean_dn = jnp.mean(d_normal * normal, axis=1, keepdims=True)
    return inv * (d_normal - mean_d - normal * mean_dn)


def rows_sum(values):
    return jnp.sum(values, axis=0, keepdims=True)


def gelu_parts(v):
    size = jnp.abs(v)
    bell = jnp.exp(-0.5 * v * v)
    t = 1.0 / (1.0 + (0.3275911 * 0.7071067811865476) * size)
    poly = t * (
        0.127414796
        + t * (-0.142248368 + t * (0.7107068705 + t * (-0.7265760135 + t * 0.5307027145)))
    )
    tail = poly * bell
    phi = jnp.where(v < 0, tail, 1.0 - tail)
    return v * phi, phi + v * bell * 0.3989422804014327


(
    FIRST_GAIN,
    FIRST_SHIFT,
    QUERY_BIAS,
    VALUE_BIAS,
    OUTPUT_BIAS,
    ATTEND_SCALE,
    SECOND_GAIN,
    SECOND_SHIFT,
    REDUCE_BIAS,
    FEED_SCALE,
) = range(10)


def vec(ref, idx):
    return ref[idx : idx + 1, :]


def project_kernel(tok_ref, vec_ref, w_ref, normed_ref, out_ref):
    part = pl.program_id(0)

    @pl.when(part == 0)
    def _():
        normal, _ = norm_stats(tok_ref[...].astype(f32))
        normed_ref[...] = (normal * vec(vec_ref, FIRST_GAIN) + vec(vec_ref, FIRST_SHIFT)).astype(
            bf16
        )

    bias = jnp.where(
        part == 0,
        vec(vec_ref, QUERY_BIAS),
        jnp.where(part == 2, vec(vec_ref, VALUE_BIAS), 0.0),
    )
    scale = jnp.where(part == 0, 0.125, 1.0)
    triple = mm(normed_ref[...], w_ref[...]) + bias
    out_ref[...] = (triple.astype(bf16).astype(f32) * scale).astype(bf16)


def project(tokens, vecs, weight):
    rows, width = tokens.shape
    return pl.pallas_call(
        project_kernel,
        grid=(3,),
        in_specs=[
            whole(tokens.shape),
            whole(vecs.shape),
            pl.BlockSpec((width, width), lambda i: (0, i)),
        ],
        out_specs=[whole(tokens.shape), pl.BlockSpec((rows, width), lambda i: (0, i))],
        out_shape=[
            jax.ShapeDtypeStruct((rows, width), bf16),
            jax.ShapeDtypeStruct((rows, 3 * width), bf16),
        ],
        compiler_params=params,
        name="project",
    )(tokens, vecs, weight)


def half_mask(rows):
    return iota((rows, 128), 1) < 64


def attend_kernel(q_ref, k_ref, v_ref, b_ref, mixed_ref, p_ref):
    q, k, v = q_ref[...], k_ref[...], v_ref[...]
    lower = half_mask(q.shape[0])
    mixed = []
    for t in range(2):
        keep = lower if t == 0 else ~lower
        scores = mm(jnp.where(keep, q, jnp.zeros_like(q)), k, NT) + b_ref[t].astype(f32)
        top = jnp.max(scores, axis=1, keepdims=True)
        exps = jnp.exp(scores - top)
        total = jnp.sum(exps, axis=1, keepdims=True)
        probs = (exps * (1.0 / total)).astype(bf16)
        p_ref[t] = probs
        mixed.append(mm(probs, v))
    mixed_ref[...] = jnp.where(lower, mixed[0], mixed[1]).astype(bf16)


def attend(triple, bias):
    rows = triple.shape[0]
    heads = bias.shape[0]
    pairs = heads // 2
    cols = lambda part: pl.BlockSpec((rows, 128), lambda i: (0, i + part * pairs))
    square = pl.BlockSpec((2, rows, rows), lambda i: (i, 0, 0))
    return pl.pallas_call(
        attend_kernel,
        grid=(pairs,),
        in_specs=[cols(0), cols(1), cols(2), square],
        out_specs=[cols(0), square],
        out_shape=[
            jax.ShapeDtypeStruct((rows, 64 * heads), bf16),
            jax.ShapeDtypeStruct((heads, rows, rows), bf16),
        ],
        compiler_params=params,
        name="attend",
    )(triple, triple, triple, bias)


def attend_back_kernel(q_ref, k_ref, v_ref, do_ref, m_ref, p_ref, dq_ref, dk_ref, dv_ref, ds_ref):
    q, k, v, do = q_ref[...], k_ref[...], v_ref[...], do_ref[...]
    lower = half_mask(q.shape[0])
    prod = do.astype(f32) * m_ref[...].astype(f32)
    dq, dk, dv = [], [], []
    for t in range(2):
        keep = lower if t == 0 else ~lower
        d_mixed = jnp.where(keep, do, jnp.zeros_like(do))
        delta = jnp.sum(jnp.where(keep, prod, 0.0), axis=1, keepdims=True)
        d_probs = mm(d_mixed, v, NT)
        probs = p_ref[t]
        d_scores = (probs.astype(f32) * (d_probs - delta)).astype(bf16)
        ds_ref[t] = d_scores
        dq.append(mm(d_scores, k))
        dk.append(mm(d_scores, q, TN))
        dv.append(mm(probs, do, TN))
    dq_ref[...] = (jnp.where(lower, dq[0], dq[1]) * 0.125).astype(bf16)
    dk_ref[...] = jnp.where(lower, dk[0], dk[1]).astype(bf16)
    dv_ref[...] = jnp.where(lower, dv[0], dv[1]).astype(bf16)


def attend_back(triple, d_mixed, mixed, probs):
    heads, rows, _ = probs.shape
    pairs = heads // 2
    cols = lambda part: pl.BlockSpec((rows, 128), lambda i: (0, i + part * pairs))
    square = pl.BlockSpec((2, rows, rows), lambda i: (i, 0, 0))
    wide = jax.ShapeDtypeStruct((rows, 64 * heads), bf16)
    return pl.pallas_call(
        attend_back_kernel,
        grid=(pairs,),
        in_specs=[cols(0), cols(1), cols(2), cols(0), cols(0), square],
        out_specs=[cols(0), cols(0), cols(0), square],
        out_shape=[wide, wide, wide, jax.ShapeDtypeStruct(probs.shape, bf16)],
        compiler_params=params,
        name="attend_back",
    )(triple, triple, triple, d_mixed, mixed, probs)


def feed_kernel(
    plan,
    kind_ref,
    tok_ref,
    cot_ref,
    mixed_ref,
    wo_ref,
    vec_ref,
    be_ref,
    we_ref,
    wr_ref,
    out_ref,
    dmid_ref,
    dmix_ref,
    dwo_ref,
    dwe_ref,
    dwr_ref,
    small_ref,
    dbe_ref,
    middle_ref,
    branch_ref,
    second_ref,
    dfeed_ref,
    feed_ref,
    dsec_ref,
):
    step = pl.program_id(0)
    rows = plan.rows

    def masked_cot():
        limit = jnp.where(kind_ref[0] == 1, plan.large_len, 3 * plan.small_len)
        live = iota((rows, 1), 0) < limit
        return jnp.where(live, cot_ref[...].astype(f32), 0.0)

    @pl.when(step == 0)
    def _():
        branch = mm(mixed_ref[...], wo_ref[...]) + vec(vec_ref, OUTPUT_BIAS)
        branch_ref[...] = branch
        middle = tok_ref[...].astype(f32) + vec(vec_ref, ATTEND_SCALE) * branch
        middle_ref[...] = middle
        normal, _ = norm_stats(middle)
        second_ref[...] = (
            normal * vec(vec_ref, SECOND_GAIN) + vec(vec_ref, SECOND_SHIFT)
        ).astype(bf16)
        dfeed_ref[...] = (vec(vec_ref, FEED_SCALE) * masked_cot()).astype(bf16)
        feed_ref[...] = jnp.zeros_like(feed_ref)
        dsec_ref[...] = jnp.zeros_like(dsec_ref)

    second, d_feed = second_ref[...], dfeed_ref[...]
    we, wr = we_ref[...], wr_ref[...]
    pre = mm(second, we) + be_ref[...]
    value, slope = gelu_parts(pre)
    activated = value.astype(bf16)
    feed_ref[...] += mm(activated, wr)
    d_pre = (mm(d_feed, wr, NT) * slope).astype(bf16)
    dsec_ref[...] += mm(d_pre, we, NT)
    dwr_ref[...] = mm(activated, d_feed, TN).astype(bf16)
    dwe_ref[...] = mm(second, d_pre, TN).astype(bf16)
    dbe_ref[...] = rows_sum(d_pre.astype(f32))

    @pl.when(step == pl.num_programs(0) - 1)
    def _():
        feed_out = feed_ref[...] + vec(vec_ref, REDUCE_BIAS)
        middle = middle_ref[...]
        out_ref[...] = (middle + vec(vec_ref, FEED_SCALE) * feed_out).astype(bf16)
        grad = masked_cot()
        d_second = dsec_ref[...]
        normal, inv = norm_stats(middle)
        d_middle = grad + norm_back(d_second, vec(vec_ref, SECOND_GAIN), normal, inv)
        dmid_ref[...] = d_middle
        d_branch = (vec(vec_ref, ATTEND_SCALE) * d_middle).astype(bf16)
        dwo_ref[...] = mm(mixed_ref[...], d_branch, TN).astype(bf16)
        dmix_ref[...] = mm(d_branch, wo_ref[...], NT).astype(bf16)
        small_ref[...] = jnp.zeros_like(small_ref)
        small_ref[FEED_SCALE : FEED_SCALE + 1, :] = rows_sum(grad * feed_out)
        small_ref[REDUCE_BIAS : REDUCE_BIAS + 1, :] = rows_sum(dfeed_ref[...].astype(f32))
        small_ref[SECOND_GAIN : SECOND_GAIN + 1, :] = rows_sum(d_second * normal)
        small_ref[SECOND_SHIFT : SECOND_SHIFT + 1, :] = rows_sum(d_second)
        small_ref[ATTEND_SCALE : ATTEND_SCALE + 1, :] = rows_sum(d_middle * branch_ref[...])
        small_ref[OUTPUT_BIAS : OUTPUT_BIAS + 1, :] = rows_sum(d_branch.astype(f32))


def feed(plan, kind, tokens, cot, mixed, wo, vecs, be, we, wr):
    rows, width = tokens.shape
    hidden = we.shape[1]
    tile = 512
    sds = jax.ShapeDtypeStruct
    return pl.pallas_call(
        functools.partial(feed_kernel, plan),
        grid=(hidden // tile,),
        in_specs=[
            smem_spec,
            whole(tokens.shape),
            whole(cot.shape),
            whole(mixed.shape),
            whole(wo.shape),
            whole(vecs.shape),
            pl.BlockSpec((1, tile), lambda i: (0, i)),
            pl.BlockSpec((width, tile), lambda i: (0, i)),
            pl.BlockSpec((tile, width), lambda i: (i, 0)),
        ],
        out_specs=[
            whole((rows, width)),
            whole((rows, width)),
            whole((rows, width)),
            whole((width, width)),
            pl.BlockSpec((width, tile), lambda i: (0, i)),
            pl.BlockSpec((tile, width), lambda i: (i, 0)),
            whole(vecs.shape),
            pl.BlockSpec((1, tile), lambda i: (0, i)),
        ],
        out_shape=[
            sds((rows, width), bf16),
            sds((rows, width), f32),
            sds((rows, width), bf16),
            sds((width, width), bf16),
            sds((width, hidden), bf16),
            sds((hidden, width), bf16),
            sds(vecs.shape, f32),
            sds((1, hidden), f32),
        ],
        scratch_shapes=[
            pltpu.VMEM((rows, width), f32),
            pltpu.VMEM((rows, width), f32),
            pltpu.VMEM((rows, width), bf16),
            pltpu.VMEM((rows, width), bf16),
            pltpu.VMEM((rows, width), f32),
            pltpu.VMEM((rows, width), f32),
        ],
        compiler_params=params,
        name="feed",
    )(kind, tokens, cot, mixed, wo, vecs, be, we, wr)


def finish_kernel(
    tok_ref, dmid_ref, normed_ref, vec_ref, dt_ref, w_ref, dw_ref, out_ref, small_ref, acc_ref
):
    part = pl.program_id(0)

    @pl.when(part == 0)
    def _():
        acc_ref[...] = jnp.zeros_like(acc_ref)
        small_ref[...] = jnp.zeros_like(small_ref)

    d_part = dt_ref[0]
    dw_ref[...] = mm(normed_ref[...], d_part, TN).astype(bf16)
    acc_ref[...] += mm(d_part, w_ref[...], NT)
    sums = rows_sum(d_part.astype(f32))

    @pl.when(part == 0)
    def _():
        small_ref[QUERY_BIAS : QUERY_BIAS + 1, :] = sums

    @pl.when(part == 2)
    def _():
        small_ref[VALUE_BIAS : VALUE_BIAS + 1, :] = sums
        d_normed = acc_ref[...]
        normal, inv = norm_stats(tok_ref[...].astype(f32))
        back = norm_back(d_normed, vec(vec_ref, FIRST_GAIN), normal, inv)
        out_ref[...] = (dmid_ref[...] + back).astype(bf16)
        small_ref[FIRST_GAIN : FIRST_GAIN + 1, :] = rows_sum(d_normed * normal)
        small_ref[FIRST_SHIFT : FIRST_SHIFT + 1, :] = rows_sum(d_normed)


def finish(tokens, d_middle, normed, vecs, d_triple, weight):
    rows, width = tokens.shape
    sds = jax.ShapeDtypeStruct
    return pl.pallas_call(
        finish_kernel,
        grid=(3,),
        in_specs=[
            whole(tokens.shape),
            whole(d_middle.shape),
            whole(normed.shape),
            whole(vecs.shape),
            pl.BlockSpec((1, rows, width), lambda i: (i, 0, 0)),
            pl.BlockSpec((width, width), lambda i: (0, i)),
        ],
        out_specs=[
            pl.BlockSpec((width, width), lambda i: (0, i)),
            whole(tokens.shape),
            whole(vecs.shape),
        ],
        out_shape=[
            sds(weight.shape, bf16),
            sds(tokens.shape, bf16),
            sds(vecs.shape, f32),
        ],
        scratch_shapes=[pltpu.VMEM((rows, width), f32)],
        compiler_params=params,
        name="finish",
    )(tokens, d_middle, normed, vecs, d_triple, weight)


def per_device(
    tokens,
    slot_kinds,
    small_index,
    large_index,
    first_gain,
    first_shift,
    triple_weight,
    query_bias,
    value_bias,
    bias_table,
    output_weight,
    output_bias,
    attend_scale,
    second_gain,
    second_shift,
    expand_weight,
    expand_bias,
    reduce_weight,
    reduce_bias,
    feed_scale,
    cotangent,
):
    _, rows, width = tokens.shape
    heads = bias_table.shape[2]
    plan = Plan(small_index.shape[0], large_index.shape[0], rows)
    tokens, cotangent = tokens[0], cotangent[0]
    gather = lambda value: lax.all_gather(value, "fsdp", axis=0, tiled=True)

    short = [
        first_gain,
        first_shift,
        query_bias,
        value_bias,
        output_bias,
        attend_scale,
        second_gain,
        second_shift,
        reduce_bias,
        feed_scale,
    ]
    share = first_gain.shape[1]
    wide_share = expand_bias.shape[1]
    bucket_share = bias_table.shape[1]
    packed = jnp.concatenate(
        [v[0] for v in short] + [expand_bias[0], bias_table[0].T.reshape(-1)], axis=0
    )
    packed = lax.all_gather(packed, "fsdp", axis=0, tiled=False)
    n = packed.shape[0]
    cut = len(short) * share
    vecs = packed[:, :cut].reshape(n, len(short), share).transpose(1, 0, 2)
    vecs = jnp.pad(vecs.reshape(len(short), width).astype(f32), ((0, 16 - len(short)), (0, 0)))
    be = packed[:, cut : cut + wide_share].reshape(1, n * wide_share).astype(f32)
    table = packed[:, cut + wide_share :].reshape(n, heads, bucket_share).transpose(1, 0, 2)
    table = table.reshape(heads, n * bucket_share)

    wt = gather(triple_weight[0])
    wo = gather(output_weight[0])
    we = gather(expand_weight[0])
    wr = gather(reduce_weight[0])

    rowsel, colsel = plan.selectors()
    labels = table_labels(plan, large_index, slot_kinds[0])
    bias = pair_bias(plan, slot_kinds, labels, table, rowsel, colsel)

    normed, triple = project(tokens, vecs, wt)
    mixed, probs = attend(triple, bias)
    block_output, d_middle, d_mixed, dwo, dwe, dwr, small_a, dbe = feed(
        plan, slot_kinds, tokens, cotangent, mixed, wo, vecs, be, we, wr
    )
    dq, dk, dv, d_scores = attend_back(triple, d_mixed, mixed, probs)
    d_table = table_gradient(plan, slot_kinds, d_scores, labels, rowsel, colsel, table.shape[1])
    dwt, token_grad, small_b = finish(
        tokens, d_middle, normed, vecs, jnp.stack([dq, dk, dv]), wt
    )

    def reduce_weight_part(value):
        value = lax.psum_scatter(value, "fsdp", scatter_dimension=0, tiled=True)
        return lax.psum(value, "rep").astype(f32)[None]

    smalls = (small_a + small_b)[: len(short)]
    smalls = lax.psum((smalls, dbe, d_table[:heads]), ("rep", "fsdp"))
    me = lax.axis_index("fsdp")
    cut_of = lambda value, size: lax.dynamic_slice_in_dim(value, me * size, size, axis=1)
    small = cut_of(smalls[0], share)
    d_be = cut_of(smalls[1], wide_share)
    d_tab = cut_of(smalls[2], bucket_share).T[None]
    row = lambda idx: small[idx : idx + 1]
    return (
        block_output[None],
        token_grad[None],
        row(FIRST_GAIN),
        row(FIRST_SHIFT),
        reduce_weight_part(dwt),
        row(QUERY_BIAS),
        row(VALUE_BIAS),
        d_tab,
        reduce_weight_part(dwo),
        row(OUTPUT_BIAS),
        row(ATTEND_SCALE),
        row(SECOND_GAIN),
        row(SECOND_SHIFT),
        reduce_weight_part(dwe),
        d_be,
        reduce_weight_part(dwr),
        row(REDUCE_BIAS),
        row(FEED_SCALE),
    )


def solution(mesh):
    rows = P(("rep", "fsdp"), None, None)
    vector = P(None, "fsdp")
    matrix = P(None, "fsdp", None)
    weights = (
        vector,
        vector,
        matrix,
        vector,
        vector,
        matrix,
        matrix,
        vector,
        vector,
        vector,
        vector,
        matrix,
        vector,
        matrix,
        vector,
        vector,
    )
    return jax.shard_map(
        per_device,
        mesh=mesh,
        in_specs=(rows, P(("rep", "fsdp")), P(), P()) + weights + (rows,),
        out_specs=(rows, rows) + weights,
        check_vma=False,
    )
```

```python
import functools

import jax
import jax.numpy as jnp
import numpy as np
from jax import lax
from jax.experimental import pallas as pl
from jax.experimental.pallas import tpu as pltpu
from jax.sharding import PartitionSpec as P

f32 = jnp.float32
bf16 = jnp.bfloat16
norm_eps = 1e-06
neg_fill = -1000000000.0
vmem_bytes = 60 << 20

NN = (((1,), (0,)), ((), ()))
NT = (((1,), (1,)), ((), ()))
TN = (((0,), (0,)), ((), ()))


def mm(left, right, dims=NN):
    return lax.dot_general(left, right, dims, preferred_element_type=f32)


def round_up(value, unit):
    return -(-value // unit) * unit


class Plan:
    def __init__(self, small_len, large_len, rows, heads):
        self.heads = heads
        self.rows = rows
        self.small_len, self.large_len = small_len, large_len
        self.gs = int(round((small_len - 1) ** 0.5))
        self.gl = int(round((large_len - 1) ** 0.5))
        gl, gs = self.gl, self.gs
        self.strip_l = round_up(2 * gl * gl, 128)
        self.strip_s = round_up(2 * gs * (2 * gs - 1) + gs, 128)
        self.line = 2 * self.strip_l
        self.lanes = self.line + 128
        self.pad_cols = round_up(2 * gs * gs + 1, 128)
        self.pad_rows = 16 * gs
        self.cls_col = 2 * gs * gs
        self.cls_row = gs

    def place(self, di, dj, limit):
        gl = self.gl
        good = (np.abs(di) < limit) & (np.abs(dj) < limit)
        row = 1 + gl * np.maximum(di, 0) + np.maximum(dj, 0)
        col = 1 + gl * np.maximum(-di, 0) + np.maximum(-dj, 0)
        return np.where(good, row, 0), np.where(good, col, 0), good

    def positions(self):
        gl, gs = self.gl, self.gs
        x = np.arange(self.strip_l)
        rows, cols, goods = [], [], []
        for parity in range(2):
            m = 2 * ((x + gl) // (2 * gl)) if parity == 0 else 2 * (x // (2 * gl)) + 1
            t = x - gl * m
            r, c, g = self.place(gl - m, -t, gl)
            rows.append(r), cols.append(c), goods.append(g)
        large = [np.concatenate(v) for v in (rows, cols, goods)]
        x = np.arange(self.strip_s)
        m = x // (2 * gs)
        t = x - 2 * gs * m - gs
        small = [np.resize(np.zeros(1, v.dtype), self.line) for v in large]
        for dst, src in zip(small, self.place(gs - 1 - m, -t, gs)):
            dst[: self.strip_s] = src
        tail_r, tail_c, tail_g = np.zeros(128, int), np.zeros(128, int), np.zeros(128, bool)
        tail_r[:3], tail_c[:3], tail_g[:3] = (0, 1, 0), (1, 0, 0), True
        out = []
        for base in (large, small):
            out.append([np.concatenate(v) for v in zip(base, (tail_r, tail_c, tail_g))])
        return out

    def selectors(self):
        gs = self.gs
        rows = np.zeros((self.rows, self.pad_rows), np.float32)
        cols = np.zeros((self.pad_cols, self.rows), np.float32)
        for image in range(3):
            for tok in range(self.small_len):
                r = image * self.small_len + tok
                i, j = divmod(tok - 1, gs)
                rows[r, self.cls_row if tok == 0 else 16 * i + j] = 1
                cols[self.cls_col if tok == 0 else 2 * gs * i + j, r] = 1
        return jnp.asarray(rows, bf16), jnp.asarray(cols, bf16)


def pick_plan(plan):
    out = []
    for r, c, good in plan.positions():
        down = r > c
        down = np.where(good, (r - 1) // plan.gl >= (c - 1) // plan.gl, False)
        key = np.where(down, r, c)
        sub = np.where(down, c, r) - 1
        valid = good.copy()
        valid[plan.line :] = False
        out.append(np.stack([key, sub, down.astype(int), valid.astype(int)]))
    return jnp.asarray(np.concatenate(out), jnp.int32)


def read_labels(plan, is_large, idx_ref, pick_ref, lab_ref):
    size, gl = idx_ref.shape[0], plan.gl
    across = idx_ref[1 : 1 + gl, :]
    down = idx_ref[:, 1 : 1 + gl]
    digits = lambda v: [(v >> 6).astype(f32).astype(bf16), (v & 63).astype(f32).astype(bf16)]
    across, down = digits(across), digits(down)
    for chunk in range(plan.line // 128):
        lanes = slice(chunk * 128, (chunk + 1) * 128)
        key, sub, use_down, valid = [
            jnp.where(is_large, pick_ref[i : i + 1, lanes], pick_ref[4 + i : 5 + i, lanes])
            for i in range(4)
        ]
        hot = jnp.where(iota((size, 128), 0) == key, 1.0, 0.0).astype(bf16)
        here = iota((gl, 128), 0) == sub
        found = []
        for digit in range(2):
            rows = jnp.where(use_down == 1, mm(down[digit], hot, TN), mm(across[digit], hot))
            found.append(jnp.sum(jnp.where(here, rows, 0.0), axis=0, keepdims=True))
        label = (found[0] * 64.0 + found[1]).astype(jnp.int32)
        lab_ref[:, lanes] = jnp.where(valid == 1, label, -1)
    lane = iota((1, 128), 1)
    tail = jnp.where(lane == 0, idx_ref[0:1, 1:2], -1)
    tail = jnp.where(lane == 1, idx_ref[1:2, 0:1], tail)
    tail = jnp.where(lane == 2, idx_ref[0:1, 0:1], tail)
    lab_ref[:, plan.line : plan.line + 128] = tail


def iota(shape, dim):
    return lax.broadcasted_iota(jnp.int32, shape, dim)


def one_hot(lab_ref, chunk, buckets):
    lab = lab_ref[:, chunk * 128 : (chunk + 1) * 128]
    return jnp.where(iota((buckets, 128), 0) == lab, 1.0, 0.0).astype(bf16)


def row_roll(value, first, step, span):
    shape = value.shape
    out = pltpu.roll(value, first % span, axis=1) if first % span else value
    bit = 1
    while bit < shape[0]:
        moved = pltpu.roll(out, (step * bit) % span, axis=1)
        out = jnp.where((iota(shape, 0) & bit) != 0, moved, out)
        bit *= 2
    return out


def bias_large(plan, line_ref, h, out_ref):
    gl, rows, span = plan.gl, plan.rows, plan.strip_l
    f0 = jnp.broadcast_to(line_ref[h, :, 0:span], (gl, span))
    f1 = jnp.broadcast_to(line_ref[h, :, span : 2 * span], (gl, span))
    tail = line_ref[h, :, 2 * span : 2 * span + 128]
    r0 = row_roll(f0, -1, 1, span)
    r1 = row_roll(f1, -1, 1, span)
    odd = (iota((gl, span), 1) // gl) % 2
    odd = jnp.where(iota((gl, span), 0) == 0, 1 - odd, odd)
    strip = jnp.where(odd == 1, r1, r0)
    strip = jnp.concatenate([jnp.zeros((gl, 128), f32), strip, jnp.zeros((gl, 128), f32)], axis=1)
    wide = round_up(rows, 128)
    col = iota((2 * gl, wide), 1)
    bands = -(-rows // gl)
    for pair in range(-(-bands // 2)):
        parts = []
        for a in range(2 * pair, 2 * pair + 2):
            if a >= bands:
                parts.append(jnp.zeros((gl, wide), f32))
                continue
            move = 127 + gl * (gl - a)
            low = move // 128 * 128
            piece = strip[:, low : low + wide + 128]
            parts.append(pltpu.roll(piece, (wide + 128 - (move - low)) % (wide + 128), axis=1)[:, :wide])
        block = jnp.concatenate(parts, axis=0)
        row = iota((2 * gl, wide), 0) + 2 * gl * pair
        block = jnp.where(col == 0, tail[:, 1:2], block)
        if pair == 0:
            block = jnp.where(row == 0, jnp.where(col == 0, tail[:, 2:3], tail[:, 0:1]), block)
        block = jnp.where((row < plan.large_len) == (col < plan.large_len), block, neg_fill)
        block = jnp.where((row < plan.large_len) | (col < plan.large_len), block, 0.0)
        first = 2 * gl * pair
        count = min(2 * gl, rows - first)
        out_ref[0, first : first + count, :] = block[:count, :rows].astype(bf16)


def segment(plan, ids):
    n = plan.small_len
    return (
        jnp.where(ids >= n, 1, 0) + jnp.where(ids >= 2 * n, 1, 0) + jnp.where(ids >= 3 * n, 1, 0)
    )


def bias_small(plan, line_ref, rowsel_ref, colsel_ref, h, out_ref):
    gs, span, rows = plan.gs, plan.strip_s, plan.rows
    line = jnp.broadcast_to(line_ref[h, :, 0:span], (16, span))
    tail = line_ref[h, :, plan.line : plan.line + 128]
    strip = row_roll(line, -gs, 1, span)
    col = iota((16, plan.pad_cols), 1)
    row = iota((16, plan.pad_cols), 0)
    bands = []
    for i in range(gs):
        band = pltpu.roll(strip, (span - 2 * gs * (gs - 1 - i)) % span, axis=1)[:, : plan.pad_cols]
        band = jnp.where(col == plan.cls_col, tail[:, 1:2], band)
        if i == 0:
            edge = jnp.where(col == plan.cls_col, tail[:, 2:3], tail[:, 0:1])
            band = jnp.where(row == plan.cls_row, edge, band)
        bands.append(band)
    padded = jnp.concatenate(bands, axis=0).astype(bf16)
    cols = mm(padded, colsel_ref[...]).astype(bf16)
    full = mm(rowsel_ref[...], cols)
    same = segment(plan, iota((rows, rows), 0)) == segment(plan, iota((rows, rows), 1))
    out_ref[0] = jnp.where(same, full, neg_fill).astype(bf16)


def bias_kernel(
    plan, kind_ref, idx_ref, pick_ref, tab_ref, rowsel_ref, colsel_ref, out_ref, lab_ref, line_ref
):
    h = pl.program_id(0)

    @pl.when(h == 0)
    def _():
        read_labels(plan, kind_ref[0] == 1, idx_ref, pick_ref, lab_ref)
        for chunk in range(plan.lanes // 128):
            part = mm(tab_ref[...], one_hot(lab_ref, chunk, tab_ref.shape[1]))
            for i in range(line_ref.shape[0]):
                line_ref[i, :, chunk * 128 : (chunk + 1) * 128] = part[i : i + 1]

    @pl.when(kind_ref[0] == 1)
    def _():
        bias_large(plan, line_ref, h, out_ref)

    @pl.when(kind_ref[0] != 1)
    def _():
        bias_small(plan, line_ref, rowsel_ref, colsel_ref, h, out_ref)


def whole(shape):
    zeros = (0,) * len(shape)
    return pl.BlockSpec(shape, lambda i: zeros)


smem_spec = pl.BlockSpec(memory_space=pltpu.SMEM)
params = pltpu.CompilerParams(vmem_limit_bytes=vmem_bytes)


def pair_bias(plan, kind, large_index, table, rowsel, colsel):
    heads, buckets = table.shape
    heads = plan.heads
    rows = plan.rows
    picks = pick_plan(plan)
    return pl.pallas_call(
        functools.partial(bias_kernel, plan),
        grid=(heads,),
        in_specs=[
            smem_spec,
            whole(large_index.shape),
            whole(picks.shape),
            whole(table.shape),
            whole(rowsel.shape),
            whole(colsel.shape),
        ],
        out_specs=[pl.BlockSpec((1, rows, rows), lambda i: (i, 0, 0)), whole((1, plan.lanes))],
        out_shape=[
            jax.ShapeDtypeStruct((heads, rows, rows), bf16),
            jax.ShapeDtypeStruct((1, plan.lanes), jnp.int32),
        ],
        scratch_shapes=[pltpu.VMEM((16, 1, plan.lanes), f32)],
        compiler_params=params,
        name="pair_bias",
    )(kind, large_index, picks, table, rowsel, colsel)


def fold_large(plan, ds_ref, h, line_ref):
    gl, rows, span = plan.gl, plan.rows, plan.strip_l
    wide = round_up(rows, 128)
    total = jnp.zeros((gl, span + 256), f32)
    pieces = {}
    bands = -(-rows // gl)
    side = jnp.zeros((1, 1), f32)
    for pair in range(-(-bands // 2)):
        first = 2 * gl * pair
        count = min(2 * gl, rows - first)
        block = ds_ref[0, first : first + count, :].astype(f32)
        block = jnp.concatenate([block, jnp.zeros((count, wide - rows), f32)], axis=1)
        if count < 2 * gl:
            block = jnp.concatenate([block, jnp.zeros((2 * gl - count, wide), f32)], axis=0)
        shape = (2 * gl, wide)
        col = iota(shape, 1)
        if pair == 0:
            row = iota(shape, 0)
            corner = jnp.sum(jnp.where((row == 0) & (col == 0), block, 0.0), keepdims=True)
            top = jnp.sum(jnp.where((row == 0) & (col > 0), block, 0.0), keepdims=True)
            block = jnp.where(row == 0, 0.0, block)
        side = side + jnp.sum(block[:, 0:1], keepdims=True)
        block = jnp.where(col == 0, 0.0, block)
        for half in range(2):
            a = 2 * pair + half
            if a >= bands:
                continue
            move = 127 + gl * (gl - a)
            low = move // 128 * 128
            piece = block[half * gl : (half + 1) * gl]
            piece = jnp.concatenate([piece, jnp.zeros((gl, 128), f32)], axis=1)
            piece = pltpu.roll(piece, move - low, axis=1) if move > low else piece
            pieces[low] = piece if low not in pieces else pieces[low] + piece
    for low, piece in pieces.items():
        parts = [piece]
        if low:
            parts.insert(0, jnp.zeros((gl, low), f32))
        rest = span + 256 - low - wide - 128
        if rest > 0:
            parts.append(jnp.zeros((gl, rest), f32))
        total = total + jnp.concatenate(parts, axis=1)[:, : span + 256]
    strip = total[:, 128 : 128 + span]
    odd = (iota((gl, span), 1) // gl) % 2
    odd = jnp.where(iota((gl, span), 0) == 0, 1 - odd, odd)
    for parity in range(2):
        part = jnp.where(odd == parity, strip, 0.0)
        part = row_roll(part, 1, -1, span)
        line_ref[h, :, parity * span : (parity + 1) * span] = jnp.sum(
            part, axis=0, keepdims=True
        )
    store_tail(plan, line_ref, h, top, side, corner)


def store_tail(plan, line_ref, h, top, side, corner):
    lane = iota((1, 128), 1)
    tail = jnp.where(lane == 0, top, jnp.where(lane == 1, side, jnp.where(lane == 2, corner, 0.0)))
    line_ref[h, :, plan.line : plan.line + 128] = tail


def fold_small(plan, ds_ref, rowsel_ref, colsel_ref, h, line_ref):
    gs, span = plan.gs, plan.strip_s
    cols = mm(ds_ref[0], colsel_ref[...], NT).astype(bf16)
    padded = mm(rowsel_ref[...], cols, TN)
    row = iota((16, plan.pad_cols), 0)
    col = iota((16, plan.pad_cols), 1)
    total = jnp.zeros((16, span), f32)
    side = jnp.zeros((1, 1), f32)
    for i in range(gs):
        band = padded[16 * i : 16 * (i + 1)]
        if i == 0:
            is_top = row == plan.cls_row
            corner = jnp.sum(jnp.where(is_top & (col == plan.cls_col), band, 0.0), keepdims=True)
            top = jnp.sum(jnp.where(is_top & (col < plan.cls_col), band, 0.0), keepdims=True)
            band = jnp.where(is_top, 0.0, band)
        side = side + jnp.sum(jnp.where(col == plan.cls_col, band, 0.0), keepdims=True)
        band = jnp.where(col < plan.cls_col, band, 0.0)
        band = jnp.concatenate([band, jnp.zeros((16, span - plan.pad_cols), f32)], axis=1)
        move = 2 * gs * (gs - 1 - i)
        total = total + (pltpu.roll(band, move, axis=1) if move else band)
    total = row_roll(total, gs, -1, span)
    line_ref[h, :, 0 : plan.line] = jnp.zeros((1, plan.line), f32)
    line_ref[h, :, 0:span] = jnp.sum(total, axis=0, keepdims=True)
    store_tail(plan, line_ref, h, top, side, corner)


def fold_kernel(plan, kind_ref, ds_ref, lab_ref, rowsel_ref, colsel_ref, out_ref, line_ref):
    h = pl.program_id(0)

    @pl.when(h == 0)
    def _():
        line_ref[...] = jnp.zeros_like(line_ref)

    @pl.when(kind_ref[0] == 1)
    def _():
        fold_large(plan, ds_ref, h, line_ref)

    @pl.when(kind_ref[0] != 1)
    def _():
        fold_small(plan, ds_ref, rowsel_ref, colsel_ref, h, line_ref)

    @pl.when(h == pl.num_programs(0) - 1)
    def _():
        buckets = out_ref.shape[1]
        total = jnp.zeros(out_ref.shape, f32)
        for chunk in range(plan.lanes // 128):
            hot = one_hot(lab_ref, chunk, buckets)
            part = jnp.concatenate(
                [line_ref[i, :, chunk * 128 : (chunk + 1) * 128] for i in range(16)], axis=0
            )
            high = part.astype(bf16)
            low = (part - high.astype(f32)).astype(bf16)
            total = total + mm(high, hot, NT) + mm(low, hot, NT)
        out_ref[...] = total


def table_gradient(plan, kind, d_scores, labels, rowsel, colsel, buckets):
    heads, rows, _ = d_scores.shape
    return pl.pallas_call(
        functools.partial(fold_kernel, plan),
        grid=(heads,),
        in_specs=[
            smem_spec,
            pl.BlockSpec((1, rows, rows), lambda i: (i, 0, 0)),
            whole(labels.shape),
            whole(rowsel.shape),
            whole(colsel.shape),
        ],
        out_specs=whole((16, buckets)),
        out_shape=jax.ShapeDtypeStruct((16, buckets), f32),
        scratch_shapes=[pltpu.VMEM((16, 1, plan.lanes), f32)],
        compiler_params=params,
        name="table_gradient",
    )(kind, d_scores, labels, rowsel, colsel)


def norm_stats(values):
    mean = jnp.mean(values, axis=1, keepdims=True)
    centred = values - mean
    var = jnp.mean(centred * centred, axis=1, keepdims=True)
    inv = lax.rsqrt(var + norm_eps)
    return centred * inv, inv


def norm_back(d_out, gain, normal, inv):
    d_normal = d_out * gain
    mean_d = jnp.mean(d_normal, axis=1, keepdims=True)
    mean_dn = jnp.mean(d_normal * normal, axis=1, keepdims=True)
    return inv * (d_normal - mean_d - normal * mean_dn)


def rows_sum(values):
    return jnp.sum(values, axis=0, keepdims=True)


def gelu_parts(v):
    size = jnp.abs(v)
    bell = jnp.exp(-0.5 * v * v)
    t = 1.0 / (1.0 + (0.3275911 * 0.7071067811865476) * size)
    poly = t * (
        0.127414796
        + t * (-0.142248368 + t * (0.7107068705 + t * (-0.7265760135 + t * 0.5307027145)))
    )
    tail = poly * bell
    phi = jnp.where(v < 0, tail, 1.0 - tail)
    return v * phi, phi + v * bell * 0.3989422804014327


(
    FIRST_GAIN,
    FIRST_SHIFT,
    QUERY_BIAS,
    VALUE_BIAS,
    OUTPUT_BIAS,
    ATTEND_SCALE,
    SECOND_GAIN,
    SECOND_SHIFT,
    REDUCE_BIAS,
    FEED_SCALE,
) = range(10)


def vec(ref, idx):
    return ref[idx : idx + 1, :]


def project_kernel(tok_ref, vec_ref, w_ref, normed_ref, out_ref):
    part = pl.program_id(0)

    @pl.when(part == 0)
    def _():
        normal, _ = norm_stats(tok_ref[...].astype(f32))
        normed_ref[...] = (normal * vec(vec_ref, FIRST_GAIN) + vec(vec_ref, FIRST_SHIFT)).astype(
            bf16
        )

    bias = jnp.where(
        part == 0,
        vec(vec_ref, QUERY_BIAS),
        jnp.where(part == 2, vec(vec_ref, VALUE_BIAS), 0.0),
    )
    scale = jnp.where(part == 0, 0.125, 1.0)
    triple = mm(normed_ref[...], w_ref[...]) + bias
    out_ref[...] = (triple.astype(bf16).astype(f32) * scale).astype(bf16)


def project(tokens, vecs, weight):
    rows, width = tokens.shape
    return pl.pallas_call(
        project_kernel,
        grid=(3,),
        in_specs=[
            whole(tokens.shape),
            whole(vecs.shape),
            pl.BlockSpec((width, width), lambda i: (0, i)),
        ],
        out_specs=[whole(tokens.shape), pl.BlockSpec((rows, width), lambda i: (0, i))],
        out_shape=[
            jax.ShapeDtypeStruct((rows, width), bf16),
            jax.ShapeDtypeStruct((rows, 3 * width), bf16),
        ],
        compiler_params=params,
        name="project",
    )(tokens, vecs, weight)


def half_mask(rows):
    return iota((rows, 128), 1) < 64


def attend_kernel(q_ref, k_ref, v_ref, b_ref, mixed_ref, p_ref):
    q, k, v = q_ref[...], k_ref[...], v_ref[...]
    lower = half_mask(q.shape[0])
    mixed = []
    for t in range(2):
        keep = lower if t == 0 else ~lower
        scores = mm(jnp.where(keep, q, jnp.zeros_like(q)), k, NT) + b_ref[t].astype(f32)
        top = jnp.max(scores, axis=1, keepdims=True)
        exps = jnp.exp(scores - top)
        total = jnp.sum(exps, axis=1, keepdims=True)
        probs = (exps * (1.0 / total)).astype(bf16)
        p_ref[t] = probs
        mixed.append(mm(probs, v))
    mixed_ref[...] = jnp.where(lower, mixed[0], mixed[1]).astype(bf16)


def attend(triple, bias):
    rows = triple.shape[0]
    heads = bias.shape[0]
    pairs = heads // 2
    cols = lambda part: pl.BlockSpec((rows, 128), lambda i: (0, i + part * pairs))
    square = pl.BlockSpec((2, rows, rows), lambda i: (i, 0, 0))
    return pl.pallas_call(
        attend_kernel,
        grid=(pairs,),
        in_specs=[cols(0), cols(1), cols(2), square],
        out_specs=[cols(0), square],
        out_shape=[
            jax.ShapeDtypeStruct((rows, 64 * heads), bf16),
            jax.ShapeDtypeStruct((heads, rows, rows), bf16),
        ],
        compiler_params=params,
        name="attend",
    )(triple, triple, triple, bias)


def attend_back_kernel(q_ref, k_ref, v_ref, do_ref, m_ref, p_ref, dq_ref, dk_ref, dv_ref, ds_ref):
    q, k, v, do = q_ref[...], k_ref[...], v_ref[...], do_ref[...]
    lower = half_mask(q.shape[0])
    prod = do.astype(f32) * m_ref[...].astype(f32)
    dq, dk, dv = [], [], []
    for t in range(2):
        keep = lower if t == 0 else ~lower
        d_mixed = jnp.where(keep, do, jnp.zeros_like(do))
        delta = jnp.sum(jnp.where(keep, prod, 0.0), axis=1, keepdims=True)
        d_probs = mm(d_mixed, v, NT)
        probs = p_ref[t]
        d_scores = (probs.astype(f32) * (d_probs - delta)).astype(bf16)
        ds_ref[t] = d_scores
        dq.append(mm(d_scores, k))
        dk.append(mm(d_scores, q, TN))
        dv.append(mm(probs, do, TN))
    dq_ref[...] = (jnp.where(lower, dq[0], dq[1]) * 0.125).astype(bf16)
    dk_ref[...] = jnp.where(lower, dk[0], dk[1]).astype(bf16)
    dv_ref[...] = jnp.where(lower, dv[0], dv[1]).astype(bf16)


def attend_back(triple, d_mixed, mixed, probs):
    heads, rows, _ = probs.shape
    pairs = heads // 2
    cols = lambda part: pl.BlockSpec((rows, 128), lambda i: (0, i + part * pairs))
    square = pl.BlockSpec((2, rows, rows), lambda i: (i, 0, 0))
    wide = jax.ShapeDtypeStruct((rows, 64 * heads), bf16)
    return pl.pallas_call(
        attend_back_kernel,
        grid=(pairs,),
        in_specs=[cols(0), cols(1), cols(2), cols(0), cols(0), square],
        out_specs=[cols(0), cols(0), cols(0), square],
        out_shape=[wide, wide, wide, jax.ShapeDtypeStruct(probs.shape, bf16)],
        compiler_params=params,
        name="attend_back",
    )(triple, triple, triple, d_mixed, mixed, probs)


def feed_kernel(
    plan,
    kind_ref,
    tok_ref,
    cot_ref,
    mixed_ref,
    wo_ref,
    vec_ref,
    be_ref,
    we_ref,
    wr_ref,
    out_ref,
    dmid_ref,
    dmix_ref,
    dwo_ref,
    dwe_ref,
    dwr_ref,
    small_ref,
    dbe_ref,
    middle_ref,
    branch_ref,
    second_ref,
    dfeed_ref,
    feed_ref,
    dsec_ref,
):
    step = pl.program_id(0)
    rows = plan.rows

    def masked_cot():
        limit = jnp.where(kind_ref[0] == 1, plan.large_len, 3 * plan.small_len)
        live = iota((rows, 1), 0) < limit
        return jnp.where(live, cot_ref[...].astype(f32), 0.0)

    @pl.when(step == 0)
    def _():
        branch = mm(mixed_ref[...], wo_ref[...]) + vec(vec_ref, OUTPUT_BIAS)
        branch_ref[...] = branch
        middle = tok_ref[...].astype(f32) + vec(vec_ref, ATTEND_SCALE) * branch
        middle_ref[...] = middle
        normal, _ = norm_stats(middle)
        second_ref[...] = (
            normal * vec(vec_ref, SECOND_GAIN) + vec(vec_ref, SECOND_SHIFT)
        ).astype(bf16)
        dfeed_ref[...] = (vec(vec_ref, FEED_SCALE) * masked_cot()).astype(bf16)
        feed_ref[...] = jnp.zeros_like(feed_ref)
        dsec_ref[...] = jnp.zeros_like(dsec_ref)

    second, d_feed = second_ref[...], dfeed_ref[...]
    we, wr = we_ref[...], wr_ref[...]
    pre = mm(second, we) + be_ref[...]
    value, slope = gelu_parts(pre)
    activated = value.astype(bf16)
    feed_ref[...] += mm(activated, wr)
    d_pre = (mm(d_feed, wr, NT) * slope).astype(bf16)
    dsec_ref[...] += mm(d_pre, we, NT)
    dwr_ref[...] = mm(activated, d_feed, TN).astype(bf16)
    dwe_ref[...] = mm(second, d_pre, TN).astype(bf16)
    dbe_ref[...] = rows_sum(d_pre.astype(f32))

    @pl.when(step == pl.num_programs(0) - 1)
    def _():
        feed_out = feed_ref[...] + vec(vec_ref, REDUCE_BIAS)
        middle = middle_ref[...]
        out_ref[...] = (middle + vec(vec_ref, FEED_SCALE) * feed_out).astype(bf16)
        grad = masked_cot()
        d_second = dsec_ref[...]
        normal, inv = norm_stats(middle)
        d_middle = grad + norm_back(d_second, vec(vec_ref, SECOND_GAIN), normal, inv)
        dmid_ref[...] = d_middle
        d_branch = (vec(vec_ref, ATTEND_SCALE) * d_middle).astype(bf16)
        dwo_ref[...] = mm(mixed_ref[...], d_branch, TN).astype(bf16)
        dmix_ref[...] = mm(d_branch, wo_ref[...], NT).astype(bf16)
        small_ref[...] = jnp.zeros_like(small_ref)
        small_ref[FEED_SCALE : FEED_SCALE + 1, :] = rows_sum(grad * feed_out)
        small_ref[REDUCE_BIAS : REDUCE_BIAS + 1, :] = rows_sum(dfeed_ref[...].astype(f32))
        small_ref[SECOND_GAIN : SECOND_GAIN + 1, :] = rows_sum(d_second * normal)
        small_ref[SECOND_SHIFT : SECOND_SHIFT + 1, :] = rows_sum(d_second)
        small_ref[ATTEND_SCALE : ATTEND_SCALE + 1, :] = rows_sum(d_middle * branch_ref[...])
        small_ref[OUTPUT_BIAS : OUTPUT_BIAS + 1, :] = rows_sum(d_branch.astype(f32))


def feed(plan, kind, tokens, cot, mixed, wo, vecs, be, we, wr):
    rows, width = tokens.shape
    hidden = we.shape[1]
    tile = 512
    sds = jax.ShapeDtypeStruct
    return pl.pallas_call(
        functools.partial(feed_kernel, plan),
        grid=(hidden // tile,),
        in_specs=[
            smem_spec,
            whole(tokens.shape),
            whole(cot.shape),
            whole(mixed.shape),
            whole(wo.shape),
            whole(vecs.shape),
            pl.BlockSpec((1, tile), lambda i: (0, i)),
            pl.BlockSpec((width, tile), lambda i: (0, i)),
            pl.BlockSpec((tile, width), lambda i: (i, 0)),
        ],
        out_specs=[
            whole((rows, width)),
            whole((rows, width)),
            whole((rows, width)),
            whole((width, width)),
            pl.BlockSpec((width, tile), lambda i: (0, i)),
            pl.BlockSpec((tile, width), lambda i: (i, 0)),
            whole(vecs.shape),
            pl.BlockSpec((1, tile), lambda i: (0, i)),
        ],
        out_shape=[
            sds((rows, width), bf16),
            sds((rows, width), f32),
            sds((rows, width), bf16),
            sds((width, width), bf16),
            sds((width, hidden), bf16),
            sds((hidden, width), bf16),
            sds(vecs.shape, f32),
            sds((1, hidden), f32),
        ],
        scratch_shapes=[
            pltpu.VMEM((rows, width), f32),
            pltpu.VMEM((rows, width), f32),
            pltpu.VMEM((rows, width), bf16),
            pltpu.VMEM((rows, width), bf16),
            pltpu.VMEM((rows, width), f32),
            pltpu.VMEM((rows, width), f32),
        ],
        compiler_params=params,
        name="feed",
    )(kind, tokens, cot, mixed, wo, vecs, be, we, wr)


def finish_kernel(
    tok_ref,
    dmid_ref,
    normed_ref,
    vec_ref,
    dq_ref,
    dk_ref,
    dv_ref,
    w_ref,
    dw_ref,
    out_ref,
    small_ref,
    acc_ref,
):
    part = pl.program_id(0)

    @pl.when(part == 0)
    def _():
        acc_ref[...] = jnp.zeros_like(acc_ref)
        small_ref[...] = jnp.zeros_like(small_ref)

    d_part = jnp.where(part == 0, dq_ref[...], jnp.where(part == 1, dk_ref[...], dv_ref[...]))
    dw_ref[...] = mm(normed_ref[...], d_part, TN).astype(bf16)
    acc_ref[...] += mm(d_part, w_ref[...], NT)
    sums = rows_sum(d_part.astype(f32))

    @pl.when(part == 0)
    def _():
        small_ref[QUERY_BIAS : QUERY_BIAS + 1, :] = sums

    @pl.when(part == 2)
    def _():
        small_ref[VALUE_BIAS : VALUE_BIAS + 1, :] = sums
        d_normed = acc_ref[...]
        normal, inv = norm_stats(tok_ref[...].astype(f32))
        back = norm_back(d_normed, vec(vec_ref, FIRST_GAIN), normal, inv)
        out_ref[...] = (dmid_ref[...] + back).astype(bf16)
        small_ref[FIRST_GAIN : FIRST_GAIN + 1, :] = rows_sum(d_normed * normal)
        small_ref[FIRST_SHIFT : FIRST_SHIFT + 1, :] = rows_sum(d_normed)


def finish(tokens, d_middle, normed, vecs, d_triple, weight):
    rows, width = tokens.shape
    sds = jax.ShapeDtypeStruct
    return pl.pallas_call(
        finish_kernel,
        grid=(3,),
        in_specs=[
            whole(tokens.shape),
            whole(d_middle.shape),
            whole(normed.shape),
            whole(vecs.shape),
            whole(tokens.shape),
            whole(tokens.shape),
            whole(tokens.shape),
            pl.BlockSpec((width, width), lambda i: (0, i)),
        ],
        out_specs=[
            pl.BlockSpec((width, width), lambda i: (0, i)),
            whole(tokens.shape),
            whole(vecs.shape),
        ],
        out_shape=[
            sds(weight.shape, bf16),
            sds(tokens.shape, bf16),
            sds(vecs.shape, f32),
        ],
        scratch_shapes=[pltpu.VMEM((rows, width), f32)],
        compiler_params=params,
        name="finish",
    )(tokens, d_middle, normed, vecs, *d_triple, weight)


class Spot:
    def __init__(self, n):
        self.n, self.levels = n, n // 2
        self.rep, self.f = lax.axis_index("rep"), lax.axis_index("fsdp")
        self.half, self.core = self.rep // 2, self.rep % 2
        self.level, self.side = self.f // 2, self.f % 2

    def at(self, rep=None, f=None):
        return {"rep": self.rep if rep is None else rep, "fsdp": self.f if f is None else f}

    def sibling(self):
        return self.at(rep=2 * self.half + 1 - self.core)

    def across(self):
        return self.at(rep=2 * (1 - self.half) + self.core)

    def beside(self):
        return self.at(f=2 * self.level + 1 - self.side)

    def along(self, step):
        return self.at(f=2 * ((self.level + step) % self.levels) + self.side)

    def from_along(self, step, side=None):
        side = self.side if side is None else side
        return 2 * ((self.level + self.levels - step) % self.levels) + side


MESH = pl.DeviceIdType.MESH


def greet(devices, count):
    barrier = pltpu.get_barrier_semaphore()
    for device in devices:
        pl.semaphore_signal(barrier, inc=1, device_id=device, device_id_type=MESH)
    pl.semaphore_wait(barrier, count)


def send(src, dst, send_sem, recv_sem, device):
    return pltpu.make_async_remote_copy(
        src_ref=src,
        dst_ref=dst,
        send_sem=send_sem,
        recv_sem=recv_sem,
        device_id=device,
        device_id_type=MESH,
    )


def fast_shape(reps, n, shard_rows):
    return reps == 4 and n % 2 == 0 and n > 2 and all(rows % 96 == 0 for rows in shard_rows)


class Gather:
    def __init__(self, spot, shard, whole_ref, send_sems, recv_sems, local_sem):
        self.spot, self.shard, self.whole = spot, shard, whole_ref
        self.ss, self.rs = send_sems, recv_sems
        self.part = shard.shape[0] // 2
        self.third = self.part // 3
        base = spot.core * self.part
        self.plane = pl.ds(base + spot.half * self.third, 2 * self.third)
        self.mine = pl.ds(base + spot.half * 2 * self.third, self.third)
        self.core_rows = pl.ds(base, self.part)
        self.local = pltpu.make_async_copy(shard, whole_ref.at[spot.f], local_sem)
        levels = spot.levels
        self.zs, self.ys, self.xs, self.cs = [], [], [], []
        idx = 0
        for step in range(1, levels):
            self.zs.append(self.copy(shard.at[self.plane], self.plane, spot.f, idx, spot.along(step)))
            idx += 1
        for step in range(levels):
            f = spot.from_along(step)
            src = shard.at[self.plane] if step == 0 else whole_ref.at[f, self.plane]
            self.ys.append(self.copy(src, self.plane, f, idx, spot.beside()))
            idx += 1
        arrivals = [spot.from_along(step) for step in range(1, levels)]
        arrivals += [spot.from_along(step, 1 - spot.side) for step in range(levels)]
        for f in arrivals:
            self.xs.append(self.copy(whole_ref.at[f, self.mine], self.mine, f, idx, spot.across()))
            idx += 1
        for f in arrivals:
            rows = self.core_rows
            self.cs.append(self.copy(whole_ref.at[f, rows], rows, f, idx, spot.sibling()))
            idx += 1

    @staticmethod
    def count(n):
        return n // 2 - 1 + n // 2 + 2 * (n - 1)

    def copy(self, src, rows, f, idx, device):
        return send(src, self.whole.at[f, rows], self.ss.at[idx], self.rs.at[idx], device)

    def start(self):
        self.local.start()
        for copy in self.zs:
            copy.start()
        self.ys[0].start()

    def step_z(self, k):
        self.zs[k].wait_recv()
        self.ys[k + 1].start()
        self.xs[k].start()

    def step_y(self, k):
        self.ys[k].wait_recv()
        self.xs[len(self.zs) + k].start()

    def step_x(self, k):
        self.xs[k].wait_recv()
        self.cs[k].start()

    def step_c(self, k):
        self.cs[k].wait_recv()

    def finish(self):
        self.local.wait()
        for copy in self.zs + self.ys + self.xs + self.cs:
            copy.wait_send()


def spread_block(refs, block_ref):
    *vectors, be_ref, table_ref = refs
    share, heads = table_ref.shape
    eye = jnp.where(iota((16, heads), 0) == iota((16, heads), 1), 1.0, 0.0).astype(bf16)
    lanes = block_ref.shape[1]
    table = mm(eye, table_ref[...], NT)
    width = vectors[0].shape[1]
    rows = [v[...].astype(f32) for v in vectors]
    rows.append(jnp.zeros((16 - len(rows), width), f32))
    block = jnp.concatenate(
        [table, jnp.zeros((16, lanes - share - width), f32), jnp.concatenate(rows, axis=0)], axis=1
    )
    wide = jnp.broadcast_to(be_ref[...].astype(f32), (16, lanes))
    block_ref[...] = jnp.where(iota((16, lanes), 0) == heads, wide, block).astype(bf16)


def gather_kernel(n, heads, *refs):
    shorts, (wt, wo, we, wr), outs = refs[:12], refs[12:16], refs[16:23]
    wholes, (vec_ref, be_ref, tab_ref) = outs[:4], outs[4:]
    block, blocks, ss, rs, local, bss, brs = refs[23:]
    spot = Spot(n)
    peers = [spot.at(f=(spot.f + k) % n) for k in range(1, n)]
    greet(peers + [spot.sibling(), spot.across()], n + 1)
    spread_block(shorts, block)
    small = []
    for k, peer in enumerate(peers):
        small.append(send(block, blocks.at[spot.f], bss.at[k], brs.at[k], peer))
        small[k].start()
    blocks[spot.f] = block[...]
    jobs = []
    for i, (shard, out) in enumerate(zip((wt, wo, we, wr), wholes)):
        jobs.append(Gather(spot, shard, out, ss.at[i], rs.at[i], local.at[i]))
    for job in jobs:
        job.start()
    for job in jobs:
        for k in range(len(job.zs)):
            job.step_z(k)
        for k in range(len(job.ys)):
            job.step_y(k)
    for job in jobs:
        for k in range(len(job.xs)):
            job.step_x(k)
    for copy in small:
        copy.wait()
    share = shorts[0].shape[1]
    bshare = shorts[11].shape[0]
    for f in range(n):
        part = blocks[f].astype(f32)
        wide = part.shape[1]
        vec_ref[:, f * share : (f + 1) * share] = part[:, wide - share :]
        tab_ref[:, f * bshare : (f + 1) * bshare] = part[:, :bshare]
        be_ref[:, f * wide : (f + 1) * wide] = part[heads : heads + 1, :]
    for job in jobs:
        for k in range(len(job.cs)):
            job.step_c(k)
    for job in jobs:
        job.finish()


any_spec = pl.BlockSpec(memory_space=pl.ANY)
vmem_spec = pl.BlockSpec(memory_space=pltpu.VMEM)


def gather_all(shorts, shards, n):
    sds = jax.ShapeDtypeStruct
    share, wide = shorts[0].shape[1], shorts[10].shape[1]
    bshare, heads = shorts[11].shape
    count = Gather.count(n)
    outs = pl.pallas_call(
        functools.partial(gather_kernel, n, heads),
        in_specs=[vmem_spec] * 12 + [any_spec] * 4,
        out_specs=[any_spec] * 4 + [vmem_spec] * 3,
        out_shape=[sds((n,) + w.shape, bf16) for w in shards]
        + [sds((16, n * share), f32), sds((1, n * wide), f32), sds((16, n * bshare), f32)],
        scratch_shapes=[
            pltpu.VMEM((16, wide), bf16),
            pltpu.VMEM((n, 16, wide), bf16),
            pltpu.SemaphoreType.DMA((4, count)),
            pltpu.SemaphoreType.DMA((4, count)),
            pltpu.SemaphoreType.DMA((4,)),
            pltpu.SemaphoreType.DMA((n - 1,)),
            pltpu.SemaphoreType.DMA((n - 1,)),
        ],
        compiler_params=pltpu.CompilerParams(
            collective_id=1, has_side_effects=True, vmem_limit_bytes=vmem_bytes
        ),
        name="gather_all",
    )(*shorts, *shards)
    wholes = [w.reshape(-1, w.shape[2]) for w in outs[:4]]
    return wholes, outs[4], outs[5], outs[6].astype(bf16)


class Reduce:
    def __init__(self, spot, grad, out, bufs, send_sems, recv_sems, local_sem):
        self.spot, self.out, self.bufs = spot, out, bufs
        own, got_c, got_x, got_y, got_z, total, got_f = bufs
        self.part = part = own.shape[2]
        self.third = q = part // 3
        half, core, side, level, levels = spot.half, spot.core, spot.side, spot.level, spot.levels
        rows = lambda start, size: pl.ds(pl.multiple_of(start, 16), size)
        self.plane = rows(half * q, 2 * q)
        self.mine = rows(half * 2 * q, q)
        self.core_rows = rows(core * part, part)

        def copy(idx, src, dst, device):
            return send(src, dst, send_sems.at[idx], recv_sems.at[idx], device)

        self.load = pltpu.make_async_copy(grad.at[:, :, self.core_rows], own, local_sem)
        other = rows((1 - core) * part, part)
        self.c = copy(0, grad.at[:, :, other], got_c, spot.sibling())
        self.x = copy(1, own.at[:, :, rows((1 - half) * 2 * q, q)], got_x, spot.across())
        self.y = copy(2, own.at[:, 1 - side, self.plane], got_y, spot.beside())
        self.z = []
        for step in range(1, levels):
            src = own.at[(level + step) % levels, side, self.plane]
            self.z.append(copy(4 + step, src, got_z.at[step - 1], spot.along(step)))
        self.f = copy(3, total, got_f, spot.across())
        self.last = copy(4, out.at[self.core_rows], out.at[self.core_rows], spot.sibling())

    @staticmethod
    def count(n):
        return 4 + n // 2

    @staticmethod
    def buffers(n, shard_rows, cols):
        part, levels = shard_rows // 2, n // 2
        q = part // 3
        shapes = [
            (levels, 2, part, cols),
            (levels, 2, part, cols),
            (levels, 2, q, cols),
            (levels, 2 * q, cols),
            (levels - 1, 2 * q, cols),
            (2 * q, cols),
            (2 * q, cols),
        ]
        return [pltpu.VMEM(shape, bf16) for shape in shapes]

    def start(self):
        self.load.start()
        self.c.start()

    def step_c(self):
        own, got = self.bufs[0], self.bufs[1]
        self.load.wait()
        self.c.wait_recv()

        @pl.loop(0, own.shape[0])
        def _(level):
            for side in range(2):
                own[level, side] = add16(own[level, side], got[level, side])

        self.x.start()

    def step_x(self):
        own, got = self.bufs[0], self.bufs[2]
        self.x.wait_recv()

        @pl.loop(0, own.shape[0])
        def _(level):
            for side in range(2):
                own[level, side, self.mine] = add16(own[level, side, self.mine], got[level, side])

        self.y.start()

    def step_y(self):
        own, got = self.bufs[0], self.bufs[3]
        side = self.spot.side
        self.y.wait_recv()

        @pl.loop(0, own.shape[0])
        def _(level):
            own[level, side, self.plane] = add16(own[level, side, self.plane], got[level])

        for copy in self.z:
            copy.start()

    def step_z(self):
        own, got, total = self.bufs[0], self.bufs[4], self.bufs[5]
        for copy in self.z:
            copy.wait_recv()
        value = own[self.spot.level, self.spot.side, self.plane].astype(f32)
        for k in range(len(self.z)):
            value = value + got[k].astype(f32)
        total[...] = value.astype(bf16)
        self.f.start()

    def step_f(self):
        total, got, out = self.bufs[5], self.bufs[6], self.out
        q, half = self.third, self.spot.half
        base = self.spot.core * self.part
        rows = lambda start: pl.ds(pl.multiple_of(start, 16), q)
        self.f.wait_recv()
        out[rows(base + half * 2 * q)] = total[rows(half * q)]
        out[rows(base + q)] = add16(total[rows((1 - half) * q)], got[rows(half * q)])
        out[rows(base + (1 - half) * 2 * q)] = got[rows((1 - half) * q)]
        self.last.start()

    def finish(self):
        self.last.wait_recv()
        for copy in [self.c, self.x, self.y, self.f, self.last] + self.z:
            copy.wait_send()


def add16(left, right):
    return (left.astype(f32) + right.astype(f32)).astype(bf16)


def reduce_kernel(n, *refs):
    grads, (vec_ref, be_ref, tab_ref) = refs[:4], refs[4:7]
    outs, small_out = refs[7:11], refs[11]
    bufs = [refs[12 + 7 * i : 19 + 7 * i] for i in range(4)]
    block, got, reps, ss, rs, local, bss, brs = refs[40:]
    spot = Spot(n)
    peers = [spot.at(f=(spot.f + k) % n) for k in range(1, n)]
    others = [spot.at(rep=(spot.rep + k) % 4) for k in range(1, 4)]
    greet(peers + others, n + 2)
    jobs = []
    for i in range(4):
        jobs.append(Reduce(spot, grads[i], outs[i], bufs[i], ss.at[i], rs.at[i], local.at[i]))
    for job in jobs:
        job.start()
    share, bshare = vec_ref.shape[1] // n, tab_ref.shape[1] // n
    wide = be_ref.shape[1] // n
    heads = 12
    for f in range(n):
        value = jnp.concatenate(
            [
                tab_ref[:, f * bshare : (f + 1) * bshare],
                jnp.zeros((16, wide - bshare - share), f32),
                vec_ref[:, f * share : (f + 1) * share],
            ],
            axis=1,
        )
        bias = jnp.broadcast_to(be_ref[:, f * wide : (f + 1) * wide], (16, wide))
        block[f] = jnp.where(iota((16, wide), 0) == heads, bias, value)
    small = []
    for k, peer in enumerate(peers):
        dst = (spot.f + k + 1) % n
        small.append(send(block.at[dst], got.at[k], bss.at[k], brs.at[k], peer))
        small[k].start()
    steps = ["step_c", "step_x", "step_y", "step_z", "step_f", "finish"]
    second = []
    for slot in range(len(jobs) + len(steps) - 1):
        for i, job in enumerate(jobs):
            if 0 <= slot - i < len(steps):
                getattr(job, steps[slot - i])()
        if slot == 1:
            value = block[spot.f]
            for k, copy in enumerate(small):
                copy.wait_recv()
                value = value + got[k]
            reps[spot.rep] = value
            for k, other in enumerate(others):
                mine = reps.at[spot.rep]
                second.append(send(mine, mine, bss.at[n - 1 + k], brs.at[n - 1 + k], other))
                second[k].start()
        if slot == 3:
            for copy in second:
                copy.wait_recv()
            small_out[...] = (reps[0] + reps[1]) + (reps[2] + reps[3])
    for copy in small + second:
        copy.wait_send()


def reduce_all(grads, vec_sums, be_sums, table_sums, n):
    sds = jax.ShapeDtypeStruct
    grads = [g.reshape(n // 2, 2, g.shape[0] // n, g.shape[1]) for g in grads]
    wide = be_sums.shape[1] // n
    scratch = []
    for g in grads:
        scratch += Reduce.buffers(n, g.shape[2], g.shape[3])
    count = Reduce.count(n)
    outs = pl.pallas_call(
        functools.partial(reduce_kernel, n),
        in_specs=[any_spec] * 4 + [vmem_spec] * 3,
        out_specs=[vmem_spec] * 5,
        out_shape=[sds(g.shape[2:], bf16) for g in grads] + [sds((16, wide), f32)],
        scratch_shapes=scratch
        + [
            pltpu.VMEM((n, 16, wide), f32),
            pltpu.VMEM((n - 1, 16, wide), f32),
            pltpu.VMEM((4, 16, wide), f32),
            pltpu.SemaphoreType.DMA((4, count)),
            pltpu.SemaphoreType.DMA((4, count)),
            pltpu.SemaphoreType.DMA((4,)),
            pltpu.SemaphoreType.DMA((n + 2,)),
            pltpu.SemaphoreType.DMA((n + 2,)),
        ],
        compiler_params=pltpu.CompilerParams(
            collective_id=2, has_side_effects=True, vmem_limit_bytes=vmem_bytes
        ),
        name="reduce_all",
    )(*grads, vec_sums, be_sums, table_sums)
    return outs[:4], outs[4]


def gather_plain(shorts, shards, n):
    gather = lambda value, axis: lax.all_gather(value, "fsdp", axis=axis, tiled=True)
    vecs = gather(jnp.concatenate(shorts[:10], axis=0), 1).astype(f32)
    vecs = jnp.pad(vecs, ((0, 6), (0, 0)))
    table = gather(shorts[11], 0).T
    table = jnp.pad(table, ((0, 16 - table.shape[0]), (0, 0)))
    return [gather(w, 0) for w in shards], vecs, gather(shorts[10], 1).astype(f32), table


def reduce_plain(grads, vec_sums, be_sums, table_sums, n):
    def whole_sum(value):
        value = lax.psum_scatter(value, "fsdp", scatter_dimension=0, tiled=True)
        return lax.psum(value, "rep")

    sums = lax.psum((vec_sums, be_sums, table_sums), ("rep", "fsdp"))
    me = lax.axis_index("fsdp")
    cut = lambda v: lax.dynamic_slice_in_dim(v, me * (v.shape[1] // n), v.shape[1] // n, axis=1)
    vec_part, be_part, table_part = [cut(v) for v in sums]
    wide = be_part.shape[1]
    space = max(wide - vec_part.shape[1] - table_part.shape[1], 0)
    body = jnp.concatenate([table_part, jnp.zeros((16, space), f32), vec_part], axis=1)
    block = jnp.where(jnp.arange(16)[:, None] == 12, jnp.pad(be_part, ((0, 0), (0, body.shape[1] - wide))), body)
    return [whole_sum(g) for g in grads], block


def per_device(
    tokens,
    slot_kinds,
    small_index,
    large_index,
    first_gain,
    first_shift,
    triple_weight,
    query_bias,
    value_bias,
    bias_table,
    output_weight,
    output_bias,
    attend_scale,
    second_gain,
    second_shift,
    expand_weight,
    expand_bias,
    reduce_weight,
    reduce_bias,
    feed_scale,
    cotangent,
):
    _, rows, width = tokens.shape
    heads = bias_table.shape[2]
    plan = Plan(small_index.shape[0], large_index.shape[0], rows, heads)
    tokens, cotangent = tokens[0], cotangent[0]
    short = [
        first_gain,
        first_shift,
        query_bias,
        value_bias,
        output_bias,
        attend_scale,
        second_gain,
        second_shift,
        reduce_bias,
        feed_scale,
    ]
    n = width // first_gain.shape[1]
    fast = fast_shape(
        lax.axis_size("rep"), n, [w.shape[1] for w in (triple_weight, output_weight, reduce_weight)]
    )
    gathered = gather_all if fast else gather_plain
    shards = [w[0] for w in (triple_weight, output_weight, expand_weight, reduce_weight)]
    (wt, wo, we, wr), vecs, be, table = gathered(short + [expand_bias, bias_table[0]], shards, n)

    rowsel, colsel = plan.selectors()
    bias, labels = pair_bias(plan, slot_kinds, large_index, table, rowsel, colsel)

    normed, triple = project(tokens, vecs, wt)
    mixed, probs = attend(triple, bias)
    block_output, d_middle, d_mixed, dwo, dwe, dwr, small_a, dbe = feed(
        plan, slot_kinds, tokens, cotangent, mixed, wo, vecs, be, we, wr
    )
    dq, dk, dv, d_scores = attend_back(triple, d_mixed, mixed, probs)
    d_table = table_gradient(plan, slot_kinds, d_scores, labels, rowsel, colsel, table.shape[1])
    dwt, token_grad, small_b = finish(
        tokens, d_middle, normed, vecs, (dq, dk, dv), wt
    )

    reduced = reduce_all if fast else reduce_plain
    (dwr, dwe, dwo, dwt), block = reduced((dwr, dwe, dwo, dwt), small_a + small_b, dbe, d_table, n)
    share, bshare = first_gain.shape[1], bias_table.shape[1]
    row = lambda idx: block[idx : idx + 1, block.shape[1] - share :]
    full = lambda value: value.astype(f32)[None]
    return (
        block_output[None],
        token_grad[None],
        row(FIRST_GAIN),
        row(FIRST_SHIFT),
        full(dwt),
        row(QUERY_BIAS),
        row(VALUE_BIAS),
        block[:heads, :bshare].T[None],
        full(dwo),
        row(OUTPUT_BIAS),
        row(ATTEND_SCALE),
        row(SECOND_GAIN),
        row(SECOND_SHIFT),
        full(dwe),
        block[heads : heads + 1],
        full(dwr),
        row(REDUCE_BIAS),
        row(FEED_SCALE),
    )


def solution(mesh):
    rows = P(("rep", "fsdp"), None, None)
    vector = P(None, "fsdp")
    matrix = P(None, "fsdp", None)
    weights = (
        vector,
        vector,
        matrix,
        vector,
        vector,
        matrix,
        matrix,
        vector,
        vector,
        vector,
        vector,
        matrix,
        vector,
        matrix,
        vector,
        vector,
    )
    return jax.shard_map(
        per_device,
        mesh=mesh,
        in_specs=(rows, P(("rep", "fsdp")), P(), P()) + weights + (rows,),
        out_specs=(rows, rows) + weights,
        check_vma=False,
    )
```

```python
import functools

import jax
import jax.numpy as jnp
import numpy as np
from jax import lax
from jax.experimental import pallas as pl
from jax.experimental.pallas import tpu as pltpu
from jax.sharding import PartitionSpec as P

f32 = jnp.float32
bf16 = jnp.bfloat16
norm_eps = 1e-06
neg_fill = -1000000000.0
vmem_bytes = 60 << 20

NN = (((1,), (0,)), ((), ()))
NT = (((1,), (1,)), ((), ()))
TN = (((0,), (0,)), ((), ()))


def mm(left, right, dims=NN):
    return lax.dot_general(left, right, dims, preferred_element_type=f32)


def round_up(value, unit):
    return -(-value // unit) * unit


class Plan:
    def __init__(self, small_len, large_len, rows, heads, buckets):
        self.heads, self.buckets = heads, buckets
        self.rows = rows
        self.small_len, self.large_len = small_len, large_len
        self.gs = int(round((small_len - 1) ** 0.5))
        self.gl = int(round((large_len - 1) ** 0.5))
        gl, gs = self.gl, self.gs
        self.strip_l = round_up(2 * gl * gl, 128)
        self.strip_s = round_up(2 * gs * (2 * gs - 1) + gs, 128)
        self.line = 2 * self.strip_l
        self.lanes = self.line + 128
        self.pad_cols = round_up(2 * gs * gs + 1, 128)
        self.pad_rows = 16 * gs
        self.cls_col = 2 * gs * gs
        self.cls_row = gs

    def place(self, di, dj, limit):
        gl = self.gl
        good = (np.abs(di) < limit) & (np.abs(dj) < limit)
        row = 1 + gl * np.maximum(di, 0) + np.maximum(dj, 0)
        col = 1 + gl * np.maximum(-di, 0) + np.maximum(-dj, 0)
        return np.where(good, row, 0), np.where(good, col, 0), good

    def positions(self):
        gl, gs = self.gl, self.gs
        x = np.arange(self.strip_l)
        rows, cols, goods = [], [], []
        for parity in range(2):
            m = 2 * ((x + gl) // (2 * gl)) if parity == 0 else 2 * (x // (2 * gl)) + 1
            t = x - gl * m
            r, c, g = self.place(gl - m, -t, gl)
            rows.append(r), cols.append(c), goods.append(g)
        large = [np.concatenate(v) for v in (rows, cols, goods)]
        x = np.arange(self.strip_s)
        m = x // (2 * gs)
        t = x - 2 * gs * m - gs
        small = [np.resize(np.zeros(1, v.dtype), self.line) for v in large]
        for dst, src in zip(small, self.place(gs - 1 - m, -t, gs)):
            dst[: self.strip_s] = src
        tail_r, tail_c, tail_g = np.zeros(128, int), np.zeros(128, int), np.zeros(128, bool)
        tail_r[:3], tail_c[:3], tail_g[:3] = (0, 1, 0), (1, 0, 0), True
        out = []
        for base in (large, small):
            out.append([np.concatenate(v) for v in zip(base, (tail_r, tail_c, tail_g))])
        return out

    def selector_arrays(self):
        gs = self.gs
        rows = np.zeros((self.rows, self.pad_rows), np.float32)
        cols = np.zeros((self.pad_cols, self.rows), np.float32)
        for image in range(3):
            for tok in range(self.small_len):
                r = image * self.small_len + tok
                i, j = divmod(tok - 1, gs)
                rows[r, self.cls_row if tok == 0 else 16 * i + j] = 1
                cols[self.cls_col if tok == 0 else 2 * gs * i + j, r] = 1
        return rows, cols

    def selectors(self):
        rows, cols = self.selector_arrays()
        return jnp.asarray(rows, bf16), jnp.asarray(cols, bf16)


def iota(shape, dim):
    return lax.broadcasted_iota(jnp.int32, shape, dim)


def pick_plan(plan):
    out = []
    for r, c, good in plan.positions():
        down = good & ((r - 1) // plan.gl >= (c - 1) // plan.gl)
        key = np.where(down, r, c)
        sub = np.where(down, c, r) - 1
        valid = good.copy()
        valid[plan.line :] = False
        out.append(np.stack([key, sub, down.astype(int), valid.astype(int)]))
    return jnp.asarray(np.concatenate(out), jnp.int32)


def read_labels(plan, is_large, idx_ref, pick_ref, lab_ref):
    size, gl = idx_ref.shape[0], plan.gl
    across = idx_ref[1 : 1 + gl, :]
    down = idx_ref[:, 1 : 1 + gl].astype(f32).T.astype(jnp.int32)
    sides = []
    for v in (across, down):
        sides += [(v >> 6).astype(f32), (v & 63).astype(f32)]
    sides = jnp.concatenate(sides, axis=0).astype(bf16)
    for chunk in range(plan.line // 128):
        lanes = slice(chunk * 128, (chunk + 1) * 128)
        key, sub, use_down, valid = [
            jnp.where(is_large, pick_ref[i : i + 1, lanes], pick_ref[4 + i : 5 + i, lanes])
            for i in range(4)
        ]
        hot = jnp.where(iota((size, 128), 0) == key, 1.0, 0.0).astype(bf16)
        here = iota((gl, 128), 0) == sub
        rows = mm(sides, hot)
        for digit in range(2):
            a = rows[digit * gl : (digit + 1) * gl]
            b = rows[(2 + digit) * gl : (3 + digit) * gl]
            found = jnp.where(here, jnp.where(use_down == 1, b, a), 0.0)
            found = jnp.sum(found, axis=0, keepdims=True).astype(jnp.int32)
            lab_ref[digit : digit + 1, lanes] = jnp.where(valid == 1, found, -1)
    lane = iota((1, 128), 1)
    tail = jnp.where(lane == 0, idx_ref[0:1, 1:2], -1)
    tail = jnp.where(lane == 1, idx_ref[1:2, 0:1], tail)
    tail = jnp.where(lane == 2, idx_ref[0:1, 0:1], tail)
    lab_ref[0:1, plan.line : plan.line + 128] = jnp.where(tail < 0, -1, tail >> 6)
    lab_ref[1:2, plan.line : plan.line + 128] = jnp.where(tail < 0, -1, tail & 63)


def table_lines(plan, tab, lab_ref, line_ref):
    count = tab.shape[1] // 64
    split = jnp.concatenate([tab[:, 64 * i : 64 * (i + 1)] for i in range(count)], axis=0)
    split = split.astype(bf16)
    for chunk in range(plan.lanes // 128):
        lanes = slice(chunk * 128, (chunk + 1) * 128)
        first, second = lab_ref[0:1, lanes], lab_ref[1:2, lanes]
        hot = jnp.where(iota((64, 128), 0) == second, 1.0, 0.0).astype(bf16)
        rows = mm(split, hot)
        line = jnp.zeros((16, 128), f32)
        for i in range(count):
            line = jnp.where(first == i, rows[16 * i : 16 * (i + 1)], line)
        for i in range(plan.heads):
            line_ref[i, :, lanes] = line[i : i + 1]


def table_from_lines(plan, line_of, lab_ref, buckets):
    count = buckets // 64
    total = jnp.zeros((32 * count, 64), f32)
    for chunk in range(plan.lanes // 128):
        lanes = slice(chunk * 128, (chunk + 1) * 128)
        first, second = lab_ref[0:1, lanes], lab_ref[1:2, lanes]
        hot = jnp.where(iota((64, 128), 0) == second, 1.0, 0.0).astype(bf16)
        part = line_of(chunk)
        high = part.astype(bf16)
        low = (part - high.astype(f32)).astype(bf16)
        both = jnp.concatenate([high, low], axis=0)
        stack = [jnp.where(first == i, both, jnp.zeros_like(both)) for i in range(count)]
        total = total + mm(jnp.concatenate(stack, axis=0), hot, NT)
    pieces = []
    for i in range(count):
        pieces.append(total[32 * i : 32 * i + 16] + total[32 * i + 16 : 32 * i + 32])
    return jnp.concatenate(pieces, axis=1)


def segments(plan, is_large, ids):
    n = plan.small_len
    small = jnp.where(ids >= n, 1, 0) + jnp.where(ids >= 2 * n, 1, 0) + jnp.where(ids >= 3 * n, 1, 0)
    return jnp.where(is_large, jnp.where(ids < plan.large_len, 0, 3), small)


def large_strip(plan, line_ref, h):
    gl, span = plan.gl, plan.strip_l
    rolled = []
    for parity in range(2):
        line = jnp.broadcast_to(line_ref[h, :, parity * span : (parity + 1) * span], (gl, span))
        rolled.append(pltpu.roll(line, 0, axis=1, stride=1, stride_axis=0))
    odd = (iota((gl, span), 1) + span - 1) % span // gl % 2
    odd = jnp.where(iota((gl, span), 0) == 0, 1 - odd, odd)
    strip = jnp.where(odd == 1, rolled[1], rolled[0])
    return jnp.concatenate([strip, strip[:, :128]], axis=1)


def band_move(plan, a):
    return plan.gl * (plan.gl - a)


def small_padded(plan, line_ref, h, tail):
    gs, span = plan.gs, plan.strip_s
    line = jnp.broadcast_to(line_ref[h, :, 0:span], (16, span))
    strip = pltpu.roll(line, 0, axis=1, stride=1, stride_axis=0)
    col = iota((16, plan.pad_cols), 1)
    row = iota((16, plan.pad_cols), 0)
    bands = []
    for i in range(gs):
        move = 2 * gs * (gs - 1 - i) + gs
        band = pltpu.roll(strip, (span - move) % span, axis=1)[:, : plan.pad_cols]
        band = jnp.where(col == plan.cls_col, tail[:, 1:2], band)
        if i == 0:
            edge = jnp.where(col == plan.cls_col, tail[:, 2:3], tail[:, 0:1])
            band = jnp.where(row == plan.cls_row, edge, band)
        bands.append(band)
    return jnp.concatenate(bands, axis=0).astype(bf16)


def bias_head(plan, is_large, line_ref, rowsel, colsel, h, out_ref):
    gl, rows = plan.gl, plan.rows
    wide = round_up(rows, 128)
    tail = line_ref[h, :, plan.line : plan.line + 128]
    cols = mm(small_padded(plan, line_ref, h, tail), colsel[...]).astype(bf16)
    small_all = mm(rowsel[...], cols)
    strip = large_strip(plan, line_ref, h)
    span = strip.shape[1]
    col = iota((1, wide), 1)
    seg_col = segments(plan, is_large, col)
    bands = -(-rows // gl)
    for pair in range(-(-bands // 2)):
        first = 2 * gl * pair
        count = min(2 * gl, rows - first)
        parts = []
        for a in range(2 * pair, 2 * pair + 2):
            if a >= bands:
                continue
            move = band_move(plan, a)
            low = move // 128 * 128
            piece = strip[:, low : min(low + wide + 128, span)]
            if piece.shape[1] < wide + 128:
                piece = jnp.concatenate(
                    [piece, jnp.zeros((gl, wide + 128 - piece.shape[1]), f32)], axis=1
                )
            turn = (wide + 128 - (move - low)) % (wide + 128)
            parts.append((pltpu.roll(piece, turn, axis=1) if turn else piece)[:, :wide])
        block = (jnp.concatenate(parts, axis=0) if len(parts) > 1 else parts[0])[:count]
        row = iota((count, 1), 0) + first
        block = jnp.where(col == 0, tail[:, 1:2], block)
        if first == 0:
            block = jnp.where(row == 0, jnp.where(col == 0, tail[:, 2:3], tail[:, 0:1]), block)
        if first + count > plan.large_len:
            block = jnp.where(row < plan.large_len, block, 0.0)
        small = small_all[first : first + count]
        small = jnp.concatenate([small, jnp.zeros((count, wide - rows), f32)], axis=1)
        block = jnp.where(is_large, block, small)
        block = jnp.where(segments(plan, is_large, row) == seg_col, block, neg_fill)
        out_ref[h, first : first + count, :] = block[:, :rows].astype(bf16)


params = pltpu.CompilerParams(vmem_limit_bytes=vmem_bytes)


def norm_stats(values):
    mean = jnp.mean(values, axis=1, keepdims=True)
    centred = values - mean
    var = jnp.mean(centred * centred, axis=1, keepdims=True)
    inv = lax.rsqrt(var + norm_eps)
    return centred * inv, inv


def norm_back(d_out, gain, normal, inv):
    d_normal = d_out * gain
    mean_d = jnp.mean(d_normal, axis=1, keepdims=True)
    mean_dn = jnp.mean(d_normal * normal, axis=1, keepdims=True)
    return inv * (d_normal - mean_d - normal * mean_dn)


def rows_sum(values):
    return jnp.sum(values, axis=0, keepdims=True)


def gelu_parts(v):
    size = jnp.abs(v)
    bell = jnp.exp(-0.5 * v * v)
    t = 1.0 / (1.0 + (0.3275911 * 0.7071067811865476) * size)
    poly = t * (
        0.127414796
        + t * (-0.142248368 + t * (0.7107068705 + t * (-0.7265760135 + t * 0.5307027145)))
    )
    tail = poly * bell
    phi = jnp.where(v < 0, tail, 1.0 - tail)
    return v * phi, phi + v * bell * 0.3989422804014327


(
    FIRST_GAIN,
    FIRST_SHIFT,
    QUERY_BIAS,
    VALUE_BIAS,
    OUTPUT_BIAS,
    ATTEND_SCALE,
    SECOND_GAIN,
    SECOND_SHIFT,
    REDUCE_BIAS,
    FEED_SCALE,
) = range(10)


def vec(ref, idx):
    return ref[idx : idx + 1, :]


def half_mask(rows):
    return iota((rows, 128), 1) < 64


class Spot:
    def __init__(self, n):
        self.n, self.levels = n, n // 2
        self.rep, self.f = lax.axis_index("rep"), lax.axis_index("fsdp")
        self.half, self.core = self.rep // 2, self.rep % 2
        self.level, self.side = self.f // 2, self.f % 2

    def at(self, rep=None, f=None):
        return {"rep": self.rep if rep is None else rep, "fsdp": self.f if f is None else f}

    def sibling(self):
        return self.at(rep=2 * self.half + 1 - self.core)

    def across(self):
        return self.at(rep=2 * (1 - self.half) + self.core)

    def beside(self):
        return self.at(f=2 * self.level + 1 - self.side)

    def along(self, step):
        return self.at(f=2 * ((self.level + step) % self.levels) + self.side)

    def from_along(self, step, side=None):
        side = self.side if side is None else side
        return 2 * ((self.level + self.levels - step) % self.levels) + side


MESH = pl.DeviceIdType.MESH


def greet(devices, count):
    barrier = pltpu.get_barrier_semaphore()
    for device in devices:
        pl.semaphore_signal(barrier, inc=1, device_id=device, device_id_type=MESH)
    pl.semaphore_wait(barrier, count)


def send(src, dst, send_sem, recv_sem, device):
    return pltpu.make_async_remote_copy(
        src_ref=src,
        dst_ref=dst,
        send_sem=send_sem,
        recv_sem=recv_sem,
        device_id=device,
        device_id_type=MESH,
    )


def fast_shape(reps, n, shard_rows):
    return reps == 4 and n == 8 and all(rows % 96 == 0 for rows in shard_rows)


def spread_block(refs, block_ref):
    *vectors, be_ref, table_ref = refs
    share, heads = table_ref.shape
    eye = jnp.where(iota((16, heads), 0) == iota((16, heads), 1), 1.0, 0.0).astype(bf16)
    lanes = block_ref.shape[1]
    table = mm(eye, table_ref[...], NT)
    width = vectors[0].shape[1]
    rows = [v[...].astype(f32) for v in vectors]
    rows.append(jnp.zeros((16 - len(rows), width), f32))
    block = jnp.concatenate(
        [table, jnp.zeros((16, lanes - share - width), f32), jnp.concatenate(rows, axis=0)], axis=1
    )
    wide = jnp.broadcast_to(be_ref[...].astype(f32), (16, lanes))
    block_ref[...] = jnp.where(iota((16, lanes), 0) == heads, wide, block).astype(bf16)


any_spec = pl.BlockSpec(memory_space=pl.ANY)
vmem_spec = pl.BlockSpec(memory_space=pltpu.VMEM)


def add16(left, right):
    return (left.astype(f32) + right.astype(f32)).astype(bf16)


def gather_plain(shorts, shards, n):
    gather = lambda value, axis: lax.all_gather(value, "fsdp", axis=axis, tiled=True)
    vecs = gather(jnp.concatenate(shorts[:10], axis=0), 1).astype(f32)
    vecs = jnp.pad(vecs, ((0, 6), (0, 0)))
    table = gather(shorts[11], 0).T
    table = jnp.pad(table, ((0, 16 - table.shape[0]), (0, 0)))
    return [gather(w, 0) for w in shards], vecs, gather(shorts[10], 1).astype(f32), table


def reduce_plain(grads, vec_sums, be_sums, table_sums, n):
    def whole_sum(value):
        value = lax.psum_scatter(value, "fsdp", scatter_dimension=0, tiled=True)
        return lax.psum(value, "rep")

    sums = lax.psum((vec_sums, be_sums, table_sums), ("rep", "fsdp"))
    me = lax.axis_index("fsdp")
    cut = lambda v: lax.dynamic_slice_in_dim(v, me * (v.shape[1] // n), v.shape[1] // n, axis=1)
    vec_part, be_part, table_part = [cut(v) for v in sums]
    wide = be_part.shape[1]
    space = max(wide - vec_part.shape[1] - table_part.shape[1], 0)
    body = jnp.concatenate([table_part, jnp.zeros((16, space), f32), vec_part], axis=1)
    block = jnp.where(jnp.arange(16)[:, None] == 12, jnp.pad(be_part, ((0, 0), (0, body.shape[1] - wide))), body)
    return [whole_sum(g) for g in grads], block


class Piece:
    sems = 8

    def __init__(self, spot, shard, whole, row, col, cols, ss, rs, base):
        self.level, self.side = spot.level, spot.side
        levels = spot.levels
        part, q = 48, 16
        start = row + spot.core * part
        cut = pl.ds(col, cols)
        rows = lambda first, size: pl.ds(pl.multiple_of(first, 16), size)
        plane = rows(start + spot.half * q, 2 * q)
        outer = rows(start + spot.half * 2 * q, q)
        core_rows = rows(start, part)
        side = spot.side

        def copy(idx, src, dst, device):
            return send(src, dst, ss.at[base + idx], rs.at[base + idx], device)

        own = shard.at[plane, cut]
        here = whole.at[spot.level, side, plane, cut]
        self.local = pltpu.make_async_copy(own, here, ss.at[base + levels + 3])
        self.z = [copy(step - 1, own, here, spot.along(step)) for step in range(1, levels)]
        column = whole.at[:, side, plane, cut]
        self.y = copy(levels - 1, column, column, spot.beside())
        near = whole.at[:, side, outer, cut]
        far = whole.at[:, 1 - side, outer, cut]
        self.x = [
            copy(levels, near, near, spot.across()),
            copy(levels + 1, far, far, spot.across()),
        ]
        done = whole.at[:, :, core_rows, cut]
        self.c = copy(levels + 2, done, done, spot.sibling())

    def start(self):
        self.local.start()
        for copy in self.z:
            copy.start()

    def after_z(self):
        self.local.wait()
        for copy in self.z:
            copy.wait_recv()
        self.y.start()
        self.x[0].start()

    def after_y(self):
        self.y.wait_recv()
        self.x[1].start()

    def after_x(self):
        self.x[0].wait_recv()
        self.x[1].wait_recv()
        self.c.start()

    def after_c(self):
        self.c.wait_recv()

    def finish(self):
        for copy in self.z + [self.y, self.c] + self.x:
            copy.wait_send()


def piece_cuts(shard_shapes):
    cuts = []
    for idx, (rows, cols) in enumerate(shard_shapes):
        for row in range(0, rows, 96):
            tile = next(t for t in (768, 512, 384, 256, 128) if cols % t == 0)
            for col in range(0, cols, tile):
                cuts.append((idx, row, col, tile))
    return cuts


def front_kernel(plan, n, fast, cuts, *refs):
    refs = list(refs)
    take = lambda count: [refs.pop(0) for _ in range(count)]
    (kind_ref, tok_ref, idx_ref, pick_ref, rowsel_ref, colsel_ref) = take(6)
    if fast:
        shorts, shards = take(12), take(4)
        wholes = take(4)
        vec_ref, be_ref = take(2)
    else:
        vec_ref, be_ref, tab_ref = take(3)
        wholes = take(4)
    lab_ref, normed_ref, mixed_ref, middle_ref, branch_ref = take(5)
    qkv_out, probs_out, act_out, slope_out = take(4)
    line_ref, heads_ref, qkv_ref, wt_ref, wo_ref, we_ref, act_ref, slope_ref, second_ref = take(9)
    load_sems, save_sems = take(2)
    is_large = kind_ref[0] == 1
    heads = plan.heads
    pairs = heads // 2
    width = tok_ref.shape[1]

    loads = []
    for idx, ref in enumerate((wt_ref, wo_ref, we_ref)):
        for j in range(ref.shape[0]):
            cut = pl.ds(j * width, width)
            src = wholes[idx].at[:, :, :, cut]
            loads.append(pltpu.make_async_copy(src, ref.at[j], load_sems.at[len(loads)]))
    matrix = lambda ref, j: ref[j].reshape(width, width)

    if fast:
        block, blocks, ss, rs, bss, brs = refs
        spot = Spot(n)
        peers = [spot.at(f=(spot.f + k) % n) for k in range(1, n)]
        greet(peers + [spot.sibling(), spot.across()], n + 1)
        pieces = []
        for idx, row, col, cols in cuts:
            base = len(pieces) * Piece.sems
            pieces.append(Piece(spot, shards[idx], wholes[idx], row, col, cols, ss, rs, base))
        spread_block(shorts, block)
        small = []
        for k, peer in enumerate(peers):
            small.append(send(block, blocks.at[spot.f], bss.at[k], brs.at[k], peer))
            small[k].start()
        blocks[spot.f] = block[...]
        pieces[0].start()
        pieces[1].start()

    def step(k):
        if not fast:
            if k == 0:
                for load in loads:
                    load.start()
            return
        for back, action in enumerate(("after_z", "after_y", "after_x", "after_c")):
            if 0 <= k - back < len(pieces):
                getattr(pieces[k - back], action)()
                if back == 0 and k + 2 < len(pieces):
                    pieces[k + 2].start()
                if back == 3 and k - 3 < len(loads):
                    loads[k - 3].start()

    last_step = len(cuts) + 3
    read_labels(plan, is_large, idx_ref, pick_ref, lab_ref)
    step(0)
    if fast:
        for copy in small:
            copy.wait()
        share, bshare = shorts[0].shape[1], shorts[11].shape[0]
        tab = []
        for f in range(n):
            part = blocks[f].astype(f32)
            wide = part.shape[1]
            vec_ref[:, f * share : (f + 1) * share] = part[:, wide - share :]
            tab.append(part[:, :bshare])
            be_ref[:, f * wide : (f + 1) * wide] = part[heads : heads + 1, :]
        tab = jnp.concatenate(tab, axis=1)
    else:
        tab = tab_ref[...]
    table_lines(plan, tab, lab_ref, line_ref)
    step(1)
    normal, _ = norm_stats(tok_ref[...].astype(f32))
    normed = normal * vec(vec_ref, FIRST_GAIN) + vec(vec_ref, FIRST_SHIFT)
    normed_ref[...] = normed.astype(bf16)

    third = heads // 3
    for group in range(3):

        @pl.loop(group * third, (group + 1) * third)
        def _(h):
            bias_head(plan, is_large, line_ref, rowsel_ref, colsel_ref, h, heads_ref)

        step(2 + group)

    step(5)
    saves = []

    def save(src, dst):
        saves.append(pltpu.make_async_copy(src, dst, save_sems.at[len(saves)]))
        saves[-1].start()

    normed = normed_ref[...]
    for j in range(3):
        loads[j].wait()
        triple = mm(normed, matrix(wt_ref, j))
        if j == 0:
            triple = triple + vec(vec_ref, QUERY_BIAS)
        if j == 2:
            triple = triple + vec(vec_ref, VALUE_BIAS)
        triple = triple.astype(bf16)
        if j == 0:
            triple = triple * jnp.array(0.125, bf16)
        for p in range(pairs):
            qkv_ref[j * pairs + p] = triple[:, 128 * p : 128 * (p + 1)]
    save(qkv_ref, qkv_out)
    step(6)

    def attend_pair(p):
        q, k, v = qkv_ref[p], qkv_ref[pairs + p], qkv_ref[2 * pairs + p]
        lower = half_mask(q.shape[0])
        mixed = []
        for t in range(2):
            keep = lower if t == 0 else ~lower
            scores = mm(jnp.where(keep, q, jnp.zeros_like(q)), k, NT)
            scores = scores + heads_ref[2 * p + t].astype(f32)
            top = jnp.max(scores, axis=1, keepdims=True)
            exps = jnp.exp(scores - top)
            total = jnp.sum(exps, axis=1, keepdims=True)
            probs = (exps * (1.0 / total)).astype(bf16)
            heads_ref[2 * p + t] = probs
            mixed.append(mm(probs, v))
        mixed_ref[p] = jnp.where(lower, mixed[0], mixed[1]).astype(bf16)

    share_of = pairs // 3
    for group in range(3):

        @pl.loop(group * share_of, (group + 1) * share_of)
        def _(p):
            attend_pair(p)

        cut = pl.ds(group * 2 * share_of, 2 * share_of)
        save(heads_ref.at[cut], probs_out.at[cut])
        step(7 + group)

    loads[3].wait()
    mixed = jnp.concatenate([mixed_ref[p] for p in range(pairs)], axis=1)
    branch = mm(mixed, matrix(wo_ref, 0)) + vec(vec_ref, OUTPUT_BIAS)
    branch_ref[...] = branch.astype(bf16)
    middle = tok_ref[...].astype(f32) + vec(vec_ref, ATTEND_SCALE) * branch
    middle_ref[...] = middle
    normal, _ = norm_stats(middle)
    second = normal * vec(vec_ref, SECOND_GAIN) + vec(vec_ref, SECOND_SHIFT)
    second_ref[...] = second.astype(bf16)
    for j in range(we_ref.shape[0]):
        if 10 + j <= last_step:
            step(10 + j)
        loads[4 + j].wait()
        pre = mm(second_ref[...], matrix(we_ref, j)) + be_ref[:, j * width : (j + 1) * width]
        value, slope = gelu_parts(pre)
        act_ref[j] = value.astype(bf16)
        slope_ref[j] = slope.astype(bf16)
        save(act_ref.at[j], act_out.at[j])
        save(slope_ref.at[j], slope_out.at[j])
    for k in range(10 + we_ref.shape[0], last_step):
        step(k)
    for copy in saves:
        copy.wait()
    if fast:
        for piece in pieces:
            piece.finish()


def front(plan, kind, tokens, large_index, rowsel, colsel, n, fast, shorts, shards):
    rows, width = tokens.shape
    heads = plan.heads
    sds = jax.ShapeDtypeStruct
    picks = pick_plan(plan)
    levels = n // 2
    hidden = shards[2].shape[1]
    blocks = hidden // width
    cuts = piece_cuts([w.shape for w in shards]) if fast else []
    inputs = [kind, tokens, large_index, picks, rowsel, colsel]
    in_specs = [pl.BlockSpec(memory_space=pltpu.SMEM)] + [vmem_spec] * 5
    outs, out_specs = [], []
    if fast:
        inputs += shorts + shards
        in_specs += [vmem_spec] * 12 + [any_spec] * 4
        outs += [sds((levels, 2) + w.shape, bf16) for w in shards]
        outs += [sds((16, width), f32), sds((1, hidden), f32)]
        out_specs += [any_spec] * 4 + [vmem_spec] * 2
    else:
        wholes, vecs, be, table = gather_plain(shorts, shards, n)
        wholes = [w.reshape(4, 2, w.shape[0] // 8, w.shape[1]) for w in wholes]
        inputs += [vecs, be, table.astype(f32)] + wholes
        in_specs += [vmem_spec] * 3 + [any_spec] * 4
    outs += [
        sds((2, plan.lanes), jnp.int32),
        sds((rows, width), bf16),
        sds((heads // 2, rows, 128), bf16),
        sds((rows, width), f32),
        sds((rows, width), bf16),
        sds((3 * heads // 2, rows, 128), bf16),
        sds((heads, rows, rows), bf16),
        sds((blocks, rows, width), bf16),
        sds((blocks, rows, width), bf16),
    ]
    out_specs += [vmem_spec] * 5 + [any_spec] * 4
    tile = lambda count: pltpu.VMEM((count, 4, 2, width // 8, width), bf16)
    scratch = [
        pltpu.VMEM((heads, 1, plan.lanes), f32),
        pltpu.VMEM((heads, rows, rows), bf16),
        pltpu.VMEM((3 * heads // 2, rows, 128), bf16),
        tile(3),
        tile(1),
        tile(blocks),
        pltpu.VMEM((blocks, rows, width), bf16),
        pltpu.VMEM((blocks, rows, width), bf16),
        pltpu.VMEM((rows, width), bf16),
        pltpu.SemaphoreType.DMA((4 + blocks,)),
        pltpu.SemaphoreType.DMA((4 + 2 * blocks,)),
    ]
    if fast:
        wide = shorts[10].shape[1]
        scratch += [
            pltpu.VMEM((16, wide), bf16),
            pltpu.VMEM((n, 16, wide), bf16),
            pltpu.SemaphoreType.DMA((len(cuts) * Piece.sems,)),
            pltpu.SemaphoreType.DMA((len(cuts) * Piece.sems,)),
            pltpu.SemaphoreType.DMA((n - 1,)),
            pltpu.SemaphoreType.DMA((n - 1,)),
        ]
    kernel_params = dict(vmem_limit_bytes=vmem_bytes)
    if fast:
        kernel_params.update(collective_id=1, has_side_effects=True)
    result = pl.pallas_call(
        functools.partial(front_kernel, plan, n, fast, cuts),
        in_specs=in_specs,
        out_specs=out_specs,
        out_shape=outs,
        scratch_shapes=scratch,
        compiler_params=pltpu.CompilerParams(**kernel_params),
        name="front",
    )(*inputs)
    result = list(result)
    if fast:
        wholes = result[:4]
        vecs, be = result[4:6]
        result = result[6:]
    return wholes, vecs, be, result


def image_rows(plan):
    out = []
    for image in range(3):
        first, last = image * plan.small_len, (image + 1) * plan.small_len
        rows = (first // 16 * 16, round_up(last, 16))
        lanes = (first // 128 * 128, min(round_up(last, 128), plan.rows))
        out.append((rows, lanes))
    return out


def image_selectors(plan):
    rows, _ = plan.selector_arrays()
    out = []
    for image, ((low, high), _) in enumerate(image_rows(plan)):
        part = rows.copy()
        part[: image * plan.small_len] = 0
        part[(image + 1) * plan.small_len :] = 0
        out.append(np.pad(part[low:high].T, ((0, 0), (0, 256 - (high - low)))))
    return jnp.asarray(np.concatenate(out, axis=1), bf16)


def fold_head(plan, ds_ref, pick, colsel, large_ref, small_ref, tail_ref, h, is_large):
    gl, gs, rows = plan.gl, plan.gs, plan.rows
    wide = round_up(rows, 128)
    width = plan.strip_l + 128
    bands = -(-rows // gl)
    total = jnp.zeros((gl, width), f32)
    side = jnp.zeros((2 * gl, 128), f32)
    for pair in range(-(-bands // 2)):
        first = 2 * gl * pair
        count = min(2 * gl, rows - first)
        block = ds_ref[first : first + count, :].astype(f32)
        block = jnp.concatenate([block, jnp.zeros((count, wide - rows), f32)], axis=1)
        if count < 2 * gl:
            block = jnp.concatenate([block, jnp.zeros((2 * gl - count, wide), f32)], axis=0)
        if pair == 0:
            row = iota((2 * gl, wide), 0)
            top_row = jnp.where(row == 0, block, 0.0)
            block = jnp.where(row == 0, 0.0, block)
        side = side + block[:, :128]
        block = jnp.where(iota((1, wide), 1) == 0, 0.0, block)
        for half in range(2):
            a = 2 * pair + half
            if a >= bands:
                continue
            move = band_move(plan, a)
            low = move // 128 * 128
            piece = block[half * gl : (half + 1) * gl]
            if move > low:
                piece = jnp.concatenate([piece, jnp.zeros((gl, 128), f32)], axis=1)
                piece = pltpu.roll(piece, move - low, axis=1)
            piece = piece[:, : width - low]
            parts = [jnp.zeros((gl, low), f32)] if low else []
            parts.append(piece)
            if low + piece.shape[1] < width:
                parts.append(jnp.zeros((gl, width - low - piece.shape[1]), f32))
            total = total + (jnp.concatenate(parts, axis=1) if len(parts) > 1 else piece)
    large_ref[h] = jnp.concatenate(
        [total[:, :128] + total[:, plan.strip_l :], total[:, 128 : plan.strip_l]], axis=1
    )
    lane = iota((1, wide), 1)
    full = lambda v: jnp.sum(jnp.sum(v, axis=0, keepdims=True), axis=1, keepdims=True)
    corner = full(jnp.where(lane == 0, top_row, 0.0))
    top = full(jnp.where(lane == 0, 0.0, top_row))
    side = full(jnp.where(iota((1, 128), 1) == 0, side, 0.0))

    padded, start = None, 0
    for (r0, r1), (l0, l1) in image_rows(plan):
        cols = mm(ds_ref[r0:r1, l0:l1], colsel[:, l0:l1], NT).astype(bf16)
        part = mm(pick[:, start : start + r1 - r0], cols)
        padded = part if padded is None else padded + part
        start += 256
    span = plan.strip_s
    col = iota((1, plan.pad_cols), 1)
    row = iota((16, 1), 0)
    acc = jnp.zeros((16, span), f32)
    edge = jnp.zeros((16, plan.pad_cols), f32)
    for i in range(gs):
        band = padded[16 * i : 16 * (i + 1)]
        if i == 0:
            top_s = jnp.where(row == plan.cls_row, band, 0.0)
            band = jnp.where(row == plan.cls_row, 0.0, band)
        edge = edge + band
        band = jnp.where(col < plan.cls_col, band, 0.0)
        band = jnp.concatenate([band, jnp.zeros((16, span - plan.pad_cols), f32)], axis=1)
        acc = acc + pltpu.roll(band, 2 * gs * (gs - 1 - i) + gs, axis=1)
    small_ref[h] = acc
    corner_s = full(jnp.where(col == plan.cls_col, top_s, 0.0))
    top_s = full(jnp.where(col < plan.cls_col, top_s, 0.0))
    side_s = full(jnp.where(col == plan.cls_col, edge, 0.0))
    lane = iota((1, 128), 1)
    picks = [(top, top_s), (side, side_s), (corner, corner_s)]
    tail = jnp.zeros((1, 128), f32)
    for i, (a, b) in enumerate(picks):
        tail = jnp.where(lane == i, jnp.where(is_large, a, b), tail)
    tail_ref[h] = tail


def fold_lines(plan, large_ref, small_ref, tail_ref, is_large):
    gl, heads, span = plan.gl, plan.heads, plan.strip_l
    odd = (iota((1, span), 1) + span - 1) % span // gl % 2
    lines = [None, None]
    for i in reversed(range(gl)):
        row = large_ref[:, i, :]
        for parity in range(2):
            want = parity if i else 1 - parity
            part = jnp.where(odd == want, row, 0.0)
            if lines[parity] is not None:
                part = part + pltpu.roll(lines[parity], span - 1, axis=1)
            lines[parity] = part
    small = None
    for i in reversed(range(16)):
        part = small_ref[:, i, :]
        small = part if small is None else part + pltpu.roll(small, plan.strip_s - 1, axis=1)
    small = jnp.concatenate([small, jnp.zeros((heads, plan.line - plan.strip_s), f32)], axis=1)
    line = jnp.where(is_large, jnp.concatenate(lines, axis=1), small)
    tail = tail_ref[:, 0, :]
    line = jnp.concatenate([line, tail], axis=1)
    return jnp.concatenate([line, jnp.zeros((16 - heads, plan.lanes), f32)], axis=0)


class Sum:
    sems = 9

    def __init__(self, spot, grad, out, row, cut, bufs, ss, rs, base):
        self.spot, self.grad = spot, grad
        self.out = out
        self.row, self.cut = row, cut
        self.acc, self.got_x, self.got_y, self.got_z, self.total, self.got_f = bufs
        half, core, side, level, levels = spot.half, spot.core, spot.side, spot.level, spot.levels
        q, part = 16, 48
        rows = lambda first, size: pl.ds(pl.multiple_of(first, 16), size)
        self.rows = rows
        self.plane = rows(half * q, 2 * q)
        self.mine = rows(half * 2 * q, q)
        self.own = rows(core * part, part)
        self.sent = self.joined = False

        def copy(idx, src, dst, device):
            return send(src, dst, ss.at[base + idx], rs.at[base + idx], device)

        acc = self.acc
        self.c = copy(0, grad.at[:, :, rows((1 - core) * part, part)], acc, spot.sibling())
        self.x = copy(1, acc.at[:, :, rows((1 - half) * 2 * q, q)], self.got_x, spot.across())
        self.y = copy(2, acc.at[:, 1 - side, self.plane], self.got_y, spot.beside())
        self.z = []
        for step in range(1, levels):
            src = acc.at[(level + step) % levels, side, self.plane]
            self.z.append(copy(4 + step, src, self.got_z.at[step - 1], spot.along(step)))
        self.f = copy(3, self.total, self.got_f, spot.across())
        mine = out.at[rows(row + core * part, part), cut]
        self.last = copy(4, mine, mine, spot.sibling())

    @staticmethod
    def buffers(levels, cols):
        shapes = [
            (levels, 2, 48, cols),
            (levels, 2, 16, cols),
            (levels, 32, cols),
            (levels - 1, 32, cols),
            (32, cols),
            (32, cols),
        ]
        return [pltpu.VMEM(shape, bf16) for shape in shapes]

    def start(self):
        self.c.start()

    def free(self):
        self.join()
        if not self.sent:
            self.c.wait_send()
            self.sent = True

    def stage(self, k):
        getattr(self, ("go", "after_x", "after_y", "after_z", "after_f", "after_last")[k])()

    def join(self):
        if self.joined:
            return
        self.joined = True
        self.c.wait_recv()

        @pl.loop(0, self.acc.shape[0])
        def _(level):
            for side in range(2):
                own = self.grad[level, side, self.own]
                self.acc[level, side] = add16(self.acc[level, side], own)

    def go(self):
        self.join()
        self.x.start()

    def after_x(self):
        self.x.wait_recv()

        @pl.loop(0, self.acc.shape[0])
        def _(level):
            for side in range(2):
                mine = self.acc[level, side, self.mine]
                self.acc[level, side, self.mine] = add16(mine, self.got_x[level, side])

        self.y.start()

    def after_y(self):
        side = self.spot.side
        self.y.wait_recv()

        @pl.loop(0, self.acc.shape[0])
        def _(level):
            mine = self.acc[level, side, self.plane]
            self.acc[level, side, self.plane] = add16(mine, self.got_y[level])

        for copy in self.z:
            copy.start()

    def after_z(self):
        for copy in self.z:
            copy.wait_recv()
        value = self.acc[self.spot.level, self.spot.side, self.plane].astype(f32)
        for k in range(len(self.z)):
            value = value + self.got_z[k].astype(f32)
        self.total[...] = value.astype(bf16)
        self.f.start()

    def after_f(self):
        q, half = 16, self.spot.half
        base = self.row + self.spot.core * 48
        rows = self.rows
        total, got, out, cut = self.total, self.got_f, self.out, self.cut
        self.f.wait_recv()
        out[rows(base + half * 2 * q, q), cut] = total[rows(half * q, q)]
        both = add16(total[rows((1 - half) * q, q)], got[rows(half * q, q)])
        out[rows(base + q, q), cut] = both
        out[rows(base + (1 - half) * 2 * q, q), cut] = got[rows((1 - half) * q, q)]
        self.last.start()

    def after_last(self):
        self.last.wait_recv()

    def finish(self):
        self.free()
        for copy in [self.x, self.y, self.f, self.last] + self.z:
            copy.wait_send()


def back_kernel(plan, n, fast, blocks, *refs):
    refs = list(refs)
    take = lambda count: [refs.pop(0) for _ in range(count)]
    kind_ref, cot_ref, vec_ref, lab_ref, colsel_ref, pick_ref = take(6)
    middle_in, branch_in, normed_in, mixed_in, tok_in = take(5)
    act_in, slope_in, qkv_in, probs_in = take(4)
    wt_in, wo_in, we_in, wr_in = take(4)
    out_ref, tok_out = take(2)
    if fast:
        sum_wt, sum_wo, sum_we, sum_wr, small_out = take(5)
    else:
        sum_wt, sum_wo, sum_we, sum_wr, vec_out, be_out, tab_out = take(7)
    ds_out = take(1)[0]
    (
        tile_ref,
        act_ref,
        slope_ref,
        middle_ref,
        feed_ref,
        dsec_ref,
        gwr_ref,
        stage_ref,
        qkv_ref,
        probs_ref,
        pair_ref,
        large_ref,
        strip_ref,
        tail_ref,
        small_ref,
    ) = take(15)
    tile_sems, act_sems, pair_sems, ds_sems, stage_sems = take(5)
    is_large = kind_ref[0] == 1
    heads, rows = plan.heads, plan.rows
    pairs = heads // 2
    width = cot_ref.shape[1]
    spot = Spot(n) if fast else None
    half_ref, dfeed_ref = pair_ref.at[0], pair_ref.at[1]
    branch_ref, late_ref = act_ref.at[0], dfeed_ref
    dtri = [act_ref.at[1 + j] for j in range(3)]
    dmix_ref, tok_ref = slope_ref.at[0], slope_ref.at[1]

    order = []
    for j in range(blocks):
        order += [(wr_in, j), (we_in, j)]
    order += [(wo_in, 0), (wt_in, 0), (wt_in, 1), (wt_in, 2)]
    tiles = []
    for i, (src, j) in enumerate(order):
        if src is wr_in:
            view, dst = src.at[j], tile_ref.at[i % 3].reshape(2, 4 * width // 8, width)
        else:
            view, dst = src.at[:, :, :, pl.ds(j * width, width)], tile_ref.at[i % 3]
        tiles.append(pltpu.make_async_copy(view, dst, tile_sems.at[i % 3]))

    def tile(i):
        tiles[i].wait()
        return tile_ref[i % 3].reshape(width, width)

    def more(i):
        if i + 3 < len(tiles):
            tiles[i + 3].start()

    def fetch(src, dst, idx):
        copy = pltpu.make_async_copy(src, dst, act_sems.at[idx])
        copy.start()
        return copy

    acts = [fetch(act_in.at[j], act_ref.at[j], j) for j in range(blocks)]
    for i in range(3):
        tiles[i].start()
    slopes = [pltpu.make_async_copy(slope_in.at[j], slope_ref.at[j % 2], act_sems.at[blocks + j]) for j in range(blocks)]
    slopes[0].start()
    slopes[1].start()
    base = 2 * blocks
    mid_copy = fetch(middle_in, middle_ref, base)

    jobs, waiting, done = [], [], []
    if fast:
        bufs, (block, got, reps, ss, rs, bss, brs) = refs[: 6 * 12], refs[6 * 12 :]
        peers = [spot.at(f=(spot.f + k) % n) for k in range(1, n)]
        others = [spot.at(rep=(spot.rep + k) % 4) for k in range(1, 4)]
        greet(peers + others, n + 2)

        def push(grad, out, row, cut):
            k = len(jobs)
            job = Sum(spot, grad, out, row, cut, bufs[6 * k : 6 * k + 6], ss, rs, k * Sum.sems)
            jobs.append(job)
            waiting.append([job, 0])
            job.start()
    else:

        def push(grad, out, row, cut):
            if out is sum_wr:
                if row == 0:
                    copy = pltpu.make_async_copy(gwr_ref, out, stage_sems.at[0])
                    copy.start()
                    copy.wait()
                return
            copy = pltpu.make_async_copy(grad, out.at[:, :, :, cut], stage_sems.at[0])
            copy.start()
            copy.wait()

    active = []

    def beat():
        if waiting:
            active.append(waiting.pop(0))
        for job, _ in waiting:
            job.join()
        for entry in list(active):
            entry[0].stage(entry[1])
            entry[1] += 1
            if entry[1] == 6:
                active.remove(entry)

    stage_count = [0]

    def stage(value):
        k = stage_count[0]
        stage_count[0] += 1
        slot = stage_ref.at[k % 2]
        if fast and k >= 2:
            jobs[k - 2 + 4].free()
        slot[...] = value.astype(bf16).reshape(4, 2, width // 8, width)
        return slot

    limit = jnp.where(is_large, plan.large_len, 3 * plan.small_len)
    live = iota((rows, 1), 0) < limit
    grad = jnp.where(live, cot_ref[...].astype(f32), 0.0)
    dfeed_ref[...] = (vec(vec_ref, FEED_SCALE) * grad).astype(bf16)
    d_feed = dfeed_ref[...]
    small_ref[...] = jnp.zeros_like(small_ref)
    small_ref[REDUCE_BIAS : REDUCE_BIAS + 1, 0:width] = rows_sum(d_feed.astype(f32))
    for j in range(blocks):
        acts[j].wait()
        gwr_ref[j] = mm(act_ref[j], d_feed, TN).astype(bf16).reshape(2, 4 * width // 8, width)
    for m in range(blocks):
        push(gwr_ref.at[:, :, pl.ds(96 * m, 96)], sum_wr, 96 * m, slice(0, width))

    mid_copy.wait()
    normal, _ = norm_stats(middle_ref[...])
    second = normal * vec(vec_ref, SECOND_GAIN) + vec(vec_ref, SECOND_SHIFT)
    half_ref[...] = second.astype(bf16)
    be_row = 10
    for j in range(blocks):
        second, d_feed = half_ref[...], dfeed_ref[...]
        wr = tile(2 * j)
        feed = mm(act_ref[j], wr)
        d_act = mm(d_feed, wr, NT)
        more(2 * j)
        slopes[j].wait()
        d_pre = (d_act * slope_ref[j % 2].astype(f32)).astype(bf16)
        if j + 2 < blocks:
            slopes[j + 2].start()
        we = tile(2 * j + 1)
        d_second = mm(d_pre, we, NT)
        more(2 * j + 1)
        if j == 0:
            branch_copy = fetch(branch_in, branch_ref, base + 1)
            feed_ref[...] = feed
            dsec_ref[...] = d_second
        else:
            feed_ref[...] += feed
            dsec_ref[...] += d_second
        small_ref[be_row + j : be_row + j + 1, 0:width] = rows_sum(d_pre.astype(f32))
        beat()
        push(stage(mm(second, d_pre, TN)), sum_we, 0, slice(j * width, (j + 1) * width))

    def pair_loads(p):
        slot = p % 3
        copies = [pltpu.make_async_copy(probs_in.at[pl.ds(2 * p, 2)], probs_ref.at[slot], pair_sems.at[slot, 3])]
        for part in range(3):
            copies.append(
                pltpu.make_async_copy(
                    qkv_in.at[part * pairs + p], qkv_ref.at[slot, part], pair_sems.at[slot, part]
                )
            )
        return copies

    for copy in pair_loads(0):
        copy.start()

    branch_copy.wait()
    feed_out = feed_ref[...] + vec(vec_ref, REDUCE_BIAS)
    middle = middle_ref[...]
    half_ref[...] = (middle + vec(vec_ref, FEED_SCALE) * feed_out).astype(bf16)
    out_copy = fetch(half_ref, out_ref, base)
    grad = jnp.where(live, cot_ref[...].astype(f32), 0.0)
    d_second = dsec_ref[...]
    normal, inv = norm_stats(middle)
    d_middle = grad + norm_back(d_second, vec(vec_ref, SECOND_GAIN), normal, inv)
    d_branch = (vec(vec_ref, ATTEND_SCALE) * d_middle).astype(bf16)

    def note(idx, value):
        small_ref[idx : idx + 1, 0:width] = value

    note(FEED_SCALE, rows_sum(grad * feed_out))
    note(SECOND_GAIN, rows_sum(d_second * normal))
    note(SECOND_SHIFT, rows_sum(d_second))
    note(ATTEND_SCALE, rows_sum(d_middle * branch_ref[...].astype(f32)))
    note(OUTPUT_BIAS, rows_sum(d_branch.astype(f32)))
    dsec_ref[...] = d_middle
    mixed = jnp.concatenate([mixed_in[p] for p in range(pairs)], axis=1)
    push(stage(mm(mixed, d_branch, TN)), sum_wo, 0, slice(0, width))
    dmix_ref[...] = mm(d_branch, tile(2 * blocks), NT).astype(bf16)
    more(2 * blocks)
    late = [fetch(normed_in, late_ref, 0), fetch(tok_in, tok_ref, 1)]
    beat()

    def ds_copy(p):
        slot = p % 3
        return pltpu.make_async_copy(probs_ref.at[slot], ds_out.at[pl.ds(2 * p, 2)], ds_sems.at[slot])

    def pair_back(p):
        slot = p % 3
        for copy in pair_loads(p):
            copy.wait()

        @pl.when(p >= 2)
        def _():
            ds_copy(p - 2).wait()

        @pl.when(p + 1 < pairs)
        def _():
            for copy in pair_loads(p + 1):
                copy.start()

        lanes = pl.ds(pl.multiple_of(128 * p, 128), 128)
        q, k, v = qkv_ref[slot, 0], qkv_ref[slot, 1], qkv_ref[slot, 2]
        do = dmix_ref[:, lanes]
        lower = half_mask(rows)
        prod = do.astype(f32) * mixed_in[p].astype(f32)
        dq, dk, dv = [], [], []
        for t in range(2):
            keep = lower if t == 0 else ~lower
            d_out = jnp.where(keep, do, jnp.zeros_like(do))
            delta = jnp.sum(jnp.where(keep, prod, 0.0), axis=1, keepdims=True)
            d_probs = mm(d_out, v, NT)
            probs = probs_ref[slot, t]
            dv.append(mm(probs, do, TN))
            d_scores = (probs.astype(f32) * (d_probs - delta)).astype(bf16)
            probs_ref[slot, t] = d_scores
            dq.append(mm(d_scores, k))
            dk.append(mm(d_scores, q, TN))
        dtri[0][:, lanes] = (jnp.where(lower, dq[0], dq[1]) * 0.125).astype(bf16)
        dtri[1][:, lanes] = jnp.where(lower, dk[0], dk[1]).astype(bf16)
        dtri[2][:, lanes] = jnp.where(lower, dv[0], dv[1]).astype(bf16)
        ds_copy(p).start()

    for group in range(3):

        @pl.loop(2 * group, 2 * group + 2)
        def _(p):
            pair_back(p)

        beat()

    d_normed = None
    for copy in late:
        copy.wait()
    for j in range(3):
        d_part = dtri[j][...]
        push(stage(mm(late_ref[...], d_part, TN)), sum_wt, 0, slice(j * width, (j + 1) * width))
        w = tile(2 * blocks + 1 + j)
        part = mm(d_part, w, NT)
        d_normed = part if d_normed is None else d_normed + part
        if j != 1:
            note(QUERY_BIAS if j == 0 else VALUE_BIAS, rows_sum(d_part.astype(f32)))
        beat()
    normal, inv = norm_stats(tok_ref[...].astype(f32))
    back = norm_back(d_normed, vec(vec_ref, FIRST_GAIN), normal, inv)
    late_ref[...] = (dsec_ref[...] + back).astype(bf16)
    tok_copy = fetch(late_ref, tok_out, base + 1)
    note(FIRST_GAIN, rows_sum(d_normed * normal))
    note(FIRST_SHIFT, rows_sum(d_normed))

    ds_copy(pairs - 2).wait()
    ds_copy(pairs - 1).wait()

    def ds_load(p):
        slot = p % 2
        return pltpu.make_async_copy(ds_out.at[pl.ds(2 * p, 2)], probs_ref.at[slot], pair_sems.at[slot, 3])

    ds_load(0).start()
    for group in range(3):

        @pl.loop(2 * group, 2 * group + 2)
        def _(p):
            ds_load(p).wait()

            @pl.when(p + 1 < pairs)
            def _():
                ds_load(p + 1).start()

            @pl.loop(0, 2)
            def _(t):
                fold_head(
                    plan,
                    probs_ref.at[p % 2, t],
                    pick_ref,
                    colsel_ref,
                    large_ref,
                    strip_ref,
                    tail_ref,
                    2 * p + t,
                    is_large,
                )

        beat()
    out_copy.wait()
    tok_copy.wait()
    lines = fold_lines(plan, large_ref, strip_ref, tail_ref, is_large)
    line_of = lambda chunk: lines[:, 128 * chunk : 128 * (chunk + 1)]
    buckets = plan.buckets
    d_table = table_from_lines(plan, line_of, lab_ref, buckets)

    if not fast:
        vec_out[...] = small_ref[:, 0:width]
        for j in range(blocks):
            be_out[:, j * width : (j + 1) * width] = small_ref[be_row + j : be_row + j + 1, 0:width]
        tab_out[...] = d_table
        return

    share, bshare = width // n, buckets // n
    wide = blocks * width // n
    per = width // wide
    for f in range(n):
        value = jnp.concatenate(
            [
                d_table[:, f * bshare : (f + 1) * bshare],
                jnp.zeros((16, wide - bshare - share), f32),
                small_ref[:, f * share : (f + 1) * share],
            ],
            axis=1,
        )
        where = f % per * wide
        bias = small_ref[be_row + f // per : be_row + f // per + 1, where : where + wide]
        bias = jnp.broadcast_to(bias, (16, wide))
        block[f] = jnp.where(iota((16, wide), 0) == heads, bias, value)
    small = []
    for k, peer in enumerate(peers):
        dst = (spot.f + k + 1) % n
        small.append(send(block.at[dst], got.at[k], bss.at[k], brs.at[k], peer))
        small[k].start()
    beat()
    value = block[spot.f]
    for k, copy in enumerate(small):
        copy.wait_recv()
        value = value + got[k]
    reps[spot.rep] = value
    second = []
    for k, other in enumerate(others):
        mine = reps.at[spot.rep]
        second.append(send(mine, mine, bss.at[n - 1 + k], brs.at[n - 1 + k], other))
        second[k].start()
    beat()
    for copy in second:
        copy.wait_recv()
    small_out[...] = (reps[0] + reps[1]) + (reps[2] + reps[3])
    while waiting or active:
        beat()
    for job in jobs:
        job.finish()
    for copy in small + second:
        copy.wait_send()


def back(plan, kind, tokens, cot, wholes, vecs, saved, colsel, n, fast):
    labs, normed, mixed, middle, branch, qkv, probs, acts, slopes = saved
    rows, width = tokens.shape
    heads = plan.heads
    pairs = heads // 2
    blocks = acts.shape[0]
    sds = jax.ShapeDtypeStruct
    picks = image_selectors(plan)
    wt, wo, we, wr = wholes
    inputs = [kind, cot, vecs, labs, colsel, picks, middle, branch, normed, mixed, tokens]
    inputs += [acts, slopes, qkv, probs, wt, wo, we, wr]
    in_specs = [pl.BlockSpec(memory_space=pltpu.SMEM)] + [vmem_spec] * 5
    in_specs += [any_spec] * 3 + [vmem_spec] + [any_spec] * 9
    outs = [sds((rows, width), bf16), sds((rows, width), bf16)]
    out_specs = [any_spec] * 2
    if fast:
        outs += [sds(w.shape[2:], bf16) for w in wholes]
        outs += [sds((16, blocks * width // n), f32)]
        out_specs += [vmem_spec] * 5
    else:
        outs += [sds(w.shape, bf16) for w in wholes]
        outs += [sds((16, width), f32), sds((1, blocks * width), f32), sds((16, plan.buckets), f32)]
        out_specs += [any_spec] * 4 + [vmem_spec] * 3
    outs += [sds(probs.shape, bf16)]
    out_specs += [any_spec]
    row_tile = lambda dtype: pltpu.VMEM((rows, width), dtype)
    scratch = [
        pltpu.VMEM((3, 4, 2, width // 8, width), bf16),
        pltpu.VMEM((blocks, rows, width), bf16),
        pltpu.VMEM((2, rows, width), bf16),
        row_tile(f32),
        row_tile(f32),
        row_tile(f32),
        pltpu.VMEM((4, 2, blocks * width // 8, width), bf16),
        pltpu.VMEM((2, 4, 2, width // 8, width), bf16),
        pltpu.VMEM((3, 3, rows, 128), bf16),
        pltpu.VMEM((3, 2, rows, rows), bf16),
        pltpu.VMEM((2, rows, width), bf16),
        pltpu.VMEM((heads, plan.gl, plan.strip_l), f32),
        pltpu.VMEM((heads, 16, plan.strip_s), f32),
        pltpu.VMEM((heads, 1, 128), f32),
        pltpu.VMEM((16, width), f32),
        pltpu.SemaphoreType.DMA((4,)),
        pltpu.SemaphoreType.DMA((2 * blocks + 2,)),
        pltpu.SemaphoreType.DMA((3, 4)),
        pltpu.SemaphoreType.DMA((3,)),
        pltpu.SemaphoreType.DMA((1,)),
    ]
    kernel_params = dict(vmem_limit_bytes=vmem_bytes)
    if fast:
        wide = blocks * width // n
        for _ in range(12):
            scratch += Sum.buffers(n // 2, width)
        scratch += [
            pltpu.VMEM((n, 16, wide), f32),
            pltpu.VMEM((n - 1, 16, wide), f32),
            pltpu.VMEM((4, 16, wide), f32),
            pltpu.SemaphoreType.DMA((12 * Sum.sems,)),
            pltpu.SemaphoreType.DMA((12 * Sum.sems,)),
            pltpu.SemaphoreType.DMA((n + 2,)),
            pltpu.SemaphoreType.DMA((n + 2,)),
        ]
        kernel_params.update(collective_id=2, has_side_effects=True)
    result = pl.pallas_call(
        functools.partial(back_kernel, plan, n, fast, blocks),
        in_specs=in_specs,
        out_specs=out_specs,
        out_shape=outs,
        scratch_shapes=scratch,
        compiler_params=pltpu.CompilerParams(**kernel_params),
        name="back",
    )(*inputs)
    out, token_grad = result[:2]
    if fast:
        return out, token_grad, result[2:6], result[6]
    grads = [g.reshape(-1, g.shape[3]) for g in result[2:6]]
    sums, block = reduce_plain(grads, result[6], result[7], result[8], n)
    return out, token_grad, sums, block


def per_device(
    tokens,
    slot_kinds,
    small_index,
    large_index,
    first_gain,
    first_shift,
    triple_weight,
    query_bias,
    value_bias,
    bias_table,
    output_weight,
    output_bias,
    attend_scale,
    second_gain,
    second_shift,
    expand_weight,
    expand_bias,
    reduce_weight,
    reduce_bias,
    feed_scale,
    cotangent,
):
    _, rows, width = tokens.shape
    heads = bias_table.shape[2]
    buckets = bias_table.shape[1] * lax.axis_size("fsdp")
    plan = Plan(small_index.shape[0], large_index.shape[0], rows, heads, buckets)
    tokens, cotangent = tokens[0], cotangent[0]
    short = [
        first_gain,
        first_shift,
        query_bias,
        value_bias,
        output_bias,
        attend_scale,
        second_gain,
        second_shift,
        reduce_bias,
        feed_scale,
    ]
    n = width // first_gain.shape[1]
    fast = fast_shape(
        lax.axis_size("rep"), n, [w.shape[1] for w in (triple_weight, output_weight, reduce_weight)]
    )
    shards = [w[0] for w in (triple_weight, output_weight, expand_weight, reduce_weight)]
    shorts = short + [expand_bias, bias_table[0]]
    rowsel, colsel = plan.selectors()
    wholes, vecs, be, saved = front(
        plan, slot_kinds, tokens, large_index, rowsel, colsel, n, fast, shorts, shards
    )
    block_output, token_grad, sums, block = back(
        plan, slot_kinds, tokens, cotangent, wholes, vecs, saved, colsel, n, fast
    )
    dwt, dwo, dwe, dwr = sums
    share, bshare = first_gain.shape[1], bias_table.shape[1]
    row = lambda idx: block[idx : idx + 1, block.shape[1] - share :]
    full = lambda value: value.astype(f32)[None]
    return (
        block_output[None],
        token_grad[None],
        row(FIRST_GAIN),
        row(FIRST_SHIFT),
        full(dwt),
        row(QUERY_BIAS),
        row(VALUE_BIAS),
        block[:heads, :bshare].T[None],
        full(dwo),
        row(OUTPUT_BIAS),
        row(ATTEND_SCALE),
        row(SECOND_GAIN),
        row(SECOND_SHIFT),
        full(dwe),
        block[heads : heads + 1],
        full(dwr),
        row(REDUCE_BIAS),
        row(FEED_SCALE),
    )


def solution(mesh):
    rows = P(("rep", "fsdp"), None, None)
    vector = P(None, "fsdp")
    matrix = P(None, "fsdp", None)
    weights = (
        vector,
        vector,
        matrix,
        vector,
        vector,
        matrix,
        matrix,
        vector,
        vector,
        vector,
        vector,
        matrix,
        vector,
        matrix,
        vector,
        vector,
    )
    return jax.shard_map(
        per_device,
        mesh=mesh,
        in_specs=(rows, P(("rep", "fsdp")), P(), P()) + weights + (rows,),
        out_specs=(rows, rows) + weights,
        check_vma=False,
    )
```

```python
import functools

import jax
import jax.numpy as jnp
import numpy as np
from jax import lax
from jax.experimental import pallas as pl
from jax.experimental.pallas import tpu as pltpu
from jax.sharding import PartitionSpec as P

f32 = jnp.float32
bf16 = jnp.bfloat16
norm_eps = 1e-06
neg_fill = -1000000000.0
vmem_bytes = 60 << 20

NN = (((1,), (0,)), ((), ()))
NT = (((1,), (1,)), ((), ()))
TN = (((0,), (0,)), ((), ()))


def mm(left, right, dims=NN):
    return lax.dot_general(left, right, dims, preferred_element_type=f32)


def round_up(value, unit):
    return -(-value // unit) * unit


class Plan:
    def __init__(self, small_len, large_len, rows, heads, buckets):
        self.heads, self.buckets = heads, buckets
        self.rows = rows
        self.small_len, self.large_len = small_len, large_len
        self.gs = int(round((small_len - 1) ** 0.5))
        self.gl = int(round((large_len - 1) ** 0.5))
        gl, gs = self.gl, self.gs
        self.strip_l = round_up(2 * gl * gl, 128)
        self.strip_s = round_up(2 * gs * (2 * gs - 1) + gs, 128)
        self.line = 2 * self.strip_l
        self.lanes = self.line + 128
        self.pad_cols = round_up(2 * gs * gs + 1, 128)
        self.pad_rows = 16 * gs
        self.cls_col = 2 * gs * gs
        self.cls_row = gs

    def place(self, di, dj, limit):
        gl = self.gl
        good = (np.abs(di) < limit) & (np.abs(dj) < limit)
        row = 1 + gl * np.maximum(di, 0) + np.maximum(dj, 0)
        col = 1 + gl * np.maximum(-di, 0) + np.maximum(-dj, 0)
        return np.where(good, row, 0), np.where(good, col, 0), good

    def positions(self):
        gl, gs = self.gl, self.gs
        x = np.arange(self.strip_l)
        rows, cols, goods = [], [], []
        for parity in range(2):
            m = 2 * ((x + gl) // (2 * gl)) if parity == 0 else 2 * (x // (2 * gl)) + 1
            t = x - gl * m
            r, c, g = self.place(gl - m, -t, gl)
            rows.append(r), cols.append(c), goods.append(g)
        large = [np.concatenate(v) for v in (rows, cols, goods)]
        x = np.arange(self.strip_s)
        m = x // (2 * gs)
        t = x - 2 * gs * m - gs
        small = [np.resize(np.zeros(1, v.dtype), self.line) for v in large]
        for dst, src in zip(small, self.place(gs - 1 - m, -t, gs)):
            dst[: self.strip_s] = src
        tail_r, tail_c, tail_g = np.zeros(128, int), np.zeros(128, int), np.zeros(128, bool)
        tail_r[:3], tail_c[:3], tail_g[:3] = (0, 1, 0), (1, 0, 0), True
        out = []
        for base in (large, small):
            out.append([np.concatenate(v) for v in zip(base, (tail_r, tail_c, tail_g))])
        return out

    def selector_arrays(self):
        gs = self.gs
        rows = np.zeros((self.rows, self.pad_rows), np.float32)
        cols = np.zeros((self.pad_cols, self.rows), np.float32)
        for image in range(3):
            for tok in range(self.small_len):
                r = image * self.small_len + tok
                i, j = divmod(tok - 1, gs)
                rows[r, self.cls_row if tok == 0 else 16 * i + j] = 1
                cols[self.cls_col if tok == 0 else 2 * gs * i + j, r] = 1
        return rows, cols

    def selectors(self):
        rows, cols = self.selector_arrays()
        return jnp.asarray(rows, bf16), jnp.asarray(cols, bf16)


def iota(shape, dim):
    return lax.broadcasted_iota(jnp.int32, shape, dim)


def pick_plan(plan):
    out = []
    for r, c, good in plan.positions():
        down = good & ((r - 1) // plan.gl >= (c - 1) // plan.gl)
        key = np.where(down, r, c)
        sub = np.where(down, c, r) - 1
        valid = good.copy()
        valid[plan.line :] = False
        out.append(np.stack([key, sub, down.astype(int), valid.astype(int)]))
    return jnp.asarray(np.concatenate(out), jnp.int32)


def lane_chunks(lanes, size=512):
    return [(low, min(low + size, lanes)) for low in range(0, lanes, size)]


def read_labels(plan, is_large, idx_ref, pick_ref, lab_ref):
    size, gl = idx_ref.shape[0], plan.gl
    across = idx_ref[1 : 1 + gl, :]
    down = idx_ref[:, 1 : 1 + gl].astype(f32).T.astype(jnp.int32)
    sides = []
    for v in (across, down):
        sides += [(v >> 6).astype(f32), (v & 63).astype(f32)]
    sides = jnp.concatenate(sides, axis=0).astype(bf16)
    for low, high in lane_chunks(plan.line):
        lanes, count = slice(low, high), high - low
        key, sub, use_down, valid = [
            jnp.where(is_large, pick_ref[i : i + 1, lanes], pick_ref[4 + i : 5 + i, lanes])
            for i in range(4)
        ]
        hot = jnp.where(iota((size, count), 0) == key, 1.0, 0.0).astype(bf16)
        here = iota((gl, count), 0) == sub
        rows = mm(sides, hot)
        for digit in range(2):
            a = rows[digit * gl : (digit + 1) * gl]
            b = rows[(2 + digit) * gl : (3 + digit) * gl]
            found = jnp.where(here, jnp.where(use_down == 1, b, a), 0.0)
            found = jnp.sum(found, axis=0, keepdims=True).astype(jnp.int32)
            lab_ref[digit : digit + 1, lanes] = jnp.where(valid == 1, found, -1)
    lane = iota((1, 128), 1)
    tail = jnp.where(lane == 0, idx_ref[0:1, 1:2], -1)
    tail = jnp.where(lane == 1, idx_ref[1:2, 0:1], tail)
    tail = jnp.where(lane == 2, idx_ref[0:1, 0:1], tail)
    lab_ref[0:1, plan.line : plan.line + 128] = jnp.where(tail < 0, -1, tail >> 6)
    lab_ref[1:2, plan.line : plan.line + 128] = jnp.where(tail < 0, -1, tail & 63)


def table_lines(plan, tab, lab_ref, line_ref):
    count = tab.shape[1] // 64
    split = jnp.concatenate([tab[:, 64 * i : 64 * (i + 1)] for i in range(count)], axis=0)
    split = split.astype(bf16)
    for low, high in lane_chunks(plan.lanes):
        first, second = lab_ref[0:1, low:high], lab_ref[1:2, low:high]
        hot = jnp.where(iota((64, high - low), 0) == second, 1.0, 0.0).astype(bf16)
        rows = mm(split, hot)
        parts = [jnp.zeros((16, high - low), f32)] * 4
        for i in range(count):
            parts[i % 4] = jnp.where(first == i, rows[16 * i : 16 * (i + 1)], parts[i % 4])
        line_ref[:, low:high] = (parts[0] + parts[1]) + (parts[2] + parts[3])


def table_from_lines(plan, line_of, lab_ref, buckets):
    count = buckets // 64
    total = jnp.zeros((32 * count, 64), f32)
    for chunk in range(plan.lanes // 128):
        lanes = slice(chunk * 128, (chunk + 1) * 128)
        first, second = lab_ref[0:1, lanes], lab_ref[1:2, lanes]
        hot = jnp.where(iota((64, 128), 0) == second, 1.0, 0.0).astype(bf16)
        part = line_of(chunk)
        high = part.astype(bf16)
        low = (part - high.astype(f32)).astype(bf16)
        both = jnp.concatenate([high, low], axis=0)
        stack = [jnp.where(first == i, both, jnp.zeros_like(both)) for i in range(count)]
        total = total + mm(jnp.concatenate(stack, axis=0), hot, NT)
    pieces = []
    for i in range(count):
        pieces.append(total[32 * i : 32 * i + 16] + total[32 * i + 16 : 32 * i + 32])
    return jnp.concatenate(pieces, axis=1)


def segments(plan, is_large, ids):
    n = plan.small_len
    small = jnp.where(ids >= n, 1, 0) + jnp.where(ids >= 2 * n, 1, 0) + jnp.where(ids >= 3 * n, 1, 0)
    return jnp.where(is_large, jnp.where(ids < plan.large_len, 0, 3), small)


def line_of_head(ref, h):
    return jnp.sum(jnp.where(iota((16, 1), 0) == h, ref[...], 0.0), axis=0, keepdims=True)


def large_strip(plan, line):
    gl, span = plan.gl, plan.strip_l
    rolled = []
    for parity in range(2):
        part = jnp.broadcast_to(line[:, parity * span : (parity + 1) * span], (gl, span))
        rolled.append(pltpu.roll(part, 0, axis=1, stride=1, stride_axis=0))
    odd = (iota((1, span), 1) + span - 1) % span // gl % 2
    odd = jnp.where(iota((gl, 1), 0) == 0, 1 - odd, odd)
    strip = jnp.where(odd == 1, rolled[1], rolled[0])
    return jnp.concatenate([strip, strip[:, :128]], axis=1)


def band_move(plan, a):
    return plan.gl * (plan.gl - a)


def small_padded(plan, line, tail):
    gs, span = plan.gs, plan.strip_s
    line = jnp.broadcast_to(line[:, 0:span], (16, span))
    strip = pltpu.roll(line, 0, axis=1, stride=1, stride_axis=0)
    col = iota((1, plan.pad_cols), 1)
    is_col = col == plan.cls_col
    is_row = iota((16, 1), 0) == plan.cls_row
    bands = []
    for i in range(gs):
        move = 2 * gs * (gs - 1 - i) + gs
        band = pltpu.roll(strip, (span - move) % span, axis=1)[:, : plan.pad_cols]
        band = jnp.where(is_col, tail[:, 1:2], band)
        if i == 0:
            edge = jnp.where(is_col, tail[:, 2:3], tail[:, 0:1])
            band = jnp.where(is_row, edge, band)
        bands.append(band)
    return jnp.concatenate(bands, axis=0).astype(bf16)


def small_blocks(plan, line, tail, pick, colsel):
    rows = plan.rows
    wide = round_up(rows, 128)
    cols = mm(small_padded(plan, line, tail), colsel[:, 0:256]).astype(bf16)
    out = []
    for image, ((r0, r1), (l0, _)) in enumerate(image_rows(plan)):
        start = 256 * image
        block = mm(pick[:, start : start + r1 - r0], cols, TN)
        shift = image * plan.small_len - l0
        last = l0 + round_up(shift + plan.small_len, 128)
        if last - l0 > 256:
            block = jnp.concatenate([block, jnp.zeros((r1 - r0, last - l0 - 256), f32)], axis=1)
        if shift:
            block = pltpu.roll(block, shift, axis=1)
        parts = [block]
        if l0:
            parts.insert(0, jnp.zeros((r1 - r0, l0), f32))
        if last < wide:
            parts.append(jnp.zeros((r1 - r0, wide - last), f32))
        out.append((r0, r1, jnp.concatenate(parts, axis=1)))
    return out


def bias_head(plan, is_large, line_ref, pick, colsel, h, out_ref):
    gl, rows = plan.gl, plan.rows
    wide = round_up(rows, 128)
    line = line_of_head(line_ref, h)
    tail = line[:, plan.line : plan.line + 128]
    blocks = small_blocks(plan, line, tail, pick, colsel)
    strip = large_strip(plan, line)
    span = strip.shape[1]
    col = iota((1, wide), 1)
    seg_col = segments(plan, is_large, col)
    bands = -(-rows // gl)
    for pair in range(-(-bands // 2)):
        first = 2 * gl * pair
        count = min(2 * gl, rows - first)
        parts = []
        for a in range(2 * pair, 2 * pair + 2):
            if a >= bands:
                continue
            move = band_move(plan, a)
            low = move // 128 * 128
            piece = strip[:, low : min(low + wide + 128, span)]
            if piece.shape[1] < wide + 128:
                piece = jnp.concatenate(
                    [piece, jnp.zeros((gl, wide + 128 - piece.shape[1]), f32)], axis=1
                )
            turn = (wide + 128 - (move - low)) % (wide + 128)
            parts.append((pltpu.roll(piece, turn, axis=1) if turn else piece)[:, :wide])
        block = (jnp.concatenate(parts, axis=0) if len(parts) > 1 else parts[0])[:count]
        row = iota((count, 1), 0) + first
        edge = jnp.where(col[:, :128] == 0, tail[:, 1:2], block[:, :128])
        block = jnp.concatenate([edge, block[:, 128:]], axis=1)
        if first == 0:
            block = jnp.where(row == 0, jnp.where(col == 0, tail[:, 2:3], tail[:, 0:1]), block)
        if first + count > plan.large_len:
            block = jnp.where(row < plan.large_len, block, 0.0)
        small = None
        for r0, r1, value in blocks:
            low, high = max(first, r0), min(first + count, r1)
            if low >= high:
                continue
            part = [value[low - r0 : high - r0]]
            if low > first:
                part.insert(0, jnp.zeros((low - first, wide), f32))
            if high < first + count:
                part.append(jnp.zeros((first + count - high, wide), f32))
            part = jnp.concatenate(part, axis=0) if len(part) > 1 else part[0]
            small = part if small is None else small + part
        block = jnp.where(is_large, block, small)
        block = jnp.where(segments(plan, is_large, row) == seg_col, block, neg_fill)
        out_ref[h, first : first + count, :] = block[:, :rows].astype(bf16)


def norm_stats(values):
    mean = jnp.mean(values, axis=1, keepdims=True)
    centred = values - mean
    var = jnp.mean(centred * centred, axis=1, keepdims=True)
    inv = lax.rsqrt(var + norm_eps)
    return centred * inv, inv


def norm_back(d_out, gain, normal, inv):
    d_normal = d_out * gain
    mean_d = jnp.mean(d_normal, axis=1, keepdims=True)
    mean_dn = jnp.mean(d_normal * normal, axis=1, keepdims=True)
    return inv * (d_normal - mean_d - normal * mean_dn)


def rows_sum(values):
    return jnp.sum(values, axis=0, keepdims=True)


def gelu_parts(v):
    size = jnp.abs(v)
    bell = jnp.exp(-0.5 * v * v)
    t = 1.0 / (1.0 + (0.3275911 * 0.7071067811865476) * size)
    poly = t * (
        0.127414796
        + t * (-0.142248368 + t * (0.7107068705 + t * (-0.7265760135 + t * 0.5307027145)))
    )
    tail = poly * bell
    phi = jnp.where(v < 0, tail, 1.0 - tail)
    return v * phi, phi + v * bell * 0.3989422804014327


BE_ROW = 10
(
    FIRST_GAIN,
    FIRST_SHIFT,
    QUERY_BIAS,
    VALUE_BIAS,
    OUTPUT_BIAS,
    ATTEND_SCALE,
    SECOND_GAIN,
    SECOND_SHIFT,
    REDUCE_BIAS,
    FEED_SCALE,
) = range(10)


def vec(ref, idx):
    return ref[idx : idx + 1, :]


def half_mask(rows):
    return iota((rows, 128), 1) < 64


class Spot:
    def __init__(self, n):
        self.n, self.levels = n, n // 2
        self.rep, self.f = lax.axis_index("rep"), lax.axis_index("fsdp")
        self.half, self.core = self.rep // 2, self.rep % 2
        self.level, self.side = self.f // 2, self.f % 2

    def at(self, rep=None, f=None):
        return {"rep": self.rep if rep is None else rep, "fsdp": self.f if f is None else f}

    def sibling(self):
        return self.at(rep=2 * self.half + 1 - self.core)

    def across(self):
        return self.at(rep=2 * (1 - self.half) + self.core)

    def beside(self):
        return self.at(f=2 * self.level + 1 - self.side)

    def along(self, step):
        return self.at(f=2 * ((self.level + step) % self.levels) + self.side)

    def from_along(self, step, side=None):
        side = self.side if side is None else side
        return 2 * ((self.level + self.levels - step) % self.levels) + side


MESH = pl.DeviceIdType.MESH


def greet(devices, count):
    barrier = pltpu.get_barrier_semaphore()
    for device in devices:
        pl.semaphore_signal(barrier, inc=1, device_id=device, device_id_type=MESH)
    pl.semaphore_wait(barrier, count)


def send(src, dst, send_sem, recv_sem, device):
    return pltpu.make_async_remote_copy(
        src_ref=src,
        dst_ref=dst,
        send_sem=send_sem,
        recv_sem=recv_sem,
        device_id=device,
        device_id_type=MESH,
    )


def fast_shape(reps, n, shard_rows):
    return reps == 4 and n == 8 and all(rows % 96 == 0 for rows in shard_rows)


def spread_block(refs, block_ref):
    *vectors, be_ref, table_ref = refs
    heads, share = table_ref.shape
    lanes = block_ref.shape[1]
    table = jnp.concatenate([table_ref[...].astype(f32), jnp.zeros((16 - heads, share), f32)], axis=0)
    width = vectors[0].shape[1]
    rows = [v[...].astype(f32) for v in vectors]
    rows.append(jnp.zeros((16 - len(rows), width), f32))
    block = jnp.concatenate(
        [table, jnp.zeros((16, lanes - share - width), f32), jnp.concatenate(rows, axis=0)], axis=1
    )
    wide = jnp.broadcast_to(be_ref[...].astype(f32), (16, lanes))
    block_ref[...] = jnp.where(iota((16, lanes), 0) == heads, wide, block).astype(bf16)


smem_spec = pl.BlockSpec(memory_space=pltpu.SMEM)
any_spec = pl.BlockSpec(memory_space=pl.ANY)
vmem_spec = pl.BlockSpec(memory_space=pltpu.VMEM)


def add16(left, right):
    return (left.astype(f32) + right.astype(f32)).astype(bf16)


def gather_plain(shorts, shards, n):
    gather = lambda value, axis: lax.all_gather(value, "fsdp", axis=axis, tiled=True)
    vecs = gather(jnp.concatenate(shorts[:10], axis=0), 1).astype(f32)
    vecs = jnp.pad(vecs, ((0, 6), (0, 0)))
    table = gather(shorts[11], 1)
    table = jnp.pad(table, ((0, 16 - table.shape[0]), (0, 0)))
    return [gather(w, 0) for w in shards], vecs, gather(shorts[10], 1).astype(f32), table


def reduce_plain(grads, vec_sums, be_sums, table_sums, n):
    def whole_sum(value):
        value = lax.psum_scatter(value, "fsdp", scatter_dimension=0, tiled=True)
        return lax.psum(value, "rep")

    sums = lax.psum((vec_sums, be_sums, table_sums), ("rep", "fsdp"))
    me = lax.axis_index("fsdp")
    cut = lambda v: lax.dynamic_slice_in_dim(v, me * (v.shape[1] // n), v.shape[1] // n, axis=1)
    vec_part, be_part, table_part = [cut(v) for v in sums]
    wide = be_part.shape[1]
    space = max(wide - vec_part.shape[1] - table_part.shape[1], 0)
    body = jnp.concatenate([table_part, jnp.zeros((16, space), f32), vec_part], axis=1)
    block = jnp.where(jnp.arange(16)[:, None] == 12, jnp.pad(be_part, ((0, 0), (0, body.shape[1] - wide))), body)
    return [whole_sum(g) for g in grads], block


class Piece:
    sems = 8

    def __init__(self, spot, shard, whole, row, col, cols, ss, rs, base):
        self.level, self.side = spot.level, spot.side
        levels = spot.levels
        part, q = 48, 16
        start = row + spot.core * part
        cut = pl.ds(col, cols)
        rows = lambda first, size: pl.ds(pl.multiple_of(first, 16), size)
        plane = rows(start + spot.half * q, 2 * q)
        outer = rows(start + spot.half * 2 * q, q)
        core_rows = rows(start, part)
        side = spot.side

        def copy(idx, src, dst, device):
            return send(src, dst, ss.at[base + idx], rs.at[base + idx], device)

        own = shard.at[plane, cut]
        here = whole.at[spot.level, side, plane, cut]
        self.local = pltpu.make_async_copy(own, here, ss.at[base + levels + 3])
        self.z = [copy(step - 1, own, here, spot.along(step)) for step in range(1, levels)]
        column = whole.at[:, side, plane, cut]
        self.y = copy(levels - 1, column, column, spot.beside())
        near = whole.at[:, side, outer, cut]
        far = whole.at[:, 1 - side, outer, cut]
        self.x = [
            copy(levels, near, near, spot.across()),
            copy(levels + 1, far, far, spot.across()),
        ]
        done = whole.at[:, :, core_rows, cut]
        self.c = copy(levels + 2, done, done, spot.sibling())

    def start(self):
        self.local.start()
        for copy in self.z:
            copy.start()

    def after_z(self):
        self.local.wait()
        for copy in self.z:
            copy.wait_recv()
        self.y.start()
        self.x[0].start()

    def after_y(self):
        self.y.wait_recv()
        self.x[1].start()

    def after_x(self):
        self.x[0].wait_recv()
        self.x[1].wait_recv()
        self.c.start()

    def after_c(self):
        self.c.wait_recv()

    def finish(self):
        for copy in self.z + [self.y, self.c] + self.x:
            copy.wait_send()


def piece_cuts(shard_shapes):
    cuts = []
    for idx, (rows, cols) in enumerate(shard_shapes):
        for row in range(0, rows, 96):
            tile = 384 if idx == 0 else 768
            for col in range(0, cols, tile):
                cuts.append((idx, row, col, tile))
    return cuts


def image_rows(plan):
    out = []
    for image in range(3):
        first, last = image * plan.small_len, (image + 1) * plan.small_len
        rows = (first // 16 * 16, round_up(last, 16))
        lanes = (first // 128 * 128, min(round_up(last, 128), plan.rows))
        out.append((rows, lanes))
    return out


def image_selectors(plan):
    rows, _ = plan.selector_arrays()
    out = []
    for image, ((low, high), _) in enumerate(image_rows(plan)):
        part = rows.copy()
        part[: image * plan.small_len] = 0
        part[(image + 1) * plan.small_len :] = 0
        out.append(np.pad(part[low:high].T, ((0, 0), (0, 256 - (high - low)))))
    return jnp.asarray(np.concatenate(out, axis=1), bf16)


def fold_head(plan, ds_ref, pick, colsel, large_ref, small_ref, tail_ref, h, is_large):
    gl, gs, rows = plan.gl, plan.gs, plan.rows
    wide = round_up(rows, 128)
    width = plan.strip_l + 128
    bands = -(-rows // gl)
    total = jnp.zeros((gl, width), f32)
    side = jnp.zeros((2 * gl, 128), f32)
    for pair in range(-(-bands // 2)):
        first = 2 * gl * pair
        count = min(2 * gl, rows - first)
        block = ds_ref[first : first + count, :].astype(f32)
        block = jnp.concatenate([block, jnp.zeros((count, wide - rows), f32)], axis=1)
        if count < 2 * gl:
            block = jnp.concatenate([block, jnp.zeros((2 * gl - count, wide), f32)], axis=0)
        if pair == 0:
            row = iota((2 * gl, 1), 0)
            top_row = jnp.where(row == 0, block, 0.0)
            block = jnp.where(row == 0, 0.0, block)
        side = side + block[:, :128]
        block = jnp.concatenate(
            [jnp.where(iota((1, 128), 1) == 0, 0.0, block[:, :128]), block[:, 128:]], axis=1
        )
        for half in range(2):
            a = 2 * pair + half
            if a >= bands:
                continue
            move = band_move(plan, a)
            low = move // 128 * 128
            piece = block[half * gl : (half + 1) * gl]
            if move > low:
                piece = jnp.concatenate([piece, jnp.zeros((gl, 128), f32)], axis=1)
                piece = pltpu.roll(piece, move - low, axis=1)
            piece = piece[:, : width - low]
            high = low + piece.shape[1]
            parts = [total[:, low:high] + piece]
            if low:
                parts.insert(0, total[:, :low])
            if high < width:
                parts.append(total[:, high:])
            total = jnp.concatenate(parts, axis=1) if len(parts) > 1 else parts[0]
    large_ref[h] = jnp.concatenate(
        [total[:, :128] + total[:, plan.strip_l :], total[:, 128 : plan.strip_l]], axis=1
    )
    lane = iota((1, wide), 1)
    full = lambda v: jnp.sum(jnp.sum(v, axis=0, keepdims=True), axis=1, keepdims=True)
    corner = full(jnp.where(lane == 0, top_row, 0.0))
    top = full(jnp.where(lane == 0, 0.0, top_row))
    side = full(jnp.where(iota((1, 128), 1) == 0, side, 0.0))

    gathered = jnp.zeros((plan.pad_rows, 256), f32)
    for image, ((r0, r1), (l0, l1)) in enumerate(image_rows(plan)):
        block = ds_ref[r0:r1, l0:l1]
        shift = image * plan.small_len - l0
        if shift:
            pad = round_up(l1 - l0, 128) - (l1 - l0)
            block = block.astype(f32)
            if pad:
                block = jnp.concatenate([block, jnp.zeros((r1 - r0, pad), f32)], axis=1)
            block = pltpu.roll(block, block.shape[1] - shift, axis=1)[:, :256].astype(bf16)
        start = 256 * image
        gathered = gathered + mm(pick[:, start : start + r1 - r0], block)
    high = gathered.astype(bf16)
    low = (gathered - high.astype(f32)).astype(bf16)
    select = colsel[:, 0:256]
    padded = mm(high, select, NT) + mm(low, select, NT)
    span = plan.strip_s
    col = iota((1, plan.pad_cols), 1)
    row = iota((16, 1), 0)
    acc = jnp.zeros((16, span), f32)
    edge = jnp.zeros((16, plan.pad_cols), f32)
    for i in range(gs):
        band = padded[16 * i : 16 * (i + 1)]
        if i == 0:
            top_s = jnp.where(row == plan.cls_row, band, 0.0)
            band = jnp.where(row == plan.cls_row, 0.0, band)
        edge = edge + band
        band = jnp.where(col < plan.cls_col, band, 0.0)
        band = jnp.concatenate([band, jnp.zeros((16, span - plan.pad_cols), f32)], axis=1)
        acc = acc + pltpu.roll(band, 2 * gs * (gs - 1 - i) + gs, axis=1)
    small_ref[h] = acc
    corner_s = full(jnp.where(col == plan.cls_col, top_s, 0.0))
    top_s = full(jnp.where(col < plan.cls_col, top_s, 0.0))
    side_s = full(jnp.where(col == plan.cls_col, edge, 0.0))
    lane = iota((1, 128), 1)
    picks = [(top, top_s), (side, side_s), (corner, corner_s)]
    tail = jnp.zeros((1, 128), f32)
    for i, (a, b) in enumerate(picks):
        tail = jnp.where(lane == i, jnp.where(is_large, a, b), tail)
    tail_ref[h] = tail


def fold_lines(plan, large_ref, small_ref, tail_ref, is_large):
    gl, heads, span = plan.gl, plan.heads, plan.strip_l
    odd = (iota((1, span), 1) + span - 1) % span // gl % 2
    lines = [None, None]
    for i in reversed(range(gl)):
        row = large_ref[:, i, :]
        for parity in range(2):
            want = parity if i else 1 - parity
            part = jnp.where(odd == want, row, 0.0)
            if lines[parity] is not None:
                part = part + pltpu.roll(lines[parity], span - 1, axis=1)
            lines[parity] = part
    small = None
    for i in reversed(range(16)):
        part = small_ref[:, i, :]
        small = part if small is None else part + pltpu.roll(small, plan.strip_s - 1, axis=1)
    small = jnp.concatenate([small, jnp.zeros((heads, plan.line - plan.strip_s), f32)], axis=1)
    line = jnp.where(is_large, jnp.concatenate(lines, axis=1), small)
    tail = tail_ref[:, 0, :]
    line = jnp.concatenate([line, tail], axis=1)
    return jnp.concatenate([line, jnp.zeros((16 - heads, plan.lanes), f32)], axis=0)


class Sum:
    sems = 9

    def __init__(self, spot, grad, out, row, cut, bufs, ss, rs, base):
        self.spot, self.grad = spot, grad
        self.out = out
        self.row, self.cut = row, cut
        self.acc, self.got_x, self.got_y, self.got_z, self.total, self.got_f = bufs
        half, core, side, level, levels = spot.half, spot.core, spot.side, spot.level, spot.levels
        q, part = 16, 48
        rows = lambda first, size: pl.ds(pl.multiple_of(first, 16), size)
        self.rows = rows
        self.plane = rows(half * q, 2 * q)
        self.mine = rows(half * 2 * q, q)
        self.own = rows(core * part, part)
        self.sent = self.joined = False

        def copy(idx, src, dst, device):
            return send(src, dst, ss.at[base + idx], rs.at[base + idx], device)

        acc = self.acc
        self.c = copy(0, grad.at[:, :, rows((1 - core) * part, part)], acc, spot.sibling())
        self.x = copy(1, acc.at[:, :, rows((1 - half) * 2 * q, q)], self.got_x, spot.across())
        self.y = copy(2, acc.at[:, 1 - side, self.plane], self.got_y, spot.beside())
        self.z = []
        for step in range(1, levels):
            src = acc.at[(level + step) % levels, side, self.plane]
            self.z.append(copy(4 + step, src, self.got_z.at[step - 1], spot.along(step)))
        self.f = copy(3, self.total, self.got_f, spot.across())
        mine = out.at[rows(row + core * part, part), cut]
        self.last = copy(4, mine, mine, spot.sibling())

    @staticmethod
    def buffers(levels, cols):
        shapes = [
            (levels, 2, 48, cols),
            (levels, 2, 16, cols),
            (levels, 32, cols),
            (levels - 1, 32, cols),
            (32, cols),
            (32, cols),
        ]
        return [pltpu.VMEM(shape, bf16) for shape in shapes]

    def start(self):
        self.c.start()

    def free(self):
        self.join()
        if not self.sent:
            self.c.wait_send()
            self.sent = True

    def stage(self, k):
        getattr(self, ("go", "after_x", "after_y", "after_z", "after_f", "after_last")[k])()

    def join(self):
        if self.joined:
            return
        self.joined = True
        self.c.wait_recv()

        @pl.loop(0, self.acc.shape[0])
        def _(level):
            for side in range(2):
                own = self.grad[level, side, self.own]
                self.acc[level, side] = add16(self.acc[level, side], own)

    def go(self):
        self.join()
        self.x.start()

    def after_x(self):
        self.x.wait_recv()

        @pl.loop(0, self.acc.shape[0])
        def _(level):
            for side in range(2):
                mine = self.acc[level, side, self.mine]
                self.acc[level, side, self.mine] = add16(mine, self.got_x[level, side])

        self.y.start()

    def after_y(self):
        side = self.spot.side
        self.y.wait_recv()

        @pl.loop(0, self.acc.shape[0])
        def _(level):
            mine = self.acc[level, side, self.plane]
            self.acc[level, side, self.plane] = add16(mine, self.got_y[level])

        for copy in self.z:
            copy.start()

    def after_z(self):
        for copy in self.z:
            copy.wait_recv()
        value = self.acc[self.spot.level, self.spot.side, self.plane].astype(f32)
        for k in range(len(self.z)):
            value = value + self.got_z[k].astype(f32)
        self.total[...] = value.astype(bf16)
        self.f.start()

    def after_f(self):
        q, half = 16, self.spot.half
        base = self.row + self.spot.core * 48
        rows = self.rows
        total, got, out, cut = self.total, self.got_f, self.out, self.cut
        self.f.wait_recv()
        out[rows(base + half * 2 * q, q), cut] = total[rows(half * q, q)]
        both = add16(total[rows((1 - half) * q, q)], got[rows(half * q, q)])
        out[rows(base + q, q), cut] = both
        out[rows(base + (1 - half) * 2 * q, q), cut] = got[rows((1 - half) * q, q)]
        self.last.start()

    def after_last(self):
        self.last.wait_recv()

    def finish(self):
        self.free()
        for copy in [self.x, self.y, self.f, self.last] + self.z:
            copy.wait_send()


ADMIT, HOLD = 2, 2


class Queue:
    def __init__(self):
        self.waiting, self.active, self.beats, self.last = [], [], 0, -9

    def add(self, job):
        self.waiting.append([job, 0])
        job.start()

    def beat(self, hold=None):
        hold = HOLD if hold is None else hold
        self.beats += 1
        for entry in self.waiting:
            if entry[1] >= hold - 1:
                entry[0].join()
            entry[1] += 1
        for entry in list(self.active):
            entry[1] += 1
            if entry[1] >= hold:
                entry[1] = 0
                entry[2] += 1
                entry[0].stage(entry[2])
                if entry[2] == 5:
                    self.active.remove(entry)
        admit = ADMIT if hold > 1 else 1
        if self.waiting and self.waiting[0][0].joined and self.beats - self.last >= admit:
            self.last = self.beats
            job, _ = self.waiting.pop(0)
            self.active.append([job, 0, 0])
            job.stage(0)

    def drain(self):
        while self.waiting or self.active:
            self.beat(1)


def layer_kernel(plan, n, fast, cuts, blocks, *refs):
    refs = list(refs)
    take = lambda count: [refs.pop(0) for _ in range(count)]
    kind_ref, tok_in, cot_in, idx_in, pick_ref, colsel_ref, image_ref = take(7)
    if fast:
        shorts, shards = take(12), take(4)
    else:
        vec_in, be_in, tab_in = take(3)
        wholes = take(4)
    out_ref, tok_out = take(2)
    sum_wt, sum_wo, sum_we, sum_wr = take(4)
    if fast:
        (small_out,) = take(1)
        wholes = take(4)
    else:
        vec_out, be_out, tab_out = take(3)
    normed_out, branch_out, qkv_out, probs_out, slope_out, ds_out = take(6)
    vec_ref, be_ref, lab_ref, act_ref, slope_ref, middle_ref, pair_ref, mixed_ref, small_ref = take(9)
    load_sems, save_sems, tile_sems, slope_sems, late_sems, pair_sems, ds_sems, stage_sems = take(8)
    wt_in, wo_in, we_in, wr_in = wholes
    is_large = kind_ref[0] == 1
    heads, rows = plan.heads, plan.rows
    pairs = heads // 2
    width = tok_in.shape[1]
    eighth = width // 8
    matrix = lambda ref: ref[...].reshape(width, width)
    half_ref, dfeed_ref = pair_ref.at[0], pair_ref.at[1]
    branch_ref, late_ref, cot_ref = act_ref.at[0], dfeed_ref, act_ref.at[1]
    dtri = [act_ref.at[1 + j] for j in range(3)]
    dmix_ref, tok_ref = slope_ref.at[0], slope_ref.at[1]

    def fetch(src, dst, sem):
        copy = pltpu.make_async_copy(src, dst, sem)
        copy.start()
        return copy

    saves = []

    def save(src, dst):
        copy = fetch(src, dst, save_sems.at[len(saves)])
        saves.append(copy)
        return copy

    queue = Queue()
    jobs, pieces = [], []
    if fast:
        bufs = take(6 * (blocks + blocks + 4))
        short, shorts_got, block, got, reps = take(5)
        gss, grs, ass, ars, rss, rrs, bss, brs = take(8)
        spot = Spot(n)
        peers = [spot.at(f=(spot.f + k) % n) for k in range(1, n)]
        others = [spot.at(rep=(spot.rep + k) % 4) for k in range(1, 4)]
        greet(peers + others, n + 2)
        for idx, row, col, cols in cuts:
            base = len(pieces) * Piece.sems
            pieces.append(Piece(spot, shards[idx], wholes[idx], row, col, cols, gss, grs, base))
        spread_block(shorts, short)
        small = []
        for k, peer in enumerate(peers):
            small.append(send(short, shorts_got.at[spot.f], ass.at[k], ars.at[k], peer))
            small[k].start()
        pieces[0].start()
        pieces[1].start()
        shorts_got[spot.f] = short[...]


    def forward(line_ref, heads_ref, qkv_ref, wt_ref, wo_ref, we_ref, idx_ref, tok, normed_ref):
        idx_copy = fetch(idx_in, idx_ref, late_sems.at[0])
        tok_copy = fetch(tok_in, tok, late_sems.at[1])
        loads = []
        for src, ref, span in zip((wt_in, wo_in, we_in), (wt_ref, wo_ref, we_ref), (384, width, width)):
            for col in range(0, src.shape[3], span):
                dst = ref.at[col // width, :, :, :, pl.ds(col % width, span)]
                view = src.at[:, :, :, pl.ds(col, span)]
                loads.append(pltpu.make_async_copy(view, dst, load_sems.at[len(loads)]))
        wt_loads, wo_load, we_loads = loads[: 6], loads[6], loads[7:]
        if not fast:
            for load in loads:
                load.start()

        def step(k):
            gather_step(k)
            if fast and 0 <= k - 3 < len(loads):
                loads[k - 3].start()

        idx_copy.wait()
        read_labels(plan, is_large, idx_ref, pick_ref, lab_ref)
        if fast:
            for copy in small:
                copy.wait()
            share, bshare = shorts[0].shape[1], shorts[11].shape[1]
            tab = []
            for f in range(n):
                part = shorts_got[f].astype(f32)
                wide = part.shape[1]
                vec_ref[:, f * share : (f + 1) * share] = part[:, wide - share :]
                tab.append(part[:, :bshare])
                be_ref[:, f * wide : (f + 1) * wide] = part[heads : heads + 1, :]
            tab = jnp.concatenate(tab, axis=1)
        else:
            vec_ref[...] = vec_in[...]
            be_ref[...] = be_in[...]
            tab = tab_in[...]
        table_lines(plan, tab, lab_ref, line_ref)
        step(0)
        tok_copy.wait()
        normal, _ = norm_stats(tok[...].astype(f32))
        normed = normal * vec(vec_ref, FIRST_GAIN) + vec(vec_ref, FIRST_SHIFT)
        normed_ref[...] = normed.astype(bf16)
        save(normed_ref, normed_out)
        step(1)
        for group in range(heads // 2):

            @pl.loop(2 * group, 2 * group + 2)
            def _(h):
                bias_head(plan, is_large, line_ref, image_ref, colsel_ref, h, heads_ref)

            step(2 + group)

        step(8)
        normed = normed_ref[...]
        for j in range(3):
            wt_loads[2 * j].wait()
            wt_loads[2 * j + 1].wait()
            triple = mm(normed, matrix(wt_ref.at[j]))
            if j == 0:
                triple = triple + vec(vec_ref, QUERY_BIAS)
            if j == 2:
                triple = triple + vec(vec_ref, VALUE_BIAS)
            triple = triple.astype(bf16)
            if j == 0:
                triple = triple * jnp.array(0.125, bf16)
            for p in range(pairs):
                qkv_ref[j * pairs + p] = triple[:, 128 * p : 128 * (p + 1)]
        save(qkv_ref, qkv_out)
        step(9)

        def attend_pair(p):
            q, k, v = qkv_ref[p], qkv_ref[pairs + p], qkv_ref[2 * pairs + p]
            lower = half_mask(rows)
            mixed = []
            for t in range(2):
                keep = lower if t == 0 else ~lower
                scores = mm(jnp.where(keep, q, jnp.zeros_like(q)), k, NT)
                scores = scores + heads_ref[2 * p + t].astype(f32)
                top = jnp.max(scores, axis=1, keepdims=True)
                exps = jnp.exp(scores - top)
                total = jnp.sum(exps, axis=1, keepdims=True)
                probs = (exps * (1.0 / total)).astype(bf16)
                heads_ref[2 * p + t] = probs
                mixed.append(mm(probs, v))
            mixed_ref[p] = jnp.where(lower, mixed[0], mixed[1]).astype(bf16)

        share_of = pairs // 3
        for group in range(3):

            @pl.loop(group * share_of, (group + 1) * share_of)
            def _(p):
                attend_pair(p)

            cut = pl.ds(group * 2 * share_of, 2 * share_of)
            save(heads_ref.at[cut], probs_out.at[cut])
            step(10 + group)

        wo_load.wait()
        mixed = jnp.concatenate([mixed_ref[p] for p in range(pairs)], axis=1)
        branch = mm(mixed, matrix(wo_ref.at[0])) + vec(vec_ref, OUTPUT_BIAS)
        saves[0].wait()
        normed_ref[...] = branch.astype(bf16)
        save(normed_ref, branch_out)
        middle = tok[...].astype(f32) + vec(vec_ref, ATTEND_SCALE) * branch
        middle_ref[...] = middle
        normal, _ = norm_stats(middle)
        second = normal * vec(vec_ref, SECOND_GAIN) + vec(vec_ref, SECOND_SHIFT)
        half_ref[...] = second.astype(bf16)
        slope_saves = []
        for j in range(blocks):
            if j == blocks - 2:
                step(13)
            we_loads[j].wait()
            pre = mm(half_ref[...], matrix(we_ref.at[j])) + be_ref[:, j * width : (j + 1) * width]
            value, slope = gelu_parts(pre)
            act_ref[j] = value.astype(bf16)
            if j >= 2:
                slope_saves[j - 2].wait()
            slope_ref[j % 2] = slope.astype(bf16)
            slope_saves.append(fetch(slope_ref.at[j % 2], slope_out.at[j], slope_sems.at[j % 2]))
        for copy in slope_saves[-2:]:
            copy.wait()
        for copy in saves[1:]:
            copy.wait()

    def gather_step(k):
        for back, action in enumerate(("after_z", "after_y", "after_x", "after_c")):
            if 0 <= k - back < len(pieces):
                getattr(pieces[k - back], action)()
                if back == 0 and k + 2 < len(pieces):
                    pieces[k + 2].start()

    pl.run_scoped(
        forward,
        pltpu.VMEM((16, plan.lanes), f32),
        pltpu.VMEM((heads, rows, rows), bf16),
        pltpu.VMEM((3 * pairs, rows, 128), bf16),
        pltpu.VMEM((3, 4, 2, eighth, width), bf16),
        pltpu.VMEM((1, 4, 2, eighth, width), bf16),
        pltpu.VMEM((blocks, 4, 2, eighth, width), bf16),
        pltpu.VMEM(idx_in.shape, jnp.int32),
        pltpu.VMEM((rows, width), bf16),
        pltpu.VMEM((rows, width), bf16),
    )


    def backward(
        tile_ref, feed_ref, dsec_ref, gwr_ref, stage_ref, qkv_ref, probs_ref, large_ref, strip_ref, tail_ref
    ):
        order = []
        for j in range(blocks):
            order += [(wr_in, j), (we_in, j)]
        order += [(wo_in, 0), (wt_in, 0), (wt_in, 1), (wt_in, 2)]
        tiles = []
        for i, (src, j) in enumerate(order):
            slot = i % 3
            if src is wr_in:
                view, dst = src.at[j], tile_ref.at[slot].reshape(2, 4 * eighth, width)
            else:
                view, dst = src.at[:, :, :, pl.ds(j * width, width)], tile_ref.at[slot]
            tiles.append(pltpu.make_async_copy(view, dst, tile_sems.at[slot]))

        def tile(i):
            tiles[i].wait()
            return matrix(tile_ref.at[i % 3])

        def more(i):
            if i + 3 < len(tiles):
                tiles[i + 3].start()

        def push(grad, out, row, cut):
            if fast:
                k = len(jobs)
                job = Sum(spot, grad, out, row, cut, bufs[6 * k : 6 * k + 6], rss, rrs, k * Sum.sems)
                jobs.append(job)
                queue.add(job)
            elif out is sum_wr:
                if row == 0:
                    fetch(gwr_ref, out, stage_sems.at[0]).wait()
            else:
                dst = out[0] if isinstance(out, tuple) else out.at[:, :, :, cut]
                fetch(grad, dst, stage_sems.at[0]).wait()

        stage_count = [0]

        def stage(value):
            k = stage_count[0]
            stage_count[0] += 1
            slot = stage_ref.at[k % 2]
            if fast and k >= 2:
                jobs[k - 2 + blocks].free()
            slot[...] = value.astype(bf16).reshape(4, 2, eighth, width)
            return slot

        def note(idx, value):
            small_ref[idx : idx + 1, 0:width] = value

        first_cot = stage_ref.at[1].reshape(width, width).at[pl.ds(0, rows)]
        cot_copy = fetch(cot_in, first_cot, late_sems.at[0])
        if fast:
            for i in (1,):
                tiles[i].start()
        else:
            tiles[0].start()
            tiles[1].start()
            tiles[2].start()
        slopes = []
        for j in range(blocks):
            copy = pltpu.make_async_copy(slope_out.at[j], slope_ref.at[j % 2], slope_sems.at[j % 2])
            slopes.append(copy)
        slopes[0].start()
        slopes[1].start()
        limit = jnp.where(is_large, plan.large_len, 3 * plan.small_len)
        live = iota((rows, 1), 0) < limit
        cot_copy.wait()
        grad = jnp.where(live, first_cot[...].astype(f32), 0.0)
        dfeed_ref[...] = (vec(vec_ref, FEED_SCALE) * grad).astype(bf16)
        small_ref[...] = jnp.zeros_like(small_ref)
        note(REDUCE_BIAS, rows_sum(dfeed_ref[...].astype(f32)))
        gather_step(14)
        for j in range(blocks):
            d_feed = dfeed_ref[...]
            value = mm(act_ref[j], d_feed, TN).astype(bf16)
            gwr_ref[j] = value.reshape(2, 4 * eighth, width)
            if j == 1:
                gather_step(15)
        for m in range(blocks):
            push(gwr_ref.at[:, :, pl.ds(eighth * m, eighth)], sum_wr, eighth * m, slice(0, width))
        gather_step(16)
        queue.beat()
        gather_step(17)
        if fast:
            tiles[0].start()
            tiles[2].start()
        for j in range(blocks):
            second, d_feed = half_ref[...], dfeed_ref[...]
            wr = tile(2 * j)
            feed = mm(act_ref[j], wr)
            d_act = mm(d_feed, wr, NT)
            more(2 * j)
            slopes[j].wait()
            d_pre = (d_act * slope_ref[j % 2].astype(f32)).astype(bf16)
            if j + 2 < blocks:
                slopes[j + 2].start()
            queue.beat()
            we = tile(2 * j + 1)
            d_second = mm(d_pre, we, NT)
            more(2 * j + 1)
            if j == 0:
                branch_copy = fetch(branch_out, branch_ref, late_sems.at[1])
                feed_ref[...] = feed
                dsec_ref[...] = d_second
            else:
                feed_ref[...] += feed
                dsec_ref[...] += d_second
            if j == 1:
                cot_copy = fetch(cot_in, cot_ref, late_sems.at[0])
            note(BE_ROW + j, rows_sum(d_pre.astype(f32)))
            push(stage(mm(second, d_pre, TN)), sum_we, 0, slice(j * width, (j + 1) * width))
            queue.beat()

        def pair_loads(p):
            slot = p % 3
            probs = probs_out.at[pl.ds(2 * p, 2)]
            copies = [pltpu.make_async_copy(probs, probs_ref.at[slot], pair_sems.at[slot, 3])]
            for part in range(3):
                src, dst = qkv_out.at[part * pairs + p], qkv_ref.at[slot, part]
                copies.append(pltpu.make_async_copy(src, dst, pair_sems.at[slot, part]))
            return copies

        for copy in pair_loads(0):
            copy.start()

        branch_copy.wait()
        cot_copy.wait()
        feed_out = feed_ref[...] + vec(vec_ref, REDUCE_BIAS)
        middle = middle_ref[...]
        half_ref[...] = (middle + vec(vec_ref, FEED_SCALE) * feed_out).astype(bf16)
        out_copy = fetch(half_ref, out_ref, slope_sems.at[0])
        grad = jnp.where(live, cot_ref[...].astype(f32), 0.0)
        d_second = dsec_ref[...]
        normal, inv = norm_stats(middle)
        d_middle = grad + norm_back(d_second, vec(vec_ref, SECOND_GAIN), normal, inv)
        d_branch = (vec(vec_ref, ATTEND_SCALE) * d_middle).astype(bf16)
        note(FEED_SCALE, rows_sum(grad * feed_out))
        note(SECOND_GAIN, rows_sum(d_second * normal))
        note(SECOND_SHIFT, rows_sum(d_second))
        note(ATTEND_SCALE, rows_sum(d_middle * branch_ref[...].astype(f32)))
        note(OUTPUT_BIAS, rows_sum(d_branch.astype(f32)))
        dsec_ref[...] = d_middle
        dmix_ref[...] = mm(d_branch, tile(2 * blocks), NT).astype(bf16)
        more(2 * blocks)
        mixed = jnp.concatenate([mixed_ref[p] for p in range(pairs)], axis=1)
        push(stage(mm(mixed, d_branch, TN)), sum_wo, 0, slice(0, width))
        late = [fetch(normed_out, late_ref, late_sems.at[0]), fetch(tok_in, tok_ref, late_sems.at[1])]
        queue.beat()

        def ds_copy(p):
            slot = p % 3
            dst = ds_out.at[pl.ds(2 * p, 2)]
            return pltpu.make_async_copy(probs_ref.at[slot], dst, ds_sems.at[slot])

        def pair_back(p):
            slot = p % 3
            for copy in pair_loads(p):
                copy.wait()

            @pl.when(p >= 2)
            def _():
                ds_copy(p - 2).wait()

            @pl.when(p + 1 < pairs)
            def _():
                for copy in pair_loads(p + 1):
                    copy.start()

            lanes = pl.ds(pl.multiple_of(128 * p, 128), 128)
            q, k, v = qkv_ref[slot, 0], qkv_ref[slot, 1], qkv_ref[slot, 2]
            do = dmix_ref[:, lanes]
            lower = half_mask(rows)
            prod = do.astype(f32) * mixed_ref[p].astype(f32)
            dq, dk, dv = [], [], []
            for t in range(2):
                keep = lower if t == 0 else ~lower
                d_out = jnp.where(keep, do, jnp.zeros_like(do))
                delta = jnp.sum(jnp.where(keep, prod, 0.0), axis=1, keepdims=True)
                d_probs = mm(d_out, v, NT)
                probs = probs_ref[slot, t]
                dv.append(mm(probs, do, TN))
                d_scores = (probs.astype(f32) * (d_probs - delta)).astype(bf16)
                probs_ref[slot, t] = d_scores
                dq.append(mm(d_scores, k))
                dk.append(mm(d_scores, q, TN))
            dtri[0][:, lanes] = (jnp.where(lower, dq[0], dq[1]) * 0.125).astype(bf16)
            dtri[1][:, lanes] = jnp.where(lower, dk[0], dk[1]).astype(bf16)
            dtri[2][:, lanes] = jnp.where(lower, dv[0], dv[1]).astype(bf16)
            ds_copy(p).start()

        span = width // 3
        for group in range(3):

            @pl.loop(2 * group, 2 * group + 2)
            def _(p):
                pair_back(p)

                @pl.when(p == 2 * group)
                def _():
                    queue.beat()

            if group == 0:
                for copy in late:
                    copy.wait()
            d_part = [dtri[j][:, group * span : (group + 1) * span] for j in range(3)]
            d_part = jnp.concatenate(d_part, axis=1)
            cut = slice(0, width)
            value = stage(mm(late_ref[...], d_part, TN))
            push(value, sum_wt.at[group] if fast else (sum_wt.at[group],), 0, cut)
            queue.beat()

        d_normed = None
        for j in range(3):
            d_part = dtri[j][...]
            part = mm(d_part, tile(2 * blocks + 1 + j), NT)
            d_normed = part if d_normed is None else d_normed + part
            if j != 1:
                note(QUERY_BIAS if j == 0 else VALUE_BIAS, rows_sum(d_part.astype(f32)))
            if j == 1:
                queue.beat()
        normal, inv = norm_stats(tok_ref[...].astype(f32))
        back = norm_back(d_normed, vec(vec_ref, FIRST_GAIN), normal, inv)
        late_ref[...] = (dsec_ref[...] + back).astype(bf16)
        tok_copy = fetch(late_ref, tok_out, slope_sems.at[1])
        note(FIRST_GAIN, rows_sum(d_normed * normal))
        note(FIRST_SHIFT, rows_sum(d_normed))
        queue.beat()

        ds_copy(pairs - 2).wait()
        ds_copy(pairs - 1).wait()

        def ds_load(p):
            src, slot = ds_out.at[pl.ds(2 * p, 2)], p % 3
            return pltpu.make_async_copy(src, probs_ref.at[slot], pair_sems.at[slot, 3])

        ds_load(0).start()

        @pl.loop(0, pairs)
        def _(p):
            ds_load(p).wait()

            @pl.when(p + 1 < pairs)
            def _():
                ds_load(p + 1).start()

            for t in range(2):
                ds = probs_ref.at[p % 3, t]
                args = (image_ref, colsel_ref, large_ref, strip_ref, tail_ref, 2 * p + t, is_large)
                fold_head(plan, ds, *args)

            for i in range(pairs):

                @pl.when(p == i)
                def _():
                    queue.beat()

        out_copy.wait()
        tok_copy.wait()
        lines = fold_lines(plan, large_ref, strip_ref, tail_ref, is_large)
        line_of = lambda chunk: lines[:, 128 * chunk : 128 * (chunk + 1)]
        buckets = plan.buckets
        d_table = table_from_lines(plan, line_of, lab_ref, buckets)
        if not fast:
            vec_out[...] = small_ref[:, 0:width]
            for j in range(blocks):
                be_out[:, j * width : (j + 1) * width] = small_ref[BE_ROW + j : BE_ROW + j + 1, 0:width]
            tab_out[...] = d_table
            return

        share, bshare = width // n, buckets // n
        wide = blocks * width // n
        per = width // wide
        for f in range(n):
            value = jnp.concatenate(
                [
                    d_table[:, f * bshare : (f + 1) * bshare],
                    jnp.zeros((16, wide - bshare - share), f32),
                    small_ref[:, f * share : (f + 1) * share],
                ],
                axis=1,
            )
            where, row = f % per * wide, BE_ROW + f // per
            bias = jnp.broadcast_to(small_ref[row : row + 1, where : where + wide], (16, wide))
            block[f] = jnp.where(iota((16, wide), 0) == heads, bias, value)
        sums = []
        for k, peer in enumerate(peers):
            dst = (spot.f + k + 1) % n
            sums.append(send(block.at[dst], got.at[k], bss.at[k], brs.at[k], peer))
            sums[k].start()
        queue.beat(1)
        value = block[spot.f]
        for k, copy in enumerate(sums):
            copy.wait_recv()
            value = value + got[k]
        reps[spot.rep] = value
        for k, other in enumerate(others):
            mine = reps.at[spot.rep]
            sums.append(send(mine, mine, bss.at[n - 1 + k], brs.at[n - 1 + k], other))
            sums[-1].start()
        queue.beat(1)
        for copy in sums[n - 1 :]:
            copy.wait_recv()
        small_out[...] = (reps[0] + reps[1]) + (reps[2] + reps[3])
        queue.drain()
        for copy in sums:
            copy.wait_send()
        for job in jobs:
            job.finish()
        for piece in pieces:
            piece.finish()

    pl.run_scoped(
        backward,
        pltpu.VMEM((3, 4, 2, eighth, width), bf16),
        pltpu.VMEM((rows, width), f32),
        pltpu.VMEM((rows, width), f32),
        pltpu.VMEM((4, 2, blocks * eighth, width), bf16),
        pltpu.VMEM((2, 4, 2, eighth, width), bf16),
        pltpu.VMEM((3, 3, rows, 128), bf16),
        pltpu.VMEM((3, 2, rows, rows), bf16),
        pltpu.VMEM((heads, plan.gl, plan.strip_l), f32),
        pltpu.VMEM((heads, 16, plan.strip_s), f32),
        pltpu.VMEM((heads, 1, 128), f32),
    )


def layer(plan, kind, tokens, cot, large_index, n, fast, shorts, shards):
    rows, width = tokens.shape
    heads = plan.heads
    pairs = heads // 2
    sds = jax.ShapeDtypeStruct
    hidden = shards[2].shape[1]
    blocks = hidden // width
    cuts = piece_cuts([w.shape for w in shards]) if fast else []
    colsel = jnp.asarray(plan.selector_arrays()[1], bf16)
    inputs = [kind, tokens, cot, large_index, pick_plan(plan), colsel, image_selectors(plan)]
    in_specs = [smem_spec] + [any_spec] * 3 + [vmem_spec] * 3
    outs, out_specs = [sds((rows, width), bf16)] * 2, [any_spec] * 2
    group = (3, width // 8, width)
    if fast:
        wide = hidden // n
        inputs += shorts + shards
        in_specs += [vmem_spec] * 12 + [any_spec] * 4
        outs += [sds(group, bf16)] + [sds(w.shape, bf16) for w in shards[1:]]
        outs += [sds((16, wide), f32)]
        out_specs += [vmem_spec] * 5
        outs += [sds((4, 2) + w.shape, bf16) for w in shards]
        out_specs += [any_spec] * 4
    else:
        wholes, vecs, be, table = gather_plain(shorts, shards, n)
        wholes = [w.reshape(4, 2, w.shape[0] // 8, w.shape[1]) for w in wholes]
        inputs += [vecs, be, table.astype(f32)] + wholes
        in_specs += [vmem_spec] * 3 + [any_spec] * 4
        outs += [sds((3, 4, 2, width // 8, width), bf16)] + [sds(w.shape, bf16) for w in wholes[1:]]
        outs += [sds((16, width), f32), sds((1, hidden), f32), sds((16, plan.buckets), f32)]
        out_specs += [any_spec] * 4 + [vmem_spec] * 3
    kept = len(outs)
    square = sds((heads, rows, rows), bf16)
    flat = sds((rows, width), bf16)
    outs += [flat, flat, sds((3 * pairs, rows, 128), bf16), square]
    outs += [sds((blocks, rows, width), bf16), square]
    out_specs += [any_spec] * 6
    dma = pltpu.SemaphoreType.DMA
    scratch = [
        pltpu.VMEM((16, width), f32),
        pltpu.VMEM((1, hidden), f32),
        pltpu.VMEM((2, plan.lanes), jnp.int32),
        pltpu.VMEM((blocks, rows, width), bf16),
        pltpu.VMEM((2, rows, width), bf16),
        pltpu.VMEM((rows, width), f32),
        pltpu.VMEM((2, rows, width), bf16),
        pltpu.VMEM((pairs, rows, 128), bf16),
        pltpu.VMEM((16, width), f32),
        dma((7 + blocks,)),
        dma((8,)),
        dma((3,)),
        dma((2,)),
        dma((3,)),
        dma((3, 4)),
        dma((3,)),
        dma((1,)),
    ]
    kernel_params = dict(vmem_limit_bytes=vmem_bytes)
    if fast:
        sums = 2 * blocks + 4
        for _ in range(sums):
            scratch += Sum.buffers(n // 2, width)
        scratch += [
            pltpu.VMEM((16, wide), bf16),
            pltpu.VMEM((n, 16, wide), bf16),
            pltpu.VMEM((n, 16, wide), f32),
            pltpu.VMEM((n - 1, 16, wide), f32),
            pltpu.VMEM((4, 16, wide), f32),
            dma((len(cuts) * Piece.sems,)),
            dma((len(cuts) * Piece.sems,)),
            dma((n - 1,)),
            dma((n - 1,)),
            dma((sums * Sum.sems,)),
            dma((sums * Sum.sems,)),
            dma((n + 2,)),
            dma((n + 2,)),
        ]
        kernel_params.update(collective_id=1, has_side_effects=True)
    result = pl.pallas_call(
        functools.partial(layer_kernel, plan, n, fast, cuts, blocks),
        in_specs=in_specs,
        out_specs=out_specs,
        out_shape=outs,
        scratch_shapes=scratch,
        compiler_params=pltpu.CompilerParams(**kernel_params),
        name="layer",
    )(*inputs)[:kept]
    out, token_grad, wt = result[:3]
    if fast:
        return out, token_grad, result[2:6], result[6]
    wt = wt.reshape(3, width, 3, width // 3).transpose(1, 2, 0, 3).reshape(width, 3 * width)
    grads = [wt] + [g.reshape(-1, g.shape[3]) for g in result[3:6]]
    sums, block = reduce_plain(grads, *result[6:9], n)
    wt = sums[0].reshape(-1, 3, 3, width // 3).transpose(2, 0, 1, 3).reshape(3, -1, width)
    return out, token_grad, [wt] + sums[1:], block


def per_device(
    tokens,
    slot_kinds,
    small_index,
    large_index,
    first_gain,
    first_shift,
    triple_weight,
    query_bias,
    value_bias,
    bias_table,
    output_weight,
    output_bias,
    attend_scale,
    second_gain,
    second_shift,
    expand_weight,
    expand_bias,
    reduce_weight,
    reduce_bias,
    feed_scale,
    cotangent,
):
    _, rows, width = tokens.shape
    heads = bias_table.shape[2]
    buckets = bias_table.shape[1] * lax.axis_size("fsdp")
    plan = Plan(small_index.shape[0], large_index.shape[0], rows, heads, buckets)
    tokens, cotangent = tokens[0], cotangent[0]
    short = [
        first_gain,
        first_shift,
        query_bias,
        value_bias,
        output_bias,
        attend_scale,
        second_gain,
        second_shift,
        reduce_bias,
        feed_scale,
    ]
    n = width // first_gain.shape[1]
    fast = fast_shape(
        lax.axis_size("rep"), n, [w.shape[1] for w in (triple_weight, output_weight, reduce_weight)]
    )
    shards = [w[0] for w in (triple_weight, output_weight, expand_weight, reduce_weight)]
    shorts = short + [expand_bias, bias_table[0].T]
    block_output, token_grad, sums, block = layer(
        plan, slot_kinds, tokens, cotangent, large_index, n, fast, shorts, shards
    )
    return wrap(block_output, token_grad, sums, block, first_gain.shape[1], bias_table.shape[1:])


def wrap_kernel(share, heads, out_in, tok_in, wt_in, wo_in, we_in, wr_in, block_ref, *outs):
    (
        out,
        tok,
        first_gain,
        first_shift,
        triple_weight,
        query_bias,
        value_bias,
        bias_table,
        output_weight,
        output_bias,
        attend_scale,
        second_gain,
        second_shift,
        expand_weight,
        expand_bias,
        reduce_weight,
        reduce_bias,
        feed_scale,
    ) = outs
    out[0] = out_in[...]
    tok[0] = tok_in[...]
    groups, _, width = wt_in.shape
    span = width // groups
    for g in range(groups):
        for part in range(3):
            value = wt_in[g, :, part * span : (part + 1) * span].astype(f32)
            triple_weight[0, :, part * width + g * span : part * width + (g + 1) * span] = value
    output_weight[0] = wo_in[...].astype(f32)
    expand_weight[0] = we_in[...].astype(f32)
    reduce_weight[0] = wr_in[...].astype(f32)
    first = block_ref.shape[1] - share
    rows = {
        FIRST_GAIN: first_gain,
        FIRST_SHIFT: first_shift,
        QUERY_BIAS: query_bias,
        VALUE_BIAS: value_bias,
        OUTPUT_BIAS: output_bias,
        ATTEND_SCALE: attend_scale,
        SECOND_GAIN: second_gain,
        SECOND_SHIFT: second_shift,
        REDUCE_BIAS: reduce_bias,
        FEED_SCALE: feed_scale,
    }
    for idx, ref in rows.items():
        ref[...] = block_ref[idx : idx + 1, first:]
    expand_bias[...] = block_ref[heads : heads + 1, :]
    for h in range(heads):
        bias_table[h] = block_ref[h : h + 1, : bias_table.shape[2]]


def wrap(block_output, token_grad, sums, block, share, table_shape):
    wt, wo, we, wr = sums
    sds = jax.ShapeDtypeStruct
    vector = sds((1, share), f32)
    whole_of = lambda w: sds((1,) + w.shape, f32)
    bshare, heads = table_shape
    triple = sds((1, wt.shape[1], 3 * wt.shape[2]), f32)
    outs = [sds((1,) + block_output.shape, bf16)] * 2
    outs += [vector, vector, triple, vector, vector, sds((heads, 1, bshare), f32)]
    outs += [whole_of(wo)] + [vector] * 4 + [whole_of(we), sds((1, block.shape[1]), f32)]
    outs += [whole_of(wr), vector, vector]
    result = pl.pallas_call(
        functools.partial(wrap_kernel, share, heads),
        in_specs=[vmem_spec] * 7,
        out_specs=[vmem_spec] * 18,
        out_shape=outs,
        compiler_params=pltpu.CompilerParams(vmem_limit_bytes=vmem_bytes),
        name="wrap",
    )(block_output, token_grad, wt, wo, we, wr, block)
    result = list(result)
    result[7] = result[7].transpose(1, 2, 0)
    return tuple(result)


def solution(mesh):
    rows = P(("rep", "fsdp"), None, None)
    vector = P(None, "fsdp")
    matrix = P(None, "fsdp", None)
    weights = (
        vector,
        vector,
        matrix,
        vector,
        vector,
        matrix,
        matrix,
        vector,
        vector,
        vector,
        vector,
        matrix,
        vector,
        matrix,
        vector,
        vector,
    )
    return jax.shard_map(
        per_device,
        mesh=mesh,
        in_specs=(rows, P(("rep", "fsdp")), P(), P()) + weights + (rows,),
        out_specs=(rows, rows) + weights,
        check_vma=False,
    )
```

```python
import functools

import jax
import jax.numpy as jnp
import numpy as np
from jax import lax
from jax.experimental import pallas as pl
from jax.experimental.pallas import tpu as pltpu
from jax.sharding import PartitionSpec as P

f32 = jnp.float32
bf16 = jnp.bfloat16
norm_eps = 1e-06
neg_fill = -1000000000.0
vmem_bytes = 62 << 20

NN = (((1,), (0,)), ((), ()))
NT = (((1,), (1,)), ((), ()))
TN = (((0,), (0,)), ((), ()))


def mm(left, right, dims=NN):
    return lax.dot_general(left, right, dims, preferred_element_type=f32)


def round_up(value, unit):
    return -(-value // unit) * unit


class Plan:
    def __init__(self, small_len, large_len, rows, heads, buckets):
        self.heads, self.buckets = heads, buckets
        self.rows = rows
        self.small_len, self.large_len = small_len, large_len
        self.gs = int(round((small_len - 1) ** 0.5))
        self.gl = int(round((large_len - 1) ** 0.5))
        gl, gs = self.gl, self.gs
        self.strip_l = round_up(2 * gl * gl, 128)
        self.strip_s = round_up(2 * gs * (2 * gs - 1) + gs, 128)
        self.line = 2 * self.strip_l
        self.lanes = self.line + 128
        self.pad_cols = round_up(2 * gs * gs + 1, 128)
        self.pad_rows = 16 * gs
        self.cls_col = 2 * gs * gs
        self.cls_row = gs

    def place(self, di, dj, limit):
        gl = self.gl
        good = (np.abs(di) < limit) & (np.abs(dj) < limit)
        row = 1 + gl * np.maximum(di, 0) + np.maximum(dj, 0)
        col = 1 + gl * np.maximum(-di, 0) + np.maximum(-dj, 0)
        return np.where(good, row, 0), np.where(good, col, 0), good

    def positions(self):
        gl, gs = self.gl, self.gs
        x = np.arange(self.strip_l)
        rows, cols, goods = [], [], []
        for parity in range(2):
            m = 2 * ((x + gl) // (2 * gl)) if parity == 0 else 2 * (x // (2 * gl)) + 1
            t = x - gl * m
            r, c, g = self.place(gl - m, -t, gl)
            rows.append(r), cols.append(c), goods.append(g)
        large = [np.concatenate(v) for v in (rows, cols, goods)]
        x = np.arange(self.strip_s)
        m = x // (2 * gs)
        t = x - 2 * gs * m - gs
        small = [np.resize(np.zeros(1, v.dtype), self.line) for v in large]
        for dst, src in zip(small, self.place(gs - 1 - m, -t, gs)):
            dst[: self.strip_s] = src
        tail_r, tail_c, tail_g = np.zeros(128, int), np.zeros(128, int), np.zeros(128, bool)
        tail_r[:3], tail_c[:3], tail_g[:3] = (0, 1, 0), (1, 0, 0), True
        out = []
        for base in (large, small):
            out.append([np.concatenate(v) for v in zip(base, (tail_r, tail_c, tail_g))])
        return out

    def selector_arrays(self):
        gs = self.gs
        rows = np.zeros((self.rows, self.pad_rows), np.float32)
        cols = np.zeros((self.pad_cols, self.rows), np.float32)
        for image in range(3):
            for tok in range(self.small_len):
                r = image * self.small_len + tok
                i, j = divmod(tok - 1, gs)
                rows[r, self.cls_row if tok == 0 else 16 * i + j] = 1
                cols[self.cls_col if tok == 0 else 2 * gs * i + j, r] = 1
        return rows, cols

    def selectors(self):
        rows, cols = self.selector_arrays()
        return jnp.asarray(rows, bf16), jnp.asarray(cols, bf16)


def iota(shape, dim):
    return lax.broadcasted_iota(jnp.int32, shape, dim)


def pick_plan(plan):
    out = []
    for r, c, good in plan.positions():
        down = good & ((r - 1) // plan.gl >= (c - 1) // plan.gl)
        key = np.where(down, r, c)
        sub = np.where(down, c, r) - 1
        valid = good.copy()
        valid[plan.line :] = False
        out.append(np.stack([key, sub, down.astype(int), valid.astype(int)]))
    return jnp.asarray(np.concatenate(out), jnp.int32)


def lane_chunks(lanes, size=512):
    return [(low, min(low + size, lanes)) for low in range(0, lanes, size)]


def read_labels(plan, is_large, idx_ref, pick_ref, lab_ref):
    size, gl = idx_ref.shape[0], plan.gl
    across = idx_ref[1 : 1 + gl, :]
    down = idx_ref[:, 1 : 1 + gl].astype(f32).T.astype(jnp.int32)
    sides = []
    for v in (across, down):
        sides += [(v >> 6).astype(f32), (v & 63).astype(f32)]
    sides = jnp.concatenate(sides, axis=0).astype(bf16)
    for low, high in lane_chunks(plan.line):
        lanes, count = slice(low, high), high - low
        key, sub, use_down, valid = [
            jnp.where(is_large, pick_ref[i : i + 1, lanes], pick_ref[4 + i : 5 + i, lanes])
            for i in range(4)
        ]
        hot = jnp.where(iota((size, count), 0) == key, 1.0, 0.0).astype(bf16)
        here = iota((gl, count), 0) == sub
        rows = mm(sides, hot)
        for digit in range(2):
            a = rows[digit * gl : (digit + 1) * gl]
            b = rows[(2 + digit) * gl : (3 + digit) * gl]
            found = jnp.where(here, jnp.where(use_down == 1, b, a), 0.0)
            found = jnp.sum(found, axis=0, keepdims=True).astype(jnp.int32)
            lab_ref[digit : digit + 1, lanes] = jnp.where(valid == 1, found, -1)
    lane = iota((1, 128), 1)
    tail = jnp.where(lane == 0, idx_ref[0:1, 1:2], -1)
    tail = jnp.where(lane == 1, idx_ref[1:2, 0:1], tail)
    tail = jnp.where(lane == 2, idx_ref[0:1, 0:1], tail)
    lab_ref[0:1, plan.line : plan.line + 128] = jnp.where(tail < 0, -1, tail >> 6)
    lab_ref[1:2, plan.line : plan.line + 128] = jnp.where(tail < 0, -1, tail & 63)


def table_lines(plan, tab, lab_ref, line_ref):
    count = tab.shape[1] // 64
    split = jnp.concatenate([tab[:, 64 * i : 64 * (i + 1)] for i in range(count)], axis=0)
    split = split.astype(bf16)
    for low, high in lane_chunks(plan.lanes):
        first, second = lab_ref[0:1, low:high], lab_ref[1:2, low:high]
        hot = jnp.where(iota((64, high - low), 0) == second, 1.0, 0.0).astype(bf16)
        rows = mm(split, hot)
        parts = [jnp.zeros((16, high - low), f32)] * 4
        for i in range(count):
            parts[i % 4] = jnp.where(first == i, rows[16 * i : 16 * (i + 1)], parts[i % 4])
        line_ref[:, low:high] = (parts[0] + parts[1]) + (parts[2] + parts[3])


def table_from_lines(plan, line_of, lab_ref, buckets):
    count = buckets // 64
    total = jnp.zeros((32 * count, 64), f32)
    for chunk in range(plan.lanes // 128):
        lanes = slice(chunk * 128, (chunk + 1) * 128)
        first, second = lab_ref[0:1, lanes], lab_ref[1:2, lanes]
        hot = jnp.where(iota((64, 128), 0) == second, 1.0, 0.0).astype(bf16)
        part = line_of(chunk)
        high = part.astype(bf16)
        low = (part - high.astype(f32)).astype(bf16)
        both = jnp.concatenate([high, low], axis=0)
        stack = [jnp.where(first == i, both, jnp.zeros_like(both)) for i in range(count)]
        total = total + mm(jnp.concatenate(stack, axis=0), hot, NT)
    pieces = []
    for i in range(count):
        pieces.append(total[32 * i : 32 * i + 16] + total[32 * i + 16 : 32 * i + 32])
    return jnp.concatenate(pieces, axis=1)


def segments(plan, is_large, ids):
    n = plan.small_len
    small = jnp.where(ids >= n, 1, 0) + jnp.where(ids >= 2 * n, 1, 0) + jnp.where(ids >= 3 * n, 1, 0)
    return jnp.where(is_large, jnp.where(ids < plan.large_len, 0, 3), small)


def line_of_head(ref, h):
    return jnp.sum(jnp.where(iota((16, 1), 0) == h, ref[...], 0.0), axis=0, keepdims=True)


def large_strip(plan, line):
    gl, span = plan.gl, plan.strip_l
    rolled = []
    for parity in range(2):
        part = jnp.broadcast_to(line[:, parity * span : (parity + 1) * span], (gl, span))
        rolled.append(pltpu.roll(part, 0, axis=1, stride=1, stride_axis=0))
    odd = (iota((1, span), 1) + span - 1) % span // gl % 2
    odd = jnp.where(iota((gl, 1), 0) == 0, 1 - odd, odd)
    strip = jnp.where(odd == 1, rolled[1], rolled[0])
    return jnp.concatenate([strip, strip[:, :128]], axis=1)


def band_move(plan, a):
    return plan.gl * (plan.gl - a)


def small_padded(plan, line, tail):
    gs, span = plan.gs, plan.strip_s
    line = jnp.broadcast_to(line[:, 0:span], (16, span))
    strip = pltpu.roll(line, 0, axis=1, stride=1, stride_axis=0)
    col = iota((1, plan.pad_cols), 1)
    is_col = col == plan.cls_col
    is_row = iota((16, 1), 0) == plan.cls_row
    bands = []
    for i in range(gs):
        move = 2 * gs * (gs - 1 - i) + gs
        band = pltpu.roll(strip, (span - move) % span, axis=1)[:, : plan.pad_cols]
        band = jnp.where(is_col, tail[:, 1:2], band)
        if i == 0:
            edge = jnp.where(is_col, tail[:, 2:3], tail[:, 0:1])
            band = jnp.where(is_row, edge, band)
        bands.append(band)
    return jnp.concatenate(bands, axis=0).astype(bf16)


def small_blocks(plan, line, tail, pick, colsel):
    rows = plan.rows
    wide = round_up(rows, 128)
    cols = mm(small_padded(plan, line, tail), colsel[:, 0:256]).astype(bf16)
    out = []
    for image, ((r0, r1), (l0, _)) in enumerate(image_rows(plan)):
        start = 256 * image
        block = mm(pick[:, start : start + r1 - r0], cols, TN)
        shift = image * plan.small_len - l0
        last = l0 + round_up(shift + plan.small_len, 128)
        if last - l0 > 256:
            block = jnp.concatenate([block, jnp.zeros((r1 - r0, last - l0 - 256), f32)], axis=1)
        if shift:
            block = pltpu.roll(block, shift, axis=1)
        parts = [block]
        if l0:
            parts.insert(0, jnp.zeros((r1 - r0, l0), f32))
        if last < wide:
            parts.append(jnp.zeros((r1 - r0, wide - last), f32))
        out.append((r0, r1, jnp.concatenate(parts, axis=1)))
    return out


def bias_head(plan, is_large, line_ref, pick, colsel, h, out_ref):
    gl, rows = plan.gl, plan.rows
    wide = round_up(rows, 128)
    line = line_of_head(line_ref, h)
    tail = line[:, plan.line : plan.line + 128]
    blocks = small_blocks(plan, line, tail, pick, colsel)
    strip = large_strip(plan, line)
    span = strip.shape[1]
    col = iota((1, wide), 1)
    seg_col = segments(plan, is_large, col)
    bands = -(-rows // gl)
    for pair in range(-(-bands // 2)):
        first = 2 * gl * pair
        count = min(2 * gl, rows - first)
        parts = []
        for a in range(2 * pair, 2 * pair + 2):
            if a >= bands:
                continue
            move = band_move(plan, a)
            low = move // 128 * 128
            piece = strip[:, low : min(low + wide + 128, span)]
            if piece.shape[1] < wide + 128:
                piece = jnp.concatenate(
                    [piece, jnp.zeros((gl, wide + 128 - piece.shape[1]), f32)], axis=1
                )
            turn = (wide + 128 - (move - low)) % (wide + 128)
            parts.append((pltpu.roll(piece, turn, axis=1) if turn else piece)[:, :wide])
        block = (jnp.concatenate(parts, axis=0) if len(parts) > 1 else parts[0])[:count]
        row = iota((count, 1), 0) + first
        edge = jnp.where(col[:, :128] == 0, tail[:, 1:2], block[:, :128])
        block = jnp.concatenate([edge, block[:, 128:]], axis=1)
        if first == 0:
            block = jnp.where(row == 0, jnp.where(col == 0, tail[:, 2:3], tail[:, 0:1]), block)
        if first + count > plan.large_len:
            block = jnp.where(row < plan.large_len, block, 0.0)
        small = None
        for r0, r1, value in blocks:
            low, high = max(first, r0), min(first + count, r1)
            if low >= high:
                continue
            part = [value[low - r0 : high - r0]]
            if low > first:
                part.insert(0, jnp.zeros((low - first, wide), f32))
            if high < first + count:
                part.append(jnp.zeros((first + count - high, wide), f32))
            part = jnp.concatenate(part, axis=0) if len(part) > 1 else part[0]
            small = part if small is None else small + part
        block = jnp.where(is_large, block, small)
        block = jnp.where(segments(plan, is_large, row) == seg_col, block, neg_fill)
        out_ref[h, first : first + count, :] = block[:, :rows].astype(bf16)


def norm_stats(values):
    mean = jnp.mean(values, axis=1, keepdims=True)
    centred = values - mean
    var = jnp.mean(centred * centred, axis=1, keepdims=True)
    inv = lax.rsqrt(var + norm_eps)
    return centred * inv, inv


def norm_back(d_out, gain, normal, inv):
    d_normal = d_out * gain
    mean_d = jnp.mean(d_normal, axis=1, keepdims=True)
    mean_dn = jnp.mean(d_normal * normal, axis=1, keepdims=True)
    return inv * (d_normal - mean_d - normal * mean_dn)


def rows_sum(values):
    return jnp.sum(values, axis=0, keepdims=True)


def gelu_parts(v):
    size = jnp.abs(v)
    bell = jnp.exp(-0.5 * v * v)
    below = 1.0 + (0.3275911 * 0.7071067811865476) * size
    t = pl.reciprocal(below, approx=True)
    t = t * (2.0 - below * t)
    poly = t * (
        0.127414796
        + t * (-0.142248368 + t * (0.7107068705 + t * (-0.7265760135 + t * 0.5307027145)))
    )
    tail = poly * bell
    phi = jnp.where(v < 0, tail, 1.0 - tail)
    return v * phi, phi + v * bell * 0.3989422804014327


BE_ROW = 10
(
    FIRST_GAIN,
    FIRST_SHIFT,
    QUERY_BIAS,
    VALUE_BIAS,
    OUTPUT_BIAS,
    ATTEND_SCALE,
    SECOND_GAIN,
    SECOND_SHIFT,
    REDUCE_BIAS,
    FEED_SCALE,
) = range(10)


def vec(ref, idx):
    return ref[idx : idx + 1, :]


def half_mask(rows):
    return iota((rows, 128), 1) < 64


class Spot:
    def __init__(self, n):
        self.n, self.levels = n, n // 2
        self.rep, self.f = lax.axis_index("rep"), lax.axis_index("fsdp")
        self.half, self.core = self.rep // 2, self.rep % 2
        self.level, self.side = self.f // 2, self.f % 2

    def at(self, rep=None, f=None):
        return {"rep": self.rep if rep is None else rep, "fsdp": self.f if f is None else f}

    def sibling(self):
        return self.at(rep=2 * self.half + 1 - self.core)

    def across(self):
        return self.at(rep=2 * (1 - self.half) + self.core)

    def beside(self):
        return self.at(f=2 * self.level + 1 - self.side)

    def along(self, step):
        return self.at(f=2 * ((self.level + step) % self.levels) + self.side)

    def from_along(self, step, side=None):
        side = self.side if side is None else side
        return 2 * ((self.level + self.levels - step) % self.levels) + side


MESH = pl.DeviceIdType.MESH


def greet(devices):
    for device in devices:
        barrier = pltpu.get_barrier_semaphore()
        pl.semaphore_signal(barrier, inc=1, device_id=device, device_id_type=MESH)


def met(count):
    pl.semaphore_wait(pltpu.get_barrier_semaphore(), count)


def send(src, dst, send_sem, recv_sem, device):
    return pltpu.make_async_remote_copy(
        src_ref=src,
        dst_ref=dst,
        send_sem=send_sem,
        recv_sem=recv_sem,
        device_id=device,
        device_id_type=MESH,
    )


def fast_shape(reps, n, shard_rows):
    return reps == 4 and n == 8 and all(rows % 96 == 0 for rows in shard_rows)


def spread_block(refs, block_ref):
    *vectors, be_ref, table_ref = refs
    heads, share = table_ref.shape
    lanes = block_ref.shape[1]
    table = jnp.concatenate([table_ref[...].astype(f32), jnp.zeros((16 - heads, share), f32)], axis=0)
    width = vectors[0].shape[1]
    rows = [v[...].astype(f32) for v in vectors]
    rows.append(jnp.zeros((16 - len(rows), width), f32))
    block = jnp.concatenate(
        [table, jnp.zeros((16, lanes - share - width), f32), jnp.concatenate(rows, axis=0)], axis=1
    )
    wide = jnp.broadcast_to(be_ref[...].astype(f32), (16, lanes))
    block_ref[...] = jnp.where(iota((16, lanes), 0) == heads, wide, block).astype(bf16)


smem_spec = pl.BlockSpec(memory_space=pltpu.SMEM)
any_spec = pl.BlockSpec(memory_space=pl.ANY)
vmem_spec = pl.BlockSpec(memory_space=pltpu.VMEM)


def add16(left, right):
    return (left.astype(f32) + right.astype(f32)).astype(bf16)


def gather_plain(shorts, shards, n):
    gather = lambda value, axis: lax.all_gather(value, "fsdp", axis=axis, tiled=True)
    vecs = gather(jnp.concatenate(shorts[:10], axis=0), 1).astype(f32)
    vecs = jnp.pad(vecs, ((0, 6), (0, 0)))
    table = gather(shorts[11], 1)
    table = jnp.pad(table, ((0, 16 - table.shape[0]), (0, 0)))
    return [gather(w, 0) for w in shards], vecs, gather(shorts[10], 1).astype(f32), table


def reduce_plain(grads, vec_sums, be_sums, table_sums, n):
    def whole_sum(value):
        value = lax.psum_scatter(value, "fsdp", scatter_dimension=0, tiled=True)
        return lax.psum(value, "rep")

    sums = lax.psum((vec_sums, be_sums, table_sums), ("rep", "fsdp"))
    me = lax.axis_index("fsdp")
    cut = lambda v: lax.dynamic_slice_in_dim(v, me * (v.shape[1] // n), v.shape[1] // n, axis=1)
    vec_part, be_part, table_part = [cut(v) for v in sums]
    wide = be_part.shape[1]
    space = max(wide - vec_part.shape[1] - table_part.shape[1], 0)
    body = jnp.concatenate([table_part, jnp.zeros((16, space), f32), vec_part], axis=1)
    block = jnp.where(jnp.arange(16)[:, None] == 12, jnp.pad(be_part, ((0, 0), (0, body.shape[1] - wide))), body)
    return [whole_sum(g) for g in grads], block


class Piece:
    sems = 6

    def __init__(self, spot, shard, whole, row, col, cols, sent, rs, base):
        self.size = cols // 384
        levels = spot.levels
        part, q = 48, 16
        start = row + spot.core * part
        cut = slice(col, col + cols)
        rows = lambda first, size: pl.ds(pl.multiple_of(first, 16), size)
        plane = rows(start + spot.half * q, 2 * q)
        outer = rows(start + spot.half * 2 * q, q)
        core_rows = rows(start, part)
        side = spot.side

        def copy(idx, kind, src, dst, device):
            return send(src, dst, sent.at[kind], rs.at[base + idx], device)

        own = shard.at[plane, cut]
        here = whole.at[spot.level, side, plane, cut]
        self.local = pltpu.make_async_copy(own, here, rs.at[base + 5])
        self.z = [copy(0, 0, own, here, spot.along(step)) for step in range(1, levels)]
        three = whole.at[0 : levels - 1, 0, 0 : 2 * q, cut]
        self.z_all = pltpu.make_async_copy(three, three, rs.at[base])
        column = whole.at[:, side, plane, cut]
        self.y = copy(1, 1, column, column, spot.beside())
        near = whole.at[:, side, outer, cut]
        far = whole.at[:, 1 - side, outer, cut]
        self.x = [copy(2, 2, near, near, spot.across()), copy(3, 2, far, far, spot.across())]
        done = whole.at[:, :, core_rows, cut]
        self.c = copy(4, 3, done, done, spot.sibling())

    @staticmethod
    def sent_waits(levels, whole, sent):
        part = whole.shape[2] // 96
        views = [
            whole.at[0 : levels - 1, 0, 0 : 32 * part],
            whole.at[:, 0, 0 : 32 * part],
            whole.at[:, :, 0 : 16 * part],
            whole.at[:, :, 0 : 48 * part],
        ]
        return [pltpu.make_async_copy(v, v, sent.at[kind]) for kind, v in enumerate(views)]

    def start(self):
        self.local.start()
        for copy in self.z:
            copy.start()

    def after_z(self):
        self.local.wait()
        self.z_all.wait()
        self.y.start()
        self.x[0].start()

    def after_y(self):
        self.y.wait_recv()
        self.x[1].start()

    def after_x(self):
        self.x[0].wait_recv()
        self.x[1].wait_recv()
        self.c.start()

    def after_c(self):
        self.c.wait_recv()


def piece_cuts(shard_shapes):
    cuts = []
    for idx, (rows, cols) in enumerate(shard_shapes):
        for row in range(0, rows, 96):
            starts = list(range(0, cols, 384))
            if idx == 0:
                starts = starts[0::2] + starts[1::2]
            for col in starts:
                cuts.append((idx, row, col, 384))
    return cuts


def image_rows(plan):
    out = []
    for image in range(3):
        first, last = image * plan.small_len, (image + 1) * plan.small_len
        rows = (first // 16 * 16, round_up(last, 16))
        lanes = (first // 128 * 128, min(round_up(last, 128), plan.rows))
        out.append((rows, lanes))
    return out


def image_selectors(plan):
    rows, _ = plan.selector_arrays()
    out = []
    for image, ((low, high), _) in enumerate(image_rows(plan)):
        part = rows.copy()
        part[: image * plan.small_len] = 0
        part[(image + 1) * plan.small_len :] = 0
        out.append(np.pad(part[low:high].T, ((0, 0), (0, 256 - (high - low)))))
    return jnp.asarray(np.concatenate(out, axis=1), bf16)


def fold_head(plan, ds_ref, pick, colsel, large_ref, small_ref, tail_ref, h, is_large):
    gl, gs, rows = plan.gl, plan.gs, plan.rows
    wide = round_up(rows, 128)
    width = plan.strip_l + 128
    bands = -(-rows // gl)
    total = jnp.zeros((gl, width), f32)
    side = jnp.zeros((2 * gl, 128), f32)
    for pair in range(-(-bands // 2)):
        first = 2 * gl * pair
        count = min(2 * gl, rows - first)
        block = ds_ref[first : first + count, :].astype(f32)
        block = jnp.concatenate([block, jnp.zeros((count, wide - rows), f32)], axis=1)
        if count < 2 * gl:
            block = jnp.concatenate([block, jnp.zeros((2 * gl - count, wide), f32)], axis=0)
        if pair == 0:
            row = iota((2 * gl, 1), 0)
            top_row = jnp.where(row == 0, block, 0.0)
            block = jnp.where(row == 0, 0.0, block)
        side = side + block[:, :128]
        block = jnp.concatenate(
            [jnp.where(iota((1, 128), 1) == 0, 0.0, block[:, :128]), block[:, 128:]], axis=1
        )
        for half in range(2):
            a = 2 * pair + half
            if a >= bands:
                continue
            move = band_move(plan, a)
            low = move // 128 * 128
            piece = block[half * gl : (half + 1) * gl]
            if move > low:
                piece = jnp.concatenate([piece, jnp.zeros((gl, 128), f32)], axis=1)
                piece = pltpu.roll(piece, move - low, axis=1)
            piece = piece[:, : width - low]
            high = low + piece.shape[1]
            parts = [total[:, low:high] + piece]
            if low:
                parts.insert(0, total[:, :low])
            if high < width:
                parts.append(total[:, high:])
            total = jnp.concatenate(parts, axis=1) if len(parts) > 1 else parts[0]
    large_ref[h] = jnp.concatenate(
        [total[:, :128] + total[:, plan.strip_l :], total[:, 128 : plan.strip_l]], axis=1
    )
    lane = iota((1, wide), 1)
    full = lambda v: jnp.sum(jnp.sum(v, axis=0, keepdims=True), axis=1, keepdims=True)
    corner = full(jnp.where(lane == 0, top_row, 0.0))
    top = full(jnp.where(lane == 0, 0.0, top_row))
    side = full(jnp.where(iota((1, 128), 1) == 0, side, 0.0))

    gathered = jnp.zeros((plan.pad_rows, 256), f32)
    for image, ((r0, r1), (l0, l1)) in enumerate(image_rows(plan)):
        block = ds_ref[r0:r1, l0:l1]
        shift = image * plan.small_len - l0
        if shift:
            pad = round_up(l1 - l0, 128) - (l1 - l0)
            block = block.astype(f32)
            if pad:
                block = jnp.concatenate([block, jnp.zeros((r1 - r0, pad), f32)], axis=1)
            block = pltpu.roll(block, block.shape[1] - shift, axis=1)[:, :256].astype(bf16)
        start = 256 * image
        gathered = gathered + mm(pick[:, start : start + r1 - r0], block)
    high = gathered.astype(bf16)
    low = (gathered - high.astype(f32)).astype(bf16)
    select = colsel[:, 0:256]
    padded = mm(high, select, NT) + mm(low, select, NT)
    span = plan.strip_s
    col = iota((1, plan.pad_cols), 1)
    row = iota((16, 1), 0)
    acc = jnp.zeros((16, span), f32)
    edge = jnp.zeros((16, plan.pad_cols), f32)
    for i in range(gs):
        band = padded[16 * i : 16 * (i + 1)]
        if i == 0:
            top_s = jnp.where(row == plan.cls_row, band, 0.0)
            band = jnp.where(row == plan.cls_row, 0.0, band)
        edge = edge + band
        band = jnp.where(col < plan.cls_col, band, 0.0)
        band = jnp.concatenate([band, jnp.zeros((16, span - plan.pad_cols), f32)], axis=1)
        acc = acc + pltpu.roll(band, 2 * gs * (gs - 1 - i) + gs, axis=1)
    small_ref[h] = acc
    corner_s = full(jnp.where(col == plan.cls_col, top_s, 0.0))
    top_s = full(jnp.where(col < plan.cls_col, top_s, 0.0))
    side_s = full(jnp.where(col == plan.cls_col, edge, 0.0))
    lane = iota((1, 128), 1)
    picks = [(top, top_s), (side, side_s), (corner, corner_s)]
    tail = jnp.zeros((1, 128), f32)
    for i, (a, b) in enumerate(picks):
        tail = jnp.where(lane == i, jnp.where(is_large, a, b), tail)
    tail_ref[h] = tail


def fold_lines(plan, large_ref, small_ref, tail_ref, is_large):
    gl, heads, span = plan.gl, plan.heads, plan.strip_l
    odd = (iota((1, span), 1) + span - 1) % span // gl % 2
    lines = [None, None]
    for i in reversed(range(gl)):
        row = large_ref[:, i, :]
        for parity in range(2):
            want = parity if i else 1 - parity
            part = jnp.where(odd == want, row, 0.0)
            if lines[parity] is not None:
                part = part + pltpu.roll(lines[parity], span - 1, axis=1)
            lines[parity] = part
    small = None
    for i in reversed(range(16)):
        part = small_ref[:, i, :]
        small = part if small is None else part + pltpu.roll(small, plan.strip_s - 1, axis=1)
    small = jnp.concatenate([small, jnp.zeros((heads, plan.line - plan.strip_s), f32)], axis=1)
    line = jnp.where(is_large, jnp.concatenate(lines, axis=1), small)
    tail = tail_ref[:, 0, :]
    line = jnp.concatenate([line, tail], axis=1)
    return jnp.concatenate([line, jnp.zeros((16 - heads, plan.lanes), f32)], axis=0)


class Sum:
    sems = 6
    outer = 16

    def __init__(self, spot, grad, out, row, cut, bufs, sent, c_sem, rs, base):
        self.spot, self.grad, self.out = spot, grad, out
        self.row, self.cut = row, cut
        self.acc, self.got_x, self.got_y, self.got_z, self.total, self.got_f = bufs
        half, core, side, level, levels = spot.half, spot.core, spot.side, spot.level, spot.levels
        q, part = self.outer, self.acc.shape[2]
        self.middle = m = part - 2 * q
        rows = lambda first, size: pl.ds(pl.multiple_of(first, 16), size)
        self.rows = rows
        self.plane = rows(half * q, q + m)
        self.mine = rows(half * (q + m), q)
        self.own = rows(core * part, part)
        self.sent = self.joined = False

        def copy(idx, src, dst, device):
            out_sem = sent.at[idx] if idx else c_sem
            return send(src, dst, out_sem, rs.at[base + idx], device)

        acc = self.acc
        other = rows((1 - core) * part, part)
        self.c = copy(0, grad.at[:, :, other, cut[0]], acc, spot.sibling())
        self.x = copy(1, acc.at[:, :, rows((1 - half) * (q + m), q)], self.got_x, spot.across())
        self.y = copy(2, acc.at[:, 1 - side, self.plane], self.got_y, spot.beside())
        self.z = []
        for step in range(1, levels):
            src = acc.at[(level + step) % levels, side, self.plane]
            self.z.append(copy(5, src, self.got_z.at[step - 1], spot.along(step)))
        self.z_all = pltpu.make_async_copy(self.got_z, self.got_z, rs.at[base + 5])
        self.f = copy(3, self.total, self.got_f, spot.across())
        mine = out.at[rows(row + core * part, part), cut[1]]
        self.last = copy(4, mine, mine, spot.sibling())

    @classmethod
    def buffers(cls, levels, shard_rows, cols):
        part = shard_rows // 2
        kept = part - cls.outer
        shapes = [
            (levels, 2, part, cols),
            (levels, 2, cls.outer, cols),
            (levels, kept, cols),
            (levels - 1, kept, cols),
            (kept, cols),
            (kept, cols),
        ]
        return [pltpu.VMEM(shape, bf16) for shape in shapes]

    def start(self):
        self.c.start()

    def free(self):
        self.join()
        if not self.sent:
            self.c.wait_send()
            self.sent = True

    def stage(self, k):
        getattr(self, ("go", "after_x", "after_y", "after_z", "after_f", "after_last")[k])()

    def join(self):
        if self.joined:
            return
        self.joined = True
        self.c.wait_recv()

        @pl.loop(0, self.acc.shape[0])
        def _(level):
            for side in range(2):
                own = self.grad[level, side, self.own, self.cut[0]]
                self.acc[level, side] = add16(self.acc[level, side], own)

    def go(self):
        self.join()
        self.x.start()

    def after_x(self):
        self.x.wait_recv()

        @pl.loop(0, self.acc.shape[0])
        def _(level):
            for side in range(2):
                mine = self.acc[level, side, self.mine]
                self.acc[level, side, self.mine] = add16(mine, self.got_x[level, side])

        self.y.start()

    def after_y(self):
        side = self.spot.side
        self.y.wait_recv()

        @pl.loop(0, self.acc.shape[0])
        def _(level):
            mine = self.acc[level, side, self.plane]
            self.acc[level, side, self.plane] = add16(mine, self.got_y[level])

        for copy in self.z:
            copy.start()

    def after_z(self):
        self.z_all.wait()
        value = self.acc[self.spot.level, self.spot.side, self.plane].astype(f32)
        for k in range(len(self.z)):
            value = value + self.got_z[k].astype(f32)
        self.total[...] = value.astype(bf16)
        self.f.start()

    def after_f(self):
        q, m, half = self.outer, self.middle, self.spot.half
        base = self.row + self.spot.core * self.acc.shape[2]
        rows = self.rows
        total, got, out, cut = self.total, self.got_f, self.out, self.cut[1]
        self.f.wait_recv()
        out[rows(base + half * (q + m), q), cut] = total[rows(half * m, q)]
        both = add16(total[rows((1 - half) * q, m)], got[rows(half * q, m)])
        out[rows(base + q, m), cut] = both
        out[rows(base + (1 - half) * (q + m), q), cut] = got[rows((1 - half) * m, q)]
        self.last.start()

    def after_last(self):
        self.last.wait_recv()

    @classmethod
    def sent_rows(cls, levels, shard_rows):
        part = shard_rows // 2
        kept = part - cls.outer
        return [2 * levels * cls.outer, levels * kept, kept, part, (levels - 1) * kept]


ADMIT, HOLD = 1, 3
HIDDEN_BLOCKS = 3


class Queue:
    def __init__(self):
        self.waiting, self.active, self.beats, self.last = [], [], 0, -9

    def add(self, job):
        self.waiting.append([job, 0])
        job.start()

    def beat(self, hold=None):
        hold = HOLD if hold is None else hold
        self.beats += 1
        for entry in self.waiting:
            if entry[1] >= hold - 1:
                entry[0].join()
            entry[1] += 1
        for entry in list(self.active):
            entry[1] += 1
            if entry[1] >= hold:
                entry[1] = 0
                entry[2] += 1
                entry[0].stage(entry[2])
                if entry[2] == 5:
                    self.active.remove(entry)
        admit = ADMIT if hold > 1 else 1
        if self.waiting and self.waiting[0][0].joined and self.beats - self.last >= admit:
            self.last = self.beats
            job, _ = self.waiting.pop(0)
            self.active.append([job, 0, 0])
            job.stage(0)

    def drain(self):
        while self.waiting or self.active:
            self.beat(1)


def layer_kernel(plan, n, fast, cuts, sum_shapes, *refs):
    refs = list(refs)
    take = lambda count: [refs.pop(0) for _ in range(count)]
    kind_ref, tok_in, cot_in, idx_in, pick_ref, colsel_ref, image_ref = take(7)
    if fast:
        shorts, shards = take(12), take(4)
    else:
        vec_in, be_in, tab_in = take(3)
        wholes = take(4)
    out_ref, tok_out = take(2)
    sum_wt, sum_wo, sum_we, sum_wr = take(4)
    if fast:
        (small_out,) = take(1)
        wholes = take(4)
    else:
        vec_out, be_out, tab_out = take(3)
    normed_out, branch_out, qkv_out, probs_out, ds_out = take(5)
    vec_ref, be_ref, lab_ref, middle_ref, pair_ref, mixed_ref, small_ref, dbe_ref = take(8)
    rows_ref, cols_ref = take(2)
    load_sems, save_sems, tile_sems, late_sems, pair_sems, ds_sems, stage_sems = take(7)
    wt_in, wo_in, we_in, wr_in = wholes
    is_large = kind_ref[0] == 1
    heads, rows = plan.heads, plan.rows
    pairs = heads // 2
    width = tok_in.shape[1]
    eighth = width // 8
    hidden = wr_in.shape[2] * 8
    unit = hidden // 8 // HIDDEN_BLOCKS
    tile_cols = 8 * unit
    matrix = lambda ref: ref[...].reshape(width, width)
    half_ref, dfeed_ref = pair_ref.at[0], pair_ref.at[1]

    def fetch(src, dst, sem):
        copy = pltpu.make_async_copy(src, dst, sem)
        copy.start()
        return copy

    saves = []

    def save(src, dst):
        copy = fetch(src, dst, save_sems.at[len(saves)])
        saves.append(copy)
        return copy

    queue = Queue()
    jobs, pieces = [], []
    if fast:
        bufs = take(6 * len(sum_shapes))
        sum_kinds = sorted(set(sum_shapes))
        short, shorts_got, block, got, reps = take(5)
        gss, grs, ass, ars, rss, css, rrs, bss, brs = take(9)
        spot = Spot(n)
        peers = [spot.at(f=(spot.f + k) % n) for k in range(1, n)]
        others = [spot.at(rep=(spot.rep + k) % 4) for k in range(1, 4)]
        greet(peers + others)
        for idx, row, col, cols in cuts:
            base = len(pieces) * Piece.sems
            at = GATHER_ORDER[idx]
            args = (row, col, cols, gss.at[at], grs, base)
            pieces.append(Piece(spot, shards[at], wholes[at], *args))
        formed = []
        for j in range(HIDDEN_BLOCKS):
            formed.append((rows_ref, sum_wr, j * unit, 0))
            formed.append((cols_ref, sum_we, 0, j * tile_cols))
        formed.append((rows_ref, sum_wo, 0, 0))
        for j in range(3):
            formed.append((rows_ref, sum_wt, 0, j * width))
        counts = {}
        for ring, out, row, col in formed:
            k = counts[id(ring)] = counts.get(id(ring), -1) + 1
            cols = ring.shape[4] // 2
            for first in (0, cols):
                i = len(jobs)
                cut = (slice(first, first + cols), slice(col + first, col + first + cols))
                kind = sum_kinds.index(sum_shapes[i])
                args = (bufs[6 * i : 6 * i + 6], rss.at[kind], css.at[i], rrs, i * Sum.sems)
                jobs.append(Sum(spot, ring.at[k % 2], out, row, cut, *args))
        spread_block(shorts, short)
        small = []
        for k, peer in enumerate(peers):
            small.append(send(short, shorts_got.at[spot.f], ass.at[k], ars.at[k], peer))

    def set_out():
        met(n + 2)
        for copy in small:
            copy.start()
        pieces[0].start()
        shorts_got[spot.f] = short[...]

    events = []
    for i in range(len(pieces)):
        for kind, lag in enumerate((0,) + LAGS):
            events.append((i + lag, kind, i))
    events.sort()
    gone = [0]
    whole_at = {i: pos for pos, (_, kind, i) in enumerate(events) if kind == 3}
    on_whole = []

    def run_event():
        _, kind, i = events[gone[0]]
        gone[0] += 1
        getattr(pieces[i], ("after_z", "after_y", "after_x", "after_c")[kind])()
        if kind == 0:
            for ahead in (range(2, AHEAD + 1) if i == 0 else (i + AHEAD,)):
                if ahead < len(pieces):
                    pieces[ahead].start()
        if kind == 3:
            for call in on_whole:
                call(i)

    now = [-1]

    def step(count=1):
        now[0] += count
        while gone[0] < len(events) and events[gone[0]][0] <= now[0]:
            run_event()

    def gather_until(piece):
        while events and gone[0] <= whole_at[min(piece, len(pieces) - 1)]:
            step()


    def forward(line_ref, heads_ref, qkv_ref, wt_ref, wo_ref, idx_ref, tok, normed_ref):
        idx_copy = fetch(idx_in, idx_ref, late_sems.at[0])
        tok_copy = fetch(tok_in, tok, late_sems.at[1])
        loads = []
        for src, ref in ((wt_in, wt_ref), (wo_in, wo_ref)):
            starts = range(0, src.shape[3], width // 2)
            for col in list(starts[0::2]) + list(starts[1::2]):
                first = col % width
                dst = ref.at[col // width, :, :, :, first : first + width // 2]
                view = src.at[:, :, :, col : col + width // 2]
                loads.append(pltpu.make_async_copy(view, dst, load_sems.at[len(loads)]))
        if not fast:
            for load in loads:
                load.start()

        def begin(i):
            if i < len(loads):
                loads[i].start()

        on_whole.append(begin)
        idx_copy.wait()
        read_labels(plan, is_large, idx_ref, pick_ref, lab_ref)
        if fast:
            set_out()
        tok_copy.wait()
        normal, _ = norm_stats(tok[...].astype(f32))
        if fast:
            pieces[1].start()
            for copy in small:
                copy.wait()
            step()
            share, bshare = shorts[0].shape[1], shorts[11].shape[1]
            tab = []
            for f in range(n):
                part = shorts_got[f].astype(f32)
                wide = part.shape[1]
                vec_ref[:, f * share : (f + 1) * share] = part[:, wide - share :]
                tab.append(part[:, :bshare])
                be_ref[:, f * wide : (f + 1) * wide] = part[heads : heads + 1, :]
            tab = jnp.concatenate(tab, axis=1)
        else:
            vec_ref[...] = vec_in[...]
            be_ref[...] = be_in[...]
            tab = tab_in[...]
        table_lines(plan, tab, lab_ref, line_ref)
        step()
        normed = normal * vec(vec_ref, FIRST_GAIN) + vec(vec_ref, FIRST_SHIFT)
        normed_ref[...] = normed.astype(bf16)
        save(normed_ref, normed_out)
        for group in range(heads // 2):

            @pl.loop(2 * group, 2 * group + 2)
            def _(h):
                bias_head(plan, is_large, line_ref, image_ref, colsel_ref, h, heads_ref)

            step()
        def project(group):
            low, high = group * width // 2, (group + 1) * width // 2
            normed = normed_ref[...]
            gather_until(3 * group + 2)
            for j in range(3):
                loads[3 * group + j].wait()
                triple = mm(normed, wt_ref[j, :, :, :, low:high].reshape(width, width // 2))
                if j == 0:
                    triple = triple + vec_ref[QUERY_BIAS : QUERY_BIAS + 1, low:high]
                if j == 2:
                    triple = triple + vec_ref[VALUE_BIAS : VALUE_BIAS + 1, low:high]
                triple = triple.astype(bf16)
                if j == 0:
                    triple = triple * jnp.array(0.125, bf16)
                for p in range(pairs // 2):
                    where = j * pairs + group * (pairs // 2) + p
                    qkv_ref[where] = triple[:, 128 * p : 128 * (p + 1)]

        def attend_pair(p):
            q, k, v = qkv_ref[p], qkv_ref[pairs + p], qkv_ref[2 * pairs + p]
            lower = half_mask(rows)
            mixed = []
            for t in range(2):
                keep = lower if t == 0 else ~lower
                scores = mm(jnp.where(keep, q, jnp.zeros_like(q)), k, NT)
                scores = scores + heads_ref[2 * p + t].astype(f32)
                top = jnp.max(scores, axis=1, keepdims=True)
                exps = jnp.exp(scores - top)
                total = jnp.sum(exps, axis=1, keepdims=True)
                probs = (exps * (1.0 / total)).astype(bf16)
                heads_ref[2 * p + t] = probs
                mixed.append(mm(probs, v))
            mixed_ref[p] = jnp.where(lower, mixed[0], mixed[1]).astype(bf16)

        for group in range(2):
            project(group)
            step()

            @pl.loop(group * pairs // 2, (group + 1) * pairs // 2)
            def _(p):
                attend_pair(p)
                for i in range(group * pairs // 2, (group + 1) * pairs // 2):

                    @pl.when(p == i)
                    def _():
                        step()

                cut = pl.ds(2 * p, 2)
                dst = probs_out.at[cut]
                pltpu.make_async_copy(heads_ref.at[cut], dst, pair_sems.at[0, 3]).start()

        save(qkv_ref, qkv_out)

        gather_until(7)
        loads[6].wait()
        loads[7].wait()
        mixed = jnp.concatenate([mixed_ref[p] for p in range(pairs)], axis=1)
        branch = mm(mixed, matrix(wo_ref.at[0])) + vec(vec_ref, OUTPUT_BIAS)
        saves[0].wait()
        normed_ref[...] = branch.astype(bf16)
        save(normed_ref, branch_out)
        middle = tok[...].astype(f32) + vec(vec_ref, ATTEND_SCALE) * branch
        middle_ref[...] = middle
        normal, _ = norm_stats(middle)
        second = normal * vec(vec_ref, SECOND_GAIN) + vec(vec_ref, SECOND_SHIFT)
        half_ref[...] = second.astype(bf16)
        gather_until(7)
        on_whole.pop()
        step()
        pltpu.make_async_copy(heads_ref, probs_out, pair_sems.at[0, 3]).wait()
        for copy in saves[1:]:
            copy.wait()

    pl.run_scoped(
        forward,
        pltpu.VMEM((16, plan.lanes), f32),
        pltpu.VMEM((heads, rows, rows), bf16),
        pltpu.VMEM((3 * pairs, rows, 128), bf16),
        pltpu.VMEM((3, 4, 2, eighth, width), bf16),
        pltpu.VMEM((1, 4, 2, eighth, width), bf16),
        pltpu.VMEM(idx_in.shape, jnp.int32),
        pltpu.VMEM((rows, width), bf16),
        pltpu.VMEM((rows, width), bf16),
    )


    def note(idx, value):
        small_ref[idx : idx + 1, 0:width] = value

    limit = jnp.where(is_large, plan.large_len, 3 * plan.small_len)
    live = iota((rows, 1), 0) < limit

    def backward(feed_ref, dsec_ref, dtri_ref, lines_ref):
        used = {"rows": [], "cols": [], "all": 0}

        def push(kind, value, out, row, col):
            k = used[kind]
            if fast and len(k) >= 2:
                for job in k[-2]:
                    job.free()
            slot = (rows_ref if kind == "rows" else cols_ref).at[len(k) % 2]
            shard, cols = value.shape[0] // 8, value.shape[1]
            slot[:, :, 0:shard, :] = value.astype(bf16).reshape(4, 2, shard, cols)
            added = []
            if fast:
                added = jobs[used["all"] : used["all"] + 2]
                used["all"] += 2
                for job in added:
                    queue.add(job)
            else:
                view = out.at[:, :, pl.ds(row, shard), pl.ds(col, cols)]
                fetch(slot.at[:, :, pl.ds(0, shard)], view, stage_sems.at[0]).wait()
            k.append(added)

        branch_ref, cot_ref = dtri_ref.at[0], dtri_ref.at[1]
        cot_copy = fetch(cot_in, cot_ref, late_sems.at[0])
        branch_copy = fetch(branch_out, branch_ref, late_sems.at[1])

        def feed_forward(we_ref, wr_ref, pre_ref, act_ref, slope_ref):

            def we_loads(j):
                copies = []
                for f in range(8):
                    src = we_in.at[:, :, :, pl.ds((f * HIDDEN_BLOCKS + j) * unit, unit)]
                    dst = we_ref.at[j % 2, :, :, :, pl.ds(f * unit, unit)]
                    copies.append(pltpu.make_async_copy(src, dst, tile_sems.at[j % 2, f]))
                return copies

            def wr_load(j):
                src = wr_in.at[:, :, pl.ds(j * unit, unit)]
                return pltpu.make_async_copy(src, wr_ref.at[j % 2], tile_sems.at[j % 2, 8])

            gather_until(15)
            for j in range(2):
                for copy in we_loads(j):
                    copy.start()
            cot_copy.wait()
            grad = jnp.where(live, cot_ref[...].astype(f32), 0.0)
            dfeed_ref[...] = (vec(vec_ref, FEED_SCALE) * grad).astype(bf16)
            small_ref[...] = jnp.zeros_like(small_ref)
            note(REDUCE_BIAS, rows_sum(dfeed_ref[...].astype(f32)))

            def we_tile(j):
                return we_ref[j % 2].reshape(width, tile_cols)

            def before(j):
                for copy in we_loads(j):
                    copy.wait()
                bias = []
                for f in range(8):
                    first = (f * HIDDEN_BLOCKS + j) * unit
                    bias.append(be_ref[:, first : first + unit])
                pre_ref[...] = mm(half_ref[...], we_tile(j)) + jnp.concatenate(bias, axis=1)

            part = 16 * (-(-rows // 64))
            spans = [(low, min(low + part, rows)) for low in range(0, rows, part)]

            def activate(j, which):
                low, high = spans[which]
                value, slope = gelu_parts(pre_ref[low:high, :])
                act_ref[j % 2, low:high, :] = value.astype(bf16)
                slope_ref[j % 2, low:high, :] = slope.astype(bf16)

            before(0)
            for i in range(len(spans)):
                activate(0, i)
                step()
            for j in range(HIDDEN_BLOCKS):
                ahead = j + 1 < HIDDEN_BLOCKS
                gather_until(16 + 2 * (((j + 1) * unit - 1) // 96) + 1)
                wr_load(j).start()
                if ahead:
                    before(j + 1)
                d_feed = dfeed_ref[...]
                act = act_ref[j % 2]
                push("rows", mm(act, d_feed, TN), sum_wr, j * unit, 0)
                if ahead:
                    activate(j + 1, 0)
                queue.beat()
                step()
                wr_load(j).wait()
                wr = wr_ref[j % 2].reshape(tile_cols, width)
                feed = mm(act, wr)
                feed_ref[...] = feed if j == 0 else feed_ref[...] + feed
                if ahead:
                    activate(j + 1, 1)
                queue.beat()
                step()
                d_act = mm(d_feed, wr, NT)
                d_pre = (d_act * slope_ref[j % 2].astype(f32)).astype(bf16)
                dbe_ref[j : j + 1, :] = rows_sum(d_pre.astype(f32))
                if ahead:
                    activate(j + 1, 2)
                queue.beat()
                step()
                push("cols", mm(half_ref[...], d_pre, TN), sum_we, 0, j * tile_cols)
                if ahead:
                    activate(j + 1, 3)
                queue.beat()
                step()
                d_second = mm(d_pre, we_tile(j), NT)
                dsec_ref[...] = d_second if j == 0 else dsec_ref[...] + d_second
                if j + 2 < HIDDEN_BLOCKS:
                    for copy in we_loads(j + 2):
                        copy.start()
                queue.beat()

        pl.run_scoped(
            feed_forward,
            pltpu.VMEM((2, 4, 2, eighth, tile_cols), bf16),
            pltpu.VMEM((2, 4, 2, unit, width), bf16),
            pltpu.VMEM((rows, tile_cols), f32),
            pltpu.VMEM((2, rows, tile_cols), bf16),
            pltpu.VMEM((2, rows, tile_cols), bf16),
        )

        def attention(
            tile_ref, qkv_ref, probs_ref, dmix_ref, large_ref, strip_ref, tail_ref
        ):
            def pair_loads(p):
                slot = p % 3
                probs = probs_out.at[pl.ds(2 * p, 2)]
                copies = [pltpu.make_async_copy(probs, probs_ref.at[slot], pair_sems.at[slot, 3])]
                for part in range(3):
                    src, dst = qkv_out.at[part * pairs + p], qkv_ref.at[p % 2, part]
                    copies.append(pltpu.make_async_copy(src, dst, pair_sems.at[slot, part]))
                return copies

            tiles = [pltpu.make_async_copy(wo_in, tile_ref.at[0], tile_sems.at[0, 0])]
            for j in range(3):
                src = wt_in.at[:, :, :, pl.ds(j * width, width)]
                slot = (1 + j) % 2
                tiles.append(pltpu.make_async_copy(src, tile_ref.at[slot], tile_sems.at[slot, 0]))

            def tile(i):
                tiles[i].wait()
                return matrix(tile_ref.at[i % 2])

            tiles[0].start()
            tiles[1].start()
            for copy in pair_loads(0):
                copy.start()
            branch_copy.wait()
            feed_out = feed_ref[...] + vec(vec_ref, REDUCE_BIAS)
            middle = middle_ref[...]
            half_ref[...] = (middle + vec(vec_ref, FEED_SCALE) * feed_out).astype(bf16)
            out_copy = fetch(half_ref, out_ref, save_sems.at[0])
            grad = jnp.where(live, cot_ref[...].astype(f32), 0.0)
            d_second = dsec_ref[...]
            normal, inv = norm_stats(middle)
            d_middle = grad + norm_back(d_second, vec(vec_ref, SECOND_GAIN), normal, inv)
            d_branch = (vec(vec_ref, ATTEND_SCALE) * d_middle).astype(bf16)
            queue.beat()
            note(FEED_SCALE, rows_sum(grad * feed_out))
            note(SECOND_GAIN, rows_sum(d_second * normal))
            note(SECOND_SHIFT, rows_sum(d_second))
            note(ATTEND_SCALE, rows_sum(d_middle * branch_ref[...].astype(f32)))
            note(OUTPUT_BIAS, rows_sum(d_branch.astype(f32)))
            dsec_ref[...] = d_middle
            dmix_ref[...] = mm(d_branch, tile(0), NT).astype(bf16)
            tiles[2].start()
            mixed = jnp.concatenate([mixed_ref[p] for p in range(pairs)], axis=1)
            push("rows", mm(mixed, d_branch, TN), sum_wo, 0, 0)
            normed_ref = dfeed_ref
            normed_copy = fetch(normed_out, normed_ref, late_sems.at[0])
            queue.beat()

            def ds_copy(p):
                slot = p % 3
                dst = ds_out.at[pl.ds(2 * p, 2)]
                return pltpu.make_async_copy(probs_ref.at[slot], dst, ds_sems.at[slot])

            def pair_back(p):
                slot = p % 3
                for copy in pair_loads(p):
                    copy.wait()

                @pl.when(p >= 2)
                def _():
                    ds_copy(p - 2).wait()

                @pl.when(p + 1 < pairs)
                def _():
                    for copy in pair_loads(p + 1):
                        copy.start()

                lanes = pl.ds(pl.multiple_of(128 * p, 128), 128)
                q, k, v = [qkv_ref[p % 2, part] for part in range(3)]
                do = dmix_ref[:, lanes]
                lower = half_mask(rows)
                prod = do.astype(f32) * mixed_ref[p].astype(f32)
                dq, dk, dv = [], [], []
                for t in range(2):
                    keep = lower if t == 0 else ~lower
                    d_out = jnp.where(keep, do, jnp.zeros_like(do))
                    delta = jnp.sum(jnp.where(keep, prod, 0.0), axis=1, keepdims=True)
                    d_probs = mm(d_out, v, NT)
                    probs = probs_ref[slot, t]
                    dv.append(mm(probs, do, TN))
                    d_scores = (probs.astype(f32) * (d_probs - delta)).astype(bf16)
                    probs_ref[slot, t] = d_scores
                    dq.append(mm(d_scores, k))
                    dk.append(mm(d_scores, q, TN))
                dtri_ref[0, :, lanes] = (jnp.where(lower, dq[0], dq[1]) * 0.125).astype(bf16)
                dtri_ref[1, :, lanes] = jnp.where(lower, dk[0], dk[1]).astype(bf16)
                dtri_ref[2, :, lanes] = jnp.where(lower, dv[0], dv[1]).astype(bf16)
                ds_copy(p).start()

            span = width // 3
            for group in range(3):

                @pl.loop(2 * group, 2 * group + 2)
                def _(p):
                    pair_back(p)

                    @pl.when(p == 2 * group)
                    def _():
                        queue.beat()

                queue.beat()
                if group == 0:
                    normed_copy.wait()
                d_part = [dtri_ref[j, :, group * span : (group + 1) * span] for j in range(3)]
                d_part = jnp.concatenate(d_part, axis=1)
                push("rows", mm(normed_ref[...], d_part, TN), sum_wt, 0, group * width)
                queue.beat()

            out_copy.wait()
            tok_ref = half_ref
            tok_copy = fetch(tok_in, tok_ref, late_sems.at[1])
            for j in range(3):
                d_part = dtri_ref[j]
                part = mm(d_part, tile(1 + j), NT)
                feed_ref[...] = part if j == 0 else feed_ref[...] + part
                if j == 0:
                    tiles[3].start()
                if j != 1:
                    note(QUERY_BIAS if j == 0 else VALUE_BIAS, rows_sum(d_part.astype(f32)))
                queue.beat()
            tok_copy.wait()
            normal, inv = norm_stats(tok_ref[...].astype(f32))
            note(FIRST_GAIN, rows_sum(feed_ref[...] * normal))
            note(FIRST_SHIFT, rows_sum(feed_ref[...]))
            queue.beat()

            ds_copy(pairs - 2).wait()
            ds_copy(pairs - 1).wait()

            def ds_load(p):
                src, slot = ds_out.at[pl.ds(2 * p, 2)], p % 3
                return pltpu.make_async_copy(src, probs_ref.at[slot], pair_sems.at[slot, 3])

            ds_load(0).start()

            @pl.loop(0, pairs)
            def _(p):
                ds_load(p).wait()

                @pl.when(p + 1 < pairs)
                def _():
                    ds_load(p + 1).start()

                for t in range(2):
                    ds = probs_ref.at[p % 3, t]
                    args = (image_ref, colsel_ref, large_ref, strip_ref, tail_ref, 2 * p + t, is_large)
                    fold_head(plan, ds, *args)
                for i in range(pairs):

                    @pl.when(p == i)
                    def _():
                        queue.beat()

            lines_ref[...] = fold_lines(plan, large_ref, strip_ref, tail_ref, is_large)

        def first_norm_back():
            tok_ref, normed_ref = half_ref, dfeed_ref
            normal, inv = norm_stats(tok_ref[...].astype(f32))
            back = norm_back(feed_ref[...], vec(vec_ref, FIRST_GAIN), normal, inv)
            normed_ref[...] = (dsec_ref[...] + back).astype(bf16)
            return fetch(normed_ref, tok_out, save_sems.at[1])

        pl.run_scoped(
            attention,
            pltpu.VMEM((2, 4, 2, eighth, width), bf16),
            pltpu.VMEM((2, 3, rows, 128), bf16),
            pltpu.VMEM((3, 2, rows, rows), bf16),
            pltpu.VMEM((rows, width), bf16),
            pltpu.VMEM((heads, plan.gl, plan.strip_l), f32),
            pltpu.VMEM((heads, 16, plan.strip_s), f32),
            pltpu.VMEM((heads, 1, 128), f32),
        )
        queue.beat()
        line_of = lambda chunk: lines_ref[:, 128 * chunk : 128 * (chunk + 1)]
        d_table = table_from_lines(plan, line_of, lab_ref, plan.buckets)
        wide = hidden // 8

        def bias_sum(f):
            parts = [dbe_ref[j : j + 1, f * unit : (f + 1) * unit] for j in range(HIDDEN_BLOCKS)]
            return jnp.concatenate(parts, axis=1)

        if not fast:
            vec_out[...] = small_ref[...]
            for f in range(8):
                be_out[:, f * wide : (f + 1) * wide] = bias_sum(f)
            tab_out[...] = d_table
            first_norm_back().wait()
            return

        share, bshare = width // n, plan.buckets // n
        for f in range(n):
            value = jnp.concatenate(
                [
                    d_table[:, f * bshare : (f + 1) * bshare],
                    jnp.zeros((16, wide - bshare - share), f32),
                    small_ref[:, f * share : (f + 1) * share],
                ],
                axis=1,
            )
            bias = jnp.broadcast_to(bias_sum(f), (16, wide))
            block[f] = jnp.where(iota((16, wide), 0) == heads, bias, value)
        sums = []
        for k, peer in enumerate(peers):
            dst = (spot.f + k + 1) % n
            sums.append(send(block.at[dst], got.at[k], bss.at[k], brs.at[k], peer))
            sums[k].start()
        tok_copy = first_norm_back()
        queue.beat()
        value = block[spot.f]
        for k, copy in enumerate(sums):
            copy.wait_recv()
            value = value + got[k]
        reps[spot.rep] = value
        for k, other in enumerate(others):
            mine = reps.at[spot.rep]
            sums.append(send(mine, mine, bss.at[n - 1 + k], brs.at[n - 1 + k], other))
            sums[-1].start()
        queue.beat()
        for copy in sums[n - 1 :]:
            copy.wait_recv()
        small_out[...] = (reps[0] + reps[1]) + (reps[2] + reps[3])
        queue.drain()
        tok_copy.wait()
        for copy in sums:
            copy.wait_send()
        for job in jobs:
            job.free()
        flat = normed_out
        for kind, shape in enumerate(sum_kinds):
            count = sum_shapes.count(shape)
            for idx, out_rows in enumerate(Sum.sent_rows(n // 2, shape[0])):
                total = count * out_rows * shape[1] // width
                view = flat.at[pl.ds(0, total)]
                pltpu.make_async_copy(view, view, rss.at[kind, idx + 1]).wait()
        for at, whole in enumerate(wholes):
            for copy in Piece.sent_waits(n // 2, whole, gss.at[at]):
                copy.wait()

    pl.run_scoped(
        backward,
        pltpu.VMEM((rows, width), f32),
        pltpu.VMEM((rows, width), f32),
        pltpu.VMEM((3, rows, width), bf16),
        pltpu.VMEM((16, plan.lanes), f32),
    )


AHEAD, LAGS = 3, (2, 4, 5)
GATHER_ORDER = (0, 1, 2, 3)


def layer(plan, kind, tokens, cot, large_index, n, fast, shorts, shards):
    rows, width = tokens.shape
    heads = plan.heads
    pairs = heads // 2
    sds = jax.ShapeDtypeStruct
    hidden = shards[2].shape[1]
    unit = hidden // 8 // HIDDEN_BLOCKS
    eighth = width // 8
    cuts = piece_cuts([w.shape for w in shards]) if fast else []
    sum_shapes = [(unit, width // 2)] * 2 + [(eighth, 4 * unit)] * 2
    sum_shapes = sum_shapes * HIDDEN_BLOCKS + [(eighth, width // 2)] * 8
    colsel = jnp.asarray(plan.selector_arrays()[1], bf16)
    inputs = [kind, tokens, cot, large_index, pick_plan(plan), colsel, image_selectors(plan)]
    in_specs = [smem_spec] + [any_spec] * 3 + [vmem_spec] * 3
    outs, out_specs = [sds((rows, width), bf16)] * 2, [any_spec] * 2
    if fast:
        wide = hidden // n
        inputs += shorts + shards
        in_specs += [vmem_spec] * 12 + [any_spec] * 4
        outs += [sds(w.shape, bf16) for w in shards]
        outs += [sds((16, wide), f32)]
        out_specs += [vmem_spec] * 5
        outs += [sds((4, 2) + w.shape, bf16) for w in shards]
        out_specs += [any_spec] * 4
    else:
        wholes, vecs, be, table = gather_plain(shorts, shards, n)
        wholes = [w.reshape(4, 2, w.shape[0] // 8, w.shape[1]) for w in wholes]
        inputs += [vecs, be, table.astype(f32)] + wholes
        in_specs += [vmem_spec] * 3 + [any_spec] * 4
        outs += [sds(w.shape, bf16) for w in wholes]
        outs += [sds((16, width), f32), sds((1, hidden), f32), sds((16, plan.buckets), f32)]
        out_specs += [any_spec] * 4 + [vmem_spec] * 3
    kept = len(outs)
    square = sds((heads, rows, rows), bf16)
    flat = sds((rows, width), bf16)
    outs += [flat, flat, sds((3 * pairs, rows, 128), bf16), square, square]
    out_specs += [any_spec] * 5
    dma = pltpu.SemaphoreType.DMA
    scratch = [
        pltpu.VMEM((16, width), f32),
        pltpu.VMEM((1, hidden), f32),
        pltpu.VMEM((2, plan.lanes), jnp.int32),
        pltpu.VMEM((rows, width), f32),
        pltpu.VMEM((2, rows, width), bf16),
        pltpu.VMEM((pairs, rows, 128), bf16),
        pltpu.VMEM((16, width), f32),
        pltpu.VMEM((8, 8 * unit), f32),
        pltpu.VMEM((2, 4, 2, unit, width), bf16),
        pltpu.VMEM((2, 4, 2, eighth, 8 * unit), bf16),
        dma((8,)),
        dma((4,)),
        dma((2, 9)),
        dma((2,)),
        dma((3, 4)),
        dma((3,)),
        dma((1,)),
    ]
    kernel_params = dict(vmem_limit_bytes=vmem_bytes)
    if fast:
        for shape in sum_shapes:
            scratch += Sum.buffers(n // 2, *shape)
        scratch += [
            pltpu.VMEM((16, wide), bf16),
            pltpu.VMEM((n, 16, wide), bf16),
            pltpu.VMEM((n, 16, wide), f32),
            pltpu.VMEM((n - 1, 16, wide), f32),
            pltpu.VMEM((4, 16, wide), f32),
            dma((4, 4)),
            dma((len(cuts) * Piece.sems,)),
            dma((n - 1,)),
            dma((n - 1,)),
            dma((len(set(sum_shapes)), 6)),
            dma((len(sum_shapes),)),
            dma((len(sum_shapes) * Sum.sems,)),
            dma((n + 2,)),
            dma((n + 2,)),
        ]
        kernel_params.update(collective_id=1, has_side_effects=True)
    result = pl.pallas_call(
        functools.partial(layer_kernel, plan, n, fast, cuts, sum_shapes),
        in_specs=in_specs,
        out_specs=out_specs,
        out_shape=outs,
        scratch_shapes=scratch,
        compiler_params=pltpu.CompilerParams(**kernel_params),
        name="layer",
    )(*inputs)[:kept]
    out, token_grad = result[:2]
    if fast:
        return out, token_grad, result[2:6], result[6]
    wt, wo, we, wr = [g.reshape(-1, g.shape[3]) for g in result[2:6]]
    wt = wt.reshape(width, 3, 3, width // 3).transpose(0, 2, 1, 3).reshape(width, 3 * width)
    we = we.reshape(width, HIDDEN_BLOCKS, 8, unit).transpose(0, 2, 1, 3).reshape(width, hidden)
    sums, block = reduce_plain([wt, wo, we, wr], *result[6:9], n)
    wt, wo, we, wr = sums
    wt = wt.reshape(-1, 3, 3, width // 3).transpose(0, 2, 1, 3).reshape(wt.shape)
    we = we.reshape(-1, 8, HIDDEN_BLOCKS, unit).transpose(0, 2, 1, 3).reshape(we.shape)
    return out, token_grad, [wt, wo, we, wr], block


def per_device(
    tokens,
    slot_kinds,
    small_index,
    large_index,
    first_gain,
    first_shift,
    triple_weight,
    query_bias,
    value_bias,
    bias_table,
    output_weight,
    output_bias,
    attend_scale,
    second_gain,
    second_shift,
    expand_weight,
    expand_bias,
    reduce_weight,
    reduce_bias,
    feed_scale,
    cotangent,
):
    _, rows, width = tokens.shape
    heads = bias_table.shape[2]
    buckets = bias_table.shape[1] * lax.axis_size("fsdp")
    plan = Plan(small_index.shape[0], large_index.shape[0], rows, heads, buckets)
    tokens, cotangent = tokens[0], cotangent[0]
    short = [
        first_gain,
        first_shift,
        query_bias,
        value_bias,
        output_bias,
        attend_scale,
        second_gain,
        second_shift,
        reduce_bias,
        feed_scale,
    ]
    n = width // first_gain.shape[1]
    fast = fast_shape(
        lax.axis_size("rep"), n, [w.shape[1] for w in (triple_weight, output_weight, reduce_weight)]
    )
    shards = [w[0] for w in (triple_weight, output_weight, expand_weight, reduce_weight)]
    shorts = short + [expand_bias, bias_table[0].T]
    block_output, token_grad, sums, block = layer(
        plan, slot_kinds, tokens, cotangent, large_index, n, fast, shorts, shards
    )
    return wrap(block_output, token_grad, sums, block, first_gain.shape[1], bias_table.shape[1:])


def wrap_kernel(share, heads, out_in, tok_in, wt_in, wo_in, we_in, wr_in, block_ref, *outs):
    (
        out,
        tok,
        first_gain,
        first_shift,
        triple_weight,
        query_bias,
        value_bias,
        bias_table,
        output_weight,
        output_bias,
        attend_scale,
        second_gain,
        second_shift,
        expand_weight,
        expand_bias,
        reduce_weight,
        reduce_bias,
        feed_scale,
    ) = outs
    out[0] = out_in[...]
    tok[0] = tok_in[...]
    width = wt_in.shape[1] // 3
    span = width // 3
    for g in range(3):
        for part in range(3):
            first = g * width + part * span
            value = wt_in[:, first : first + span].astype(f32)
            triple_weight[0, :, part * width + g * span : part * width + (g + 1) * span] = value
    output_weight[0] = wo_in[...].astype(f32)
    reduce_weight[0] = wr_in[...].astype(f32)
    unit = 128
    count = we_in.shape[1] // (unit * HIDDEN_BLOCKS)
    for g in range(HIDDEN_BLOCKS):
        for f in range(count):
            value = we_in[:, (g * count + f) * unit : (g * count + f + 1) * unit].astype(f32)
            first = (f * HIDDEN_BLOCKS + g) * unit
            expand_weight[0, :, first : first + unit] = value
    first = block_ref.shape[1] - share
    rows = {
        FIRST_GAIN: first_gain,
        FIRST_SHIFT: first_shift,
        QUERY_BIAS: query_bias,
        VALUE_BIAS: value_bias,
        OUTPUT_BIAS: output_bias,
        ATTEND_SCALE: attend_scale,
        SECOND_GAIN: second_gain,
        SECOND_SHIFT: second_shift,
        REDUCE_BIAS: reduce_bias,
        FEED_SCALE: feed_scale,
    }
    for idx, ref in rows.items():
        ref[...] = block_ref[idx : idx + 1, first:]
    expand_bias[...] = block_ref[heads : heads + 1, :]
    for h in range(heads):
        bias_table[h] = block_ref[h : h + 1, : bias_table.shape[2]]


def wrap(block_output, token_grad, sums, block, share, table_shape):
    wt, wo, we, wr = sums
    sds = jax.ShapeDtypeStruct
    vector = sds((1, share), f32)
    whole_of = lambda w: sds((1,) + w.shape, f32)
    bshare, heads = table_shape
    triple = whole_of(wt)
    outs = [sds((1,) + block_output.shape, bf16)] * 2
    outs += [vector, vector, triple, vector, vector, sds((heads, 1, bshare), f32)]
    outs += [whole_of(wo)] + [vector] * 4 + [whole_of(we), sds((1, block.shape[1]), f32)]
    outs += [whole_of(wr), vector, vector]
    result = pl.pallas_call(
        functools.partial(wrap_kernel, share, heads),
        in_specs=[vmem_spec] * 7,
        out_specs=[vmem_spec] * 18,
        out_shape=outs,
        compiler_params=pltpu.CompilerParams(vmem_limit_bytes=vmem_bytes),
        name="wrap",
    )(block_output, token_grad, wt, wo, we, wr, block)
    result = list(result)
    result[7] = result[7].transpose(1, 2, 0)
    return tuple(result)


def solution(mesh):
    rows = P(("rep", "fsdp"), None, None)
    vector = P(None, "fsdp")
    matrix = P(None, "fsdp", None)
    weights = (
        vector,
        vector,
        matrix,
        vector,
        vector,
        matrix,
        matrix,
        vector,
        vector,
        vector,
        vector,
        matrix,
        vector,
        matrix,
        vector,
        vector,
    )
    return jax.shard_map(
        per_device,
        mesh=mesh,
        in_specs=(rows, P(("rep", "fsdp")), P(), P()) + weights + (rows,),
        out_specs=(rows, rows) + weights,
        check_vma=False,
    )
```

```python
import functools

import jax
import jax.numpy as jnp
import numpy as np
from jax import lax
from jax.experimental import pallas as pl
from jax.experimental.pallas import tpu as pltpu
from jax.sharding import PartitionSpec as P

f32 = jnp.float32
bf16 = jnp.bfloat16
norm_eps = 1e-06
neg_fill = -1000000000.0
vmem_bytes = 62 << 20

NN = (((1,), (0,)), ((), ()))
NT = (((1,), (1,)), ((), ()))
TN = (((0,), (0,)), ((), ()))


def mm(left, right, dims=NN):
    return lax.dot_general(left, right, dims, preferred_element_type=f32)


def round_up(value, unit):
    return -(-value // unit) * unit


class Plan:
    def __init__(self, small_len, large_len, rows, heads, buckets):
        self.heads, self.buckets = heads, buckets
        self.rows = rows
        self.small_len, self.large_len = small_len, large_len
        self.gs = int(round((small_len - 1) ** 0.5))
        self.gl = int(round((large_len - 1) ** 0.5))
        gl, gs = self.gl, self.gs
        self.strip_l = round_up(2 * gl * gl, 128)
        self.strip_s = round_up(2 * gs * (2 * gs - 1) + gs, 128)
        self.line = 2 * self.strip_l
        self.lanes = self.line + 128
        self.pad_cols = round_up(2 * gs * gs + 1, 128)
        self.pad_rows = 16 * gs
        self.cls_col = 2 * gs * gs
        self.cls_row = gs

    def place(self, di, dj, limit):
        gl = self.gl
        good = (np.abs(di) < limit) & (np.abs(dj) < limit)
        row = 1 + gl * np.maximum(di, 0) + np.maximum(dj, 0)
        col = 1 + gl * np.maximum(-di, 0) + np.maximum(-dj, 0)
        return np.where(good, row, 0), np.where(good, col, 0), good

    def positions(self):
        gl, gs = self.gl, self.gs
        x = np.arange(self.strip_l)
        rows, cols, goods = [], [], []
        for parity in range(2):
            m = 2 * ((x + gl) // (2 * gl)) if parity == 0 else 2 * (x // (2 * gl)) + 1
            t = x - gl * m
            r, c, g = self.place(gl - m, -t, gl)
            rows.append(r), cols.append(c), goods.append(g)
        large = [np.concatenate(v) for v in (rows, cols, goods)]
        x = np.arange(self.strip_s)
        m = x // (2 * gs)
        t = x - 2 * gs * m - gs
        small = [np.resize(np.zeros(1, v.dtype), self.line) for v in large]
        for dst, src in zip(small, self.place(gs - 1 - m, -t, gs)):
            dst[: self.strip_s] = src
        tail_r, tail_c, tail_g = np.zeros(128, int), np.zeros(128, int), np.zeros(128, bool)
        tail_r[:3], tail_c[:3], tail_g[:3] = (0, 1, 0), (1, 0, 0), True
        out = []
        for base in (large, small):
            out.append([np.concatenate(v) for v in zip(base, (tail_r, tail_c, tail_g))])
        return out

    def selector_arrays(self):
        gs = self.gs
        rows = np.zeros((self.rows, self.pad_rows), np.float32)
        cols = np.zeros((self.pad_cols, self.rows), np.float32)
        for image in range(3):
            for tok in range(self.small_len):
                r = image * self.small_len + tok
                i, j = divmod(tok - 1, gs)
                rows[r, self.cls_row if tok == 0 else 16 * i + j] = 1
                cols[self.cls_col if tok == 0 else 2 * gs * i + j, r] = 1
        return rows, cols

    def selectors(self):
        rows, cols = self.selector_arrays()
        return jnp.asarray(rows, bf16), jnp.asarray(cols, bf16)


def iota(shape, dim):
    return lax.broadcasted_iota(jnp.int32, shape, dim)


def pick_plan(plan):
    out = []
    for r, c, good in plan.positions():
        down = good & ((r - 1) // plan.gl >= (c - 1) // plan.gl)
        key = np.where(down, r, c)
        sub = np.where(down, c, r) - 1
        valid = good.copy()
        valid[plan.line :] = False
        out.append(np.stack([key, sub, down.astype(int), valid.astype(int)]))
    return jnp.asarray(np.concatenate(out), jnp.int32)


def lane_chunks(lanes, size=512):
    return [(low, min(low + size, lanes)) for low in range(0, lanes, size)]


def read_labels(plan, is_large, idx_ref, pick_ref, lab_ref):
    size, gl = idx_ref.shape[0], plan.gl
    across = idx_ref[1 : 1 + gl, :]
    down = idx_ref[:, 1 : 1 + gl].astype(f32).T.astype(jnp.int32)
    sides = []
    for v in (across, down):
        sides += [(v >> 6).astype(f32), (v & 63).astype(f32)]
    sides = jnp.concatenate(sides, axis=0).astype(bf16)
    for low, high in lane_chunks(plan.line):
        lanes, count = slice(low, high), high - low
        key, sub, use_down, valid = [
            jnp.where(is_large, pick_ref[i : i + 1, lanes], pick_ref[4 + i : 5 + i, lanes])
            for i in range(4)
        ]
        hot = jnp.where(iota((size, count), 0) == key, 1.0, 0.0).astype(bf16)
        here = iota((gl, count), 0) == sub
        rows = mm(sides, hot)
        for digit in range(2):
            a = rows[digit * gl : (digit + 1) * gl]
            b = rows[(2 + digit) * gl : (3 + digit) * gl]
            found = jnp.where(here, jnp.where(use_down == 1, b, a), 0.0)
            found = jnp.sum(found, axis=0, keepdims=True).astype(jnp.int32)
            lab_ref[digit : digit + 1, lanes] = jnp.where(valid == 1, found, -1)
    lane = iota((1, 128), 1)
    tail = jnp.where(lane == 0, idx_ref[0:1, 1:2], -1)
    tail = jnp.where(lane == 1, idx_ref[1:2, 0:1], tail)
    tail = jnp.where(lane == 2, idx_ref[0:1, 0:1], tail)
    lab_ref[0:1, plan.line : plan.line + 128] = jnp.where(tail < 0, -1, tail >> 6)
    lab_ref[1:2, plan.line : plan.line + 128] = jnp.where(tail < 0, -1, tail & 63)


def table_lines(plan, tab, lab_ref, line_ref):
    count = tab.shape[1] // 64
    split = jnp.concatenate([tab[:, 64 * i : 64 * (i + 1)] for i in range(count)], axis=0)
    split = split.astype(bf16)
    for low, high in lane_chunks(plan.lanes):
        first, second = lab_ref[0:1, low:high], lab_ref[1:2, low:high]
        hot = jnp.where(iota((64, high - low), 0) == second, 1.0, 0.0).astype(bf16)
        rows = mm(split, hot)
        parts = [jnp.zeros((16, high - low), f32)] * 4
        for i in range(count):
            parts[i % 4] = jnp.where(first == i, rows[16 * i : 16 * (i + 1)], parts[i % 4])
        line_ref[:, low:high] = (parts[0] + parts[1]) + (parts[2] + parts[3])


def table_from_lines(plan, line_of, lab_ref, buckets):
    count = buckets // 64
    total = jnp.zeros((32 * count, 64), f32)
    for chunk in range(plan.lanes // 128):
        lanes = slice(chunk * 128, (chunk + 1) * 128)
        first, second = lab_ref[0:1, lanes], lab_ref[1:2, lanes]
        hot = jnp.where(iota((64, 128), 0) == second, 1.0, 0.0).astype(bf16)
        part = line_of(chunk)
        high = part.astype(bf16)
        low = (part - high.astype(f32)).astype(bf16)
        both = jnp.concatenate([high, low], axis=0)
        stack = [jnp.where(first == i, both, jnp.zeros_like(both)) for i in range(count)]
        total = total + mm(jnp.concatenate(stack, axis=0), hot, NT)
    pieces = []
    for i in range(count):
        pieces.append(total[32 * i : 32 * i + 16] + total[32 * i + 16 : 32 * i + 32])
    return jnp.concatenate(pieces, axis=1)


def segments(plan, is_large, ids):
    n = plan.small_len
    small = jnp.where(ids >= n, 1, 0) + jnp.where(ids >= 2 * n, 1, 0) + jnp.where(ids >= 3 * n, 1, 0)
    return jnp.where(is_large, jnp.where(ids < plan.large_len, 0, 3), small)


def line_of_head(ref, h):
    return jnp.sum(jnp.where(iota((16, 1), 0) == h, ref[...], 0.0), axis=0, keepdims=True)


def large_strip(plan, line):
    gl, span = plan.gl, plan.strip_l
    rolled = []
    for parity in range(2):
        part = jnp.broadcast_to(line[:, parity * span : (parity + 1) * span], (gl, span))
        rolled.append(pltpu.roll(part, 0, axis=1, stride=1, stride_axis=0))
    odd = (iota((1, span), 1) + span - 1) % span // gl % 2
    odd = jnp.where(iota((gl, 1), 0) == 0, 1 - odd, odd)
    strip = jnp.where(odd == 1, rolled[1], rolled[0])
    return jnp.concatenate([strip, strip[:, :128]], axis=1)


def band_move(plan, a):
    return plan.gl * (plan.gl - a)


def small_padded(plan, line, tail):
    gs, span = plan.gs, plan.strip_s
    line = jnp.broadcast_to(line[:, 0:span], (16, span))
    strip = pltpu.roll(line, 0, axis=1, stride=1, stride_axis=0)
    col = iota((1, plan.pad_cols), 1)
    is_col = col == plan.cls_col
    is_row = iota((16, 1), 0) == plan.cls_row
    bands = []
    for i in range(gs):
        move = 2 * gs * (gs - 1 - i) + gs
        band = pltpu.roll(strip, (span - move) % span, axis=1)[:, : plan.pad_cols]
        band = jnp.where(is_col, tail[:, 1:2], band)
        if i == 0:
            edge = jnp.where(is_col, tail[:, 2:3], tail[:, 0:1])
            band = jnp.where(is_row, edge, band)
        bands.append(band)
    return jnp.concatenate(bands, axis=0).astype(bf16)


def small_blocks(plan, line, tail, pick, colsel):
    rows = plan.rows
    wide = round_up(rows, 128)
    cols = mm(small_padded(plan, line, tail), colsel[:, 0:256]).astype(bf16)
    out = []
    for image, ((r0, r1), (l0, _)) in enumerate(image_rows(plan)):
        start = 256 * image
        block = mm(pick[:, start : start + r1 - r0], cols, TN)
        shift = image * plan.small_len - l0
        last = l0 + round_up(shift + plan.small_len, 128)
        if last - l0 > 256:
            block = jnp.concatenate([block, jnp.zeros((r1 - r0, last - l0 - 256), f32)], axis=1)
        if shift:
            block = pltpu.roll(block, shift, axis=1)
        parts = [block]
        if l0:
            parts.insert(0, jnp.zeros((r1 - r0, l0), f32))
        if last < wide:
            parts.append(jnp.zeros((r1 - r0, wide - last), f32))
        out.append((r0, r1, jnp.concatenate(parts, axis=1)))
    return out


def bias_head(plan, is_large, line_ref, pick, colsel, h, out_ref):
    gl, rows = plan.gl, plan.rows
    wide = round_up(rows, 128)
    line = line_of_head(line_ref, h)
    tail = line[:, plan.line : plan.line + 128]
    blocks = small_blocks(plan, line, tail, pick, colsel)
    strip = large_strip(plan, line)
    span = strip.shape[1]
    col = iota((1, wide), 1)
    seg_col = segments(plan, is_large, col)
    bands = -(-rows // gl)
    for pair in range(-(-bands // 2)):
        first = 2 * gl * pair
        count = min(2 * gl, rows - first)
        parts = []
        for a in range(2 * pair, 2 * pair + 2):
            if a >= bands:
                continue
            move = band_move(plan, a)
            low = move // 128 * 128
            piece = strip[:, low : min(low + wide + 128, span)]
            if piece.shape[1] < wide + 128:
                piece = jnp.concatenate(
                    [piece, jnp.zeros((gl, wide + 128 - piece.shape[1]), f32)], axis=1
                )
            turn = (wide + 128 - (move - low)) % (wide + 128)
            parts.append((pltpu.roll(piece, turn, axis=1) if turn else piece)[:, :wide])
        block = (jnp.concatenate(parts, axis=0) if len(parts) > 1 else parts[0])[:count]
        row = iota((count, 1), 0) + first
        edge = jnp.where(col[:, :128] == 0, tail[:, 1:2], block[:, :128])
        block = jnp.concatenate([edge, block[:, 128:]], axis=1)
        if first == 0:
            block = jnp.where(row == 0, jnp.where(col == 0, tail[:, 2:3], tail[:, 0:1]), block)
        if first + count > plan.large_len:
            block = jnp.where(row < plan.large_len, block, 0.0)
        small = None
        for r0, r1, value in blocks:
            low, high = max(first, r0), min(first + count, r1)
            if low >= high:
                continue
            part = [value[low - r0 : high - r0]]
            if low > first:
                part.insert(0, jnp.zeros((low - first, wide), f32))
            if high < first + count:
                part.append(jnp.zeros((first + count - high, wide), f32))
            part = jnp.concatenate(part, axis=0) if len(part) > 1 else part[0]
            small = part if small is None else small + part
        block = jnp.where(is_large, block, small)
        block = jnp.where(segments(plan, is_large, row) == seg_col, block, neg_fill)
        out_ref[h, first : first + count, :] = block[:, :rows].astype(bf16)


def norm_stats(values):
    mean = jnp.mean(values, axis=1, keepdims=True)
    centred = values - mean
    var = jnp.mean(centred * centred, axis=1, keepdims=True)
    inv = lax.rsqrt(var + norm_eps)
    return centred * inv, inv


def norm_back(d_out, gain, normal, inv):
    d_normal = d_out * gain
    mean_d = jnp.mean(d_normal, axis=1, keepdims=True)
    mean_dn = jnp.mean(d_normal * normal, axis=1, keepdims=True)
    return inv * (d_normal - mean_d - normal * mean_dn)


def rows_sum(values):
    return jnp.sum(values, axis=0, keepdims=True)


def gelu_parts(v):
    size = jnp.abs(v)
    bell = jnp.exp(-0.5 * v * v)
    below = 1.0 + (0.3275911 * 0.7071067811865476) * size
    t = pl.reciprocal(below, approx=True)
    t = t * (2.0 - below * t)
    poly = t * (
        0.127414796
        + t * (-0.142248368 + t * (0.7107068705 + t * (-0.7265760135 + t * 0.5307027145)))
    )
    tail = poly * bell
    phi = jnp.where(v < 0, tail, 1.0 - tail)
    return v * phi, phi + v * bell * 0.3989422804014327


BE_ROW = 10
(
    FIRST_GAIN,
    FIRST_SHIFT,
    QUERY_BIAS,
    VALUE_BIAS,
    OUTPUT_BIAS,
    ATTEND_SCALE,
    SECOND_GAIN,
    SECOND_SHIFT,
    REDUCE_BIAS,
    FEED_SCALE,
) = range(10)


def vec(ref, idx):
    return ref[idx : idx + 1, :]


def half_mask(rows):
    return iota((rows, 128), 1) < 64


class Spot:
    def __init__(self, n):
        self.n, self.levels = n, n // 2
        self.rep, self.f = lax.axis_index("rep"), lax.axis_index("fsdp")
        self.half, self.core = self.rep // 2, self.rep % 2
        self.level, self.side = self.f // 2, self.f % 2

    def at(self, rep=None, f=None):
        return {"rep": self.rep if rep is None else rep, "fsdp": self.f if f is None else f}

    def sibling(self):
        return self.at(rep=2 * self.half + 1 - self.core)

    def across(self):
        return self.at(rep=2 * (1 - self.half) + self.core)

    def beside(self):
        return self.at(f=2 * self.level + 1 - self.side)

    def along(self, step):
        return self.at(f=2 * ((self.level + step) % self.levels) + self.side)

    def from_along(self, step, side=None):
        side = self.side if side is None else side
        return 2 * ((self.level + self.levels - step) % self.levels) + side


MESH = pl.DeviceIdType.MESH


def greet(devices):
    for device in devices:
        barrier = pltpu.get_barrier_semaphore()
        pl.semaphore_signal(barrier, inc=1, device_id=device, device_id_type=MESH)


def met(count):
    pl.semaphore_wait(pltpu.get_barrier_semaphore(), count)


def send(src, dst, send_sem, recv_sem, device):
    return pltpu.make_async_remote_copy(
        src_ref=src,
        dst_ref=dst,
        send_sem=send_sem,
        recv_sem=recv_sem,
        device_id=device,
        device_id_type=MESH,
    )


def fast_shape(reps, n, shard_rows):
    return reps == 4 and n == 8 and all(rows % 96 == 0 for rows in shard_rows)


def spread_block(refs, block_ref):
    *vectors, be_ref, table_ref = refs
    heads, share = table_ref.shape
    lanes = block_ref.shape[1]
    table = jnp.concatenate([table_ref[...].astype(f32), jnp.zeros((16 - heads, share), f32)], axis=0)
    width = vectors[0].shape[1]
    rows = [v[...].astype(f32) for v in vectors]
    rows.append(jnp.zeros((16 - len(rows), width), f32))
    block = jnp.concatenate(
        [table, jnp.zeros((16, lanes - share - width), f32), jnp.concatenate(rows, axis=0)], axis=1
    )
    wide = jnp.broadcast_to(be_ref[...].astype(f32), (16, lanes))
    block_ref[...] = jnp.where(iota((16, lanes), 0) == heads, wide, block).astype(bf16)


smem_spec = pl.BlockSpec(memory_space=pltpu.SMEM)
any_spec = pl.BlockSpec(memory_space=pl.ANY)
vmem_spec = pl.BlockSpec(memory_space=pltpu.VMEM)


def add16(left, right):
    return (left.astype(f32) + right.astype(f32)).astype(bf16)


def gather_plain(shorts, shards, n):
    gather = lambda value, axis: lax.all_gather(value, "fsdp", axis=axis, tiled=True)
    vecs = gather(jnp.concatenate(shorts[:10], axis=0), 1).astype(f32)
    vecs = jnp.pad(vecs, ((0, 6), (0, 0)))
    table = gather(shorts[11], 1)
    table = jnp.pad(table, ((0, 16 - table.shape[0]), (0, 0)))
    return [gather(w, 0) for w in shards], vecs, gather(shorts[10], 1).astype(f32), table


def reduce_plain(grads, vec_sums, be_sums, table_sums, n):
    def whole_sum(value):
        value = lax.psum_scatter(value, "fsdp", scatter_dimension=0, tiled=True)
        return lax.psum(value, "rep")

    sums = lax.psum((vec_sums, be_sums, table_sums), ("rep", "fsdp"))
    me = lax.axis_index("fsdp")
    cut = lambda v: lax.dynamic_slice_in_dim(v, me * (v.shape[1] // n), v.shape[1] // n, axis=1)
    vec_part, be_part, table_part = [cut(v) for v in sums]
    wide = be_part.shape[1]
    space = max(wide - vec_part.shape[1] - table_part.shape[1], 0)
    body = jnp.concatenate([table_part, jnp.zeros((16, space), f32), vec_part], axis=1)
    block = jnp.where(jnp.arange(16)[:, None] == 12, jnp.pad(be_part, ((0, 0), (0, body.shape[1] - wide))), body)
    return [whole_sum(g) for g in grads], block


class Piece:
    sems = 6

    def __init__(self, spot, shard, whole, row, col, cols, sent, rs, base):
        self.size = cols // 384
        levels = spot.levels
        part, q = 48, 16
        start = row + spot.core * part
        cut = slice(col, col + cols)
        rows = lambda first, size: pl.ds(pl.multiple_of(first, 16), size)
        plane = rows(start + spot.half * q, 2 * q)
        outer = rows(start + spot.half * 2 * q, q)
        core_rows = rows(start, part)
        side = spot.side

        def copy(idx, kind, src, dst, device):
            return send(src, dst, sent.at[kind], rs.at[base + idx], device)

        own = shard.at[plane, cut]
        here = whole.at[spot.level, side, plane, cut]
        self.local = pltpu.make_async_copy(own, here, rs.at[base + 5])
        self.z = [copy(0, 0, own, here, spot.along(step)) for step in range(1, levels)]
        three = whole.at[0 : levels - 1, 0, 0 : 2 * q, cut]
        self.z_all = pltpu.make_async_copy(three, three, rs.at[base])
        column = whole.at[:, side, plane, cut]
        self.y = copy(1, 1, column, column, spot.beside())
        near = whole.at[:, side, outer, cut]
        far = whole.at[:, 1 - side, outer, cut]
        self.x = [copy(2, 2, near, near, spot.across()), copy(3, 2, far, far, spot.across())]
        done = whole.at[:, :, core_rows, cut]
        self.c = copy(4, 3, done, done, spot.sibling())

    @staticmethod
    def sent_waits(levels, whole, sent):
        part = whole.shape[2] // 96
        views = [
            whole.at[0 : levels - 1, 0, 0 : 32 * part],
            whole.at[:, 0, 0 : 32 * part],
            whole.at[:, :, 0 : 16 * part],
            whole.at[:, :, 0 : 48 * part],
        ]
        return [pltpu.make_async_copy(v, v, sent.at[kind]) for kind, v in enumerate(views)]

    def start(self):
        self.local.start()
        for copy in self.z:
            copy.start()

    def after_z(self):
        self.local.wait()
        self.z_all.wait()
        self.y.start()
        self.x[0].start()

    def after_y(self):
        self.y.wait_recv()
        self.x[1].start()

    def after_x(self):
        self.x[0].wait_recv()
        self.x[1].wait_recv()
        self.c.start()

    def after_c(self):
        self.c.wait_recv()


def piece_cuts(shard_shapes):
    cuts = []
    for idx, (rows, cols) in enumerate(shard_shapes):
        for row in range(0, rows, 96):
            starts = list(range(0, cols, 384))
            if idx == 0:
                starts = starts[0::2] + starts[1::2]
            for col in starts:
                cuts.append((idx, row, col, 384))
    return cuts


def image_rows(plan):
    out = []
    for image in range(3):
        first, last = image * plan.small_len, (image + 1) * plan.small_len
        rows = (first // 16 * 16, round_up(last, 16))
        lanes = (first // 128 * 128, min(round_up(last, 128), plan.rows))
        out.append((rows, lanes))
    return out


def image_selectors(plan):
    rows, _ = plan.selector_arrays()
    out = []
    for image, ((low, high), _) in enumerate(image_rows(plan)):
        part = rows.copy()
        part[: image * plan.small_len] = 0
        part[(image + 1) * plan.small_len :] = 0
        out.append(np.pad(part[low:high].T, ((0, 0), (0, 256 - (high - low)))))
    return jnp.asarray(np.concatenate(out, axis=1), bf16)


def fold_head(plan, ds_ref, pick, colsel, large_ref, small_ref, tail_ref, h, is_large):
    gl, gs, rows = plan.gl, plan.gs, plan.rows
    wide = round_up(rows, 128)
    width = plan.strip_l + 128
    bands = -(-rows // gl)
    total = jnp.zeros((gl, width), f32)
    side = jnp.zeros((2 * gl, 128), f32)
    for pair in range(-(-bands // 2)):
        first = 2 * gl * pair
        count = min(2 * gl, rows - first)
        block = ds_ref[first : first + count, :].astype(f32)
        block = jnp.concatenate([block, jnp.zeros((count, wide - rows), f32)], axis=1)
        if count < 2 * gl:
            block = jnp.concatenate([block, jnp.zeros((2 * gl - count, wide), f32)], axis=0)
        if pair == 0:
            row = iota((2 * gl, 1), 0)
            top_row = jnp.where(row == 0, block, 0.0)
            block = jnp.where(row == 0, 0.0, block)
        side = side + block[:, :128]
        block = jnp.concatenate(
            [jnp.where(iota((1, 128), 1) == 0, 0.0, block[:, :128]), block[:, 128:]], axis=1
        )
        for half in range(2):
            a = 2 * pair + half
            if a >= bands:
                continue
            move = band_move(plan, a)
            low = move // 128 * 128
            piece = block[half * gl : (half + 1) * gl]
            if move > low:
                piece = jnp.concatenate([piece, jnp.zeros((gl, 128), f32)], axis=1)
                piece = pltpu.roll(piece, move - low, axis=1)
            piece = piece[:, : width - low]
            high = low + piece.shape[1]
            parts = [total[:, low:high] + piece]
            if low:
                parts.insert(0, total[:, :low])
            if high < width:
                parts.append(total[:, high:])
            total = jnp.concatenate(parts, axis=1) if len(parts) > 1 else parts[0]
    large_ref[h] = jnp.concatenate(
        [total[:, :128] + total[:, plan.strip_l :], total[:, 128 : plan.strip_l]], axis=1
    )
    lane = iota((1, wide), 1)
    full = lambda v: jnp.sum(jnp.sum(v, axis=0, keepdims=True), axis=1, keepdims=True)
    corner = full(jnp.where(lane == 0, top_row, 0.0))
    top = full(jnp.where(lane == 0, 0.0, top_row))
    side = full(jnp.where(iota((1, 128), 1) == 0, side, 0.0))

    gathered = jnp.zeros((plan.pad_rows, 256), f32)
    for image, ((r0, r1), (l0, l1)) in enumerate(image_rows(plan)):
        block = ds_ref[r0:r1, l0:l1]
        shift = image * plan.small_len - l0
        if shift:
            pad = round_up(l1 - l0, 128) - (l1 - l0)
            block = block.astype(f32)
            if pad:
                block = jnp.concatenate([block, jnp.zeros((r1 - r0, pad), f32)], axis=1)
            block = pltpu.roll(block, block.shape[1] - shift, axis=1)[:, :256].astype(bf16)
        start = 256 * image
        gathered = gathered + mm(pick[:, start : start + r1 - r0], block)
    high = gathered.astype(bf16)
    low = (gathered - high.astype(f32)).astype(bf16)
    select = colsel[:, 0:256]
    padded = mm(high, select, NT) + mm(low, select, NT)
    span = plan.strip_s
    col = iota((1, plan.pad_cols), 1)
    row = iota((16, 1), 0)
    acc = jnp.zeros((16, span), f32)
    edge = jnp.zeros((16, plan.pad_cols), f32)
    for i in range(gs):
        band = padded[16 * i : 16 * (i + 1)]
        if i == 0:
            top_s = jnp.where(row == plan.cls_row, band, 0.0)
            band = jnp.where(row == plan.cls_row, 0.0, band)
        edge = edge + band
        band = jnp.where(col < plan.cls_col, band, 0.0)
        band = jnp.concatenate([band, jnp.zeros((16, span - plan.pad_cols), f32)], axis=1)
        acc = acc + pltpu.roll(band, 2 * gs * (gs - 1 - i) + gs, axis=1)
    small_ref[h] = acc
    corner_s = full(jnp.where(col == plan.cls_col, top_s, 0.0))
    top_s = full(jnp.where(col < plan.cls_col, top_s, 0.0))
    side_s = full(jnp.where(col == plan.cls_col, edge, 0.0))
    lane = iota((1, 128), 1)
    picks = [(top, top_s), (side, side_s), (corner, corner_s)]
    tail = jnp.zeros((1, 128), f32)
    for i, (a, b) in enumerate(picks):
        tail = jnp.where(lane == i, jnp.where(is_large, a, b), tail)
    tail_ref[h] = tail


def fold_lines(plan, large_ref, small_ref, tail_ref, is_large):
    gl, heads, span = plan.gl, plan.heads, plan.strip_l
    odd = (iota((1, span), 1) + span - 1) % span // gl % 2
    lines = [None, None]
    for i in reversed(range(gl)):
        row = large_ref[:, i, :]
        for parity in range(2):
            want = parity if i else 1 - parity
            part = jnp.where(odd == want, row, 0.0)
            if lines[parity] is not None:
                part = part + pltpu.roll(lines[parity], span - 1, axis=1)
            lines[parity] = part
    small = None
    for i in reversed(range(16)):
        part = small_ref[:, i, :]
        small = part if small is None else part + pltpu.roll(small, plan.strip_s - 1, axis=1)
    small = jnp.concatenate([small, jnp.zeros((heads, plan.line - plan.strip_s), f32)], axis=1)
    line = jnp.where(is_large, jnp.concatenate(lines, axis=1), small)
    tail = tail_ref[:, 0, :]
    line = jnp.concatenate([line, tail], axis=1)
    return jnp.concatenate([line, jnp.zeros((16 - heads, plan.lanes), f32)], axis=0)


class Sum:
    sems = 6
    outer = 16

    def __init__(self, spot, grad, out, row, cut, bufs, sent, c_sem, rs, base):
        self.spot, self.grad, self.out = spot, grad, out
        self.row, self.cut = row, cut
        self.acc, self.got_x, self.got_y, self.got_z, self.total, self.got_f = bufs
        half, core, side, level, levels = spot.half, spot.core, spot.side, spot.level, spot.levels
        q, part = self.outer, self.acc.shape[2]
        self.middle = m = part - 2 * q
        rows = lambda first, size: pl.ds(pl.multiple_of(first, 16), size)
        self.rows = rows
        self.plane = rows(half * q, q + m)
        self.mine = rows(half * (q + m), q)
        self.own = rows(core * part, part)
        self.sent = self.joined = False
        unit = 4 * self.acc.shape[3] / LINK_BYTES_PER_US
        self.link_us = (2 * levels * q * unit, levels * (q + m) * unit, (q + m) * unit)

        def copy(idx, src, dst, device):
            out_sem = sent.at[idx] if idx else c_sem
            return send(src, dst, out_sem, rs.at[base + idx], device)

        acc = self.acc
        other = rows((1 - core) * part, part)
        self.c = copy(0, grad.at[:, :, other, cut[0]], acc, spot.sibling())
        self.x = copy(1, acc.at[:, :, rows((1 - half) * (q + m), q)], self.got_x, spot.across())
        self.y = copy(2, acc.at[:, 1 - side, self.plane], self.got_y, spot.beside())
        self.z = []
        for step in range(1, levels):
            src = acc.at[(level + step) % levels, side, self.plane]
            self.z.append(copy(5, src, self.got_z.at[step - 1], spot.along(step)))
        self.z_all = pltpu.make_async_copy(self.got_z, self.got_z, rs.at[base + 5])
        self.f = copy(3, self.total, self.got_f, spot.across())
        mine = out.at[rows(row + core * part, part), cut[1]]
        self.last = copy(4, mine, mine, spot.sibling())

    @classmethod
    def buffers(cls, levels, shard_rows, cols):
        part = shard_rows // 2
        kept = part - cls.outer
        shapes = [
            (levels, 2, part, cols),
            (levels, 2, cls.outer, cols),
            (levels, kept, cols),
            (levels - 1, kept, cols),
            (kept, cols),
            (kept, cols),
        ]
        return [pltpu.VMEM(shape, bf16) for shape in shapes]

    def start(self):
        self.c.start()

    def free(self):
        self.join()
        if not self.sent:
            self.c.wait_send()
            self.sent = True

    def stage(self, k):
        getattr(self, ("go", "after_x", "after_y", "after_z", "after_f", "after_last")[k])()

    def join(self):
        if self.joined:
            return
        self.joined = True
        self.c.wait_recv()

        @pl.loop(0, self.acc.shape[0])
        def _(level):
            for side in range(2):
                own = self.grad[level, side, self.own, self.cut[0]]
                self.acc[level, side] = add16(self.acc[level, side], own)

    def go(self):
        self.join()
        self.x.start()

    def after_x(self):
        self.x.wait_recv()

        @pl.loop(0, self.acc.shape[0])
        def _(level):
            for side in range(2):
                mine = self.acc[level, side, self.mine]
                self.acc[level, side, self.mine] = add16(mine, self.got_x[level, side])

        self.y.start()

    def after_y(self):
        side = self.spot.side
        self.y.wait_recv()

        @pl.loop(0, self.acc.shape[0])
        def _(level):
            mine = self.acc[level, side, self.plane]
            self.acc[level, side, self.plane] = add16(mine, self.got_y[level])

        for copy in self.z:
            copy.start()

    def after_z(self):
        self.z_all.wait()
        value = self.acc[self.spot.level, self.spot.side, self.plane].astype(f32)
        for k in range(len(self.z)):
            value = value + self.got_z[k].astype(f32)
        self.total[...] = value.astype(bf16)
        self.f.start()

    def after_f(self):
        q, m, half = self.outer, self.middle, self.spot.half
        base = self.row + self.spot.core * self.acc.shape[2]
        rows = self.rows
        total, got, out, cut = self.total, self.got_f, self.out, self.cut[1]
        self.f.wait_recv()
        out[rows(base + half * (q + m), q), cut] = total[rows(half * m, q)]
        both = add16(total[rows((1 - half) * q, m)], got[rows(half * q, m)])
        out[rows(base + q, m), cut] = both
        out[rows(base + (1 - half) * (q + m), q), cut] = got[rows((1 - half) * m, q)]
        self.last.start()

    def after_last(self):
        self.last.wait_recv()

    @classmethod
    def sent_rows(cls, levels, shard_rows):
        part = shard_rows // 2
        kept = part - cls.outer
        return [2 * levels * cls.outer, levels * kept, kept, part, (levels - 1) * kept]


LATENCY_US, LINK_BYTES_PER_US = 2.2, 82e3
HIDDEN_BLOCKS = 3
BLOCK_ORDER = [("rows", 0), ("rows", 1), ("cols", 0), ("rows", 2), ("cols", 1), ("cols", 2)]


class Queue:
    def __init__(self):
        self.clock, self.entries = 0.0, []
        self.free = {"x": 0.0, "y": 0.0, "z": 0.0, "core": 0.0}

    def book(self, link, us):
        begin = max(self.clock, self.free[link])
        self.free[link] = begin + us
        return begin + us + LATENCY_US

    def add(self, job):
        job.start()
        self.entries.append([self.book("core", 1.0), 0, job])

    def take(self, entry):
        _, stage, job = entry
        if stage == 0:
            job.join()
        else:
            job.stage(stage)
        x, y, f = job.link_us
        if stage == 0:
            job.stage(0)
            entry[0] = self.book("x", x)
        elif stage == 1:
            entry[0] = self.book("y", y)
        elif stage == 2:
            entry[0] = self.book("z", y)
        elif stage == 3:
            entry[0] = self.book("x", f)
        elif stage == 4:
            entry[0] = self.book("core", 0.3)
        entry[1] += 1
        if stage == 5:
            self.entries.remove(entry)

    def beat(self, us):
        self.clock += us
        while self.entries:
            entry = min(self.entries, key=lambda item: item[0])
            if entry[0] > self.clock:
                break
            self.take(entry)

    def drain(self):
        while self.entries:
            entry = min(self.entries, key=lambda item: item[0])
            self.clock = max(self.clock, entry[0])
            self.take(entry)


def layer_kernel(plan, n, fast, cuts, sum_shapes, *refs):
    refs = list(refs)
    take = lambda count: [refs.pop(0) for _ in range(count)]
    kind_ref, tok_in, cot_in, idx_in, pick_ref, colsel_ref, image_ref = take(7)
    if fast:
        shorts, shards = take(12), take(4)
    else:
        vec_in, be_in, tab_in = take(3)
        wholes = take(4)
    out_ref, tok_out = take(2)
    sum_wt, sum_wo, sum_we, sum_wr = take(4)
    if fast:
        (small_out,) = take(1)
        wholes = take(4)
    else:
        vec_out, be_out, tab_out = take(3)
    normed_out, branch_out, qkv_out, probs_out, ds_out = take(5)
    vec_ref, be_ref, lab_ref, middle_ref, pair_ref, mixed_ref, small_ref, dbe_ref = take(8)
    rows_ref, cols_ref = take(2)
    load_sems, save_sems, tile_sems, late_sems, pair_sems, ds_sems, stage_sems = take(7)
    wt_in, wo_in, we_in, wr_in = wholes
    is_large = kind_ref[0] == 1
    heads, rows = plan.heads, plan.rows
    pairs = heads // 2
    width = tok_in.shape[1]
    eighth = width // 8
    hidden = wr_in.shape[2] * 8
    unit = hidden // 8 // HIDDEN_BLOCKS
    tile_cols = 8 * unit
    matrix = lambda ref: ref[...].reshape(width, width)
    half_ref, dfeed_ref = pair_ref.at[0], pair_ref.at[1]

    def fetch(src, dst, sem):
        copy = pltpu.make_async_copy(src, dst, sem)
        copy.start()
        return copy

    saves = []

    def save(src, dst):
        copy = fetch(src, dst, save_sems.at[len(saves)])
        saves.append(copy)
        return copy

    queue = Queue()
    jobs, pieces = [], []
    if fast:
        bufs = take(6 * len(sum_shapes))
        sum_kinds = sorted(set(sum_shapes))
        short, shorts_got, block, got, reps = take(5)
        gss, grs, ass, ars, rss, css, rrs, bss, brs = take(9)
        spot = Spot(n)
        peers = [spot.at(f=(spot.f + k) % n) for k in range(1, n)]
        others = [spot.at(rep=(spot.rep + k) % 4) for k in range(1, 4)]
        greet(peers + others)
        for idx, row, col, cols in cuts:
            base = len(pieces) * Piece.sems
            at = GATHER_ORDER[idx]
            args = (row, col, cols, gss.at[at], grs, base)
            pieces.append(Piece(spot, shards[at], wholes[at], *args))
        formed = []
        for ring, j in BLOCK_ORDER:
            if ring == "rows":
                formed.append((rows_ref, sum_wr, j * unit, 0))
            else:
                formed.append((cols_ref, sum_we, 0, j * tile_cols))
        formed.append((rows_ref, sum_wo, 0, 0))
        for j in range(3):
            formed.append((rows_ref, sum_wt, 0, j * width))
        counts = {}
        for ring, out, row, col in formed:
            k = counts[id(ring)] = counts.get(id(ring), -1) + 1
            cols = ring.shape[4] // 2
            for first in (0, cols):
                i = len(jobs)
                cut = (slice(first, first + cols), slice(col + first, col + first + cols))
                kind = sum_kinds.index(sum_shapes[i])
                args = (bufs[6 * i : 6 * i + 6], rss.at[kind], css.at[i], rrs, i * Sum.sems)
                jobs.append(Sum(spot, ring.at[k % 2], out, row, cut, *args))
        spread_block(shorts, short)
        small = []
        for k, peer in enumerate(peers):
            small.append(send(short, shorts_got.at[spot.f], ass.at[k], ars.at[k], peer))

    def set_out():
        met(n + 2)
        for copy in small:
            copy.start()
        pieces[0].start()
        shorts_got[spot.f] = short[...]

    events = []
    for i in range(len(pieces)):
        for kind, lag in enumerate((0,) + LAGS):
            events.append((i + lag, kind, i))
    events.sort()
    gone = [0]
    whole_at = {i: pos for pos, (_, kind, i) in enumerate(events) if kind == 3}
    on_whole = []

    def run_event():
        _, kind, i = events[gone[0]]
        gone[0] += 1
        getattr(pieces[i], ("after_z", "after_y", "after_x", "after_c")[kind])()
        if kind == 0:
            for ahead in (range(2, AHEAD + 1) if i == 0 else (i + AHEAD,)):
                if ahead < len(pieces):
                    pieces[ahead].start()
        if kind == 3:
            for call in on_whole:
                call(i)

    now = [-1]

    def step(count=1):
        now[0] += count
        while gone[0] < len(events) and events[gone[0]][0] <= now[0]:
            run_event()

    def gather_until(piece):
        while events and gone[0] <= whole_at[min(piece, len(pieces) - 1)]:
            step()


    def forward(line_ref, heads_ref, qkv_ref, wt_ref, wo_ref, idx_ref, tok, normed_ref):
        idx_copy = fetch(idx_in, idx_ref, late_sems.at[0])
        tok_copy = fetch(tok_in, tok, late_sems.at[1])
        loads = []
        for src, ref in ((wt_in, wt_ref), (wo_in, wo_ref)):
            starts = range(0, src.shape[3], width // 2)
            for col in list(starts[0::2]) + list(starts[1::2]):
                first = col % width
                dst = ref.at[col // width, :, :, :, first : first + width // 2]
                view = src.at[:, :, :, col : col + width // 2]
                loads.append(pltpu.make_async_copy(view, dst, load_sems.at[len(loads)]))
        if not fast:
            for load in loads:
                load.start()

        def begin(i):
            if i < len(loads):
                loads[i].start()

        on_whole.append(begin)
        idx_copy.wait()
        read_labels(plan, is_large, idx_ref, pick_ref, lab_ref)
        if fast:
            set_out()
        tok_copy.wait()
        normal, _ = norm_stats(tok[...].astype(f32))
        if fast:
            pieces[1].start()
            for copy in small:
                copy.wait()
            step()
            share, bshare = shorts[0].shape[1], shorts[11].shape[1]
            tab = []
            for f in range(n):
                part = shorts_got[f].astype(f32)
                wide = part.shape[1]
                vec_ref[:, f * share : (f + 1) * share] = part[:, wide - share :]
                tab.append(part[:, :bshare])
                be_ref[:, f * wide : (f + 1) * wide] = part[heads : heads + 1, :]
            tab = jnp.concatenate(tab, axis=1)
        else:
            vec_ref[...] = vec_in[...]
            be_ref[...] = be_in[...]
            tab = tab_in[...]
        table_lines(plan, tab, lab_ref, line_ref)
        step()
        normed = normal * vec(vec_ref, FIRST_GAIN) + vec(vec_ref, FIRST_SHIFT)
        normed_ref[...] = normed.astype(bf16)
        save(normed_ref, normed_out)
        for group in range(heads // 2):

            @pl.loop(2 * group, 2 * group + 2)
            def _(h):
                bias_head(plan, is_large, line_ref, image_ref, colsel_ref, h, heads_ref)

            step()
        def project(group):
            low, high = group * width // 2, (group + 1) * width // 2
            normed = normed_ref[...]
            gather_until(3 * group + 2)
            for j in range(3):
                loads[3 * group + j].wait()
                triple = mm(normed, wt_ref[j, :, :, :, low:high].reshape(width, width // 2))
                if j == 0:
                    triple = triple + vec_ref[QUERY_BIAS : QUERY_BIAS + 1, low:high]
                if j == 2:
                    triple = triple + vec_ref[VALUE_BIAS : VALUE_BIAS + 1, low:high]
                triple = triple.astype(bf16)
                if j == 0:
                    triple = triple * jnp.array(0.125, bf16)
                for p in range(pairs // 2):
                    where = j * pairs + group * (pairs // 2) + p
                    qkv_ref[where] = triple[:, 128 * p : 128 * (p + 1)]

        def attend_pair(p):
            q, k, v = qkv_ref[p], qkv_ref[pairs + p], qkv_ref[2 * pairs + p]
            lower = half_mask(rows)
            mixed = []
            for t in range(2):
                keep = lower if t == 0 else ~lower
                scores = mm(jnp.where(keep, q, jnp.zeros_like(q)), k, NT)
                scores = scores + heads_ref[2 * p + t].astype(f32)
                top = jnp.max(scores, axis=1, keepdims=True)
                exps = jnp.exp(scores - top)
                total = jnp.sum(exps, axis=1, keepdims=True)
                probs = (exps * (1.0 / total)).astype(bf16)
                heads_ref[2 * p + t] = probs
                mixed.append(mm(probs, v))
            mixed_ref[p] = jnp.where(lower, mixed[0], mixed[1]).astype(bf16)

        for group in range(2):
            project(group)
            step()

            @pl.loop(group * pairs // 2, (group + 1) * pairs // 2)
            def _(p):
                attend_pair(p)
                for i in range(group * pairs // 2, (group + 1) * pairs // 2):

                    @pl.when(p == i)
                    def _():
                        step()

                cut = pl.ds(2 * p, 2)
                dst = probs_out.at[cut]
                pltpu.make_async_copy(heads_ref.at[cut], dst, pair_sems.at[0, 3]).start()

        save(qkv_ref, qkv_out)

        gather_until(7)
        loads[6].wait()
        loads[7].wait()
        mixed = jnp.concatenate([mixed_ref[p] for p in range(pairs)], axis=1)
        branch = mm(mixed, matrix(wo_ref.at[0])) + vec(vec_ref, OUTPUT_BIAS)
        saves[0].wait()
        normed_ref[...] = branch.astype(bf16)
        save(normed_ref, branch_out)
        middle = tok[...].astype(f32) + vec(vec_ref, ATTEND_SCALE) * branch
        middle_ref[...] = middle
        normal, _ = norm_stats(middle)
        second = normal * vec(vec_ref, SECOND_GAIN) + vec(vec_ref, SECOND_SHIFT)
        half_ref[...] = second.astype(bf16)
        gather_until(7)
        on_whole.pop()
        step()
        pltpu.make_async_copy(heads_ref, probs_out, pair_sems.at[0, 3]).wait()
        for copy in saves[1:]:
            copy.wait()

    pl.run_scoped(
        forward,
        pltpu.VMEM((16, plan.lanes), f32),
        pltpu.VMEM((heads, rows, rows), bf16),
        pltpu.VMEM((3 * pairs, rows, 128), bf16),
        pltpu.VMEM((3, 4, 2, eighth, width), bf16),
        pltpu.VMEM((1, 4, 2, eighth, width), bf16),
        pltpu.VMEM(idx_in.shape, jnp.int32),
        pltpu.VMEM((rows, width), bf16),
        pltpu.VMEM((rows, width), bf16),
    )


    def note(idx, value):
        small_ref[idx : idx + 1, 0:width] = value

    limit = jnp.where(is_large, plan.large_len, 3 * plan.small_len)
    live = iota((rows, 1), 0) < limit

    def backward(feed_ref, dsec_ref, dtri_ref, lines_ref):
        used = {"rows": [], "cols": [], "all": 0}

        def push(kind, value, out, row, col):
            k = used[kind]
            if fast and len(k) >= 2:
                for job in k[-2]:
                    job.free()
            slot = (rows_ref if kind == "rows" else cols_ref).at[len(k) % 2]
            shard, cols = value.shape[0] // 8, value.shape[1]
            slot[:, :, 0:shard, :] = value.astype(bf16).reshape(4, 2, shard, cols)
            added = []
            if fast:
                added = jobs[used["all"] : used["all"] + 2]
                used["all"] += 2
                for job in added:
                    queue.add(job)
            else:
                view = out.at[:, :, pl.ds(row, shard), pl.ds(col, cols)]
                fetch(slot.at[:, :, pl.ds(0, shard)], view, stage_sems.at[0]).wait()
            k.append(added)

        branch_ref, cot_ref = dtri_ref.at[0], dtri_ref.at[1]
        cot_copy = fetch(cot_in, cot_ref, late_sems.at[0])
        branch_copy = fetch(branch_out, branch_ref, late_sems.at[1])

        def feed_forward(we_ref, wr_ref, pre_ref, act_ref, slope_ref):

            def we_loads(j):
                copies = []
                for f in range(8):
                    src = we_in.at[:, :, :, pl.ds((f * HIDDEN_BLOCKS + j) * unit, unit)]
                    dst = we_ref.at[j % 2, :, :, :, pl.ds(f * unit, unit)]
                    copies.append(pltpu.make_async_copy(src, dst, tile_sems.at[j % 2, f]))
                return copies

            def wr_load(j):
                src = wr_in.at[:, :, pl.ds(j * unit, unit)]
                return pltpu.make_async_copy(src, wr_ref.at[j % 2], tile_sems.at[j % 2, 8])

            gather_until(15)
            for j in range(2):
                for copy in we_loads(j):
                    copy.start()
            cot_copy.wait()
            grad = jnp.where(live, cot_ref[...].astype(f32), 0.0)
            dfeed_ref[...] = (vec(vec_ref, FEED_SCALE) * grad).astype(bf16)
            small_ref[...] = jnp.zeros_like(small_ref)
            note(REDUCE_BIAS, rows_sum(dfeed_ref[...].astype(f32)))

            def we_tile(j):
                return we_ref[j % 2].reshape(width, tile_cols)

            def before(j):
                for copy in we_loads(j):
                    copy.wait()
                bias = []
                for f in range(8):
                    first = (f * HIDDEN_BLOCKS + j) * unit
                    bias.append(be_ref[:, first : first + unit])
                pre_ref[...] = mm(half_ref[...], we_tile(j)) + jnp.concatenate(bias, axis=1)

            part = 16 * (-(-rows // 64))
            spans = [(low, min(low + part, rows)) for low in range(0, rows, part)]

            def activate(j, which):
                low, high = spans[which]
                value, slope = gelu_parts(pre_ref[low:high, :])
                act_ref[j % 2, low:high, :] = value.astype(bf16)
                slope_ref[j % 2, low:high, :] = slope.astype(bf16)

            def first_part(j):
                before(j)
                for i in range(len(spans)):
                    activate(j, i)
                    step()
                queue.beat(4.0)
                push("rows", mm(act_ref[j % 2], dfeed_ref[...], TN), sum_wr, j * unit, 0)

            def second_part(j):
                gather_until(16 + 2 * (((j + 1) * unit - 1) // 96) + 1)
                wr_load(j).start()
                queue.beat(1.5)
                wr_load(j).wait()
                d_feed, act = dfeed_ref[...], act_ref[j % 2]
                wr = wr_ref[j % 2].reshape(tile_cols, width)
                d_act = mm(d_feed, wr, NT)
                d_pre = (d_act * slope_ref[j % 2].astype(f32)).astype(bf16)
                dbe_ref[j : j + 1, :] = rows_sum(d_pre.astype(f32))
                step()
                queue.beat(1.5)
                push("cols", mm(half_ref[...], d_pre, TN), sum_we, 0, j * tile_cols)
                step()
                queue.beat(1.5)
                feed = mm(act, wr)
                feed_ref[...] = feed if j == 0 else feed_ref[...] + feed
                step()
                queue.beat(1.5)
                d_second = mm(d_pre, we_tile(j), NT)
                dsec_ref[...] = d_second if j == 0 else dsec_ref[...] + d_second
                if j + 2 < HIDDEN_BLOCKS:
                    for copy in we_loads(j + 2):
                        copy.start()
                step()
                queue.beat(1.5)

            first_part(0)
            for j in range(HIDDEN_BLOCKS):
                if j + 1 < HIDDEN_BLOCKS:
                    first_part(j + 1)
                second_part(j)

        pl.run_scoped(
            feed_forward,
            pltpu.VMEM((2, 4, 2, eighth, tile_cols), bf16),
            pltpu.VMEM((2, 4, 2, unit, width), bf16),
            pltpu.VMEM((rows, tile_cols), f32),
            pltpu.VMEM((2, rows, tile_cols), bf16),
            pltpu.VMEM((2, rows, tile_cols), bf16),
        )

        def attention(
            tile_ref, qkv_ref, probs_ref, dmix_ref, large_ref, strip_ref, tail_ref
        ):
            def pair_loads(p):
                slot = p % 3
                probs = probs_out.at[pl.ds(2 * p, 2)]
                copies = [pltpu.make_async_copy(probs, probs_ref.at[slot], pair_sems.at[slot, 3])]
                for part in range(3):
                    src, dst = qkv_out.at[part * pairs + p], qkv_ref.at[p % 2, part]
                    copies.append(pltpu.make_async_copy(src, dst, pair_sems.at[slot, part]))
                return copies

            tiles = [pltpu.make_async_copy(wo_in, tile_ref.at[0], tile_sems.at[0, 0])]
            for j in range(3):
                src = wt_in.at[:, :, :, pl.ds(j * width, width)]
                slot = (1 + j) % 2
                tiles.append(pltpu.make_async_copy(src, tile_ref.at[slot], tile_sems.at[slot, 0]))

            def tile(i):
                tiles[i].wait()
                return matrix(tile_ref.at[i % 2])

            tiles[0].start()
            tiles[1].start()
            for copy in pair_loads(0):
                copy.start()
            branch_copy.wait()
            feed_out = feed_ref[...] + vec(vec_ref, REDUCE_BIAS)
            middle = middle_ref[...]
            half_ref[...] = (middle + vec(vec_ref, FEED_SCALE) * feed_out).astype(bf16)
            out_copy = fetch(half_ref, out_ref, save_sems.at[0])
            grad = jnp.where(live, cot_ref[...].astype(f32), 0.0)
            d_second = dsec_ref[...]
            normal, inv = norm_stats(middle)
            d_middle = grad + norm_back(d_second, vec(vec_ref, SECOND_GAIN), normal, inv)
            d_branch = (vec(vec_ref, ATTEND_SCALE) * d_middle).astype(bf16)
            queue.beat(3.5)
            note(FEED_SCALE, rows_sum(grad * feed_out))
            note(SECOND_GAIN, rows_sum(d_second * normal))
            note(SECOND_SHIFT, rows_sum(d_second))
            note(ATTEND_SCALE, rows_sum(d_middle * branch_ref[...].astype(f32)))
            note(OUTPUT_BIAS, rows_sum(d_branch.astype(f32)))
            dsec_ref[...] = d_middle
            dmix_ref[...] = mm(d_branch, tile(0), NT).astype(bf16)
            tiles[2].start()
            mixed = jnp.concatenate([mixed_ref[p] for p in range(pairs)], axis=1)
            push("rows", mm(mixed, d_branch, TN), sum_wo, 0, 0)
            normed_ref = dfeed_ref
            normed_copy = fetch(normed_out, normed_ref, late_sems.at[0])
            queue.beat(4.0)

            def ds_copy(p):
                slot = p % 3
                dst = ds_out.at[pl.ds(2 * p, 2)]
                return pltpu.make_async_copy(probs_ref.at[slot], dst, ds_sems.at[slot])

            def pair_back(p):
                slot = p % 3
                for copy in pair_loads(p):
                    copy.wait()

                @pl.when(p >= 2)
                def _():
                    ds_copy(p - 2).wait()

                @pl.when(p + 1 < pairs)
                def _():
                    for copy in pair_loads(p + 1):
                        copy.start()

                lanes = pl.ds(pl.multiple_of(128 * p, 128), 128)
                q, k, v = [qkv_ref[p % 2, part] for part in range(3)]
                do = dmix_ref[:, lanes]
                lower = half_mask(rows)
                prod = do.astype(f32) * mixed_ref[p].astype(f32)
                dq, dk, dv = [], [], []
                for t in range(2):
                    keep = lower if t == 0 else ~lower
                    d_out = jnp.where(keep, do, jnp.zeros_like(do))
                    delta = jnp.sum(jnp.where(keep, prod, 0.0), axis=1, keepdims=True)
                    d_probs = mm(d_out, v, NT)
                    probs = probs_ref[slot, t]
                    dv.append(mm(probs, do, TN))
                    d_scores = (probs.astype(f32) * (d_probs - delta)).astype(bf16)
                    probs_ref[slot, t] = d_scores
                    dq.append(mm(d_scores, k))
                    dk.append(mm(d_scores, q, TN))
                dtri_ref[0, :, lanes] = (jnp.where(lower, dq[0], dq[1]) * 0.125).astype(bf16)
                dtri_ref[1, :, lanes] = jnp.where(lower, dk[0], dk[1]).astype(bf16)
                dtri_ref[2, :, lanes] = jnp.where(lower, dv[0], dv[1]).astype(bf16)
                ds_copy(p).start()

            span = width // 3
            for group in range(3):

                @pl.loop(2 * group, 2 * group + 2)
                def _(p):
                    pair_back(p)

                    @pl.when(p == 2 * group)
                    def _():
                        queue.beat(2.3)

                queue.beat(2.3)
                if group == 0:
                    normed_copy.wait()
                d_part = [dtri_ref[j, :, group * span : (group + 1) * span] for j in range(3)]
                d_part = jnp.concatenate(d_part, axis=1)
                push("rows", mm(normed_ref[...], d_part, TN), sum_wt, 0, group * width)
                queue.beat(1.6)

            out_copy.wait()
            tok_ref = half_ref
            tok_copy = fetch(tok_in, tok_ref, late_sems.at[1])
            for j in range(3):
                d_part = dtri_ref[j]
                part = mm(d_part, tile(1 + j), NT)
                feed_ref[...] = part if j == 0 else feed_ref[...] + part
                if j == 0:
                    tiles[3].start()
                if j != 1:
                    note(QUERY_BIAS if j == 0 else VALUE_BIAS, rows_sum(d_part.astype(f32)))
                queue.beat(1.3)
            tok_copy.wait()
            normal, inv = norm_stats(tok_ref[...].astype(f32))
            note(FIRST_GAIN, rows_sum(feed_ref[...] * normal))
            note(FIRST_SHIFT, rows_sum(feed_ref[...]))
            queue.beat(1.0)

            ds_copy(pairs - 2).wait()
            ds_copy(pairs - 1).wait()

            def ds_load(p):
                src, slot = ds_out.at[pl.ds(2 * p, 2)], p % 3
                return pltpu.make_async_copy(src, probs_ref.at[slot], pair_sems.at[slot, 3])

            ds_load(0).start()

            @pl.loop(0, pairs)
            def _(p):
                ds_load(p).wait()

                @pl.when(p + 1 < pairs)
                def _():
                    ds_load(p + 1).start()

                for t in range(2):
                    ds = probs_ref.at[p % 3, t]
                    args = (image_ref, colsel_ref, large_ref, strip_ref, tail_ref, 2 * p + t, is_large)
                    fold_head(plan, ds, *args)
                for i in range(pairs):

                    @pl.when(p == i)
                    def _():
                        queue.beat(1.9)

            lines_ref[...] = fold_lines(plan, large_ref, strip_ref, tail_ref, is_large)

        def first_norm_back():
            tok_ref, normed_ref = half_ref, dfeed_ref
            normal, inv = norm_stats(tok_ref[...].astype(f32))
            back = norm_back(feed_ref[...], vec(vec_ref, FIRST_GAIN), normal, inv)
            normed_ref[...] = (dsec_ref[...] + back).astype(bf16)
            return fetch(normed_ref, tok_out, save_sems.at[1])

        pl.run_scoped(
            attention,
            pltpu.VMEM((2, 4, 2, eighth, width), bf16),
            pltpu.VMEM((2, 3, rows, 128), bf16),
            pltpu.VMEM((3, 2, rows, rows), bf16),
            pltpu.VMEM((rows, width), bf16),
            pltpu.VMEM((heads, plan.gl, plan.strip_l), f32),
            pltpu.VMEM((heads, 16, plan.strip_s), f32),
            pltpu.VMEM((heads, 1, 128), f32),
        )
        queue.beat(1.9)
        line_of = lambda chunk: lines_ref[:, 128 * chunk : 128 * (chunk + 1)]
        d_table = table_from_lines(plan, line_of, lab_ref, plan.buckets)
        wide = hidden // 8

        def bias_sum(f):
            parts = [dbe_ref[j : j + 1, f * unit : (f + 1) * unit] for j in range(HIDDEN_BLOCKS)]
            return jnp.concatenate(parts, axis=1)

        if not fast:
            vec_out[...] = small_ref[...]
            for f in range(8):
                be_out[:, f * wide : (f + 1) * wide] = bias_sum(f)
            tab_out[...] = d_table
            first_norm_back().wait()
            return

        share, bshare = width // n, plan.buckets // n
        for f in range(n):
            value = jnp.concatenate(
                [
                    d_table[:, f * bshare : (f + 1) * bshare],
                    jnp.zeros((16, wide - bshare - share), f32),
                    small_ref[:, f * share : (f + 1) * share],
                ],
                axis=1,
            )
            bias = jnp.broadcast_to(bias_sum(f), (16, wide))
            block[f] = jnp.where(iota((16, wide), 0) == heads, bias, value).astype(bf16)
        sums = []
        for k, peer in enumerate(peers):
            dst = (spot.f + k + 1) % n
            sums.append(send(block.at[dst], got.at[k], bss.at[k], brs.at[k], peer))
            sums[k].start()
        tok_copy = first_norm_back()
        queue.beat(4.0)
        value = block[spot.f].astype(f32)
        for k, copy in enumerate(sums):
            copy.wait_recv()
            value = value + got[k].astype(f32)
        reps[spot.rep] = value
        for k, other in enumerate(others):
            mine = reps.at[spot.rep]
            sums.append(send(mine, mine, bss.at[n - 1 + k], brs.at[n - 1 + k], other))
            sums[-1].start()
        queue.beat(3.0)
        for copy in sums[n - 1 :]:
            copy.wait_recv()
        small_out[...] = (reps[0] + reps[1]) + (reps[2] + reps[3])
        queue.drain()
        tok_copy.wait()
        for copy in sums:
            copy.wait_send()
        for job in jobs:
            job.free()
        flat = normed_out
        for kind, shape in enumerate(sum_kinds):
            count = sum_shapes.count(shape)
            for idx, out_rows in enumerate(Sum.sent_rows(n // 2, shape[0])):
                total = count * out_rows * shape[1] // width
                view = flat.at[pl.ds(0, total)]
                pltpu.make_async_copy(view, view, rss.at[kind, idx + 1]).wait()
        for at, whole in enumerate(wholes):
            for copy in Piece.sent_waits(n // 2, whole, gss.at[at]):
                copy.wait()

    pl.run_scoped(
        backward,
        pltpu.VMEM((rows, width), f32),
        pltpu.VMEM((rows, width), f32),
        pltpu.VMEM((3, rows, width), bf16),
        pltpu.VMEM((16, plan.lanes), f32),
    )


AHEAD, LAGS = 3, (2, 4, 5)
GATHER_ORDER = (0, 1, 2, 3)


def layer(plan, kind, tokens, cot, large_index, n, fast, shorts, shards):
    rows, width = tokens.shape
    heads = plan.heads
    pairs = heads // 2
    sds = jax.ShapeDtypeStruct
    hidden = shards[2].shape[1]
    unit = hidden // 8 // HIDDEN_BLOCKS
    eighth = width // 8
    cuts = piece_cuts([w.shape for w in shards]) if fast else []
    sum_shapes = []
    for ring, _ in BLOCK_ORDER:
        sum_shapes += [(unit, width // 2) if ring == "rows" else (eighth, 4 * unit)] * 2
    sum_shapes += [(eighth, width // 2)] * 8
    colsel = jnp.asarray(plan.selector_arrays()[1], bf16)
    inputs = [kind, tokens, cot, large_index, pick_plan(plan), colsel, image_selectors(plan)]
    in_specs = [smem_spec] + [any_spec] * 3 + [vmem_spec] * 3
    outs, out_specs = [sds((rows, width), bf16)] * 2, [any_spec] * 2
    if fast:
        wide = hidden // n
        inputs += shorts + shards
        in_specs += [vmem_spec] * 12 + [any_spec] * 4
        outs += [sds(w.shape, bf16) for w in shards]
        outs += [sds((16, wide), f32)]
        out_specs += [vmem_spec] * 5
        outs += [sds((4, 2) + w.shape, bf16) for w in shards]
        out_specs += [any_spec] * 4
    else:
        wholes, vecs, be, table = gather_plain(shorts, shards, n)
        wholes = [w.reshape(4, 2, w.shape[0] // 8, w.shape[1]) for w in wholes]
        inputs += [vecs, be, table.astype(f32)] + wholes
        in_specs += [vmem_spec] * 3 + [any_spec] * 4
        outs += [sds(w.shape, bf16) for w in wholes]
        outs += [sds((16, width), f32), sds((1, hidden), f32), sds((16, plan.buckets), f32)]
        out_specs += [any_spec] * 4 + [vmem_spec] * 3
    kept = len(outs)
    square = sds((heads, rows, rows), bf16)
    flat = sds((rows, width), bf16)
    outs += [flat, flat, sds((3 * pairs, rows, 128), bf16), square, square]
    out_specs += [any_spec] * 5
    dma = pltpu.SemaphoreType.DMA
    scratch = [
        pltpu.VMEM((16, width), f32),
        pltpu.VMEM((1, hidden), f32),
        pltpu.VMEM((2, plan.lanes), jnp.int32),
        pltpu.VMEM((rows, width), f32),
        pltpu.VMEM((2, rows, width), bf16),
        pltpu.VMEM((pairs, rows, 128), bf16),
        pltpu.VMEM((16, width), f32),
        pltpu.VMEM((8, 8 * unit), f32),
        pltpu.VMEM((2, 4, 2, unit, width), bf16),
        pltpu.VMEM((2, 4, 2, eighth, 8 * unit), bf16),
        dma((8,)),
        dma((4,)),
        dma((2, 9)),
        dma((2,)),
        dma((3, 4)),
        dma((3,)),
        dma((1,)),
    ]
    kernel_params = dict(vmem_limit_bytes=vmem_bytes)
    if fast:
        for shape in sum_shapes:
            scratch += Sum.buffers(n // 2, *shape)
        scratch += [
            pltpu.VMEM((16, wide), bf16),
            pltpu.VMEM((n, 16, wide), bf16),
            pltpu.VMEM((n, 16, wide), bf16),
            pltpu.VMEM((n - 1, 16, wide), bf16),
            pltpu.VMEM((4, 16, wide), f32),
            dma((4, 4)),
            dma((len(cuts) * Piece.sems,)),
            dma((n - 1,)),
            dma((n - 1,)),
            dma((len(set(sum_shapes)), 6)),
            dma((len(sum_shapes),)),
            dma((len(sum_shapes) * Sum.sems,)),
            dma((n + 2,)),
            dma((n + 2,)),
        ]
        kernel_params.update(collective_id=1, has_side_effects=True)
    result = pl.pallas_call(
        functools.partial(layer_kernel, plan, n, fast, cuts, sum_shapes),
        in_specs=in_specs,
        out_specs=out_specs,
        out_shape=outs,
        scratch_shapes=scratch,
        compiler_params=pltpu.CompilerParams(**kernel_params),
        name="layer",
    )(*inputs)[:kept]
    out, token_grad = result[:2]
    if fast:
        return out, token_grad, result[2:6], result[6]
    wt, wo, we, wr = [g.reshape(-1, g.shape[3]) for g in result[2:6]]
    wt = wt.reshape(width, 3, 3, width // 3).transpose(0, 2, 1, 3).reshape(width, 3 * width)
    we = we.reshape(width, HIDDEN_BLOCKS, 8, unit).transpose(0, 2, 1, 3).reshape(width, hidden)
    sums, block = reduce_plain([wt, wo, we, wr], *result[6:9], n)
    wt, wo, we, wr = sums
    wt = wt.reshape(-1, 3, 3, width // 3).transpose(0, 2, 1, 3).reshape(wt.shape)
    we = we.reshape(-1, 8, HIDDEN_BLOCKS, unit).transpose(0, 2, 1, 3).reshape(we.shape)
    return out, token_grad, [wt, wo, we, wr], block


def per_device(
    tokens,
    slot_kinds,
    small_index,
    large_index,
    first_gain,
    first_shift,
    triple_weight,
    query_bias,
    value_bias,
    bias_table,
    output_weight,
    output_bias,
    attend_scale,
    second_gain,
    second_shift,
    expand_weight,
    expand_bias,
    reduce_weight,
    reduce_bias,
    feed_scale,
    cotangent,
):
    _, rows, width = tokens.shape
    heads = bias_table.shape[2]
    buckets = bias_table.shape[1] * lax.axis_size("fsdp")
    plan = Plan(small_index.shape[0], large_index.shape[0], rows, heads, buckets)
    tokens, cotangent = tokens[0], cotangent[0]
    short = [
        first_gain,
        first_shift,
        query_bias,
        value_bias,
        output_bias,
        attend_scale,
        second_gain,
        second_shift,
        reduce_bias,
        feed_scale,
    ]
    n = width // first_gain.shape[1]
    fast = fast_shape(
        lax.axis_size("rep"), n, [w.shape[1] for w in (triple_weight, output_weight, reduce_weight)]
    )
    shards = [w[0] for w in (triple_weight, output_weight, expand_weight, reduce_weight)]
    shorts = short + [expand_bias, bias_table[0].T]
    block_output, token_grad, sums, block = layer(
        plan, slot_kinds, tokens, cotangent, large_index, n, fast, shorts, shards
    )
    return wrap(block_output, token_grad, sums, block, first_gain.shape[1], bias_table.shape[1:])


def wrap_kernel(share, heads, out_in, tok_in, wt_in, wo_in, we_in, wr_in, block_ref, *outs):
    (
        out,
        tok,
        first_gain,
        first_shift,
        triple_weight,
        query_bias,
        value_bias,
        bias_table,
        output_weight,
        output_bias,
        attend_scale,
        second_gain,
        second_shift,
        expand_weight,
        expand_bias,
        reduce_weight,
        reduce_bias,
        feed_scale,
    ) = outs
    out[0] = out_in[...]
    tok[0] = tok_in[...]
    width = wt_in.shape[1] // 3
    span = width // 3
    for g in range(3):
        for part in range(3):
            first = g * width + part * span
            value = wt_in[:, first : first + span].astype(f32)
            triple_weight[0, :, part * width + g * span : part * width + (g + 1) * span] = value
    output_weight[0] = wo_in[...].astype(f32)
    reduce_weight[0] = wr_in[...].astype(f32)
    unit = 128
    count = we_in.shape[1] // (unit * HIDDEN_BLOCKS)
    for g in range(HIDDEN_BLOCKS):
        for f in range(count):
            value = we_in[:, (g * count + f) * unit : (g * count + f + 1) * unit].astype(f32)
            first = (f * HIDDEN_BLOCKS + g) * unit
            expand_weight[0, :, first : first + unit] = value
    first = block_ref.shape[1] - share
    rows = {
        FIRST_GAIN: first_gain,
        FIRST_SHIFT: first_shift,
        QUERY_BIAS: query_bias,
        VALUE_BIAS: value_bias,
        OUTPUT_BIAS: output_bias,
        ATTEND_SCALE: attend_scale,
        SECOND_GAIN: second_gain,
        SECOND_SHIFT: second_shift,
        REDUCE_BIAS: reduce_bias,
        FEED_SCALE: feed_scale,
    }
    for idx, ref in rows.items():
        ref[...] = block_ref[idx : idx + 1, first:]
    expand_bias[...] = block_ref[heads : heads + 1, :]
    for h in range(heads):
        bias_table[h] = block_ref[h : h + 1, : bias_table.shape[2]]


def wrap(block_output, token_grad, sums, block, share, table_shape):
    wt, wo, we, wr = sums
    sds = jax.ShapeDtypeStruct
    vector = sds((1, share), f32)
    whole_of = lambda w: sds((1,) + w.shape, f32)
    bshare, heads = table_shape
    triple = whole_of(wt)
    outs = [sds((1,) + block_output.shape, bf16)] * 2
    outs += [vector, vector, triple, vector, vector, sds((heads, 1, bshare), f32)]
    outs += [whole_of(wo)] + [vector] * 4 + [whole_of(we), sds((1, block.shape[1]), f32)]
    outs += [whole_of(wr), vector, vector]
    result = pl.pallas_call(
        functools.partial(wrap_kernel, share, heads),
        in_specs=[vmem_spec] * 7,
        out_specs=[vmem_spec] * 18,
        out_shape=outs,
        compiler_params=pltpu.CompilerParams(vmem_limit_bytes=vmem_bytes),
        name="wrap",
    )(block_output, token_grad, wt, wo, we, wr, block)
    result = list(result)
    result[7] = result[7].transpose(1, 2, 0)
    return tuple(result)


def solution(mesh):
    rows = P(("rep", "fsdp"), None, None)
    vector = P(None, "fsdp")
    matrix = P(None, "fsdp", None)
    weights = (
        vector,
        vector,
        matrix,
        vector,
        vector,
        matrix,
        matrix,
        vector,
        vector,
        vector,
        vector,
        matrix,
        vector,
        matrix,
        vector,
        vector,
    )
    return jax.shard_map(
        per_device,
        mesh=mesh,
        in_specs=(rows, P(("rep", "fsdp")), P(), P()) + weights + (rows,),
        out_specs=(rows, rows) + weights,
        check_vma=False,
    )
```

```python
import functools

import jax
import jax.numpy as jnp
import numpy as np
from jax import lax
from jax.experimental import pallas as pl
from jax.experimental.pallas import tpu as pltpu
from jax.sharding import PartitionSpec as P

f32 = jnp.float32
bf16 = jnp.bfloat16
norm_eps = 1e-06
neg_fill = -1000000000.0
vmem_bytes = 62 << 20

NN = (((1,), (0,)), ((), ()))
NT = (((1,), (1,)), ((), ()))
TN = (((0,), (0,)), ((), ()))


def mm(left, right, dims=NN):
    return lax.dot_general(left, right, dims, preferred_element_type=f32)


def round_up(value, unit):
    return -(-value // unit) * unit


class Plan:
    def __init__(self, small_len, large_len, rows, heads, buckets):
        self.heads, self.buckets = heads, buckets
        self.rows = rows
        self.small_len, self.large_len = small_len, large_len
        self.gs = int(round((small_len - 1) ** 0.5))
        self.gl = int(round((large_len - 1) ** 0.5))
        gl, gs = self.gl, self.gs
        self.strip_l = round_up(2 * gl * gl, 128)
        self.strip_s = round_up(2 * gs * (2 * gs - 1) + gs, 128)
        self.line = 2 * self.strip_l
        self.lanes = self.line + 128
        self.pad_cols = round_up(2 * gs * gs + 1, 128)
        self.pad_rows = 16 * gs
        self.cls_col = 2 * gs * gs
        self.cls_row = gs

    def place(self, di, dj, limit):
        gl = self.gl
        good = (np.abs(di) < limit) & (np.abs(dj) < limit)
        row = 1 + gl * np.maximum(di, 0) + np.maximum(dj, 0)
        col = 1 + gl * np.maximum(-di, 0) + np.maximum(-dj, 0)
        return np.where(good, row, 0), np.where(good, col, 0), good

    def positions(self):
        gl, gs = self.gl, self.gs
        x = np.arange(self.strip_l)
        rows, cols, goods = [], [], []
        for parity in range(2):
            m = 2 * ((x + gl) // (2 * gl)) if parity == 0 else 2 * (x // (2 * gl)) + 1
            t = x - gl * m
            r, c, g = self.place(gl - m, -t, gl)
            rows.append(r), cols.append(c), goods.append(g)
        large = [np.concatenate(v) for v in (rows, cols, goods)]
        x = np.arange(self.strip_s)
        m = x // (2 * gs)
        t = x - 2 * gs * m - gs
        small = [np.resize(np.zeros(1, v.dtype), self.line) for v in large]
        for dst, src in zip(small, self.place(gs - 1 - m, -t, gs)):
            dst[: self.strip_s] = src
        tail_r, tail_c, tail_g = np.zeros(128, int), np.zeros(128, int), np.zeros(128, bool)
        tail_r[:3], tail_c[:3], tail_g[:3] = (0, 1, 0), (1, 0, 0), True
        out = []
        for base in (large, small):
            out.append([np.concatenate(v) for v in zip(base, (tail_r, tail_c, tail_g))])
        return out

    def selector_arrays(self):
        gs = self.gs
        rows = np.zeros((self.rows, self.pad_rows), np.float32)
        cols = np.zeros((self.pad_cols, self.rows), np.float32)
        for image in range(3):
            for tok in range(self.small_len):
                r = image * self.small_len + tok
                i, j = divmod(tok - 1, gs)
                rows[r, self.cls_row if tok == 0 else 16 * i + j] = 1
                cols[self.cls_col if tok == 0 else 2 * gs * i + j, r] = 1
        return rows, cols

    def selectors(self):
        rows, cols = self.selector_arrays()
        return jnp.asarray(rows, bf16), jnp.asarray(cols, bf16)


def iota(shape, dim):
    return lax.broadcasted_iota(jnp.int32, shape, dim)


def pick_plan(plan):
    out = []
    for r, c, good in plan.positions():
        down = good & ((r - 1) // plan.gl >= (c - 1) // plan.gl)
        key = np.where(down, r, c)
        sub = np.where(down, c, r) - 1
        valid = good.copy()
        valid[plan.line :] = False
        out.append(np.stack([key, sub, down.astype(int), valid.astype(int)]))
    return jnp.asarray(np.concatenate(out), jnp.int32)


def lane_chunks(lanes, size=512):
    return [(low, min(low + size, lanes)) for low in range(0, lanes, size)]


def read_labels(plan, is_large, idx_ref, pick_ref, lab_ref):
    size, gl = idx_ref.shape[0], plan.gl
    across = idx_ref[1 : 1 + gl, :]
    down = idx_ref[:, 1 : 1 + gl].astype(f32).T.astype(jnp.int32)
    sides = []
    for v in (across, down):
        sides += [(v >> 6).astype(f32), (v & 63).astype(f32)]
    sides = jnp.concatenate(sides, axis=0).astype(bf16)
    for low, high in lane_chunks(plan.line):
        lanes, count = slice(low, high), high - low
        key, sub, use_down, valid = [
            jnp.where(is_large, pick_ref[i : i + 1, lanes], pick_ref[4 + i : 5 + i, lanes])
            for i in range(4)
        ]
        hot = jnp.where(iota((size, count), 0) == key, 1.0, 0.0).astype(bf16)
        here = iota((gl, count), 0) == sub
        rows = mm(sides, hot)
        for digit in range(2):
            a = rows[digit * gl : (digit + 1) * gl]
            b = rows[(2 + digit) * gl : (3 + digit) * gl]
            found = jnp.where(here, jnp.where(use_down == 1, b, a), 0.0)
            found = jnp.sum(found, axis=0, keepdims=True).astype(jnp.int32)
            lab_ref[digit : digit + 1, lanes] = jnp.where(valid == 1, found, -1)
    lane = iota((1, 128), 1)
    tail = jnp.where(lane == 0, idx_ref[0:1, 1:2], -1)
    tail = jnp.where(lane == 1, idx_ref[1:2, 0:1], tail)
    tail = jnp.where(lane == 2, idx_ref[0:1, 0:1], tail)
    lab_ref[0:1, plan.line : plan.line + 128] = jnp.where(tail < 0, -1, tail >> 6)
    lab_ref[1:2, plan.line : plan.line + 128] = jnp.where(tail < 0, -1, tail & 63)


def table_lines(plan, tab, lab_ref, line_ref):
    count = tab.shape[1] // 64
    split = jnp.concatenate([tab[:, 64 * i : 64 * (i + 1)] for i in range(count)], axis=0)
    split = split.astype(bf16)
    for low, high in lane_chunks(plan.lanes):
        first, second = lab_ref[0:1, low:high], lab_ref[1:2, low:high]
        hot = jnp.where(iota((64, high - low), 0) == second, 1.0, 0.0).astype(bf16)
        rows = mm(split, hot)
        parts = [jnp.zeros((16, high - low), f32)] * 4
        for i in range(count):
            parts[i % 4] = jnp.where(first == i, rows[16 * i : 16 * (i + 1)], parts[i % 4])
        line_ref[:, low:high] = (parts[0] + parts[1]) + (parts[2] + parts[3])


def table_from_lines(plan, line_of, lab_ref, buckets):
    count = buckets // 64
    total = jnp.zeros((32 * count, 64), f32)
    for chunk in range(plan.lanes // 128):
        lanes = slice(chunk * 128, (chunk + 1) * 128)
        first, second = lab_ref[0:1, lanes], lab_ref[1:2, lanes]
        hot = jnp.where(iota((64, 128), 0) == second, 1.0, 0.0).astype(bf16)
        part = line_of(chunk)
        high = part.astype(bf16)
        low = (part - high.astype(f32)).astype(bf16)
        both = jnp.concatenate([high, low], axis=0)
        stack = [jnp.where(first == i, both, jnp.zeros_like(both)) for i in range(count)]
        total = total + mm(jnp.concatenate(stack, axis=0), hot, NT)
    pieces = []
    for i in range(count):
        pieces.append(total[32 * i : 32 * i + 16] + total[32 * i + 16 : 32 * i + 32])
    return jnp.concatenate(pieces, axis=1)


def segments(plan, is_large, ids):
    n = plan.small_len
    small = jnp.where(ids >= n, 1, 0) + jnp.where(ids >= 2 * n, 1, 0) + jnp.where(ids >= 3 * n, 1, 0)
    return jnp.where(is_large, jnp.where(ids < plan.large_len, 0, 3), small)


def line_of_head(ref, h):
    return jnp.sum(jnp.where(iota((16, 1), 0) == h, ref[...], 0.0), axis=0, keepdims=True)


def large_strip(plan, line):
    gl, span = plan.gl, plan.strip_l
    rolled = []
    for parity in range(2):
        part = jnp.broadcast_to(line[:, parity * span : (parity + 1) * span], (gl, span))
        rolled.append(pltpu.roll(part, 0, axis=1, stride=1, stride_axis=0))
    odd = (iota((1, span), 1) + span - 1) % span // gl % 2
    odd = jnp.where(iota((gl, 1), 0) == 0, 1 - odd, odd)
    strip = jnp.where(odd == 1, rolled[1], rolled[0])
    return jnp.concatenate([strip, strip[:, :128]], axis=1)


def band_move(plan, a):
    return plan.gl * (plan.gl - a)


def small_padded(plan, line, tail):
    gs, span = plan.gs, plan.strip_s
    line = jnp.broadcast_to(line[:, 0:span], (16, span))
    strip = pltpu.roll(line, 0, axis=1, stride=1, stride_axis=0)
    col = iota((1, plan.pad_cols), 1)
    is_col = col == plan.cls_col
    is_row = iota((16, 1), 0) == plan.cls_row
    bands = []
    for i in range(gs):
        move = 2 * gs * (gs - 1 - i) + gs
        band = pltpu.roll(strip, (span - move) % span, axis=1)[:, : plan.pad_cols]
        band = jnp.where(is_col, tail[:, 1:2], band)
        if i == 0:
            edge = jnp.where(is_col, tail[:, 2:3], tail[:, 0:1])
            band = jnp.where(is_row, edge, band)
        bands.append(band)
    return jnp.concatenate(bands, axis=0).astype(bf16)


def small_blocks(plan, line, tail, pick, colsel):
    rows = plan.rows
    wide = round_up(rows, 128)
    cols = mm(small_padded(plan, line, tail), colsel[:, 0:256]).astype(bf16)
    out = []
    for image, ((r0, r1), (l0, _)) in enumerate(image_rows(plan)):
        start = 256 * image
        block = mm(pick[:, start : start + r1 - r0], cols, TN)
        shift = image * plan.small_len - l0
        last = l0 + round_up(shift + plan.small_len, 128)
        if last - l0 > 256:
            block = jnp.concatenate([block, jnp.zeros((r1 - r0, last - l0 - 256), f32)], axis=1)
        if shift:
            block = pltpu.roll(block, shift, axis=1)
        parts = [block]
        if l0:
            parts.insert(0, jnp.zeros((r1 - r0, l0), f32))
        if last < wide:
            parts.append(jnp.zeros((r1 - r0, wide - last), f32))
        out.append((r0, r1, jnp.concatenate(parts, axis=1)))
    return out


def bias_head(plan, is_large, line_ref, pick, colsel, h, out_ref):
    gl, rows = plan.gl, plan.rows
    wide = round_up(rows, 128)
    line = line_of_head(line_ref, h)
    tail = line[:, plan.line : plan.line + 128]
    blocks = small_blocks(plan, line, tail, pick, colsel)
    strip = large_strip(plan, line)
    span = strip.shape[1]
    col = iota((1, wide), 1)
    seg_col = segments(plan, is_large, col)
    bands = -(-rows // gl)
    for pair in range(-(-bands // 2)):
        first = 2 * gl * pair
        count = min(2 * gl, rows - first)
        parts = []
        for a in range(2 * pair, 2 * pair + 2):
            if a >= bands:
                continue
            move = band_move(plan, a)
            low = move // 128 * 128
            piece = strip[:, low : min(low + wide + 128, span)]
            if piece.shape[1] < wide + 128:
                piece = jnp.concatenate(
                    [piece, jnp.zeros((gl, wide + 128 - piece.shape[1]), f32)], axis=1
                )
            turn = (wide + 128 - (move - low)) % (wide + 128)
            parts.append((pltpu.roll(piece, turn, axis=1) if turn else piece)[:, :wide])
        block = (jnp.concatenate(parts, axis=0) if len(parts) > 1 else parts[0])[:count]
        row = iota((count, 1), 0) + first
        edge = jnp.where(col[:, :128] == 0, tail[:, 1:2], block[:, :128])
        block = jnp.concatenate([edge, block[:, 128:]], axis=1)
        if first == 0:
            block = jnp.where(row == 0, jnp.where(col == 0, tail[:, 2:3], tail[:, 0:1]), block)
        if first + count > plan.large_len:
            block = jnp.where(row < plan.large_len, block, 0.0)
        small = None
        for r0, r1, value in blocks:
            low, high = max(first, r0), min(first + count, r1)
            if low >= high:
                continue
            part = [value[low - r0 : high - r0]]
            if low > first:
                part.insert(0, jnp.zeros((low - first, wide), f32))
            if high < first + count:
                part.append(jnp.zeros((first + count - high, wide), f32))
            part = jnp.concatenate(part, axis=0) if len(part) > 1 else part[0]
            small = part if small is None else small + part
        block = jnp.where(is_large, block, small)
        block = jnp.where(segments(plan, is_large, row) == seg_col, block, neg_fill)
        out_ref[h, first : first + count, :] = block[:, :rows].astype(bf16)


def norm_stats(values):
    mean = jnp.mean(values, axis=1, keepdims=True)
    centred = values - mean
    var = jnp.mean(centred * centred, axis=1, keepdims=True)
    inv = lax.rsqrt(var + norm_eps)
    return centred * inv, inv


def norm_back(d_out, gain, normal, inv):
    d_normal = d_out * gain
    mean_d = jnp.mean(d_normal, axis=1, keepdims=True)
    mean_dn = jnp.mean(d_normal * normal, axis=1, keepdims=True)
    return inv * (d_normal - mean_d - normal * mean_dn)


def rows_sum(values):
    return jnp.sum(values, axis=0, keepdims=True)


def gelu_parts(v):
    size = jnp.abs(v)
    bell = jnp.exp(-0.5 * v * v)
    below = 1.0 + (0.3275911 * 0.7071067811865476) * size
    t = pl.reciprocal(below, approx=True)
    t = t * (2.0 - below * t)
    poly = t * (
        0.127414796
        + t * (-0.142248368 + t * (0.7107068705 + t * (-0.7265760135 + t * 0.5307027145)))
    )
    tail = poly * bell
    phi = jnp.where(v < 0, tail, 1.0 - tail)
    return v * phi, phi + v * bell * 0.3989422804014327


BE_ROW = 10
(
    FIRST_GAIN,
    FIRST_SHIFT,
    QUERY_BIAS,
    VALUE_BIAS,
    OUTPUT_BIAS,
    ATTEND_SCALE,
    SECOND_GAIN,
    SECOND_SHIFT,
    REDUCE_BIAS,
    FEED_SCALE,
) = range(10)


def vec(ref, idx):
    return ref[idx : idx + 1, :]


def half_mask(rows):
    return iota((rows, 128), 1) < 64


class Spot:
    def __init__(self, n):
        self.n, self.levels = n, n // 2
        self.rep, self.f = lax.axis_index("rep"), lax.axis_index("fsdp")
        self.half, self.core = self.rep // 2, self.rep % 2
        self.level, self.side = self.f // 2, self.f % 2

    def at(self, rep=None, f=None):
        return {"rep": self.rep if rep is None else rep, "fsdp": self.f if f is None else f}

    def sibling(self):
        return self.at(rep=2 * self.half + 1 - self.core)

    def across(self):
        return self.at(rep=2 * (1 - self.half) + self.core)

    def beside(self):
        return self.at(f=2 * self.level + 1 - self.side)

    def along(self, step):
        return self.at(f=2 * ((self.level + step) % self.levels) + self.side)

    def from_along(self, step, side=None):
        side = self.side if side is None else side
        return 2 * ((self.level + self.levels - step) % self.levels) + side


MESH = pl.DeviceIdType.MESH


def greet(devices):
    for device in devices:
        barrier = pltpu.get_barrier_semaphore()
        pl.semaphore_signal(barrier, inc=1, device_id=device, device_id_type=MESH)


def met(count):
    pl.semaphore_wait(pltpu.get_barrier_semaphore(), count)


def send(src, dst, send_sem, recv_sem, device):
    return pltpu.make_async_remote_copy(
        src_ref=src,
        dst_ref=dst,
        send_sem=send_sem,
        recv_sem=recv_sem,
        device_id=device,
        device_id_type=MESH,
    )


def fast_shape(reps, n, shard_rows):
    return reps == 4 and n == 8 and all(rows % 96 == 0 for rows in shard_rows)


def spread_block(refs, block_ref):
    *vectors, be_ref, table_ref = refs
    heads, share = table_ref.shape
    lanes = block_ref.shape[1]
    table = jnp.concatenate([table_ref[...].astype(f32), jnp.zeros((16 - heads, share), f32)], axis=0)
    width = vectors[0].shape[1]
    rows = [v[...].astype(f32) for v in vectors]
    rows.append(jnp.zeros((16 - len(rows), width), f32))
    block = jnp.concatenate(
        [table, jnp.zeros((16, lanes - share - width), f32), jnp.concatenate(rows, axis=0)], axis=1
    )
    wide = jnp.broadcast_to(be_ref[...].astype(f32), (16, lanes))
    block_ref[...] = jnp.where(iota((16, lanes), 0) == heads, wide, block).astype(bf16)


smem_spec = pl.BlockSpec(memory_space=pltpu.SMEM)
any_spec = pl.BlockSpec(memory_space=pl.ANY)
vmem_spec = pl.BlockSpec(memory_space=pltpu.VMEM)


def add16(left, right):
    return (left.astype(f32) + right.astype(f32)).astype(bf16)


def gather_plain(shorts, shards, n):
    gather = lambda value, axis: lax.all_gather(value, "fsdp", axis=axis, tiled=True)
    vecs = gather(jnp.concatenate(shorts[:10], axis=0), 1).astype(f32)
    vecs = jnp.pad(vecs, ((0, 6), (0, 0)))
    table = gather(shorts[11], 1)
    table = jnp.pad(table, ((0, 16 - table.shape[0]), (0, 0)))
    return [gather(w, 0) for w in shards], vecs, gather(shorts[10], 1).astype(f32), table


def reduce_plain(grads, vec_sums, be_sums, table_sums, n):
    def whole_sum(value):
        value = lax.psum_scatter(value, "fsdp", scatter_dimension=0, tiled=True)
        return lax.psum(value, "rep")

    sums = lax.psum((vec_sums, be_sums, table_sums), ("rep", "fsdp"))
    me = lax.axis_index("fsdp")
    cut = lambda v: lax.dynamic_slice_in_dim(v, me * (v.shape[1] // n), v.shape[1] // n, axis=1)
    vec_part, be_part, table_part = [cut(v) for v in sums]
    wide = be_part.shape[1]
    space = max(wide - vec_part.shape[1] - table_part.shape[1], 0)
    body = jnp.concatenate([table_part, jnp.zeros((16, space), f32), vec_part], axis=1)
    block = jnp.where(jnp.arange(16)[:, None] == 12, jnp.pad(be_part, ((0, 0), (0, body.shape[1] - wide))), body)
    return [whole_sum(g) for g in grads], block


class Piece:
    sems = 6

    def __init__(self, spot, shard, whole, row, col, cols, sent, rs, base):
        self.size = cols // 384
        levels = spot.levels
        part, q = 48, 16
        start = row + spot.core * part
        cut = slice(col, col + cols)
        rows = lambda first, size: pl.ds(pl.multiple_of(first, 16), size)
        plane = rows(start + spot.half * q, 2 * q)
        outer = rows(start + spot.half * 2 * q, q)
        core_rows = rows(start, part)
        side = spot.side

        def copy(idx, kind, src, dst, device):
            return send(src, dst, sent.at[kind], rs.at[base + idx], device)

        own = shard.at[plane, cut]
        here = whole.at[spot.level, side, plane, cut]
        self.local = pltpu.make_async_copy(own, here, rs.at[base + 5])
        self.z = [copy(0, 0, own, here, spot.along(step)) for step in range(1, levels)]
        three = whole.at[0 : levels - 1, 0, 0 : 2 * q, cut]
        self.z_all = pltpu.make_async_copy(three, three, rs.at[base])
        column = whole.at[:, side, plane, cut]
        self.y = copy(1, 1, column, column, spot.beside())
        near = whole.at[:, side, outer, cut]
        far = whole.at[:, 1 - side, outer, cut]
        self.x = [copy(2, 2, near, near, spot.across()), copy(3, 2, far, far, spot.across())]
        done = whole.at[:, :, core_rows, cut]
        self.c = copy(4, 3, done, done, spot.sibling())

    @staticmethod
    def sent_waits(levels, whole, sent):
        part = whole.shape[2] // 96
        views = [
            whole.at[0 : levels - 1, 0, 0 : 32 * part],
            whole.at[:, 0, 0 : 32 * part],
            whole.at[:, :, 0 : 16 * part],
            whole.at[:, :, 0 : 48 * part],
        ]
        return [pltpu.make_async_copy(v, v, sent.at[kind]) for kind, v in enumerate(views)]

    def start(self):
        self.local.start()
        for copy in self.z:
            copy.start()

    def after_z(self):
        self.local.wait()
        self.z_all.wait()
        self.y.start()
        self.x[0].start()

    def after_y(self):
        self.y.wait_recv()
        self.x[1].start()

    def after_x(self):
        self.x[0].wait_recv()
        self.x[1].wait_recv()
        self.c.start()

    def after_c(self):
        self.c.wait_recv()


def piece_cuts(shard_shapes):
    cuts = []
    for idx, (rows, cols) in enumerate(shard_shapes):
        for row in range(0, rows, 96):
            starts = list(range(0, cols, 384))
            if idx == 0:
                starts = starts[0::2] + starts[1::2]
            for col in starts:
                cuts.append((idx, row, col, 384))
    return cuts


def image_rows(plan):
    out = []
    for image in range(3):
        first, last = image * plan.small_len, (image + 1) * plan.small_len
        rows = (first // 16 * 16, round_up(last, 16))
        lanes = (first // 128 * 128, min(round_up(last, 128), plan.rows))
        out.append((rows, lanes))
    return out


def image_selectors(plan):
    rows, _ = plan.selector_arrays()
    out = []
    for image, ((low, high), _) in enumerate(image_rows(plan)):
        part = rows.copy()
        part[: image * plan.small_len] = 0
        part[(image + 1) * plan.small_len :] = 0
        out.append(np.pad(part[low:high].T, ((0, 0), (0, 256 - (high - low)))))
    return jnp.asarray(np.concatenate(out, axis=1), bf16)


def fold_head(plan, ds_ref, pick, colsel, large_ref, small_ref, tail_ref, h, is_large):
    gl, gs, rows = plan.gl, plan.gs, plan.rows
    wide = round_up(rows, 128)
    width = plan.strip_l + 128
    bands = -(-rows // gl)
    total = jnp.zeros((gl, width), f32)
    side = jnp.zeros((2 * gl, 128), f32)
    for pair in range(-(-bands // 2)):
        first = 2 * gl * pair
        count = min(2 * gl, rows - first)
        block = ds_ref[first : first + count, :].astype(f32)
        block = jnp.concatenate([block, jnp.zeros((count, wide - rows), f32)], axis=1)
        if count < 2 * gl:
            block = jnp.concatenate([block, jnp.zeros((2 * gl - count, wide), f32)], axis=0)
        if pair == 0:
            row = iota((2 * gl, 1), 0)
            top_row = jnp.where(row == 0, block, 0.0)
            block = jnp.where(row == 0, 0.0, block)
        side = side + block[:, :128]
        block = jnp.concatenate(
            [jnp.where(iota((1, 128), 1) == 0, 0.0, block[:, :128]), block[:, 128:]], axis=1
        )
        for half in range(2):
            a = 2 * pair + half
            if a >= bands:
                continue
            move = band_move(plan, a)
            low = move // 128 * 128
            piece = block[half * gl : (half + 1) * gl]
            if move > low:
                piece = jnp.concatenate([piece, jnp.zeros((gl, 128), f32)], axis=1)
                piece = pltpu.roll(piece, move - low, axis=1)
            piece = piece[:, : width - low]
            high = low + piece.shape[1]
            parts = [total[:, low:high] + piece]
            if low:
                parts.insert(0, total[:, :low])
            if high < width:
                parts.append(total[:, high:])
            total = jnp.concatenate(parts, axis=1) if len(parts) > 1 else parts[0]
    large_ref[h] = jnp.concatenate(
        [total[:, :128] + total[:, plan.strip_l :], total[:, 128 : plan.strip_l]], axis=1
    )
    lane = iota((1, wide), 1)
    full = lambda v: jnp.sum(jnp.sum(v, axis=0, keepdims=True), axis=1, keepdims=True)
    corner = full(jnp.where(lane == 0, top_row, 0.0))
    top = full(jnp.where(lane == 0, 0.0, top_row))
    side = full(jnp.where(iota((1, 128), 1) == 0, side, 0.0))

    gathered = jnp.zeros((plan.pad_rows, 256), f32)
    for image, ((r0, r1), (l0, l1)) in enumerate(image_rows(plan)):
        block = ds_ref[r0:r1, l0:l1]
        shift = image * plan.small_len - l0
        if shift:
            pad = round_up(l1 - l0, 128) - (l1 - l0)
            block = block.astype(f32)
            if pad:
                block = jnp.concatenate([block, jnp.zeros((r1 - r0, pad), f32)], axis=1)
            block = pltpu.roll(block, block.shape[1] - shift, axis=1)[:, :256].astype(bf16)
        start = 256 * image
        gathered = gathered + mm(pick[:, start : start + r1 - r0], block)
    high = gathered.astype(bf16)
    low = (gathered - high.astype(f32)).astype(bf16)
    select = colsel[:, 0:256]
    padded = mm(high, select, NT) + mm(low, select, NT)
    span = plan.strip_s
    col = iota((1, plan.pad_cols), 1)
    row = iota((16, 1), 0)
    acc = jnp.zeros((16, span), f32)
    edge = jnp.zeros((16, plan.pad_cols), f32)
    for i in range(gs):
        band = padded[16 * i : 16 * (i + 1)]
        if i == 0:
            top_s = jnp.where(row == plan.cls_row, band, 0.0)
            band = jnp.where(row == plan.cls_row, 0.0, band)
        edge = edge + band
        band = jnp.where(col < plan.cls_col, band, 0.0)
        band = jnp.concatenate([band, jnp.zeros((16, span - plan.pad_cols), f32)], axis=1)
        acc = acc + pltpu.roll(band, 2 * gs * (gs - 1 - i) + gs, axis=1)
    small_ref[h] = acc
    corner_s = full(jnp.where(col == plan.cls_col, top_s, 0.0))
    top_s = full(jnp.where(col < plan.cls_col, top_s, 0.0))
    side_s = full(jnp.where(col == plan.cls_col, edge, 0.0))
    lane = iota((1, 128), 1)
    picks = [(top, top_s), (side, side_s), (corner, corner_s)]
    tail = jnp.zeros((1, 128), f32)
    for i, (a, b) in enumerate(picks):
        tail = jnp.where(lane == i, jnp.where(is_large, a, b), tail)
    tail_ref[h] = tail


def fold_lines(plan, large_ref, small_ref, tail_ref, is_large):
    gl, heads, span = plan.gl, plan.heads, plan.strip_l
    odd = (iota((1, span), 1) + span - 1) % span // gl % 2
    lines = [None, None]
    for i in reversed(range(gl)):
        row = large_ref[:, i, :]
        for parity in range(2):
            want = parity if i else 1 - parity
            part = jnp.where(odd == want, row, 0.0)
            if lines[parity] is not None:
                part = part + pltpu.roll(lines[parity], span - 1, axis=1)
            lines[parity] = part
    small = None
    for i in reversed(range(16)):
        part = small_ref[:, i, :]
        small = part if small is None else part + pltpu.roll(small, plan.strip_s - 1, axis=1)
    small = jnp.concatenate([small, jnp.zeros((heads, plan.line - plan.strip_s), f32)], axis=1)
    line = jnp.where(is_large, jnp.concatenate(lines, axis=1), small)
    tail = tail_ref[:, 0, :]
    line = jnp.concatenate([line, tail], axis=1)
    return jnp.concatenate([line, jnp.zeros((16 - heads, plan.lanes), f32)], axis=0)


class Sum:
    sems = 6
    outer = 16

    def __init__(self, spot, grad, out, row, cut, bufs, sent, c_sem, rs, base):
        self.spot, self.grad, self.out = spot, grad, out
        self.row, self.cut = row, cut
        self.acc, self.got_x, self.got_y, self.got_z, self.total, self.got_f = bufs
        half, core, side, level, levels = spot.half, spot.core, spot.side, spot.level, spot.levels
        q, part = self.outer, self.acc.shape[2]
        self.middle = m = part - 2 * q
        rows = lambda first, size: pl.ds(pl.multiple_of(first, 16), size)
        self.rows = rows
        self.plane = rows(half * q, q + m)
        self.mine = rows(half * (q + m), q)
        self.own = rows(core * part, part)
        self.sent = self.joined = False
        unit = 4 * self.acc.shape[3] / LINK_BYTES_PER_US
        self.link_us = (2 * levels * q * unit, levels * (q + m) * unit, (q + m) * unit)

        def copy(idx, src, dst, device):
            out_sem = sent.at[idx] if idx else c_sem
            return send(src, dst, out_sem, rs.at[base + idx], device)

        acc = self.acc
        other = rows((1 - core) * part, part)
        self.c = copy(0, grad.at[:, :, other, cut[0]], acc, spot.sibling())
        self.x = copy(1, acc.at[:, :, rows((1 - half) * (q + m), q)], self.got_x, spot.across())
        self.y = copy(2, acc.at[:, 1 - side, self.plane], self.got_y, spot.beside())
        self.z = []
        for step in range(1, levels):
            src = acc.at[(level + step) % levels, side, self.plane]
            self.z.append(copy(5, src, self.got_z.at[step - 1], spot.along(step)))
        self.z_all = pltpu.make_async_copy(self.got_z, self.got_z, rs.at[base + 5])
        self.f = copy(3, self.total, self.got_f, spot.across())
        mine = out.at[rows(row + core * part, part), cut[1]]
        self.last = copy(4, mine, mine, spot.sibling())

    @classmethod
    def buffers(cls, levels, shard_rows, cols):
        part = shard_rows // 2
        kept = part - cls.outer
        shapes = [
            (levels, 2, part, cols),
            (levels, 2, cls.outer, cols),
            (levels, kept, cols),
            (levels - 1, kept, cols),
            (kept, cols),
            (kept, cols),
        ]
        return [pltpu.VMEM(shape, bf16) for shape in shapes]

    def start(self):
        self.c.start()

    def free(self):
        self.join()
        if not self.sent:
            self.c.wait_send()
            self.sent = True

    def stage(self, k):
        getattr(self, ("go", "after_x", "after_y", "after_z", "after_f", "after_last")[k])()

    def join(self):
        if self.joined:
            return
        self.joined = True
        self.c.wait_recv()

        @pl.loop(0, self.acc.shape[0])
        def _(level):
            for side in range(2):
                own = self.grad[level, side, self.own, self.cut[0]]
                self.acc[level, side] = add16(self.acc[level, side], own)

    def go(self):
        self.join()
        self.x.start()

    def after_x(self):
        self.x.wait_recv()

        @pl.loop(0, self.acc.shape[0])
        def _(level):
            for side in range(2):
                mine = self.acc[level, side, self.mine]
                self.acc[level, side, self.mine] = add16(mine, self.got_x[level, side])

        self.y.start()

    def after_y(self):
        side = self.spot.side
        self.y.wait_recv()

        @pl.loop(0, self.acc.shape[0])
        def _(level):
            mine = self.acc[level, side, self.plane]
            self.acc[level, side, self.plane] = add16(mine, self.got_y[level])

        for copy in self.z:
            copy.start()

    def after_z(self):
        self.z_all.wait()
        value = self.acc[self.spot.level, self.spot.side, self.plane].astype(f32)
        for k in range(len(self.z)):
            value = value + self.got_z[k].astype(f32)
        self.total[...] = value.astype(bf16)
        self.f.start()

    def after_f(self):
        q, m, half = self.outer, self.middle, self.spot.half
        base = self.row + self.spot.core * self.acc.shape[2]
        rows = self.rows
        total, got, out, cut = self.total, self.got_f, self.out, self.cut[1]
        self.f.wait_recv()
        out[rows(base + half * (q + m), q), cut] = total[rows(half * m, q)]
        both = add16(total[rows((1 - half) * q, m)], got[rows(half * q, m)])
        out[rows(base + q, m), cut] = both
        out[rows(base + (1 - half) * (q + m), q), cut] = got[rows((1 - half) * m, q)]
        self.last.start()

    def after_last(self):
        self.last.wait_recv()

    @classmethod
    def sent_rows(cls, levels, shard_rows):
        part = shard_rows // 2
        kept = part - cls.outer
        return [2 * levels * cls.outer, levels * kept, kept, part, (levels - 1) * kept]


LATENCY_US, LINK_BYTES_PER_US = 1.6, 85e3
HIDDEN_BLOCKS = 3
BLOCK_ORDER = [("rows", 0), ("rows", 1), ("cols", 0), ("rows", 2), ("cols", 1), ("cols", 2)]


class Queue:
    def __init__(self):
        self.clock, self.entries = 0.0, []
        self.free = {"x": 0.0, "y": 0.0, "z": 0.0, "core": 0.0}

    def book(self, link, us):
        begin = max(self.clock, self.free[link])
        self.free[link] = begin + us
        return begin + us + LATENCY_US

    def add(self, job):
        job.start()
        self.entries.append([self.book("core", 1.0), 0, job])

    def take(self, entry):
        _, stage, job = entry
        if stage == 0:
            job.join()
        else:
            job.stage(stage)
        x, y, f = job.link_us
        if stage == 0:
            job.stage(0)
            entry[0] = self.book("x", x)
        elif stage == 1:
            entry[0] = self.book("y", y)
        elif stage == 2:
            entry[0] = self.book("z", y)
        elif stage == 3:
            entry[0] = self.book("x", f)
        elif stage == 4:
            entry[0] = self.book("core", 0.3)
        entry[1] += 1
        if stage == 5:
            self.entries.remove(entry)

    def beat(self, us):
        self.clock += us
        while self.entries:
            entry = min(self.entries, key=lambda item: item[0])
            if entry[0] > self.clock:
                break
            self.take(entry)

    def drain(self):
        while self.entries:
            entry = min(self.entries, key=lambda item: item[0])
            self.clock = max(self.clock, entry[0])
            self.take(entry)


def layer_kernel(plan, n, fast, cuts, sum_shapes, *refs):
    refs = list(refs)
    take = lambda count: [refs.pop(0) for _ in range(count)]
    kind_ref, tok_in, cot_in, idx_in, pick_ref, colsel_ref, image_ref = take(7)
    if fast:
        shorts, shards = take(12), take(4)
    else:
        vec_in, be_in, tab_in = take(3)
        wholes = take(4)
    out_ref, tok_out = take(2)
    sum_wt, sum_wo, sum_we, sum_wr = take(4)
    if fast:
        (small_out,) = take(1)
        wholes = take(4)
    else:
        vec_out, be_out, tab_out = take(3)
    normed_out, branch_out, qkv_out, probs_out, ds_out = take(5)
    vec_ref, be_ref, lab_ref, middle_ref, pair_ref, mixed_ref, small_ref, dbe_ref = take(8)
    rows_ref, cols_ref = take(2)
    load_sems, save_sems, tile_sems, late_sems, pair_sems, ds_sems, stage_sems = take(7)
    wt_in, wo_in, we_in, wr_in = wholes
    is_large = kind_ref[0] == 1
    heads, rows = plan.heads, plan.rows
    pairs = heads // 2
    width = tok_in.shape[1]
    eighth = width // 8
    hidden = wr_in.shape[2] * 8
    unit = hidden // 8 // HIDDEN_BLOCKS
    tile_cols = 8 * unit
    matrix = lambda ref: ref[...].reshape(width, width)
    half_ref, dfeed_ref = pair_ref.at[0], pair_ref.at[1]

    def fetch(src, dst, sem):
        copy = pltpu.make_async_copy(src, dst, sem)
        copy.start()
        return copy

    saves = []

    def save(src, dst):
        copy = fetch(src, dst, save_sems.at[len(saves)])
        saves.append(copy)
        return copy

    queue = Queue()
    jobs, pieces = [], []
    if fast:
        bufs = take(6 * len(sum_shapes))
        sum_kinds = sorted(set(sum_shapes))
        short, shorts_got, block, got, reps = take(5)
        gss, grs, ass, ars, rss, css, rrs, bss, brs = take(9)
        spot = Spot(n)
        peers = [spot.at(f=(spot.f + k) % n) for k in range(1, n)]
        others = [spot.at(rep=(spot.rep + k) % 4) for k in range(1, 4)]
        greet(peers + others)
        for idx, row, col, cols in cuts:
            base = len(pieces) * Piece.sems
            at = GATHER_ORDER[idx]
            args = (row, col, cols, gss.at[at], grs, base)
            pieces.append(Piece(spot, shards[at], wholes[at], *args))
        formed = []
        for ring, j in BLOCK_ORDER:
            if ring == "rows":
                formed.append((rows_ref, sum_wr, j * unit, 0))
            else:
                formed.append((cols_ref, sum_we, 0, j * tile_cols))
        formed.append((rows_ref, sum_wo, 0, 0))
        for j in range(3):
            formed.append((rows_ref, sum_wt, 0, j * width))
        counts = {}
        for ring, out, row, col in formed:
            k = counts[id(ring)] = counts.get(id(ring), -1) + 1
            cols = ring.shape[4] // 2
            for first in (0, cols):
                i = len(jobs)
                cut = (slice(first, first + cols), slice(col + first, col + first + cols))
                kind = sum_kinds.index(sum_shapes[i])
                args = (bufs[6 * i : 6 * i + 6], rss.at[kind], css.at[i], rrs, i * Sum.sems)
                jobs.append(Sum(spot, ring.at[k % 2], out, row, cut, *args))
        spread_block(shorts, short)
        small = []
        for k, peer in enumerate(peers):
            small.append(send(short, shorts_got.at[spot.f], ass.at[k], ars.at[k], peer))

    def set_out():
        met(n + 2)
        for copy in small:
            copy.start()
        pieces[0].start()
        shorts_got[spot.f] = short[...]

    events = []
    for i in range(len(pieces)):
        for kind, lag in enumerate((0,) + LAGS):
            events.append((i + lag, kind, i))
    events.sort()
    gone = [0]
    whole_at = {i: pos for pos, (_, kind, i) in enumerate(events) if kind == 3}
    on_whole = []

    def run_event():
        _, kind, i = events[gone[0]]
        gone[0] += 1
        getattr(pieces[i], ("after_z", "after_y", "after_x", "after_c")[kind])()
        if kind == 0:
            for ahead in (range(2, AHEAD + 1) if i == 0 else (i + AHEAD,)):
                if ahead < len(pieces):
                    pieces[ahead].start()
        if kind == 3:
            for call in on_whole:
                call(i)

    now = [-1]

    def step(count=1):
        now[0] += count
        while gone[0] < len(events) and events[gone[0]][0] <= now[0]:
            run_event()

    def gather_until(piece):
        while events and gone[0] <= whole_at[min(piece, len(pieces) - 1)]:
            step()


    def forward(line_ref, heads_ref, qkv_ref, wt_ref, wo_ref, idx_ref, tok, normed_ref):
        idx_copy = fetch(idx_in, idx_ref, late_sems.at[0])
        tok_copy = fetch(tok_in, tok, late_sems.at[1])
        loads = []
        for src, ref in ((wt_in, wt_ref), (wo_in, wo_ref)):
            starts = range(0, src.shape[3], width // 2)
            for col in list(starts[0::2]) + list(starts[1::2]):
                first = col % width
                dst = ref.at[col // width, :, :, :, first : first + width // 2]
                view = src.at[:, :, :, col : col + width // 2]
                loads.append(pltpu.make_async_copy(view, dst, load_sems.at[len(loads)]))
        if not fast:
            for load in loads:
                load.start()

        def begin(i):
            if i < len(loads):
                loads[i].start()

        on_whole.append(begin)
        idx_copy.wait()
        read_labels(plan, is_large, idx_ref, pick_ref, lab_ref)
        if fast:
            set_out()
        tok_copy.wait()
        normal, _ = norm_stats(tok[...].astype(f32))
        if fast:
            pieces[1].start()
            for copy in small:
                copy.wait()
            step()
            share, bshare = shorts[0].shape[1], shorts[11].shape[1]
            tab = []
            for f in range(n):
                part = shorts_got[f].astype(f32)
                wide = part.shape[1]
                vec_ref[:, f * share : (f + 1) * share] = part[:, wide - share :]
                tab.append(part[:, :bshare])
                be_ref[:, f * wide : (f + 1) * wide] = part[heads : heads + 1, :]
            tab = jnp.concatenate(tab, axis=1)
        else:
            vec_ref[...] = vec_in[...]
            be_ref[...] = be_in[...]
            tab = tab_in[...]
        table_lines(plan, tab, lab_ref, line_ref)
        step()
        normed = normal * vec(vec_ref, FIRST_GAIN) + vec(vec_ref, FIRST_SHIFT)
        normed_ref[...] = normed.astype(bf16)
        save(normed_ref, normed_out)
        for group in range(heads // 2):

            @pl.loop(2 * group, 2 * group + 2)
            def _(h):
                bias_head(plan, is_large, line_ref, image_ref, colsel_ref, h, heads_ref)

            step()
        def project(group):
            low, high = group * width // 2, (group + 1) * width // 2
            normed = normed_ref[...]
            gather_until(3 * group + 2)
            for j in range(3):
                loads[3 * group + j].wait()
                triple = mm(normed, wt_ref[j, :, :, :, low:high].reshape(width, width // 2))
                if j == 0:
                    triple = triple + vec_ref[QUERY_BIAS : QUERY_BIAS + 1, low:high]
                if j == 2:
                    triple = triple + vec_ref[VALUE_BIAS : VALUE_BIAS + 1, low:high]
                triple = triple.astype(bf16)
                if j == 0:
                    triple = triple * jnp.array(0.125, bf16)
                for p in range(pairs // 2):
                    where = j * pairs + group * (pairs // 2) + p
                    qkv_ref[where] = triple[:, 128 * p : 128 * (p + 1)]

        def attend_pair(p):
            q, k, v = qkv_ref[p], qkv_ref[pairs + p], qkv_ref[2 * pairs + p]
            lower = half_mask(rows)
            mixed = []
            for t in range(2):
                keep = lower if t == 0 else ~lower
                scores = mm(jnp.where(keep, q, jnp.zeros_like(q)), k, NT)
                scores = scores + heads_ref[2 * p + t].astype(f32)
                top = jnp.max(scores, axis=1, keepdims=True)
                exps = jnp.exp(scores - top)
                total = jnp.sum(exps, axis=1, keepdims=True)
                probs = (exps * (1.0 / total)).astype(bf16)
                heads_ref[2 * p + t] = probs
                mixed.append(mm(probs, v))
            mixed_ref[p] = jnp.where(lower, mixed[0], mixed[1]).astype(bf16)

        for group in range(2):
            project(group)
            step()

            @pl.loop(group * pairs // 2, (group + 1) * pairs // 2)
            def _(p):
                attend_pair(p)
                for i in range(group * pairs // 2, (group + 1) * pairs // 2):

                    @pl.when(p == i)
                    def _():
                        step()

                cut = pl.ds(2 * p, 2)
                dst = probs_out.at[cut]
                pltpu.make_async_copy(heads_ref.at[cut], dst, pair_sems.at[0, 3]).start()

        save(qkv_ref, qkv_out)

        gather_until(7)
        loads[6].wait()
        loads[7].wait()
        mixed = jnp.concatenate([mixed_ref[p] for p in range(pairs)], axis=1)
        branch = mm(mixed, matrix(wo_ref.at[0])) + vec(vec_ref, OUTPUT_BIAS)
        saves[0].wait()
        normed_ref[...] = branch.astype(bf16)
        save(normed_ref, branch_out)
        middle = tok[...].astype(f32) + vec(vec_ref, ATTEND_SCALE) * branch
        middle_ref[...] = middle
        normal, _ = norm_stats(middle)
        second = normal * vec(vec_ref, SECOND_GAIN) + vec(vec_ref, SECOND_SHIFT)
        half_ref[...] = second.astype(bf16)
        gather_until(7)
        on_whole.pop()
        step()
        pltpu.make_async_copy(heads_ref, probs_out, pair_sems.at[0, 3]).wait()
        for copy in saves[1:]:
            copy.wait()

    pl.run_scoped(
        forward,
        pltpu.VMEM((16, plan.lanes), f32),
        pltpu.VMEM((heads, rows, rows), bf16),
        pltpu.VMEM((3 * pairs, rows, 128), bf16),
        pltpu.VMEM((3, 4, 2, eighth, width), bf16),
        pltpu.VMEM((1, 4, 2, eighth, width), bf16),
        pltpu.VMEM(idx_in.shape, jnp.int32),
        pltpu.VMEM((rows, width), bf16),
        pltpu.VMEM((rows, width), bf16),
    )


    def note(idx, value):
        small_ref[idx : idx + 1, 0:width] = value

    limit = jnp.where(is_large, plan.large_len, 3 * plan.small_len)
    live = iota((rows, 1), 0) < limit

    def backward(feed_ref, dsec_ref, dtri_ref, lines_ref):
        used = {"rows": [], "cols": [], "all": 0}

        def push(kind, value, out, row, col):
            k = used[kind]
            if fast and len(k) >= 2:
                for job in k[-2]:
                    job.free()
            slot = (rows_ref if kind == "rows" else cols_ref).at[len(k) % 2]
            shard, cols = value.shape[0] // 8, value.shape[1]
            slot[:, :, 0:shard, :] = value.astype(bf16).reshape(4, 2, shard, cols)
            added = []
            if fast:
                added = jobs[used["all"] : used["all"] + 2]
                used["all"] += 2
                for job in added:
                    queue.add(job)
            else:
                view = out.at[:, :, pl.ds(row, shard), pl.ds(col, cols)]
                fetch(slot.at[:, :, pl.ds(0, shard)], view, stage_sems.at[0]).wait()
            k.append(added)

        branch_ref, cot_ref = dtri_ref.at[0], dtri_ref.at[1]
        cot_copy = fetch(cot_in, cot_ref, late_sems.at[0])
        branch_copy = fetch(branch_out, branch_ref, late_sems.at[1])

        def feed_forward(we_ref, wr_ref, pre_ref, act_ref, slope_ref):

            def we_loads(j):
                copies = []
                for f in range(8):
                    src = we_in.at[:, :, :, pl.ds((f * HIDDEN_BLOCKS + j) * unit, unit)]
                    dst = we_ref.at[j % 2, :, :, :, pl.ds(f * unit, unit)]
                    copies.append(pltpu.make_async_copy(src, dst, tile_sems.at[j % 2, f]))
                return copies

            def wr_load(j):
                src = wr_in.at[:, :, pl.ds(j * unit, unit)]
                return pltpu.make_async_copy(src, wr_ref.at[j % 2], tile_sems.at[j % 2, 8])

            gather_until(15)
            for j in range(2):
                for copy in we_loads(j):
                    copy.start()
            cot_copy.wait()
            grad = jnp.where(live, cot_ref[...].astype(f32), 0.0)
            dfeed_ref[...] = (vec(vec_ref, FEED_SCALE) * grad).astype(bf16)
            small_ref[...] = jnp.zeros_like(small_ref)
            note(REDUCE_BIAS, rows_sum(dfeed_ref[...].astype(f32)))

            def we_tile(j):
                return we_ref[j % 2].reshape(width, tile_cols)

            def before(j):
                for copy in we_loads(j):
                    copy.wait()
                bias = []
                for f in range(8):
                    first = (f * HIDDEN_BLOCKS + j) * unit
                    bias.append(be_ref[:, first : first + unit])
                pre_ref[...] = mm(half_ref[...], we_tile(j)) + jnp.concatenate(bias, axis=1)

            part = 16 * (-(-rows // 64))
            spans = [(low, min(low + part, rows)) for low in range(0, rows, part)]

            def activate(j, which):
                low, high = spans[which]
                value, slope = gelu_parts(pre_ref[low:high, :])
                act_ref[j % 2, low:high, :] = value.astype(bf16)
                slope_ref[j % 2, low:high, :] = slope.astype(bf16)

            def first_part(j):
                before(j)
                for i in range(len(spans)):
                    activate(j, i)
                    step()
                queue.beat(4.0)
                push("rows", mm(act_ref[j % 2], dfeed_ref[...], TN), sum_wr, j * unit, 0)

            def second_part(j):
                gather_until(16 + 2 * (((j + 1) * unit - 1) // 96) + 1)
                wr_load(j).start()
                queue.beat(1.5)
                wr_load(j).wait()
                d_feed, act = dfeed_ref[...], act_ref[j % 2]
                wr = wr_ref[j % 2].reshape(tile_cols, width)
                d_act = mm(d_feed, wr, NT)
                d_pre = (d_act * slope_ref[j % 2].astype(f32)).astype(bf16)
                dbe_ref[j : j + 1, :] = rows_sum(d_pre.astype(f32))
                step()
                queue.beat(1.5)
                push("cols", mm(half_ref[...], d_pre, TN), sum_we, 0, j * tile_cols)
                step()
                queue.beat(1.5)
                feed = mm(act, wr)
                feed_ref[...] = feed if j == 0 else feed_ref[...] + feed
                step()
                queue.beat(1.5)
                d_second = mm(d_pre, we_tile(j), NT)
                dsec_ref[...] = d_second if j == 0 else dsec_ref[...] + d_second
                if j + 2 < HIDDEN_BLOCKS:
                    for copy in we_loads(j + 2):
                        copy.start()
                step()
                queue.beat(1.5)

            first_part(0)
            for j in range(HIDDEN_BLOCKS):
                if j + 1 < HIDDEN_BLOCKS:
                    first_part(j + 1)
                second_part(j)

        pl.run_scoped(
            feed_forward,
            pltpu.VMEM((2, 4, 2, eighth, tile_cols), bf16),
            pltpu.VMEM((2, 4, 2, unit, width), bf16),
            pltpu.VMEM((rows, tile_cols), f32),
            pltpu.VMEM((2, rows, tile_cols), bf16),
            pltpu.VMEM((2, rows, tile_cols), bf16),
        )

        def attention(
            tile_ref, qkv_ref, probs_ref, dmix_ref, large_ref, strip_ref, tail_ref
        ):
            def pair_loads(p):
                slot = p % 3
                probs = probs_out.at[pl.ds(2 * p, 2)]
                copies = [pltpu.make_async_copy(probs, probs_ref.at[slot], pair_sems.at[slot, 3])]
                for part in range(3):
                    src, dst = qkv_out.at[part * pairs + p], qkv_ref.at[p % 2, part]
                    copies.append(pltpu.make_async_copy(src, dst, pair_sems.at[slot, part]))
                return copies

            tiles = [pltpu.make_async_copy(wo_in, tile_ref.at[0], tile_sems.at[0, 0])]
            for j in range(3):
                src = wt_in.at[:, :, :, pl.ds(j * width, width)]
                slot = (1 + j) % 2
                tiles.append(pltpu.make_async_copy(src, tile_ref.at[slot], tile_sems.at[slot, 0]))

            def tile(i):
                tiles[i].wait()
                return matrix(tile_ref.at[i % 2])

            tiles[0].start()
            tiles[1].start()
            for copy in pair_loads(0):
                copy.start()
            branch_copy.wait()
            feed_out = feed_ref[...] + vec(vec_ref, REDUCE_BIAS)
            middle = middle_ref[...]
            half_ref[...] = (middle + vec(vec_ref, FEED_SCALE) * feed_out).astype(bf16)
            out_copy = fetch(half_ref, out_ref, save_sems.at[0])
            grad = jnp.where(live, cot_ref[...].astype(f32), 0.0)
            d_second = dsec_ref[...]
            normal, inv = norm_stats(middle)
            d_middle = grad + norm_back(d_second, vec(vec_ref, SECOND_GAIN), normal, inv)
            d_branch = (vec(vec_ref, ATTEND_SCALE) * d_middle).astype(bf16)
            queue.beat(3.5)
            note(FEED_SCALE, rows_sum(grad * feed_out))
            note(SECOND_GAIN, rows_sum(d_second * normal))
            note(SECOND_SHIFT, rows_sum(d_second))
            note(ATTEND_SCALE, rows_sum(d_middle * branch_ref[...].astype(f32)))
            note(OUTPUT_BIAS, rows_sum(d_branch.astype(f32)))
            dsec_ref[...] = d_middle
            dmix_ref[...] = mm(d_branch, tile(0), NT).astype(bf16)
            tiles[2].start()
            mixed = jnp.concatenate([mixed_ref[p] for p in range(pairs)], axis=1)
            push("rows", mm(mixed, d_branch, TN), sum_wo, 0, 0)
            normed_ref = dfeed_ref
            normed_copy = fetch(normed_out, normed_ref, late_sems.at[0])
            queue.beat(4.0)

            def ds_copy(p):
                slot = p % 3
                dst = ds_out.at[pl.ds(2 * p, 2)]
                return pltpu.make_async_copy(probs_ref.at[slot], dst, ds_sems.at[slot])

            def pair_back(p):
                slot = p % 3
                for copy in pair_loads(p):
                    copy.wait()

                @pl.when(p >= 2)
                def _():
                    ds_copy(p - 2).wait()

                @pl.when(p + 1 < pairs)
                def _():
                    for copy in pair_loads(p + 1):
                        copy.start()

                lanes = pl.ds(pl.multiple_of(128 * p, 128), 128)
                q, k, v = [qkv_ref[p % 2, part] for part in range(3)]
                do = dmix_ref[:, lanes]
                lower = half_mask(rows)
                prod = do.astype(f32) * mixed_ref[p].astype(f32)
                dq, dk, dv = [], [], []
                for t in range(2):
                    keep = lower if t == 0 else ~lower
                    d_out = jnp.where(keep, do, jnp.zeros_like(do))
                    delta = jnp.sum(jnp.where(keep, prod, 0.0), axis=1, keepdims=True)
                    d_probs = mm(d_out, v, NT)
                    probs = probs_ref[slot, t]
                    dv.append(mm(probs, do, TN))
                    d_scores = (probs.astype(f32) * (d_probs - delta)).astype(bf16)
                    probs_ref[slot, t] = d_scores
                    dq.append(mm(d_scores, k))
                    dk.append(mm(d_scores, q, TN))
                dtri_ref[0, :, lanes] = (jnp.where(lower, dq[0], dq[1]) * 0.125).astype(bf16)
                dtri_ref[1, :, lanes] = jnp.where(lower, dk[0], dk[1]).astype(bf16)
                dtri_ref[2, :, lanes] = jnp.where(lower, dv[0], dv[1]).astype(bf16)
                ds_copy(p).start()

            span = width // 3
            for group in range(3):

                @pl.loop(2 * group, 2 * group + 2)
                def _(p):
                    pair_back(p)

                    @pl.when(p == 2 * group)
                    def _():
                        queue.beat(2.3)

                queue.beat(2.3)
                if group == 0:
                    normed_copy.wait()
                d_part = [dtri_ref[j, :, group * span : (group + 1) * span] for j in range(3)]
                d_part = jnp.concatenate(d_part, axis=1)
                push("rows", mm(normed_ref[...], d_part, TN), sum_wt, 0, group * width)
                queue.beat(1.6)

            out_copy.wait()
            tok_ref = half_ref
            tok_copy = fetch(tok_in, tok_ref, late_sems.at[1])
            for j in range(3):
                d_part = dtri_ref[j]
                part = mm(d_part, tile(1 + j), NT)
                feed_ref[...] = part if j == 0 else feed_ref[...] + part
                if j == 0:
                    tiles[3].start()
                if j != 1:
                    note(QUERY_BIAS if j == 0 else VALUE_BIAS, rows_sum(d_part.astype(f32)))
                queue.beat(1.3)
            tok_copy.wait()
            normal, inv = norm_stats(tok_ref[...].astype(f32))
            note(FIRST_GAIN, rows_sum(feed_ref[...] * normal))
            note(FIRST_SHIFT, rows_sum(feed_ref[...]))
            queue.beat(1.0)

            ds_copy(pairs - 2).wait()
            ds_copy(pairs - 1).wait()

            def ds_load(p):
                src, slot = ds_out.at[pl.ds(2 * p, 2)], p % 3
                return pltpu.make_async_copy(src, probs_ref.at[slot], pair_sems.at[slot, 3])

            ds_load(0).start()

            @pl.loop(0, pairs)
            def _(p):
                ds_load(p).wait()

                @pl.when(p + 1 < pairs)
                def _():
                    ds_load(p + 1).start()

                for t in range(2):
                    ds = probs_ref.at[p % 3, t]
                    args = (image_ref, colsel_ref, large_ref, strip_ref, tail_ref, 2 * p + t, is_large)
                    fold_head(plan, ds, *args)
                for i in range(pairs):

                    @pl.when(p == i)
                    def _():
                        queue.beat(1.9)

            lines_ref[...] = fold_lines(plan, large_ref, strip_ref, tail_ref, is_large)

        def first_norm_back():
            tok_ref, normed_ref = half_ref, dfeed_ref
            normal, inv = norm_stats(tok_ref[...].astype(f32))
            back = norm_back(feed_ref[...], vec(vec_ref, FIRST_GAIN), normal, inv)
            normed_ref[...] = (dsec_ref[...] + back).astype(bf16)
            return fetch(normed_ref, tok_out, save_sems.at[1])

        pl.run_scoped(
            attention,
            pltpu.VMEM((2, 4, 2, eighth, width), bf16),
            pltpu.VMEM((2, 3, rows, 128), bf16),
            pltpu.VMEM((3, 2, rows, rows), bf16),
            pltpu.VMEM((rows, width), bf16),
            pltpu.VMEM((heads, plan.gl, plan.strip_l), f32),
            pltpu.VMEM((heads, 16, plan.strip_s), f32),
            pltpu.VMEM((heads, 1, 128), f32),
        )
        queue.beat(1.9)
        line_of = lambda chunk: lines_ref[:, 128 * chunk : 128 * (chunk + 1)]
        d_table = table_from_lines(plan, line_of, lab_ref, plan.buckets)
        wide = hidden // 8

        def bias_sum(f):
            parts = [dbe_ref[j : j + 1, f * unit : (f + 1) * unit] for j in range(HIDDEN_BLOCKS)]
            return jnp.concatenate(parts, axis=1)

        if not fast:
            vec_out[...] = small_ref[...]
            for f in range(8):
                be_out[:, f * wide : (f + 1) * wide] = bias_sum(f)
            tab_out[...] = d_table
            first_norm_back().wait()
            return

        share, bshare = width // n, plan.buckets // n
        for f in range(n):
            value = jnp.concatenate(
                [
                    d_table[:, f * bshare : (f + 1) * bshare],
                    jnp.zeros((16, wide - bshare - share), f32),
                    small_ref[:, f * share : (f + 1) * share],
                ],
                axis=1,
            )
            bias = jnp.broadcast_to(bias_sum(f), (16, wide))
            block[f] = jnp.where(iota((16, wide), 0) == heads, bias, value).astype(bf16)
        sums = []
        for k, peer in enumerate(peers):
            dst = (spot.f + k + 1) % n
            sums.append(send(block.at[dst], got.at[k], bss.at[k], brs.at[k], peer))
            sums[k].start()
        tok_copy = first_norm_back()
        queue.beat(4.0)
        for job in jobs:
            job.free()
        for at, whole in enumerate(wholes):
            for copy in Piece.sent_waits(n // 2, whole, gss.at[at]):
                copy.wait()
        value = block[spot.f].astype(f32)
        for k, copy in enumerate(sums):
            copy.wait_recv()
            value = value + got[k].astype(f32)
        reps[spot.rep] = value
        for k, other in enumerate(others):
            mine = reps.at[spot.rep]
            sums.append(send(mine, mine, bss.at[n - 1 + k], brs.at[n - 1 + k], other))
            sums[-1].start()
        queue.beat(3.0)
        for copy in sums[n - 1 :]:
            copy.wait_recv()
        small_out[...] = (reps[0] + reps[1]) + (reps[2] + reps[3])
        queue.drain()
        tok_copy.wait()
        for copy in sums:
            copy.wait_send()
        flat = normed_out
        for kind, shape in enumerate(sum_kinds):
            count = sum_shapes.count(shape)
            for idx, out_rows in enumerate(Sum.sent_rows(n // 2, shape[0])):
                total = count * out_rows * shape[1] // width
                view = flat.at[pl.ds(0, total)]
                pltpu.make_async_copy(view, view, rss.at[kind, idx + 1]).wait()

    pl.run_scoped(
        backward,
        pltpu.VMEM((rows, width), f32),
        pltpu.VMEM((rows, width), f32),
        pltpu.VMEM((3, rows, width), bf16),
        pltpu.VMEM((16, plan.lanes), f32),
    )


AHEAD, LAGS = 3, (2, 4, 5)
GATHER_ORDER = (0, 1, 2, 3)


def layer(plan, kind, tokens, cot, large_index, n, fast, shorts, shards):
    rows, width = tokens.shape
    heads = plan.heads
    pairs = heads // 2
    sds = jax.ShapeDtypeStruct
    hidden = shards[2].shape[1]
    unit = hidden // 8 // HIDDEN_BLOCKS
    eighth = width // 8
    cuts = piece_cuts([w.shape for w in shards]) if fast else []
    sum_shapes = []
    for ring, _ in BLOCK_ORDER:
        sum_shapes += [(unit, width // 2) if ring == "rows" else (eighth, 4 * unit)] * 2
    sum_shapes += [(eighth, width // 2)] * 8
    colsel = jnp.asarray(plan.selector_arrays()[1], bf16)
    inputs = [kind, tokens, cot, large_index, pick_plan(plan), colsel, image_selectors(plan)]
    in_specs = [smem_spec] + [any_spec] * 3 + [vmem_spec] * 3
    outs, out_specs = [sds((rows, width), bf16)] * 2, [any_spec] * 2
    if fast:
        wide = hidden // n
        inputs += shorts + shards
        in_specs += [vmem_spec] * 12 + [any_spec] * 4
        outs += [sds(w.shape, bf16) for w in shards]
        outs += [sds((16, wide), f32)]
        out_specs += [vmem_spec] * 5
        outs += [sds((4, 2) + w.shape, bf16) for w in shards]
        out_specs += [any_spec] * 4
    else:
        wholes, vecs, be, table = gather_plain(shorts, shards, n)
        wholes = [w.reshape(4, 2, w.shape[0] // 8, w.shape[1]) for w in wholes]
        inputs += [vecs, be, table.astype(f32)] + wholes
        in_specs += [vmem_spec] * 3 + [any_spec] * 4
        outs += [sds(w.shape, bf16) for w in wholes]
        outs += [sds((16, width), f32), sds((1, hidden), f32), sds((16, plan.buckets), f32)]
        out_specs += [any_spec] * 4 + [vmem_spec] * 3
    kept = len(outs)
    square = sds((heads, rows, rows), bf16)
    flat = sds((rows, width), bf16)
    outs += [flat, flat, sds((3 * pairs, rows, 128), bf16), square, square]
    out_specs += [any_spec] * 5
    dma = pltpu.SemaphoreType.DMA
    scratch = [
        pltpu.VMEM((16, width), f32),
        pltpu.VMEM((1, hidden), f32),
        pltpu.VMEM((2, plan.lanes), jnp.int32),
        pltpu.VMEM((rows, width), f32),
        pltpu.VMEM((2, rows, width), bf16),
        pltpu.VMEM((pairs, rows, 128), bf16),
        pltpu.VMEM((16, width), f32),
        pltpu.VMEM((8, 8 * unit), f32),
        pltpu.VMEM((2, 4, 2, unit, width), bf16),
        pltpu.VMEM((2, 4, 2, eighth, 8 * unit), bf16),
        dma((8,)),
        dma((4,)),
        dma((2, 9)),
        dma((2,)),
        dma((3, 4)),
        dma((3,)),
        dma((1,)),
    ]
    kernel_params = dict(vmem_limit_bytes=vmem_bytes)
    if fast:
        for shape in sum_shapes:
            scratch += Sum.buffers(n // 2, *shape)
        scratch += [
            pltpu.VMEM((16, wide), bf16),
            pltpu.VMEM((n, 16, wide), bf16),
            pltpu.VMEM((n, 16, wide), bf16),
            pltpu.VMEM((n - 1, 16, wide), bf16),
            pltpu.VMEM((4, 16, wide), f32),
            dma((4, 4)),
            dma((len(cuts) * Piece.sems,)),
            dma((n - 1,)),
            dma((n - 1,)),
            dma((len(set(sum_shapes)), 6)),
            dma((len(sum_shapes),)),
            dma((len(sum_shapes) * Sum.sems,)),
            dma((n + 2,)),
            dma((n + 2,)),
        ]
        kernel_params.update(collective_id=1, has_side_effects=True)
    result = pl.pallas_call(
        functools.partial(layer_kernel, plan, n, fast, cuts, sum_shapes),
        in_specs=in_specs,
        out_specs=out_specs,
        out_shape=outs,
        scratch_shapes=scratch,
        compiler_params=pltpu.CompilerParams(**kernel_params),
        name="layer",
    )(*inputs)[:kept]
    out, token_grad = result[:2]
    if fast:
        return out, token_grad, result[2:6], result[6]
    wt, wo, we, wr = [g.reshape(-1, g.shape[3]) for g in result[2:6]]
    wt = wt.reshape(width, 3, 3, width // 3).transpose(0, 2, 1, 3).reshape(width, 3 * width)
    we = we.reshape(width, HIDDEN_BLOCKS, 8, unit).transpose(0, 2, 1, 3).reshape(width, hidden)
    sums, block = reduce_plain([wt, wo, we, wr], *result[6:9], n)
    wt, wo, we, wr = sums
    wt = wt.reshape(-1, 3, 3, width // 3).transpose(0, 2, 1, 3).reshape(wt.shape)
    we = we.reshape(-1, 8, HIDDEN_BLOCKS, unit).transpose(0, 2, 1, 3).reshape(we.shape)
    return out, token_grad, [wt, wo, we, wr], block


def per_device(
    tokens,
    slot_kinds,
    small_index,
    large_index,
    first_gain,
    first_shift,
    triple_weight,
    query_bias,
    value_bias,
    bias_table,
    output_weight,
    output_bias,
    attend_scale,
    second_gain,
    second_shift,
    expand_weight,
    expand_bias,
    reduce_weight,
    reduce_bias,
    feed_scale,
    cotangent,
):
    _, rows, width = tokens.shape
    heads = bias_table.shape[2]
    buckets = bias_table.shape[1] * lax.axis_size("fsdp")
    plan = Plan(small_index.shape[0], large_index.shape[0], rows, heads, buckets)
    tokens, cotangent = tokens[0], cotangent[0]
    short = [
        first_gain,
        first_shift,
        query_bias,
        value_bias,
        output_bias,
        attend_scale,
        second_gain,
        second_shift,
        reduce_bias,
        feed_scale,
    ]
    n = width // first_gain.shape[1]
    fast = fast_shape(
        lax.axis_size("rep"), n, [w.shape[1] for w in (triple_weight, output_weight, reduce_weight)]
    )
    shards = [w[0] for w in (triple_weight, output_weight, expand_weight, reduce_weight)]
    shorts = short + [expand_bias, bias_table[0].T]
    block_output, token_grad, sums, block = layer(
        plan, slot_kinds, tokens, cotangent, large_index, n, fast, shorts, shards
    )
    return wrap(block_output, token_grad, sums, block, first_gain.shape[1], bias_table.shape[1:])


def wrap_kernel(share, heads, out_in, tok_in, wt_in, wo_in, we_in, wr_in, block_ref, *outs):
    (
        out,
        tok,
        first_gain,
        first_shift,
        triple_weight,
        query_bias,
        value_bias,
        bias_table,
        output_weight,
        output_bias,
        attend_scale,
        second_gain,
        second_shift,
        expand_weight,
        expand_bias,
        reduce_weight,
        reduce_bias,
        feed_scale,
    ) = outs
    out[0] = out_in[...]
    tok[0] = tok_in[...]
    width = wt_in.shape[1] // 3
    span = width // 3
    for g in range(3):
        for part in range(3):
            first = g * width + part * span
            value = wt_in[:, first : first + span].astype(f32)
            triple_weight[0, :, part * width + g * span : part * width + (g + 1) * span] = value
    output_weight[0] = wo_in[...].astype(f32)
    reduce_weight[0] = wr_in[...].astype(f32)
    unit = 128
    count = we_in.shape[1] // (unit * HIDDEN_BLOCKS)
    for g in range(HIDDEN_BLOCKS):
        for f in range(count):
            value = we_in[:, (g * count + f) * unit : (g * count + f + 1) * unit].astype(f32)
            first = (f * HIDDEN_BLOCKS + g) * unit
            expand_weight[0, :, first : first + unit] = value
    first = block_ref.shape[1] - share
    rows = {
        FIRST_GAIN: first_gain,
        FIRST_SHIFT: first_shift,
        QUERY_BIAS: query_bias,
        VALUE_BIAS: value_bias,
        OUTPUT_BIAS: output_bias,
        ATTEND_SCALE: attend_scale,
        SECOND_GAIN: second_gain,
        SECOND_SHIFT: second_shift,
        REDUCE_BIAS: reduce_bias,
        FEED_SCALE: feed_scale,
    }
    for idx, ref in rows.items():
        ref[...] = block_ref[idx : idx + 1, first:]
    expand_bias[...] = block_ref[heads : heads + 1, :]
    for h in range(heads):
        bias_table[h] = block_ref[h : h + 1, : bias_table.shape[2]]


def wrap(block_output, token_grad, sums, block, share, table_shape):
    wt, wo, we, wr = sums
    sds = jax.ShapeDtypeStruct
    vector = sds((1, share), f32)
    whole_of = lambda w: sds((1,) + w.shape, f32)
    bshare, heads = table_shape
    triple = whole_of(wt)
    outs = [sds((1,) + block_output.shape, bf16)] * 2
    outs += [vector, vector, triple, vector, vector, sds((heads, 1, bshare), f32)]
    outs += [whole_of(wo)] + [vector] * 4 + [whole_of(we), sds((1, block.shape[1]), f32)]
    outs += [whole_of(wr), vector, vector]
    result = pl.pallas_call(
        functools.partial(wrap_kernel, share, heads),
        in_specs=[vmem_spec] * 7,
        out_specs=[vmem_spec] * 18,
        out_shape=outs,
        compiler_params=pltpu.CompilerParams(vmem_limit_bytes=vmem_bytes),
        name="wrap",
    )(block_output, token_grad, wt, wo, we, wr, block)
    result = list(result)
    result[7] = result[7].transpose(1, 2, 0)
    return tuple(result)


def solution(mesh):
    rows = P(("rep", "fsdp"), None, None)
    vector = P(None, "fsdp")
    matrix = P(None, "fsdp", None)
    weights = (
        vector,
        vector,
        matrix,
        vector,
        vector,
        matrix,
        matrix,
        vector,
        vector,
        vector,
        vector,
        matrix,
        vector,
        matrix,
        vector,
        vector,
    )
    return jax.shard_map(
        per_device,
        mesh=mesh,
        in_specs=(rows, P(("rep", "fsdp")), P(), P()) + weights + (rows,),
        out_specs=(rows, rows) + weights,
        check_vma=False,
    )
```
